32 devices in a mesh: shell: 8 (over z, x), aux: 4 (over y, core).
Axes of the slice: x: 2, y: 2, z: 4, core: 2. Of those that a mesh axis runs over, the one named last changes fastest.
Arguments:
- integrals: bfloat16 [32, 128, 4, 128], P('shell', None, 'aux'), may hold values from -6 to 6
- pair_list: int32 [32, 3], P('shell'), may hold values from 0 to 31, as said below
- coef: bfloat16 [4096, 1024], P('shell'), may hold values from -0.5 to 0.5
- metric: bfloat16 [4, 4], replicated, may hold values from -3 to 3, as said below
- occ_slot: int32 [128], replicated, may hold values from 0 to 127, each once
Outputs:
- transformed: bfloat16 [1024, 4, 4096], P(('shell', 'aux'))
The draws below stay inside these ranges and needn't reach their ends.
Inputs may be any that keep to these rules, and one draw needn't show every extreme that they name: `pair_list`: row d * 4 + k holds slot k of index d of shell: block row, block column, live flag. The block column lies in d * 4 to (d + 1) * 4 - 1. On every index live slots come first and at least one is live; some index has all 4 live. `metric`: lower triangular, positive on the diagonal.
All inputs are finite; a program needn't handle non-finite values.
Results may differ from the reference program's by a relative error of at most 0.0054.
Values may be sent and summed in bfloat16 or wider, within the bound.
No kernel may reach another device: no remote copies, remote signals or barrier semaphores. Data moves between devices by JAX's collectives and lax.ppermute only.
A program may use at most 64 MiB of HBM per device.

```python
import jax
import jax.numpy as jnp
from jax import lax

BS = 128
NOCC = 1024
OB = 8
NB_DEV = 4
PAIRS_DEV = 4
NB = 32
NBF = 4096
SLAB = 4
PAIRS = 32
NOB = 128


def draw_pair_list(key, part):
    keys = jax.random.split(jax.random.fold_in(key, 11), 4)
    device_count = PAIRS // PAIRS_DEV
    positions = jnp.arange(PAIRS, dtype=jnp.int32)
    owner = positions // PAIRS_DEV
    within = positions % PAIRS_DEV
    block_rows = jax.random.randint(keys[0], (PAIRS,), 0, NB, dtype=jnp.int32)
    block_cols = owner * NB_DEV + jax.random.randint(keys[1], (PAIRS,), 0, NB_DEV, dtype=jnp.int32)
    counts = jax.random.randint(keys[2], (device_count,), 1, PAIRS_DEV + 1, dtype=jnp.int32)
    full_device = jax.random.randint(keys[3], (), 0, device_count, dtype=jnp.int32)
    counts = jnp.where(jnp.arange(device_count, dtype=jnp.int32) == full_device, PAIRS_DEV, counts)
    block_rows = jnp.where(positions == full_device * PAIRS_DEV, NB - 1, block_rows)
    live_flag = (within < counts[owner]).astype(jnp.int32)
    return jnp.stack([block_rows, block_cols, live_flag], axis=1).astype(jnp.int32)


def draw_metric(key, part):
    keys = jax.random.split(jax.random.fold_in(key, 7), 2)
    spread = 0.35 * jnp.clip(jax.random.normal(keys[0], (SLAB, SLAB), jnp.float32), -5.0, 5.0)
    diagonal = jax.random.uniform(keys[1], (SLAB,), jnp.float32, 0.7, 1.3)
    lower = jnp.tril(spread, -1) + jnp.diag(diagonal)
    return lower.astype(jnp.bfloat16)


def levels(key, dims, pieces, low, high):
    level, own = 1.0, jax.random.fold_in(key, 6)
    for axis_at, blocks in pieces:
        steps = jnp.exp(jax.random.uniform(jax.random.fold_in(own, axis_at), (blocks,), jnp.float32, low / len(pieces), high / len(pieces)))
        level = level * jnp.repeat(steps, dims[axis_at] // blocks).reshape([-1 if axis == axis_at else 1 for axis in range(len(dims))])
    return level


def centred(rng, extent, width, reach, cuts=(), kind=jnp.bfloat16):
    entries = width * jax.random.normal(rng, extent, jnp.float32)
    if cuts:
        entries = entries * levels(rng, extent, cuts, -0.22, 0.18)
    return jnp.clip(entries, -reach, reach).astype(kind)


def setup_inputs(seed: int = 0) -> dict:
    splits = jax.random.split(jax.random.key(seed), 6)
    return {
        "integrals": centred(splits[0], (PAIRS, BS, SLAB, BS), 1.0, 6.0, ((0, 8), (2, 4))),
        "pair_list": draw_pair_list(jax.random.fold_in(splits[5], 71), 0),
        "coef": centred(splits[2], (NBF, NOCC), BS ** -0.5, 0.5, ((0, 8),)),
        "metric": draw_metric(jax.random.fold_in(splits[5], 71), 0),
        "occ_slot": jax.random.permutation(splits[4], NOB).astype(jnp.int32),
    }


def reference(integrals, pair_list, coef, metric, occ_slot):
    inverse = jnp.zeros((NOB,), jnp.int32).at[occ_slot].set(jnp.arange(NOB, dtype=jnp.int32))
    ordered = jnp.take(coef.reshape(NBF, NOB, OB), inverse, axis=1).reshape(NBF, NOCC)

    def accumulate(running, item):
        int_block, pair_entry = item
        column = lax.dynamic_slice_in_dim(ordered, (pair_entry[1] * BS).astype(jnp.int32), BS, 0)
        product = jnp.dot(column.T, int_block.reshape(BS, SLAB * BS), preferred_element_type=jnp.float32)
        rounded = lax.optimization_barrier(product.astype(jnp.bfloat16)).astype(jnp.float32)
        rounded = rounded * pair_entry[2].astype(jnp.float32)
        offset = (pair_entry[0] * BS).astype(jnp.int32)
        anchor = jnp.zeros((), jnp.int32)
        current = lax.dynamic_slice(running, (anchor, anchor, offset), (NOCC, SLAB, BS))
        running = lax.dynamic_update_slice(running, current + rounded.reshape(NOCC, SLAB, BS), (anchor, anchor, offset))
        return running, None

    initial = jnp.zeros((NOCC, SLAB, NBF), jnp.float32)
    summed, unused = lax.scan(accumulate, initial, (integrals, pair_list))
    summed = lax.optimization_barrier(summed.astype(jnp.bfloat16))
    factor = metric.astype(jnp.float32)

    def transform_rows(rows):
        return jnp.einsum("qp,ipm->iqm", factor, rows.astype(jnp.float32)).astype(jnp.bfloat16)

    result = lax.map(transform_rows, summed.reshape(NOB, OB, SLAB, NBF))
    return result.reshape(NOCC, SLAB, NBF)
```

```python
import functools

import jax
import jax.numpy as jnp
from jax import lax
from jax.experimental import pallas as pl
from jax.experimental.pallas import tpu as pltpu
from jax.sharding import PartitionSpec as P

BS = 128
CODE = 128
GATHER_LIMIT = 16 * 2**20


def relayed_half_blocks(integrals, pair_list, coef, metric, occ_slot):
    pairs_dev = pair_list.shape[0]
    rows_local = coef.shape[0]
    occ_count = coef.shape[1]
    blocks_dev = rows_local // BS
    shell_count = lax.axis_size("shell")
    block_count = blocks_dev * shell_count
    slot_count = occ_slot.shape[0]
    aux_dev = integrals.shape[2]
    inverse = (
        jnp.zeros((slot_count,), jnp.int32)
        .at[occ_slot]
        .set(jnp.arange(slot_count, dtype=jnp.int32))
    )
    ordered = jnp.take(
        coef.reshape(rows_local, slot_count, occ_count // slot_count), inverse, axis=1
    )
    ordered = ordered.reshape(rows_local, occ_count)

    def one_slot(item):
        int_block, column_index = item
        start = column_index % blocks_dev * BS
        column = lax.dynamic_slice_in_dim(ordered, start, BS, 0)
        product = lax.dot_general(
            column,
            int_block.reshape(BS, aux_dev * BS),
            (((0,), (0,)), ((), ())),
            preferred_element_type=jnp.float32,
        )
        return product.astype(jnp.bfloat16)

    half_blocks = lax.map(one_slot, (integrals, pair_list[:, 1]))
    half_blocks = half_blocks.reshape(pairs_dev, occ_count, aux_dev, BS)
    listing = lax.all_gather(pair_list, "shell", axis=0, tiled=True)
    targets = jnp.arange(block_count, dtype=jnp.int32)[:, None]
    selector = ((listing[:, 0][None, :] == targets) & (listing[:, 2][None, :] == 1)).astype(
        jnp.bfloat16
    )
    relayed = lax.all_to_all(
        lax.all_to_all(half_blocks, "shell", split_axis=1, concat_axis=0, tiled=True),
        "aux",
        split_axis=1,
        concat_axis=2,
        tiled=True,
    )
    summed = jnp.dot(
        selector, relayed.reshape(relayed.shape[0], -1), preferred_element_type=jnp.float32
    )
    blocks = summed.astype(jnp.bfloat16).reshape((block_count,) + relayed.shape[1:])
    result = jnp.einsum("qp,bipm->iqbm", metric, blocks, preferred_element_type=jnp.float32)
    return result.reshape(result.shape[0], result.shape[1], block_count * BS).astype(jnp.bfloat16)


def pieces_kernel(occ_local, aux_count, pairs, slot_row, coef, out):
    pairs_dev = pairs.shape[0]
    blocks_dev = coef.shape[0] // BS
    occ_count = coef.shape[1]
    block_total = slot_row.shape[1]
    width = occ_count // block_total
    rows = out.shape[0]
    me = lax.axis_index("aux")

    spread = (
        lax.broadcasted_iota(jnp.int32, (block_total, occ_count), 1) // width
        == lax.broadcasted_iota(jnp.int32, (block_total, occ_count), 0)
    ).astype(jnp.bfloat16)
    slots = jnp.broadcast_to(slot_row[...], (8, block_total)).astype(jnp.float32)
    target = jnp.dot(slots.astype(jnp.bfloat16), spread, preferred_element_type=jnp.float32)
    target = target.astype(jnp.int32)[:1] * width + (
        lax.broadcasted_iota(jnp.int32, (1, occ_count), 1) % width
    )
    row = lax.broadcasted_iota(jnp.int32, (rows, 1), 0)
    wanted = (row // occ_local * aux_count + me) * occ_local + row % occ_local
    pick = (wanted == target).astype(jnp.bfloat16)

    lane = lax.broadcasted_iota(jnp.int32, (1, CODE), 1)
    code = jnp.zeros((1, CODE), jnp.int32)
    for k in range(pairs_dev):
        column = lax.rem(pairs[k, 1], blocks_dev)
        block = coef[pl.ds(pl.multiple_of(column * BS, BS), BS), :]
        piece = lax.dot_general(
            pick, block, (((1,), (1,)), ((), ())), preferred_element_type=jnp.float32
        )
        live = (pairs[k, 2] == 1).astype(jnp.float32)
        out[:, k * BS : (k + 1) * BS] = (piece * live).astype(jnp.bfloat16)
        block_row = pairs[k, 0]
        code = jnp.where(lane == k, block_row % 128, code)
        code = jnp.where(lane == pairs_dev + k, block_row // 128, code)
    out[:, pairs_dev * BS :] = jnp.broadcast_to(
        code.astype(jnp.float32), (rows, CODE)
    ).astype(jnp.bfloat16)


def transform_kernel(block_rows, metric, pieces, blocks, out, total):
    step = pl.program_id(0)
    aux_count, pairs_dev = blocks.shape[1:3]
    occ_local = pieces.shape[1]
    rows = occ_local * aux_count

    @pl.when(step == 0)
    def _():
        total[...] = jnp.zeros_like(total)

    row = lax.broadcasted_iota(jnp.int32, (rows, occ_local), 0)
    orbital = lax.broadcasted_iota(jnp.int32, (rows, occ_local), 1)
    coefs = pieces[0, :, : pairs_dev * BS]
    scaled = []
    for p in range(aux_count):
        factor = jnp.zeros((rows, occ_local), jnp.float32)
        for q in range(aux_count):
            factor = jnp.where(row % aux_count == q, metric[q, p], factor)
        factor = jnp.where(row // aux_count == orbital, factor, 0.0).astype(jnp.bfloat16)
        scaled.append(
            jnp.dot(factor, coefs, preferred_element_type=jnp.float32).astype(jnp.bfloat16)
        )
    for k in range(pairs_dev):
        left = jnp.concatenate([s[:, k * BS : (k + 1) * BS] for s in scaled], axis=1)
        right = jnp.concatenate([blocks[0, p, k] for p in range(aux_count)], axis=0)
        r = block_rows[step, k]
        total[r] += jnp.dot(left, right, preferred_element_type=jnp.float32)

    @pl.when(step == pl.num_programs(0) - 1)
    def _():
        for r in range(total.shape[0]):
            out[:, :, r * BS : (r + 1) * BS] = (
                total[r].reshape(occ_local, aux_count, BS).astype(jnp.bfloat16)
            )


def gathered_blocks(integrals, pair_list, coef, metric, occ_slot):
    pairs_dev = pair_list.shape[0]
    shell_count = lax.axis_size("shell")
    aux_count = lax.axis_size("aux")
    occ_local = coef.shape[1] // (shell_count * aux_count)
    block_count = coef.shape[0] // BS * shell_count
    width = pairs_dev * BS + CODE

    blocks = lax.all_gather(
        integrals.reshape(pairs_dev, BS, BS), ("shell", "aux"), axis=0, tiled=True
    ).reshape(shell_count, aux_count, pairs_dev, BS, BS)
    pieces = pl.pallas_call(
        functools.partial(pieces_kernel, occ_local, aux_count),
        out_shape=jax.ShapeDtypeStruct((shell_count * occ_local, width), jnp.bfloat16),
        in_specs=[
            pl.BlockSpec(memory_space=pltpu.SMEM),
            pl.BlockSpec(memory_space=pltpu.VMEM),
            pl.BlockSpec(memory_space=pltpu.VMEM),
        ],
        out_specs=pl.BlockSpec(memory_space=pltpu.VMEM),
        compiler_params=pltpu.CompilerParams(vmem_limit_bytes=32 * 2**20),
        name="pieces",
    )(pair_list, occ_slot.reshape(1, -1), coef)
    pieces = lax.all_to_all(
        pieces.reshape(shell_count, occ_local, width), "shell", split_axis=0, concat_axis=0
    )
    digits = pieces[:, 0, pairs_dev * BS : pairs_dev * (BS + 2)].astype(jnp.int32)
    block_rows = digits[:, :pairs_dev] + 128 * digits[:, pairs_dev:]
    return pl.pallas_call(
        transform_kernel,
        grid_spec=pltpu.PrefetchScalarGridSpec(
            num_scalar_prefetch=1,
            grid=(shell_count,),
            in_specs=[
                pl.BlockSpec(memory_space=pltpu.SMEM),
                pl.BlockSpec((1, occ_local, width), lambda s, rows: (s, 0, 0)),
                pl.BlockSpec(
                    (1, aux_count, pairs_dev, BS, BS), lambda s, rows: (s, 0, 0, 0, 0)
                ),
            ],
            out_specs=pl.BlockSpec(
                (occ_local, aux_count, block_count * BS), lambda s, rows: (0, 0, 0)
            ),
            scratch_shapes=[pltpu.VMEM((block_count, occ_local * aux_count, BS), jnp.float32)],
        ),
        out_shape=jax.ShapeDtypeStruct(
            (occ_local, aux_count, block_count * BS), jnp.bfloat16
        ),
        compiler_params=pltpu.CompilerParams(vmem_limit_bytes=32 * 2**20),
        name="transform",
    )(block_rows, metric.astype(jnp.float32), pieces, blocks)


def per_device(integrals, pair_list, coef, metric, occ_slot):
    gathered_bytes = integrals.size * 2 * lax.axis_size("shell") * lax.axis_size("aux")
    if gathered_bytes > GATHER_LIMIT:
        return relayed_half_blocks(integrals, pair_list, coef, metric, occ_slot)
    return gathered_blocks(integrals, pair_list, coef, metric, occ_slot)


def solution(mesh):
    placed = (P("shell", None, "aux", None), P("shell", None), P("shell", None), P(), P())
    return jax.shard_map(
        per_device,
        mesh=mesh,
        in_specs=placed,
        out_specs=P(("shell", "aux"), None, None),
        check_vma=False,
    )
```

```python
import jax
import jax.numpy as jnp
from jax import lax
from jax.experimental import pallas as pl
from jax.experimental.pallas import tpu as pltpu
from jax.sharding import PartitionSpec as P

BS = 128


def relayed_half_blocks(integrals, pair_list, coef, metric, occ_slot):
    pairs_dev = pair_list.shape[0]
    rows_local = coef.shape[0]
    occ_count = coef.shape[1]
    blocks_dev = rows_local // BS
    shell_count = lax.axis_size("shell")
    block_count = blocks_dev * shell_count
    slot_count = occ_slot.shape[0]
    aux_dev = integrals.shape[2]
    inverse = (
        jnp.zeros((slot_count,), jnp.int32)
        .at[occ_slot]
        .set(jnp.arange(slot_count, dtype=jnp.int32))
    )
    ordered = jnp.take(
        coef.reshape(rows_local, slot_count, occ_count // slot_count), inverse, axis=1
    )
    ordered = ordered.reshape(rows_local, occ_count)

    def one_slot(item):
        int_block, column_index = item
        start = column_index % blocks_dev * BS
        column = lax.dynamic_slice_in_dim(ordered, start, BS, 0)
        product = lax.dot_general(
            column,
            int_block.reshape(BS, aux_dev * BS),
            (((0,), (0,)), ((), ())),
            preferred_element_type=jnp.float32,
        )
        return product.astype(jnp.bfloat16)

    half_blocks = lax.map(one_slot, (integrals, pair_list[:, 1]))
    half_blocks = half_blocks.reshape(pairs_dev, occ_count, aux_dev, BS)
    listing = lax.all_gather(pair_list, "shell", axis=0, tiled=True)
    targets = jnp.arange(block_count, dtype=jnp.int32)[:, None]
    selector = ((listing[:, 0][None, :] == targets) & (listing[:, 2][None, :] == 1)).astype(
        jnp.bfloat16
    )
    relayed = lax.all_to_all(
        lax.all_to_all(half_blocks, "shell", split_axis=1, concat_axis=0, tiled=True),
        "aux",
        split_axis=1,
        concat_axis=2,
        tiled=True,
    )
    summed = jnp.dot(
        selector, relayed.reshape(relayed.shape[0], -1), preferred_element_type=jnp.float32
    )
    blocks = summed.astype(jnp.bfloat16).reshape((block_count,) + relayed.shape[1:])
    result = jnp.einsum("qp,bipm->iqbm", metric, blocks, preferred_element_type=jnp.float32)
    return result.reshape(result.shape[0], result.shape[1], block_count * BS).astype(jnp.bfloat16)


def half_kernel(pairs_in, slot_in, coef_in, blocks_in, out, pairs, slot_row, coef, blocks, sems):
    pairs_dev = pairs.shape[0]
    blocks_dev = coef.shape[0] // BS
    occ_count = coef.shape[1]
    block_total = slot_row.shape[1]
    width = occ_count // block_total
    devices = out.shape[0]
    occ_local = occ_count // devices

    loads = [
        pltpu.make_async_copy(source, target, sems.at[at])
        for at, (source, target) in enumerate(
            ((slot_in, slot_row), (pairs_in, pairs), (coef_in, coef), (blocks_in, blocks))
        )
    ]
    for load in loads:
        load.start()
    loads[0].wait()

    spread = (
        lax.broadcasted_iota(jnp.int32, (block_total, occ_count), 1) // width
        == lax.broadcasted_iota(jnp.int32, (block_total, occ_count), 0)
    ).astype(jnp.bfloat16)
    slots = jnp.broadcast_to(slot_row[...], (8, block_total)).astype(jnp.float32)
    target = jnp.dot(slots.astype(jnp.bfloat16), spread, preferred_element_type=jnp.float32)
    target = target.astype(jnp.int32)[:1] * width + (
        lax.broadcasted_iota(jnp.int32, (1, occ_count), 1) % width
    )
    pick = (lax.broadcasted_iota(jnp.int32, (occ_count, 1), 0) == target).astype(jnp.bfloat16)

    for load in loads[1:]:
        load.wait()
    rows = [
        coef[pl.ds(pl.multiple_of(lax.rem(pairs[k, 1], blocks_dev) * BS, BS), BS), :]
        for k in range(pairs_dev)
    ]
    ordered = lax.dot_general(
        pick,
        jnp.concatenate(rows, axis=0),
        (((1,), (1,)), ((), ())),
        preferred_element_type=jnp.float32,
    ).astype(jnp.bfloat16)
    lane = lax.broadcasted_iota(jnp.int32, (1, BS), 1)
    code = jnp.zeros((1, BS), jnp.int32)
    for k in range(pairs_dev):
        half = jnp.dot(
            ordered[:, k * BS : (k + 1) * BS], blocks[k], preferred_element_type=jnp.float32
        )
        live = (pairs[k, 2] == 1).astype(jnp.float32)
        out[:, k * occ_local : (k + 1) * occ_local, :] = (
            (half * live).astype(jnp.bfloat16).reshape(devices, occ_local, BS)
        )
        block_row = pairs[k, 0]
        code = jnp.where(lane == k, block_row % 128, code)
        code = jnp.where(lane == pairs_dev + k, block_row // 128, code)
    digits = code.astype(jnp.float32).astype(jnp.bfloat16)
    out[:, pairs_dev * occ_local :, :] = jnp.broadcast_to(digits[None], (devices, 8, BS))


def collect_kernel(block_rows, metric, received, out, total):
    shell_count, pairs_dev = block_rows.shape
    occ_local, aux_count = out.shape[:2]
    rows = occ_local * aux_count
    total[...] = jnp.zeros_like(total)
    for s in range(shell_count):
        for k in range(pairs_dev):
            r = block_rows[s, k]
            for p in range(aux_count):
                part = received[s * aux_count + p, k * occ_local : (k + 1) * occ_local, :]
                total[r, p * occ_local : (p + 1) * occ_local, :] += part.astype(jnp.float32)

    row = lax.broadcasted_iota(jnp.int32, (rows, rows), 0)
    column = lax.broadcasted_iota(jnp.int32, (rows, rows), 1)
    left = (
        lax.broadcasted_iota(jnp.int32, (rows, aux_count), 0) % aux_count
        == lax.broadcasted_iota(jnp.int32, (rows, aux_count), 1)
    ).astype(jnp.bfloat16)
    right = (
        lax.broadcasted_iota(jnp.int32, (aux_count, rows), 1) // occ_local
        == lax.broadcasted_iota(jnp.int32, (aux_count, rows), 0)
    ).astype(jnp.bfloat16)
    factor = jnp.dot(left, metric[...], preferred_element_type=jnp.float32).astype(jnp.bfloat16)
    factor = jnp.dot(factor, right, preferred_element_type=jnp.float32)
    mix = jnp.where(row // aux_count == column % occ_local, factor, 0.0).astype(jnp.bfloat16)
    for r in range(0, total.shape[0], 2):
        summed = jnp.concatenate([total[r], total[r + 1]], axis=1).astype(jnp.bfloat16)
        mixed = jnp.dot(mix, summed, preferred_element_type=jnp.float32)
        out[:, :, r * BS : (r + 2) * BS] = mixed.reshape(
            occ_local, aux_count, 2 * BS
        ).astype(jnp.bfloat16)


def direct_half_blocks(integrals, pair_list, coef, metric, occ_slot):
    pairs_dev = pair_list.shape[0]
    shell_count = lax.axis_size("shell")
    aux_count = lax.axis_size("aux")
    devices = shell_count * aux_count
    occ_local = coef.shape[1] // devices
    block_count = coef.shape[0] // BS * shell_count
    vmem = pl.BlockSpec(memory_space=pltpu.VMEM)
    smem = pl.BlockSpec(memory_space=pltpu.SMEM)
    hbm = pl.BlockSpec(memory_space=pltpu.HBM)
    half = pl.pallas_call(
        half_kernel,
        out_shape=jax.ShapeDtypeStruct((devices, pairs_dev * occ_local + 8, BS), jnp.bfloat16),
        in_specs=[hbm] * 4,
        out_specs=vmem,
        scratch_shapes=[
            pltpu.SMEM(pair_list.shape, jnp.int32),
            pltpu.VMEM((1, occ_slot.shape[0]), jnp.int32),
            pltpu.VMEM(coef.shape, jnp.bfloat16),
            pltpu.VMEM((pairs_dev, BS, BS), jnp.bfloat16),
            pltpu.SemaphoreType.DMA((4,)),
        ],
        compiler_params=pltpu.CompilerParams(vmem_limit_bytes=40 * 2**20),
        name="half_blocks",
    )(
        *(
            pltpu.with_memory_space_constraint(operand, pltpu.HBM)
            for operand in (
                pair_list,
                occ_slot.reshape(1, -1),
                coef,
                integrals.reshape(pairs_dev, BS, BS),
            )
        )
    )
    received = lax.all_to_all(half, ("shell", "aux"), split_axis=0, concat_axis=0)
    digits = received[::aux_count, pairs_dev * occ_local, : 2 * pairs_dev].astype(jnp.int32)
    block_rows = digits[:, :pairs_dev] + 128 * digits[:, pairs_dev:]
    return pl.pallas_call(
        collect_kernel,
        out_shape=jax.ShapeDtypeStruct(
            (occ_local, aux_count, block_count * BS), jnp.bfloat16
        ),
        in_specs=[smem, vmem, vmem],
        out_specs=vmem,
        scratch_shapes=[pltpu.VMEM((block_count, occ_local * aux_count, BS), jnp.float32)],
        compiler_params=pltpu.CompilerParams(vmem_limit_bytes=40 * 2**20),
        name="collect",
    )(block_rows, metric, received)


def per_device(integrals, pair_list, coef, metric, occ_slot):
    occ_local = coef.shape[1] // (lax.axis_size("shell") * lax.axis_size("aux"))
    if occ_local % 16:
        return relayed_half_blocks(integrals, pair_list, coef, metric, occ_slot)
    return direct_half_blocks(integrals, pair_list, coef, metric, occ_slot)


def solution(mesh):
    placed = (P("shell", None, "aux", None), P("shell", None), P("shell", None), P(), P())
    return jax.shard_map(
        per_device,
        mesh=mesh,
        in_specs=placed,
        out_specs=P(("shell", "aux"), None, None),
        check_vma=False,
    )
```

```python
import functools

import jax
import jax.numpy as jnp
from jax import lax
from jax.experimental import pallas as pl
from jax.experimental.pallas import tpu as pltpu
from jax.sharding import PartitionSpec as P

BS = 128


def relayed_half_blocks(integrals, pair_list, coef, metric, occ_slot):
    pairs_dev = pair_list.shape[0]
    rows_local = coef.shape[0]
    occ_count = coef.shape[1]
    blocks_dev = rows_local // BS
    shell_count = lax.axis_size("shell")
    block_count = blocks_dev * shell_count
    slot_count = occ_slot.shape[0]
    aux_dev = integrals.shape[2]
    inverse = (
        jnp.zeros((slot_count,), jnp.int32)
        .at[occ_slot]
        .set(jnp.arange(slot_count, dtype=jnp.int32))
    )
    ordered = jnp.take(
        coef.reshape(rows_local, slot_count, occ_count // slot_count), inverse, axis=1
    )
    ordered = ordered.reshape(rows_local, occ_count)

    def one_slot(item):
        int_block, column_index = item
        start = column_index % blocks_dev * BS
        column = lax.dynamic_slice_in_dim(ordered, start, BS, 0)
        product = lax.dot_general(
            column,
            int_block.reshape(BS, aux_dev * BS),
            (((0,), (0,)), ((), ())),
            preferred_element_type=jnp.float32,
        )
        return product.astype(jnp.bfloat16)

    half_blocks = lax.map(one_slot, (integrals, pair_list[:, 1]))
    half_blocks = half_blocks.reshape(pairs_dev, occ_count, aux_dev, BS)
    listing = lax.all_gather(pair_list, "shell", axis=0, tiled=True)
    targets = jnp.arange(block_count, dtype=jnp.int32)[:, None]
    selector = ((listing[:, 0][None, :] == targets) & (listing[:, 2][None, :] == 1)).astype(
        jnp.bfloat16
    )
    relayed = lax.all_to_all(
        lax.all_to_all(half_blocks, "shell", split_axis=1, concat_axis=0, tiled=True),
        "aux",
        split_axis=1,
        concat_axis=2,
        tiled=True,
    )
    summed = jnp.dot(
        selector, relayed.reshape(relayed.shape[0], -1), preferred_element_type=jnp.float32
    )
    blocks = summed.astype(jnp.bfloat16).reshape((block_count,) + relayed.shape[1:])
    result = jnp.einsum("qp,bipm->iqbm", metric, blocks, preferred_element_type=jnp.float32)
    return result.reshape(result.shape[0], result.shape[1], block_count * BS).astype(jnp.bfloat16)


def targets_of(slot_row, block_total, occ_count):
    width = occ_count // block_total
    spread = (
        lax.broadcasted_iota(jnp.int32, (block_total, occ_count), 1) // width
        == lax.broadcasted_iota(jnp.int32, (block_total, occ_count), 0)
    ).astype(jnp.bfloat16)
    slots = jnp.broadcast_to(slot_row, (8, block_total)).astype(jnp.float32)
    target = jnp.dot(slots.astype(jnp.bfloat16), spread, preferred_element_type=jnp.float32)
    return target.astype(jnp.int32)[:1] * width + (
        lax.broadcasted_iota(jnp.int32, (1, occ_count), 1) % width
    )


def pick_kernel(group, occ_local, aux_count, pairs_in, slot_in, coef_in, near, far, pairs, slot_row, coef, sems):
    pairs_dev = pairs.shape[0]
    blocks_dev = coef.shape[0] // BS
    occ_count = coef.shape[1]
    loads = [
        pltpu.make_async_copy(source, target, sems.at[at])
        for at, (source, target) in enumerate(
            ((slot_in, slot_row), (pairs_in, pairs), (coef_in, coef))
        )
    ]
    for load in loads:
        load.start()
    me = lax.axis_index("shell")
    mine = lax.axis_index("aux")
    rows = group * occ_local
    row = lax.broadcasted_iota(jnp.int32, (2 * rows, 1), 0)
    owner = jnp.bitwise_xor(row // occ_local, me)
    wanted = (owner * aux_count + mine) * occ_local + row % occ_local
    loads[0].wait()
    target = targets_of(slot_row[...], slot_row.shape[1], occ_count)
    pick = (wanted == target).astype(jnp.bfloat16)
    for load in loads[1:]:
        load.wait()
    for k in range(pairs_dev):
        start = pl.multiple_of(lax.rem(pairs[k, 1], blocks_dev) * BS, BS)
        live = (pairs[k, 2] == 1).astype(jnp.float32)
        piece = lax.dot_general(
            pick,
            coef[pl.ds(start, BS), :],
            (((1,), (1,)), ((), ())),
            preferred_element_type=jnp.float32,
        )
        piece = (piece * live).astype(jnp.bfloat16)
        near[:, k * BS : (k + 1) * BS] = piece[:rows]
        far[:, k * BS : (k + 1) * BS] = piece[rows:]


def block_kernel(aux_count, coded, *refs):
    if coded:
        pairs, far_pairs, *refs = refs
    coefs, *refs = refs
    blocks, pieces = refs[:aux_count], refs[aux_count:]
    pairs_dev = blocks[0].shape[0]
    occ_local = coefs.shape[0] // len(pieces)
    mine = lax.axis_index("aux")
    for k in range(pairs_dev):
        left = coefs[:, k * BS : (k + 1) * BS]
        for j in range(0, aux_count, 2):
            right = jnp.concatenate([blocks[j][k], blocks[j + 1][k]], axis=1)
            half = jnp.dot(left, right, preferred_element_type=jnp.float32).astype(jnp.bfloat16)
            for side in range(2):
                at = k * aux_count + jnp.bitwise_xor(mine, j + side)
                start = pl.multiple_of(at * occ_local, occ_local)
                for f, piece in enumerate(pieces):
                    piece[pl.ds(start, occ_local), :] = half[
                        f * occ_local : (f + 1) * occ_local, side * BS : (side + 1) * BS
                    ]
    if coded:
        lane = lax.broadcasted_iota(jnp.int32, (1, BS), 1)
        code = jnp.zeros((1, BS), jnp.int32)
        for at, listing in enumerate((pairs, far_pairs)):
            for k in range(pairs_dev):
                block_row = listing[k, 0]
                place = 2 * (at * pairs_dev + k)
                code = jnp.where(lane == place, block_row % 128, code)
                code = jnp.where(lane == place + 1, block_row // 128, code)
        digits = jnp.broadcast_to(code.astype(jnp.float32), (16, BS)).astype(jnp.bfloat16)
        for piece in pieces:
            piece[pairs_dev * aux_count * occ_local :, :] = digits


def collect_kernel(block_rows, metric, *refs):
    *received, out, total = refs
    occ_local, aux_count = out.shape[:2]
    rows = occ_local * aux_count
    pairs_dev = block_rows.shape[1]
    total[...] = jnp.zeros_like(total)
    for at, piece in enumerate(received):
        for k in range(pairs_dev):
            r = block_rows[at, k]
            total[r] += piece[k * rows : (k + 1) * rows, :].astype(jnp.float32)

    row = lax.broadcasted_iota(jnp.int32, (rows, rows), 0)
    column = lax.broadcasted_iota(jnp.int32, (rows, rows), 1)
    left = (
        lax.broadcasted_iota(jnp.int32, (rows, aux_count), 0) % aux_count
        == lax.broadcasted_iota(jnp.int32, (rows, aux_count), 1)
    ).astype(jnp.bfloat16)
    right = (
        lax.broadcasted_iota(jnp.int32, (aux_count, rows), 1) // occ_local
        == lax.broadcasted_iota(jnp.int32, (aux_count, rows), 0)
    ).astype(jnp.bfloat16)
    factor = jnp.dot(left, metric[...], preferred_element_type=jnp.float32).astype(jnp.bfloat16)
    factor = jnp.dot(factor, right, preferred_element_type=jnp.float32)
    mix = jnp.where(row // aux_count == column % occ_local, factor, 0.0).astype(jnp.bfloat16)
    for r in range(0, total.shape[0], 2):
        summed = jnp.concatenate([total[r], total[r + 1]], axis=1).astype(jnp.bfloat16)
        mixed = jnp.dot(mix, summed, preferred_element_type=jnp.float32)
        out[:, :, r * BS : (r + 2) * BS] = mixed.reshape(
            occ_local, aux_count, 2 * BS
        ).astype(jnp.bfloat16)


def flip(value, axis, bits):
    count = lax.axis_size(axis)
    return lax.ppermute(value, axis, [(at, at ^ bits) for at in range(count)])


def in_hbm(*operands):
    return [pltpu.with_memory_space_constraint(operand, pltpu.HBM) for operand in operands]


def exchanged_inputs(integrals, pair_list, coef, metric, occ_slot):
    pairs_dev = pair_list.shape[0]
    shell_count = lax.axis_size("shell")
    aux_count = lax.axis_size("aux")
    group = shell_count // 2
    occ_local = coef.shape[1] // (shell_count * aux_count)
    block_count = coef.shape[0] // BS * shell_count
    rows = group * occ_local
    piece_rows = pairs_dev * aux_count * occ_local
    vmem = pl.BlockSpec(memory_space=pltpu.VMEM)
    smem = pl.BlockSpec(memory_space=pltpu.SMEM)
    hbm = pl.BlockSpec(memory_space=pltpu.HBM)
    params = pltpu.CompilerParams(vmem_limit_bytes=40 * 2**20)

    blocks = integrals.reshape(pairs_dev, BS, BS)
    far_block = flip(blocks, "shell", group)
    far_pairs = flip(pair_list, "shell", group)
    near_blocks = [blocks] + [flip(blocks, "aux", j) for j in range(1, aux_count)]
    near_coef, sent_coef = pl.pallas_call(
        functools.partial(pick_kernel, group, occ_local, aux_count),
        out_shape=[jax.ShapeDtypeStruct((rows, pairs_dev * BS), jnp.bfloat16)] * 2,
        in_specs=[hbm] * 3,
        out_specs=[vmem] * 2,
        scratch_shapes=[
            pltpu.SMEM(pair_list.shape, jnp.int32),
            pltpu.VMEM((1, occ_slot.shape[0]), jnp.int32),
            pltpu.VMEM(coef.shape, jnp.bfloat16),
            pltpu.SemaphoreType.DMA((3,)),
        ],
        compiler_params=params,
        name="pick",
    )(*in_hbm(pair_list, occ_slot.reshape(1, -1), coef))
    far_coef = flip(sent_coef, "shell", group)

    def transformed(coded, name, listings, coefs, quad):
        pieces = pl.pallas_call(
            functools.partial(block_kernel, aux_count, coded),
            out_shape=[
                jax.ShapeDtypeStruct((piece_rows + 16 * coded, BS), jnp.bfloat16)
            ] * group,
            in_specs=[smem] * len(listings) + [vmem] * (1 + aux_count),
            out_specs=[vmem] * group,
            compiler_params=params,
            name=name,
        )(*listings, coefs, *quad)
        return [pieces[0]] + [flip(pieces[f], "shell", f) for f in range(1, group)]

    near = transformed(True, "near_blocks", (pair_list, far_pairs), near_coef, near_blocks)
    far_blocks = [far_block] + [flip(far_block, "aux", j) for j in range(1, aux_count)]
    far = transformed(False, "far_blocks", (), far_coef, far_blocks)
    digits = jnp.stack([piece[piece_rows, : 4 * pairs_dev] for piece in near])
    digits = digits.astype(jnp.int32).reshape(group, 2, pairs_dev, 2)
    block_rows = (digits[..., 0] + 128 * digits[..., 1]).swapaxes(0, 1)
    return pl.pallas_call(
        collect_kernel,
        out_shape=jax.ShapeDtypeStruct(
            (occ_local, aux_count, block_count * BS), jnp.bfloat16
        ),
        in_specs=[smem] + [vmem] * (1 + 2 * group),
        out_specs=vmem,
        scratch_shapes=[pltpu.VMEM((block_count, occ_local * aux_count, BS), jnp.float32)],
        compiler_params=params,
        name="collect",
    )(block_rows.reshape(2 * group, pairs_dev), metric, *near, *far)


def per_device(integrals, pair_list, coef, metric, occ_slot):
    shell_count, aux_count = lax.axis_size("shell"), lax.axis_size("aux")
    occ_local = coef.shape[1] // (shell_count * aux_count)
    if occ_local % 16 or shell_count & (shell_count - 1) or aux_count & (aux_count - 1):
        return relayed_half_blocks(integrals, pair_list, coef, metric, occ_slot)
    return exchanged_inputs(integrals, pair_list, coef, metric, occ_slot)


def solution(mesh):
    placed = (P("shell", None, "aux", None), P("shell", None), P("shell", None), P(), P())
    return jax.shard_map(
        per_device,
        mesh=mesh,
        in_specs=placed,
        out_specs=P(("shell", "aux"), None, None),
        check_vma=False,
    )
```

```python
import functools

import jax
import jax.numpy as jnp
from jax import lax
from jax.experimental import pallas as pl
from jax.experimental.pallas import tpu as pltpu
from jax.sharding import PartitionSpec as P

BS = 128


def relayed_half_blocks(integrals, pair_list, coef, metric, occ_slot):
    pairs_dev = pair_list.shape[0]
    rows_local = coef.shape[0]
    occ_count = coef.shape[1]
    blocks_dev = rows_local // BS
    shell_count = lax.axis_size("shell")
    block_count = blocks_dev * shell_count
    slot_count = occ_slot.shape[0]
    aux_dev = integrals.shape[2]
    inverse = (
        jnp.zeros((slot_count,), jnp.int32)
        .at[occ_slot]
        .set(jnp.arange(slot_count, dtype=jnp.int32))
    )
    ordered = jnp.take(
        coef.reshape(rows_local, slot_count, occ_count // slot_count), inverse, axis=1
    )
    ordered = ordered.reshape(rows_local, occ_count)

    def one_slot(item):
        int_block, column_index = item
        start = column_index % blocks_dev * BS
        column = lax.dynamic_slice_in_dim(ordered, start, BS, 0)
        product = lax.dot_general(
            column,
            int_block.reshape(BS, aux_dev * BS),
            (((0,), (0,)), ((), ())),
            preferred_element_type=jnp.float32,
        )
        return product.astype(jnp.bfloat16)

    half_blocks = lax.map(one_slot, (integrals, pair_list[:, 1]))
    half_blocks = half_blocks.reshape(pairs_dev, occ_count, aux_dev, BS)
    listing = lax.all_gather(pair_list, "shell", axis=0, tiled=True)
    targets = jnp.arange(block_count, dtype=jnp.int32)[:, None]
    selector = ((listing[:, 0][None, :] == targets) & (listing[:, 2][None, :] == 1)).astype(
        jnp.bfloat16
    )
    relayed = lax.all_to_all(
        lax.all_to_all(half_blocks, "shell", split_axis=1, concat_axis=0, tiled=True),
        "aux",
        split_axis=1,
        concat_axis=2,
        tiled=True,
    )
    summed = jnp.dot(
        selector, relayed.reshape(relayed.shape[0], -1), preferred_element_type=jnp.float32
    )
    blocks = summed.astype(jnp.bfloat16).reshape((block_count,) + relayed.shape[1:])
    result = jnp.einsum("qp,bipm->iqbm", metric, blocks, preferred_element_type=jnp.float32)
    return result.reshape(result.shape[0], result.shape[1], block_count * BS).astype(jnp.bfloat16)


def targets_of(slot_row, block_total, occ_count):
    width = occ_count // block_total
    spread = (
        lax.broadcasted_iota(jnp.int32, (block_total, occ_count), 1) // width
        == lax.broadcasted_iota(jnp.int32, (block_total, occ_count), 0)
    ).astype(jnp.bfloat16)
    slots = jnp.broadcast_to(slot_row, (8, block_total)).astype(jnp.float32)
    target = jnp.dot(slots.astype(jnp.bfloat16), spread, preferred_element_type=jnp.float32)
    return target.astype(jnp.int32)[:1] * width + (
        lax.broadcasted_iota(jnp.int32, (1, occ_count), 1) % width
    )


def pick_kernel(group, occ_local, aux_count, pairs_in, slot_in, coef_in, near, far, pairs, slot_row, coef, sems):
    pairs_dev = pairs.shape[0]
    blocks_dev = coef.shape[0] // BS
    occ_count = coef.shape[1]
    loads = [
        pltpu.make_async_copy(source, target, sems.at[at])
        for at, (source, target) in enumerate(
            ((slot_in, slot_row), (pairs_in, pairs), (coef_in, coef))
        )
    ]
    for load in loads:
        load.start()
    me = lax.axis_index("shell")
    mine = lax.axis_index("aux")
    rows = group * occ_local
    row = lax.broadcasted_iota(jnp.int32, (2 * rows, 1), 0)
    owner = jnp.bitwise_xor(row // occ_local, me)
    wanted = (owner * aux_count + mine) * occ_local + row % occ_local
    loads[0].wait()
    target = targets_of(slot_row[...], slot_row.shape[1], occ_count)
    pick = (wanted == target).astype(jnp.bfloat16)
    for load in loads[1:]:
        load.wait()
    for k in range(pairs_dev):
        start = pl.multiple_of(lax.rem(pairs[k, 1], blocks_dev) * BS, BS)
        live = (pairs[k, 2] == 1).astype(jnp.float32)
        piece = lax.dot_general(
            pick,
            coef[pl.ds(start, BS), :],
            (((1,), (1,)), ((), ())),
            preferred_element_type=jnp.float32,
        )
        piece = (piece * live).astype(jnp.bfloat16)
        near[:rows, k * BS : (k + 1) * BS] = piece[:rows]
        far[:rows, k * BS : (k + 1) * BS] = piece[rows:]
    lane = lax.broadcasted_iota(jnp.int32, (1, BS), 1)
    code = jnp.zeros((1, BS), jnp.int32)
    for k in range(pairs_dev):
        code = jnp.where(lane == k, pairs[k, 0] % 128, code)
        code = jnp.where(lane == pairs_dev + k, pairs[k, 0] // 128, code)
    code = jnp.broadcast_to(code.astype(jnp.float32), (16, BS)).astype(jnp.bfloat16)
    for piece in (near, far):
        piece[rows:, :BS] = code
        piece[rows:, BS:] = jnp.zeros((16, piece.shape[1] - BS), jnp.bfloat16)


def block_kernel(aux_count, coefs, *refs):
    blocks, pieces = refs[:aux_count], refs[aux_count:]
    pairs_dev = blocks[0].shape[0]
    rows = coefs.shape[0] - 16
    occ_local = rows // len(pieces)
    mine = lax.axis_index("aux")
    for k in range(pairs_dev):
        left = coefs[:rows, k * BS : (k + 1) * BS]
        for j in range(0, aux_count, 2):
            right = jnp.concatenate([blocks[j][k], blocks[j + 1][k]], axis=1)
            half = jnp.dot(left, right, preferred_element_type=jnp.float32).astype(jnp.bfloat16)
            for side in range(2):
                at = k * aux_count + jnp.bitwise_xor(mine, j + side)
                start = pl.multiple_of(at * occ_local, occ_local)
                for f, piece in enumerate(pieces):
                    piece[pl.ds(start, occ_local), :] = half[
                        f * occ_local : (f + 1) * occ_local, side * BS : (side + 1) * BS
                    ]
    for piece in pieces:
        piece[pairs_dev * aux_count * occ_local :, :] = coefs[rows:, :BS]


def collect_kernel(pairs_dev, metric_in, *refs):
    *received, out, total, metric, codes_v, codes, sems = refs
    occ_local, aux_count = out.shape[:2]
    rows = occ_local * aux_count
    for at, piece in enumerate(received):
        digits = piece[pairs_dev * rows :, :].astype(jnp.float32).astype(jnp.int32)
        codes_v[at : at + 1, :] = digits[:1]
    loads = [
        pltpu.make_async_copy(codes_v, codes, sems.at[0]),
        pltpu.make_async_copy(metric_in, metric, sems.at[1]),
    ]
    for load in loads:
        load.start()
    total[...] = jnp.zeros_like(total)
    for load in loads:
        load.wait()
    for at, piece in enumerate(received):
        for k in range(pairs_dev):
            r = codes[at, k] + 128 * codes[at, pairs_dev + k]
            total[r] += piece[k * rows : (k + 1) * rows, :].astype(jnp.float32)

    row = lax.broadcasted_iota(jnp.int32, (rows, rows), 0)
    column = lax.broadcasted_iota(jnp.int32, (rows, rows), 1)
    left = (
        lax.broadcasted_iota(jnp.int32, (rows, aux_count), 0) % aux_count
        == lax.broadcasted_iota(jnp.int32, (rows, aux_count), 1)
    ).astype(jnp.bfloat16)
    right = (
        lax.broadcasted_iota(jnp.int32, (aux_count, rows), 1) // occ_local
        == lax.broadcasted_iota(jnp.int32, (aux_count, rows), 0)
    ).astype(jnp.bfloat16)
    factor = jnp.dot(left, metric[...], preferred_element_type=jnp.float32).astype(jnp.bfloat16)
    factor = jnp.dot(factor, right, preferred_element_type=jnp.float32)
    mix = jnp.where(row // aux_count == column % occ_local, factor, 0.0).astype(jnp.bfloat16)
    for r in range(0, total.shape[0], 2):
        summed = jnp.concatenate([total[r], total[r + 1]], axis=1).astype(jnp.bfloat16)
        mixed = jnp.dot(mix, summed, preferred_element_type=jnp.float32)
        out[:, :, r * BS : (r + 2) * BS] = mixed.reshape(
            occ_local, aux_count, 2 * BS
        ).astype(jnp.bfloat16)


def flip(value, axis, bits):
    count = lax.axis_size(axis)
    return lax.ppermute(value, axis, [(at, at ^ bits) for at in range(count)])


def shared(block, after=None):
    held, order, bits = [block], [0], lax.axis_size("aux") // 2
    while bits:
        held += [flip(one, "aux", bits) for one in held]
        order += [at ^ bits for at in order]
        bits //= 2
        if after is not None:
            *held, after = lax.optimization_barrier((*held, after))
    return [held[order.index(at)] for at in range(len(held))]


def in_hbm(*operands):
    return [pltpu.with_memory_space_constraint(operand, pltpu.HBM) for operand in operands]


def exchanged_inputs(integrals, pair_list, coef, metric, occ_slot):
    pairs_dev = pair_list.shape[0]
    shell_count = lax.axis_size("shell")
    aux_count = lax.axis_size("aux")
    group = shell_count // 2
    occ_local = coef.shape[1] // (shell_count * aux_count)
    block_count = coef.shape[0] // BS * shell_count
    rows = group * occ_local
    piece_rows = pairs_dev * aux_count * occ_local
    vmem = pl.BlockSpec(memory_space=pltpu.VMEM)
    hbm = pl.BlockSpec(memory_space=pltpu.HBM)
    params = pltpu.CompilerParams(vmem_limit_bytes=40 * 2**20)

    blocks = integrals.reshape(pairs_dev, BS, BS)
    far_block = flip(blocks, "shell", group)
    near_coef, sent_coef = pl.pallas_call(
        functools.partial(pick_kernel, group, occ_local, aux_count),
        out_shape=[jax.ShapeDtypeStruct((rows + 16, pairs_dev * BS), jnp.bfloat16)] * 2,
        in_specs=[hbm] * 3,
        out_specs=[vmem] * 2,
        scratch_shapes=[
            pltpu.SMEM(pair_list.shape, jnp.int32),
            pltpu.VMEM((1, occ_slot.shape[0]), jnp.int32),
            pltpu.VMEM(coef.shape, jnp.bfloat16),
            pltpu.SemaphoreType.DMA((3,)),
        ],
        compiler_params=params,
        name="pick",
    )(*in_hbm(pair_list, occ_slot.reshape(1, -1), coef))
    near_blocks = shared(blocks, sent_coef)
    far_block, near_coef, sent_coef = lax.optimization_barrier((far_block, near_coef, sent_coef))
    far_coef = flip(sent_coef, "shell", group)

    def transformed(name, coefs, quad):
        pieces = pl.pallas_call(
            functools.partial(block_kernel, aux_count),
            out_shape=[jax.ShapeDtypeStruct((piece_rows + 16, BS), jnp.bfloat16)] * group,
            in_specs=[vmem] * (1 + aux_count),
            out_specs=[vmem] * group,
            compiler_params=params,
            name=name,
        )(coefs, *quad)
        return [pieces[0]] + [flip(pieces[f], "shell", f) for f in range(1, group)]

    near = transformed("near_blocks", near_coef, near_blocks)
    far_blocks = shared(far_block)
    far = transformed("far_blocks", far_coef, far_blocks)
    return pl.pallas_call(
        functools.partial(collect_kernel, pairs_dev),
        out_shape=jax.ShapeDtypeStruct(
            (occ_local, aux_count, block_count * BS), jnp.bfloat16
        ),
        in_specs=[hbm] + [vmem] * (2 * group),
        out_specs=vmem,
        scratch_shapes=[
            pltpu.VMEM((block_count, occ_local * aux_count, BS), jnp.float32),
            pltpu.VMEM(metric.shape, jnp.bfloat16),
            pltpu.VMEM((2 * group, BS), jnp.int32),
            pltpu.SMEM((2 * group, BS), jnp.int32),
            pltpu.SemaphoreType.DMA((2,)),
        ],
        compiler_params=params,
        name="collect",
    )(*in_hbm(metric), *near, *far)


def per_device(integrals, pair_list, coef, metric, occ_slot):
    shell_count, aux_count = lax.axis_size("shell"), lax.axis_size("aux")
    occ_local = coef.shape[1] // (shell_count * aux_count)
    if occ_local % 16 or shell_count & (shell_count - 1) or aux_count & (aux_count - 1):
        return relayed_half_blocks(integrals, pair_list, coef, metric, occ_slot)
    return exchanged_inputs(integrals, pair_list, coef, metric, occ_slot)


def solution(mesh):
    placed = (P("shell", None, "aux", None), P("shell", None), P("shell", None), P(), P())
    return jax.shard_map(
        per_device,
        mesh=mesh,
        in_specs=placed,
        out_specs=P(("shell", "aux"), None, None),
        check_vma=False,
    )
```

```python
import functools

import jax
import jax.numpy as jnp
from jax import lax
from jax.experimental import pallas as pl
from jax.experimental.pallas import tpu as pltpu
from jax.sharding import PartitionSpec as P

BS = 128


def relayed_half_blocks(integrals, pair_list, coef, metric, occ_slot):
    pairs_dev = pair_list.shape[0]
    rows_local = coef.shape[0]
    occ_count = coef.shape[1]
    blocks_dev = rows_local // BS
    shell_count = lax.axis_size("shell")
    block_count = blocks_dev * shell_count
    slot_count = occ_slot.shape[0]
    aux_dev = integrals.shape[2]
    inverse = (
        jnp.zeros((slot_count,), jnp.int32)
        .at[occ_slot]
        .set(jnp.arange(slot_count, dtype=jnp.int32))
    )
    ordered = jnp.take(
        coef.reshape(rows_local, slot_count, occ_count // slot_count), inverse, axis=1
    )
    ordered = ordered.reshape(rows_local, occ_count)

    def one_slot(item):
        int_block, column_index = item
        start = column_index % blocks_dev * BS
        column = lax.dynamic_slice_in_dim(ordered, start, BS, 0)
        product = lax.dot_general(
            column,
            int_block.reshape(BS, aux_dev * BS),
            (((0,), (0,)), ((), ())),
            preferred_element_type=jnp.float32,
        )
        return product.astype(jnp.bfloat16)

    half_blocks = lax.map(one_slot, (integrals, pair_list[:, 1]))
    half_blocks = half_blocks.reshape(pairs_dev, occ_count, aux_dev, BS)
    listing = lax.all_gather(pair_list, "shell", axis=0, tiled=True)
    targets = jnp.arange(block_count, dtype=jnp.int32)[:, None]
    selector = ((listing[:, 0][None, :] == targets) & (listing[:, 2][None, :] == 1)).astype(
        jnp.bfloat16
    )
    relayed = lax.all_to_all(
        lax.all_to_all(half_blocks, "shell", split_axis=1, concat_axis=0, tiled=True),
        "aux",
        split_axis=1,
        concat_axis=2,
        tiled=True,
    )
    summed = jnp.dot(
        selector, relayed.reshape(relayed.shape[0], -1), preferred_element_type=jnp.float32
    )
    blocks = summed.astype(jnp.bfloat16).reshape((block_count,) + relayed.shape[1:])
    result = jnp.einsum("qp,bipm->iqbm", metric, blocks, preferred_element_type=jnp.float32)
    return result.reshape(result.shape[0], result.shape[1], block_count * BS).astype(jnp.bfloat16)


def targets_of(slot_row, block_total, occ_count):
    width = occ_count // block_total
    spread = (
        lax.broadcasted_iota(jnp.int32, (block_total, occ_count), 1) // width
        == lax.broadcasted_iota(jnp.int32, (block_total, occ_count), 0)
    ).astype(jnp.bfloat16)
    slots = jnp.broadcast_to(slot_row, (8, block_total)).astype(jnp.float32)
    target = jnp.dot(slots.astype(jnp.bfloat16), spread, preferred_element_type=jnp.float32)
    return target.astype(jnp.int32)[:1] * width + (
        lax.broadcasted_iota(jnp.int32, (1, occ_count), 1) % width
    )


def pick_kernel(group, occ_local, aux_count, pairs_in, slot_in, coef_in, near, far, pairs, slot_row, coef, sems):
    pairs_dev = pairs.shape[0]
    blocks_dev = coef.shape[0] // BS
    occ_count = coef.shape[1]
    loads = [
        pltpu.make_async_copy(source, target, sems.at[at])
        for at, (source, target) in enumerate(
            ((slot_in, slot_row), (pairs_in, pairs), (coef_in, coef))
        )
    ]
    for load in loads:
        load.start()
    me = lax.axis_index("shell")
    mine = lax.axis_index("aux")
    rows = group * occ_local
    row = lax.broadcasted_iota(jnp.int32, (2 * rows, 1), 0)
    owner = jnp.bitwise_xor(row // occ_local, me)
    wanted = (owner * aux_count + mine) * occ_local + row % occ_local
    loads[0].wait()
    target = targets_of(slot_row[...], slot_row.shape[1], occ_count)
    pick = (wanted == target).astype(jnp.bfloat16)
    for load in loads[1:]:
        load.wait()
    for k in range(pairs_dev):
        start = pl.multiple_of(lax.rem(pairs[k, 1], blocks_dev) * BS, BS)
        live = (pairs[k, 2] == 1).astype(jnp.float32)
        piece = lax.dot_general(
            pick,
            coef[pl.ds(start, BS), :],
            (((1,), (1,)), ((), ())),
            preferred_element_type=jnp.float32,
        )
        piece = (piece * live).astype(jnp.bfloat16)
        near[:rows, k * BS : (k + 1) * BS] = piece[:rows]
        far[:rows, k * BS : (k + 1) * BS] = piece[rows:]
    lane = lax.broadcasted_iota(jnp.int32, (1, BS), 1)
    code = jnp.zeros((1, BS), jnp.int32)
    for k in range(pairs_dev):
        code = jnp.where(lane == k, pairs[k, 0] % 128, code)
        code = jnp.where(lane == pairs_dev + k, pairs[k, 0] // 128, code)
    code = jnp.broadcast_to(code.astype(jnp.float32), (16, BS)).astype(jnp.bfloat16)
    for piece in (near, far):
        piece[rows:, :BS] = code
        piece[rows:, BS:] = jnp.zeros((16, piece.shape[1] - BS), jnp.bfloat16)


def block_kernel(aux_count, coefs, *refs):
    blocks, pieces = refs[:aux_count], refs[aux_count:]
    pairs_dev = blocks[0].shape[0]
    rows = coefs.shape[0] - 16
    occ_local = rows // len(pieces)
    mine = lax.axis_index("aux")
    for k in range(pairs_dev):
        left = coefs[:rows, k * BS : (k + 1) * BS]
        for j in range(0, aux_count, 2):
            right = jnp.concatenate([blocks[j][k], blocks[j + 1][k]], axis=1)
            half = jnp.dot(left, right, preferred_element_type=jnp.float32).astype(jnp.bfloat16)
            for side in range(2):
                at = k * aux_count + jnp.bitwise_xor(mine, j + side)
                start = pl.multiple_of(at * occ_local, occ_local)
                for f, piece in enumerate(pieces):
                    piece[pl.ds(start, occ_local), :] = half[
                        f * occ_local : (f + 1) * occ_local, side * BS : (side + 1) * BS
                    ]
    for piece in pieces:
        piece[pairs_dev * aux_count * occ_local :, :] = coefs[rows:, :BS]


def collect_kernel(pairs_dev, metric_in, *refs):
    *received, out, total, metric, codes_v, codes, sems = refs
    occ_local, aux_count = out.shape[:2]
    rows = occ_local * aux_count
    for at, piece in enumerate(received):
        digits = piece[pairs_dev * rows :, :].astype(jnp.float32).astype(jnp.int32)
        codes_v[at : at + 1, :] = digits[:1]
    loads = [
        pltpu.make_async_copy(codes_v, codes, sems.at[0]),
        pltpu.make_async_copy(metric_in, metric, sems.at[1]),
    ]
    for load in loads:
        load.start()
    total[...] = jnp.zeros_like(total)
    for load in loads:
        load.wait()
    for at, piece in enumerate(received):
        for k in range(pairs_dev):
            r = codes[at, k] + 128 * codes[at, pairs_dev + k]
            total[r] += piece[k * rows : (k + 1) * rows, :].astype(jnp.float32)

    row = lax.broadcasted_iota(jnp.int32, (rows, rows), 0)
    column = lax.broadcasted_iota(jnp.int32, (rows, rows), 1)
    left = (
        lax.broadcasted_iota(jnp.int32, (rows, aux_count), 0) % aux_count
        == lax.broadcasted_iota(jnp.int32, (rows, aux_count), 1)
    ).astype(jnp.bfloat16)
    right = (
        lax.broadcasted_iota(jnp.int32, (aux_count, rows), 1) // occ_local
        == lax.broadcasted_iota(jnp.int32, (aux_count, rows), 0)
    ).astype(jnp.bfloat16)
    factor = jnp.dot(left, metric[...], preferred_element_type=jnp.float32).astype(jnp.bfloat16)
    factor = jnp.dot(factor, right, preferred_element_type=jnp.float32)
    mix = jnp.where(row // aux_count == column % occ_local, factor, 0.0).astype(jnp.bfloat16)
    for r in range(0, total.shape[0], 2):
        summed = jnp.concatenate([total[r], total[r + 1]], axis=1).astype(jnp.bfloat16)
        mixed = jnp.dot(mix, summed, preferred_element_type=jnp.float32)
        out[:, :, r * BS : (r + 2) * BS] = mixed.reshape(
            occ_local, aux_count, 2 * BS
        ).astype(jnp.bfloat16)


def flip(value, axis, bits):
    count = lax.axis_size(axis)
    return lax.ppermute(value, axis, [(at, at ^ bits) for at in range(count)])


def after(value, *others):
    return lax.optimization_barrier((value, *others))[0]


def shared(block, *others):
    held, order, bits = [block], [0], lax.axis_size("aux") // 2
    while bits:
        held += [flip(one, "aux", bits) for one in held]
        order += [at ^ bits for at in order]
        bits //= 2
        held = [after(one, *others) for one in held]
    return [held[order.index(at)] for at in range(len(held))]


def in_hbm(*operands):
    return [pltpu.with_memory_space_constraint(operand, pltpu.HBM) for operand in operands]


def exchanged_inputs(integrals, pair_list, coef, metric, occ_slot):
    pairs_dev = pair_list.shape[0]
    shell_count = lax.axis_size("shell")
    aux_count = lax.axis_size("aux")
    group = shell_count // 2
    occ_local = coef.shape[1] // (shell_count * aux_count)
    block_count = coef.shape[0] // BS * shell_count
    rows = group * occ_local
    piece_rows = pairs_dev * aux_count * occ_local
    vmem = pl.BlockSpec(memory_space=pltpu.VMEM)
    hbm = pl.BlockSpec(memory_space=pltpu.HBM)
    params = pltpu.CompilerParams(vmem_limit_bytes=40 * 2**20)

    blocks = integrals.reshape(pairs_dev, BS, BS)
    far_block = flip(blocks, "shell", group)
    near_coef, sent_coef = pl.pallas_call(
        functools.partial(pick_kernel, group, occ_local, aux_count),
        out_shape=[jax.ShapeDtypeStruct((rows + 16, pairs_dev * BS), jnp.bfloat16)] * 2,
        in_specs=[hbm] * 3,
        out_specs=[vmem] * 2,
        scratch_shapes=[
            pltpu.SMEM(pair_list.shape, jnp.int32),
            pltpu.VMEM((1, occ_slot.shape[0]), jnp.int32),
            pltpu.VMEM(coef.shape, jnp.bfloat16),
            pltpu.SemaphoreType.DMA((3,)),
        ],
        compiler_params=params,
        name="pick",
    )(*in_hbm(pair_list, occ_slot.reshape(1, -1), coef))
    near_blocks = [blocks] + [flip(blocks, "aux", j) for j in range(1, aux_count)]
    far_coef = flip(sent_coef, "shell", group)

    def transformed(name, coefs, quad):
        pieces = pl.pallas_call(
            functools.partial(block_kernel, aux_count),
            out_shape=[jax.ShapeDtypeStruct((piece_rows + 16, BS), jnp.bfloat16)] * group,
            in_specs=[vmem] * (1 + aux_count),
            out_specs=[vmem] * group,
            compiler_params=params,
            name=name,
        )(coefs, *quad)
        return pieces

    def relayed(pieces):
        return [pieces[0]] + [flip(pieces[f], "shell", f) for f in range(1, group)]

    near = transformed("near_blocks", near_coef, near_blocks)
    far_block = after(far_block, near[0])
    near = relayed(near)
    far_blocks = shared(far_block, far_coef, *near[1:3])
    far = relayed(transformed("far_blocks", after(far_coef, *near), far_blocks))
    return pl.pallas_call(
        functools.partial(collect_kernel, pairs_dev),
        out_shape=jax.ShapeDtypeStruct(
            (occ_local, aux_count, block_count * BS), jnp.bfloat16
        ),
        in_specs=[hbm] + [vmem] * (2 * group),
        out_specs=vmem,
        scratch_shapes=[
            pltpu.VMEM((block_count, occ_local * aux_count, BS), jnp.float32),
            pltpu.VMEM(metric.shape, jnp.bfloat16),
            pltpu.VMEM((2 * group, BS), jnp.int32),
            pltpu.SMEM((2 * group, BS), jnp.int32),
            pltpu.SemaphoreType.DMA((2,)),
        ],
        compiler_params=params,
        name="collect",
    )(*in_hbm(metric), *near, *far)


def per_device(integrals, pair_list, coef, metric, occ_slot):
    shell_count, aux_count = lax.axis_size("shell"), lax.axis_size("aux")
    occ_local = coef.shape[1] // (shell_count * aux_count)
    if occ_local % 16 or shell_count & (shell_count - 1) or aux_count & (aux_count - 1):
        return relayed_half_blocks(integrals, pair_list, coef, metric, occ_slot)
    return exchanged_inputs(integrals, pair_list, coef, metric, occ_slot)


def solution(mesh):
    placed = (P("shell", None, "aux", None), P("shell", None), P("shell", None), P(), P())
    return jax.shard_map(
        per_device,
        mesh=mesh,
        in_specs=placed,
        out_specs=P(("shell", "aux"), None, None),
        check_vma=False,
    )
```

```python
import functools

import jax
import jax.numpy as jnp
from jax import lax
from jax.experimental import pallas as pl
from jax.experimental.pallas import tpu as pltpu
from jax.sharding import Mesh, PartitionSpec as P

BS = 128


def relayed_half_blocks(integrals, pair_list, coef, metric, occ_slot):
    pairs_dev = pair_list.shape[0]
    rows_local = coef.shape[0]
    occ_count = coef.shape[1]
    blocks_dev = rows_local // BS
    shell_count = lax.axis_size("shell")
    block_count = blocks_dev * shell_count
    slot_count = occ_slot.shape[0]
    aux_dev = integrals.shape[2]
    inverse = (
        jnp.zeros((slot_count,), jnp.int32)
        .at[occ_slot]
        .set(jnp.arange(slot_count, dtype=jnp.int32))
    )
    ordered = jnp.take(
        coef.reshape(rows_local, slot_count, occ_count // slot_count), inverse, axis=1
    )
    ordered = ordered.reshape(rows_local, occ_count)

    def one_slot(item):
        int_block, column_index = item
        start = column_index % blocks_dev * BS
        column = lax.dynamic_slice_in_dim(ordered, start, BS, 0)
        product = lax.dot_general(
            column,
            int_block.reshape(BS, aux_dev * BS),
            (((0,), (0,)), ((), ())),
            preferred_element_type=jnp.float32,
        )
        return product.astype(jnp.bfloat16)

    half_blocks = lax.map(one_slot, (integrals, pair_list[:, 1]))
    half_blocks = half_blocks.reshape(pairs_dev, occ_count, aux_dev, BS)
    listing = lax.all_gather(pair_list, "shell", axis=0, tiled=True)
    targets = jnp.arange(block_count, dtype=jnp.int32)[:, None]
    selector = ((listing[:, 0][None, :] == targets) & (listing[:, 2][None, :] == 1)).astype(
        jnp.bfloat16
    )
    relayed = lax.all_to_all(
        lax.all_to_all(half_blocks, "shell", split_axis=1, concat_axis=0, tiled=True),
        "aux",
        split_axis=1,
        concat_axis=2,
        tiled=True,
    )
    summed = jnp.dot(
        selector, relayed.reshape(relayed.shape[0], -1), preferred_element_type=jnp.float32
    )
    blocks = summed.astype(jnp.bfloat16).reshape((block_count,) + relayed.shape[1:])
    result = jnp.einsum("qp,bipm->iqbm", metric, blocks, preferred_element_type=jnp.float32)
    return result.reshape(result.shape[0], result.shape[1], block_count * BS).astype(jnp.bfloat16)


def targets_of(slot_row, block_total, occ_count):
    width = occ_count // block_total
    spread = (
        lax.broadcasted_iota(jnp.int32, (block_total, occ_count), 1) // width
        == lax.broadcasted_iota(jnp.int32, (block_total, occ_count), 0)
    ).astype(jnp.bfloat16)
    slots = jnp.broadcast_to(slot_row, (8, block_total)).astype(jnp.float32)
    target = jnp.dot(slots.astype(jnp.bfloat16), spread, preferred_element_type=jnp.float32)
    return target.astype(jnp.int32)[:1] * width + (
        lax.broadcasted_iota(jnp.int32, (1, occ_count), 1) % width
    )


def load_all(copies, sems):
    loads = [
        pltpu.make_async_copy(source, target, sems.at[at])
        for at, (source, target) in enumerate(copies)
    ]
    for load in loads:
        load.start()
    return loads


def half_kernel(
    occ_local,
    aux_count,
    pairs_in,
    slot_in,
    coef_in,
    blocks_in,
    near,
    far_coef,
    pairs,
    slot_row,
    coef,
    blocks,
    sems,
):
    loads = load_all(
        ((slot_in, slot_row), (pairs_in, pairs), (coef_in, coef), (blocks_in, blocks)), sems
    )
    pairs_dev = pairs.shape[0]
    blocks_dev = coef.shape[0] // BS
    occ_count = coef.shape[1]
    devices = near.shape[0]
    near_rows = devices * occ_local
    far_rows = far_coef.shape[0] - 16
    half, mine = lax.axis_index("half"), lax.axis_index("aux")

    near_wanted = half * near_rows + lax.broadcasted_iota(jnp.int32, (near_rows, 1), 0)
    row = lax.broadcasted_iota(jnp.int32, (far_rows, 1), 0)
    far_wanted = (1 - half) * near_rows + (
        (row // occ_local * aux_count + mine) * occ_local + row % occ_local
    )
    loads[0].wait()
    target = targets_of(slot_row[...], slot_row.shape[1], occ_count)
    near_pick = (near_wanted == target).astype(jnp.bfloat16)
    far_pick = (far_wanted == target).astype(jnp.bfloat16)
    for load in loads[1:]:
        load.wait()
    lane = lax.broadcasted_iota(jnp.int32, (1, BS), 1)
    code = jnp.zeros((1, BS), jnp.int32)
    rows, live = [], []
    for k in range(pairs_dev):
        code = jnp.where(lane == k, pairs[k, 0] % 128, code)
        code = jnp.where(lane == pairs_dev + k, pairs[k, 0] // 128, code)
        start = pl.multiple_of(lax.rem(pairs[k, 1], blocks_dev) * BS, BS)
        rows.append(coef[pl.ds(start, BS), :])
        live.append((pairs[k, 2] == 1).astype(jnp.bfloat16))
    code = jnp.broadcast_to(code.astype(jnp.float32), (16, BS)).astype(jnp.bfloat16)
    rows = jnp.concatenate(rows, axis=0)
    contract = (((1,), (1,)), ((), ()))
    ordered = lax.dot_general(far_pick, rows, contract, preferred_element_type=jnp.float32)
    ordered = ordered.astype(jnp.bfloat16)
    for k in range(pairs_dev):
        far_coef[:far_rows, k * BS : (k + 1) * BS] = ordered[:, k * BS : (k + 1) * BS] * live[k]
        far_coef[far_rows:, k * BS : (k + 1) * BS] = code
    ordered = lax.dot_general(near_pick, rows, contract, preferred_element_type=jnp.float32)
    ordered = ordered.astype(jnp.bfloat16)
    for k in range(pairs_dev):
        block = jnp.dot(
            ordered[:, k * BS : (k + 1) * BS], blocks[k], preferred_element_type=jnp.float32
        )
        near[:, k * occ_local : (k + 1) * occ_local, :] = (
            block.astype(jnp.bfloat16) * live[k]
        ).reshape(devices, occ_local, BS)
    near[:, pairs_dev * occ_local :, :] = jnp.broadcast_to(code[None], (devices, 16, BS))


def far_kernel(aux_count, coefs, *refs):
    *blocks, out = refs
    pairs_dev = blocks[0].shape[0]
    rows = coefs.shape[0] - 16
    places = out.shape[0]
    occ_local = rows // places
    mine = lax.axis_index("aux")
    for k in range(pairs_dev):
        left = coefs[:rows, k * BS : (k + 1) * BS]
        for j in range(0, aux_count, 2):
            right = jnp.concatenate([blocks[j][k], blocks[j + 1][k]], axis=1)
            half = jnp.dot(left, right, preferred_element_type=jnp.float32).astype(jnp.bfloat16)
            for side in range(2):
                at = k * aux_count + jnp.bitwise_xor(mine, j + side)
                start = pl.multiple_of(at * occ_local, occ_local)
                out[:, pl.ds(start, occ_local), :] = half[
                    :, side * BS : (side + 1) * BS
                ].reshape(places, occ_local, BS)
    out[:, pairs_dev * aux_count * occ_local :, :] = jnp.broadcast_to(
        coefs[rows:, :BS][None], (places, 16, BS)
    )


def load_codes(received, step, codes_v, codes, sem):
    tile = received.shape[1] - 16
    for at in range(received.shape[0] // step):
        digits = received[at * step, tile:, :].astype(jnp.float32).astype(jnp.int32)
        codes_v[at : at + 1, :] = digits[:1]
    load = pltpu.make_async_copy(codes_v, codes, sem)
    load.start()
    return load


def near_sum_kernel(aux_count, received, total, codes_v, codes, sem):
    load = load_codes(received, aux_count, codes_v, codes, sem)
    occ_local = total.shape[1] // aux_count
    pairs_dev = (received.shape[1] - 16) // occ_local
    total[...] = jnp.zeros_like(total)
    load.wait()
    for at in range(received.shape[0] // aux_count):
        for k in range(pairs_dev):
            r = codes[at, k] + 128 * codes[at, pairs_dev + k]
            for p in range(aux_count):
                part = received[at * aux_count + p, k * occ_local : (k + 1) * occ_local, :]
                total[r, p * occ_local : (p + 1) * occ_local, :] += part.astype(jnp.float32)


def collect_kernel(metric_in, total_in, received, out, total, metric, codes_v, codes, sems):
    (metric_load,) = load_all(((metric_in, metric),), sems)
    load = load_codes(received, 1, codes_v, codes, sems.at[1])
    occ_local, aux_count = out.shape[:2]
    rows = occ_local * aux_count
    pairs_dev = (received.shape[1] - 16) // rows
    load.wait()
    for at in range(received.shape[0]):
        for k in range(pairs_dev):
            r = codes[at, k] + 128 * codes[at, pairs_dev + k]
            total[r] += received[at, k * rows : (k + 1) * rows, :].astype(jnp.float32)
    metric_load.wait()

    row = lax.broadcasted_iota(jnp.int32, (rows, rows), 0)
    column = lax.broadcasted_iota(jnp.int32, (rows, rows), 1)
    left = (
        lax.broadcasted_iota(jnp.int32, (rows, aux_count), 0) % aux_count
        == lax.broadcasted_iota(jnp.int32, (rows, aux_count), 1)
    ).astype(jnp.bfloat16)
    right = (
        lax.broadcasted_iota(jnp.int32, (aux_count, rows), 1) // occ_local
        == lax.broadcasted_iota(jnp.int32, (aux_count, rows), 0)
    ).astype(jnp.bfloat16)
    factor = jnp.dot(left, metric[...], preferred_element_type=jnp.float32).astype(jnp.bfloat16)
    factor = jnp.dot(factor, right, preferred_element_type=jnp.float32)
    mix = jnp.where(row // aux_count == column % occ_local, factor, 0.0).astype(jnp.bfloat16)
    for r in range(0, total.shape[0], 2):
        summed = jnp.concatenate([total[r], total[r + 1]], axis=1).astype(jnp.bfloat16)
        mixed = jnp.dot(mix, summed, preferred_element_type=jnp.float32)
        out[:, :, r * BS : (r + 2) * BS] = mixed.reshape(
            occ_local, aux_count, 2 * BS
        ).astype(jnp.bfloat16)


def flip(value, axis, bits):
    count = lax.axis_size(axis)
    return lax.ppermute(value, axis, [(at, at ^ bits) for at in range(count)])


def after(value, *others):
    return lax.optimization_barrier((value, *others))[0]


def shared(block):
    held, order, bits = [block], [0], lax.axis_size("aux") // 2
    while bits:
        held += [flip(one, "aux", bits) for one in held]
        order += [at ^ bits for at in order]
        bits //= 2
    return [held[order.index(at)] for at in range(len(held))]


def in_hbm(*operands):
    return [pltpu.with_memory_space_constraint(operand, pltpu.HBM) for operand in operands]


def crossed_inputs(integrals, pair_list, coef, metric, occ_slot):
    pairs_dev = pair_list.shape[0]
    places = lax.axis_size("place")
    aux_count = lax.axis_size("aux")
    devices = places * aux_count
    occ_local = coef.shape[1] // (2 * devices)
    block_count = coef.shape[0] // BS * 2 * places
    rows = occ_local * aux_count
    vmem = pl.BlockSpec(memory_space=pltpu.VMEM)
    hbm = pl.BlockSpec(memory_space=pltpu.HBM)
    params = pltpu.CompilerParams(vmem_limit_bytes=40 * 2**20)

    blocks = integrals.reshape(pairs_dev, BS, BS)
    far_block = flip(blocks, "half", 1)
    near, sent_coef = pl.pallas_call(
        functools.partial(half_kernel, occ_local, aux_count),
        out_shape=[
            jax.ShapeDtypeStruct((devices, pairs_dev * occ_local + 16, BS), jnp.bfloat16),
            jax.ShapeDtypeStruct((places * occ_local + 16, pairs_dev * BS), jnp.bfloat16),
        ],
        in_specs=[hbm] * 4,
        out_specs=[vmem] * 2,
        scratch_shapes=[
            pltpu.SMEM(pair_list.shape, jnp.int32),
            pltpu.VMEM((1, occ_slot.shape[0]), jnp.int32),
            pltpu.VMEM(coef.shape, jnp.bfloat16),
            pltpu.VMEM(blocks.shape, jnp.bfloat16),
            pltpu.SemaphoreType.DMA((4,)),
        ],
        compiler_params=params,
        name="near_blocks",
    )(*in_hbm(pair_list, occ_slot.reshape(1, -1), coef, blocks))
    near = lax.all_to_all(near, ("place", "aux"), split_axis=0, concat_axis=0)
    far_block = after(far_block, sent_coef)
    far_coef = flip(after(sent_coef, far_block), "half", 1)
    far_blocks = shared(far_block)

    total_shape = jax.ShapeDtypeStruct((block_count, rows, BS), jnp.float32)
    total = pl.pallas_call(
        functools.partial(near_sum_kernel, aux_count),
        out_shape=total_shape,
        in_specs=[vmem],
        out_specs=vmem,
        scratch_shapes=[
            pltpu.VMEM((places, BS), jnp.int32),
            pltpu.SMEM((places, BS), jnp.int32),
            pltpu.SemaphoreType.DMA,
        ],
        compiler_params=params,
        name="near_sum",
    )(near)
    far = pl.pallas_call(
        functools.partial(far_kernel, aux_count),
        out_shape=jax.ShapeDtypeStruct((places, pairs_dev * rows + 16, BS), jnp.bfloat16),
        in_specs=[vmem] * (1 + aux_count),
        out_specs=vmem,
        compiler_params=params,
        name="far_blocks",
    )(far_coef, *far_blocks)
    far = lax.all_to_all(far, "place", split_axis=0, concat_axis=0)
    return pl.pallas_call(
        collect_kernel,
        out_shape=[
            jax.ShapeDtypeStruct((occ_local, aux_count, block_count * BS), jnp.bfloat16),
            total_shape,
        ],
        in_specs=[hbm, vmem, vmem],
        out_specs=[vmem, vmem],
        input_output_aliases={1: 1},
        scratch_shapes=[
            pltpu.VMEM(metric.shape, jnp.bfloat16),
            pltpu.VMEM((places, BS), jnp.int32),
            pltpu.SMEM((places, BS), jnp.int32),
            pltpu.SemaphoreType.DMA((2,)),
        ],
        compiler_params=params,
        name="collect",
    )(*in_hbm(metric), total, far)[0]


def solution(mesh):
    shell_count, aux_count = mesh.shape["shell"], mesh.shape["aux"]
    halves = Mesh(
        mesh.devices.reshape(2, shell_count // 2, aux_count), ("half", "place", "aux")
    )

    def whole(*args):
        occ_local = args[2].shape[1] // (shell_count * aux_count)
        if occ_local % 16 or aux_count & (aux_count - 1):
            program, grid, shell = relayed_half_blocks, mesh, "shell"
        else:
            program, grid, shell = crossed_inputs, halves, ("half", "place")
        owners = ("shell", "aux") if grid is mesh else ("half", "place", "aux")
        return jax.shard_map(
            program,
            mesh=grid,
            in_specs=(P(shell, None, "aux", None), P(shell, None), P(shell, None), P(), P()),
            out_specs=P(owners, None, None),
            check_vma=False,
        )(*args)

    return whole
```

```python
import functools

import jax
import jax.numpy as jnp
from jax import lax
from jax.experimental import pallas as pl
from jax.experimental.pallas import tpu as pltpu
from jax.sharding import PartitionSpec as P

BS = 128


def relayed_half_blocks(integrals, pair_list, coef, metric, occ_slot):
    pairs_dev = pair_list.shape[0]
    rows_local = coef.shape[0]
    occ_count = coef.shape[1]
    blocks_dev = rows_local // BS
    shell_count = lax.axis_size("shell")
    block_count = blocks_dev * shell_count
    slot_count = occ_slot.shape[0]
    aux_dev = integrals.shape[2]
    inverse = (
        jnp.zeros((slot_count,), jnp.int32)
        .at[occ_slot]
        .set(jnp.arange(slot_count, dtype=jnp.int32))
    )
    ordered = jnp.take(
        coef.reshape(rows_local, slot_count, occ_count // slot_count), inverse, axis=1
    )
    ordered = ordered.reshape(rows_local, occ_count)

    def one_slot(item):
        int_block, column_index = item
        start = column_index % blocks_dev * BS
        column = lax.dynamic_slice_in_dim(ordered, start, BS, 0)
        product = lax.dot_general(
            column,
            int_block.reshape(BS, aux_dev * BS),
            (((0,), (0,)), ((), ())),
            preferred_element_type=jnp.float32,
        )
        return product.astype(jnp.bfloat16)

    half_blocks = lax.map(one_slot, (integrals, pair_list[:, 1]))
    half_blocks = half_blocks.reshape(pairs_dev, occ_count, aux_dev, BS)
    listing = lax.all_gather(pair_list, "shell", axis=0, tiled=True)
    targets = jnp.arange(block_count, dtype=jnp.int32)[:, None]
    selector = ((listing[:, 0][None, :] == targets) & (listing[:, 2][None, :] == 1)).astype(
        jnp.bfloat16
    )
    relayed = lax.all_to_all(
        lax.all_to_all(half_blocks, "shell", split_axis=1, concat_axis=0, tiled=True),
        "aux",
        split_axis=1,
        concat_axis=2,
        tiled=True,
    )
    summed = jnp.dot(
        selector, relayed.reshape(relayed.shape[0], -1), preferred_element_type=jnp.float32
    )
    blocks = summed.astype(jnp.bfloat16).reshape((block_count,) + relayed.shape[1:])
    result = jnp.einsum("qp,bipm->iqbm", metric, blocks, preferred_element_type=jnp.float32)
    return result.reshape(result.shape[0], result.shape[1], block_count * BS).astype(jnp.bfloat16)


def targets_of(slot_row, block_total, occ_count):
    width = occ_count // block_total
    spread = (
        lax.broadcasted_iota(jnp.int32, (block_total, occ_count), 1) // width
        == lax.broadcasted_iota(jnp.int32, (block_total, occ_count), 0)
    ).astype(jnp.bfloat16)
    slots = jnp.broadcast_to(slot_row, (8, block_total)).astype(jnp.float32)
    target = jnp.dot(slots.astype(jnp.bfloat16), spread, preferred_element_type=jnp.float32)
    return target.astype(jnp.int32)[:1] * width + (
        lax.broadcasted_iota(jnp.int32, (1, occ_count), 1) % width
    )


def pick_kernel(
    flips,
    occ_local,
    aux_count,
    pairs_in,
    slot_in,
    coef_in,
    blocks_in,
    *refs,
):
    *outs, blocks, pairs, slot_row, coef, sems = refs
    pairs_dev = pairs.shape[0]
    blocks_dev = coef.shape[0] // BS
    occ_count = coef.shape[1]
    loads = [
        pltpu.make_async_copy(source, target, sems.at[at])
        for at, (source, target) in enumerate(
            ((slot_in, slot_row), (pairs_in, pairs), (coef_in, coef), (blocks_in, blocks))
        )
    ]
    for load in loads:
        load.start()
    me = lax.axis_index("shell")
    mine = lax.axis_index("aux")
    every = sum(flips, [])
    row = lax.broadcasted_iota(jnp.int32, (len(every) * occ_local, 1), 0)
    owner = sum(jnp.where(row // occ_local == at, f, 0) for at, f in enumerate(every))
    wanted = (jnp.bitwise_xor(owner, me) * aux_count + mine) * occ_local + row % occ_local
    loads[0].wait()
    target = targets_of(slot_row[...], slot_row.shape[1], occ_count)
    pick = (wanted == target).astype(jnp.bfloat16)
    for load in loads[1:]:
        load.wait()
    lane = lax.broadcasted_iota(jnp.int32, (1, BS), 1)
    code = jnp.zeros((1, BS), jnp.int32)
    for k in range(pairs_dev):
        code = jnp.where(lane == k, pairs[k, 0] % 128, code)
        code = jnp.where(lane == pairs_dev + k, pairs[k, 0] // 128, code)
    code = jnp.broadcast_to(code.astype(jnp.float32), (16, BS)).astype(jnp.bfloat16)
    for k in range(pairs_dev):
        start = pl.multiple_of(lax.rem(pairs[k, 1], blocks_dev) * BS, BS)
        live = (pairs[k, 2] == 1).astype(jnp.float32)
        piece = lax.dot_general(
            pick,
            coef[pl.ds(start, BS), :],
            (((1,), (1,)), ((), ())),
            preferred_element_type=jnp.float32,
        )
        piece = (piece * live).astype(jnp.bfloat16)
        first = 0
        for out in outs:
            rows = out.shape[0] - 16
            out[:rows, k * BS : (k + 1) * BS] = piece[first : first + rows]
            out[rows:, k * BS : (k + 1) * BS] = code
            first += rows


def block_kernel(aux_count, coefs, *refs):
    blocks, pieces = refs[:aux_count], refs[aux_count:]
    pairs_dev = blocks[0].shape[0]
    rows = coefs.shape[0] - 16
    occ_local = rows // len(pieces)
    mine = lax.axis_index("aux")
    for k in range(pairs_dev):
        left = coefs[:rows, k * BS : (k + 1) * BS]
        for j in range(0, aux_count, 2):
            right = jnp.concatenate([blocks[j][k], blocks[j + 1][k]], axis=1)
            half = jnp.dot(left, right, preferred_element_type=jnp.float32).astype(jnp.bfloat16)
            for side in range(2):
                at = k * aux_count + jnp.bitwise_xor(mine, j + side)
                start = pl.multiple_of(at * occ_local, occ_local)
                for f, piece in enumerate(pieces):
                    piece[pl.ds(start, occ_local), :] = half[
                        f * occ_local : (f + 1) * occ_local, side * BS : (side + 1) * BS
                    ]
    for piece in pieces:
        piece[pairs_dev * aux_count * occ_local :, :] = coefs[rows:, :BS]


def add_received(total, received, codes_v, codes, sem, meanwhile):
    rows = total.shape[1]
    pairs_dev = (received[0].shape[0] - 16) // rows
    for at, piece in enumerate(received):
        digits = piece[pairs_dev * rows :, :].astype(jnp.float32).astype(jnp.int32)
        codes_v[at : at + 1, :] = digits[:1]
    load = pltpu.make_async_copy(codes_v, codes, sem)
    load.start()
    meanwhile()
    load.wait()
    for at, piece in enumerate(received):
        for k in range(pairs_dev):
            r = codes[at, k] + 128 * codes[at, pairs_dev + k]
            total[r] += piece[k * rows : (k + 1) * rows, :].astype(jnp.float32)


def near_sum_kernel(*refs):
    *received, total, codes_v, codes, sem = refs

    def clear():
        total[...] = jnp.zeros_like(total)

    add_received(total, received, codes_v, codes, sem, clear)


def collect_kernel(metric_in, total_in, *refs):
    *received, out, total, metric, codes_v, codes, sem, metric_sem = refs
    occ_local, aux_count = out.shape[:2]
    rows = occ_local * aux_count
    load = pltpu.make_async_copy(metric_in, metric, metric_sem)
    load.start()
    add_received(total, received, codes_v, codes, sem, load.wait)

    row = lax.broadcasted_iota(jnp.int32, (rows, rows), 0)
    column = lax.broadcasted_iota(jnp.int32, (rows, rows), 1)
    left = (
        lax.broadcasted_iota(jnp.int32, (rows, aux_count), 0) % aux_count
        == lax.broadcasted_iota(jnp.int32, (rows, aux_count), 1)
    ).astype(jnp.bfloat16)
    right = (
        lax.broadcasted_iota(jnp.int32, (aux_count, rows), 1) // occ_local
        == lax.broadcasted_iota(jnp.int32, (aux_count, rows), 0)
    ).astype(jnp.bfloat16)
    factor = jnp.dot(left, metric[...], preferred_element_type=jnp.float32).astype(jnp.bfloat16)
    factor = jnp.dot(factor, right, preferred_element_type=jnp.float32)
    mix = jnp.where(row // aux_count == column % occ_local, factor, 0.0).astype(jnp.bfloat16)
    for r in range(0, total.shape[0], 2):
        summed = jnp.concatenate([total[r], total[r + 1]], axis=1).astype(jnp.bfloat16)
        mixed = jnp.dot(mix, summed, preferred_element_type=jnp.float32)
        out[:, :, r * BS : (r + 2) * BS] = mixed.reshape(
            occ_local, aux_count, 2 * BS
        ).astype(jnp.bfloat16)


def flip(value, axis, bits):
    count = lax.axis_size(axis)
    return lax.ppermute(value, axis, [(at, at ^ bits) for at in range(count)])


def after(value, *others):
    return lax.optimization_barrier((value, *others))[0]


def shared(block, *others):
    held, order, bits = [block], [0], lax.axis_size("aux") // 2
    while bits:
        held += [flip(one, "aux", bits) for one in held]
        order += [at ^ bits for at in order]
        bits //= 2
        if others:
            held = [after(one, *others) for one in held]
    return [held[order.index(at)] for at in range(len(held))]


def in_hbm(*operands):
    return [pltpu.with_memory_space_constraint(operand, pltpu.HBM) for operand in operands]


def exchanged_inputs(integrals, pair_list, coef, metric, occ_slot):
    pairs_dev = pair_list.shape[0]
    shell_count = lax.axis_size("shell")
    aux_count = lax.axis_size("aux")
    group = shell_count // 2
    occ_local = coef.shape[1] // (shell_count * aux_count)
    block_count = coef.shape[0] // BS * shell_count
    rows = occ_local * aux_count
    piece = jax.ShapeDtypeStruct((pairs_dev * rows + 16, BS), jnp.bfloat16)
    vmem = pl.BlockSpec(memory_space=pltpu.VMEM)
    hbm = pl.BlockSpec(memory_space=pltpu.HBM)
    params = pltpu.CompilerParams(vmem_limit_bytes=40 * 2**20)

    def transformed(name, coefs, quad, count):
        return pl.pallas_call(
            functools.partial(block_kernel, aux_count),
            out_shape=[piece] * count,
            in_specs=[vmem] * (1 + aux_count),
            out_specs=[vmem] * count,
            compiler_params=params,
            name=name,
        )(coefs, *quad)

    def code_scratch(count):
        return [
            pltpu.VMEM((count, BS), jnp.int32),
            pltpu.SMEM((count, BS), jnp.int32),
            pltpu.SemaphoreType.DMA,
        ]

    blocks = integrals.reshape(pairs_dev, BS, BS)
    far_block = flip(blocks, "shell", group)

    flips = [list(range(group)), list(range(group, shell_count))]
    near_coef, sent_coef, near_block = pl.pallas_call(
        functools.partial(pick_kernel, flips, occ_local, aux_count),
        out_shape=[
            jax.ShapeDtypeStruct((len(f) * occ_local + 16, pairs_dev * BS), jnp.bfloat16)
            for f in flips
        ]
        + [jax.ShapeDtypeStruct(blocks.shape, jnp.bfloat16)],
        in_specs=[hbm] * 4,
        out_specs=[vmem] * (len(flips) + 1),
        scratch_shapes=[
            pltpu.SMEM(pair_list.shape, jnp.int32),
            pltpu.VMEM((1, occ_slot.shape[0]), jnp.int32),
            pltpu.VMEM(coef.shape, jnp.bfloat16),
            pltpu.SemaphoreType.DMA((4,)),
        ],
        compiler_params=params,
        name="pick",
    )(*in_hbm(pair_list, occ_slot.reshape(1, -1), coef, blocks))
    near_blocks = [near_block] + [flip(blocks, "aux", j) for j in range(1, aux_count)]

    near = transformed("near_blocks", near_coef, near_blocks, group)
    far_block = after(far_block, near[0])
    near = [near[0]] + [flip(near[f], "shell", f) for f in range(1, group)]
    far_coef = flip(after(sent_coef, far_block), "shell", group)
    far_blocks = shared(far_block, *near[1:3])
    far = transformed("far_blocks", after(far_coef, *near), far_blocks, group)
    far = [far[0]] + [flip(far[f], "shell", f) for f in range(1, group)]
    total_shape = jax.ShapeDtypeStruct((block_count, rows, BS), jnp.float32)
    total = pl.pallas_call(
        near_sum_kernel,
        out_shape=total_shape,
        in_specs=[vmem] * group,
        out_specs=vmem,
        scratch_shapes=code_scratch(group),
        compiler_params=params,
        name="near_sum",
    )(*(after(one, far[0]) for one in near))
    return pl.pallas_call(
        collect_kernel,
        out_shape=[
            jax.ShapeDtypeStruct((occ_local, aux_count, block_count * BS), jnp.bfloat16),
            total_shape,
        ],
        in_specs=[hbm] + [vmem] * (1 + group),
        out_specs=[vmem, vmem],
        input_output_aliases={1: 1},
        scratch_shapes=[pltpu.VMEM(metric.shape, jnp.bfloat16)]
        + code_scratch(group)
        + [pltpu.SemaphoreType.DMA],
        compiler_params=params,
        name="collect",
    )(*in_hbm(metric), total, *far)[0]


def per_device(integrals, pair_list, coef, metric, occ_slot):
    shell_count, aux_count = lax.axis_size("shell"), lax.axis_size("aux")
    occ_local = coef.shape[1] // (shell_count * aux_count)
    if occ_local % 16 or shell_count & (shell_count - 1) or aux_count & (aux_count - 1):
        return relayed_half_blocks(integrals, pair_list, coef, metric, occ_slot)
    return exchanged_inputs(integrals, pair_list, coef, metric, occ_slot)


def solution(mesh):
    placed = (P("shell", None, "aux", None), P("shell", None), P("shell", None), P(), P())
    return jax.shard_map(
        per_device,
        mesh=mesh,
        in_specs=placed,
        out_specs=P(("shell", "aux"), None, None),
        check_vma=False,
    )
```

```python
import functools

import jax
import jax.numpy as jnp
from jax import lax
from jax.experimental import pallas as pl
from jax.experimental.pallas import tpu as pltpu
from jax.sharding import PartitionSpec as P

BS = 128


def relayed_half_blocks(integrals, pair_list, coef, metric, occ_slot):
    pairs_dev = pair_list.shape[0]
    rows_local = coef.shape[0]
    occ_count = coef.shape[1]
    blocks_dev = rows_local // BS
    shell_count = lax.axis_size("shell")
    block_count = blocks_dev * shell_count
    slot_count = occ_slot.shape[0]
    aux_dev = integrals.shape[2]
    inverse = (
        jnp.zeros((slot_count,), jnp.int32)
        .at[occ_slot]
        .set(jnp.arange(slot_count, dtype=jnp.int32))
    )
    ordered = jnp.take(
        coef.reshape(rows_local, slot_count, occ_count // slot_count), inverse, axis=1
    )
    ordered = ordered.reshape(rows_local, occ_count)

    def one_slot(item):
        int_block, column_index = item
        start = column_index % blocks_dev * BS
        column = lax.dynamic_slice_in_dim(ordered, start, BS, 0)
        product = lax.dot_general(
            column,
            int_block.reshape(BS, aux_dev * BS),
            (((0,), (0,)), ((), ())),
            preferred_element_type=jnp.float32,
        )
        return product.astype(jnp.bfloat16)

    half_blocks = lax.map(one_slot, (integrals, pair_list[:, 1]))
    half_blocks = half_blocks.reshape(pairs_dev, occ_count, aux_dev, BS)
    listing = lax.all_gather(pair_list, "shell", axis=0, tiled=True)
    targets = jnp.arange(block_count, dtype=jnp.int32)[:, None]
    selector = ((listing[:, 0][None, :] == targets) & (listing[:, 2][None, :] == 1)).astype(
        jnp.bfloat16
    )
    relayed = lax.all_to_all(
        lax.all_to_all(half_blocks, "shell", split_axis=1, concat_axis=0, tiled=True),
        "aux",
        split_axis=1,
        concat_axis=2,
        tiled=True,
    )
    summed = jnp.dot(
        selector, relayed.reshape(relayed.shape[0], -1), preferred_element_type=jnp.float32
    )
    blocks = summed.astype(jnp.bfloat16).reshape((block_count,) + relayed.shape[1:])
    result = jnp.einsum("qp,bipm->iqbm", metric, blocks, preferred_element_type=jnp.float32)
    return result.reshape(result.shape[0], result.shape[1], block_count * BS).astype(jnp.bfloat16)


def targets_of(slot_row, block_total, occ_count):
    width = occ_count // block_total
    spread = (
        lax.broadcasted_iota(jnp.int32, (block_total, occ_count), 1) // width
        == lax.broadcasted_iota(jnp.int32, (block_total, occ_count), 0)
    ).astype(jnp.bfloat16)
    slots = jnp.broadcast_to(slot_row, (8, block_total)).astype(jnp.float32)
    target = jnp.dot(slots.astype(jnp.bfloat16), spread, preferred_element_type=jnp.float32)
    return target.astype(jnp.int32)[:1] * width + (
        lax.broadcasted_iota(jnp.int32, (1, occ_count), 1) % width
    )


def pick_kernel(
    flips,
    occ_local,
    aux_count,
    pairs_in,
    slot_in,
    coef_in,
    blocks_in,
    *refs,
):
    *outs, blocks, pairs, slot_row, coef, sems = refs
    pairs_dev = pairs.shape[0]
    blocks_dev = coef.shape[0] // BS
    occ_count = coef.shape[1]
    loads = [
        pltpu.make_async_copy(source, target, sems.at[at])
        for at, (source, target) in enumerate(
            ((slot_in, slot_row), (pairs_in, pairs), (coef_in, coef), (blocks_in, blocks))
        )
    ]
    for load in loads:
        load.start()
    me = lax.axis_index("shell")
    mine = lax.axis_index("aux")
    every = sum(flips, [])
    row = lax.broadcasted_iota(jnp.int32, (len(every) * occ_local, 1), 0)
    owner = sum(jnp.where(row // occ_local == at, f, 0) for at, f in enumerate(every))
    wanted = (jnp.bitwise_xor(owner, me) * aux_count + mine) * occ_local + row % occ_local
    loads[0].wait()
    target = targets_of(slot_row[...], slot_row.shape[1], occ_count)
    pick = (wanted == target).astype(jnp.bfloat16)
    for load in loads[1:]:
        load.wait()
    lane = lax.broadcasted_iota(jnp.int32, (1, BS), 1)
    code = jnp.zeros((1, BS), jnp.int32)
    for k in range(pairs_dev):
        code = jnp.where(lane == k, pairs[k, 0] % 128, code)
        code = jnp.where(lane == pairs_dev + k, pairs[k, 0] // 128, code)
    code = jnp.broadcast_to(code.astype(jnp.float32), (16, BS)).astype(jnp.bfloat16)
    for k in range(pairs_dev):
        start = pl.multiple_of(lax.rem(pairs[k, 1], blocks_dev) * BS, BS)
        live = (pairs[k, 2] == 1).astype(jnp.float32)
        piece = lax.dot_general(
            pick,
            coef[pl.ds(start, BS), :],
            (((1,), (1,)), ((), ())),
            preferred_element_type=jnp.float32,
        )
        piece = (piece * live).astype(jnp.bfloat16)
        first = 0
        for out in outs:
            rows = out.shape[0] - 16
            out[:rows, k * BS : (k + 1) * BS] = piece[first : first + rows]
            out[rows:, k * BS : (k + 1) * BS] = code
            first += rows


def block_kernel(aux_count, coefs, *refs):
    blocks, pieces = refs[:aux_count], refs[aux_count:]
    pairs_dev = blocks[0].shape[0]
    rows = coefs.shape[0] - 16
    occ_local = rows // len(pieces)
    mine = lax.axis_index("aux")
    for k in range(pairs_dev):
        left = coefs[:rows, k * BS : (k + 1) * BS]
        for j in range(0, aux_count, 2):
            right = jnp.concatenate([blocks[j][k], blocks[j + 1][k]], axis=1)
            half = jnp.dot(left, right, preferred_element_type=jnp.float32).astype(jnp.bfloat16)
            for side in range(2):
                at = k * aux_count + jnp.bitwise_xor(mine, j + side)
                start = pl.multiple_of(at * occ_local, occ_local)
                for f, piece in enumerate(pieces):
                    piece[pl.ds(start, occ_local), :] = half[
                        f * occ_local : (f + 1) * occ_local, side * BS : (side + 1) * BS
                    ]
    for piece in pieces:
        piece[pairs_dev * aux_count * occ_local :, :] = coefs[rows:, :BS]


def add_received(total, received, codes_v, codes, sem, meanwhile):
    rows = total.shape[1]
    pairs_dev = (received[0].shape[0] - 16) // rows
    for at, piece in enumerate(received):
        digits = piece[pairs_dev * rows :, :].astype(jnp.float32).astype(jnp.int32)
        codes_v[at : at + 1, :] = digits[:1]
    load = pltpu.make_async_copy(codes_v, codes, sem)
    load.start()
    meanwhile()
    load.wait()
    for at, piece in enumerate(received):
        for k in range(pairs_dev):
            r = codes[at, k] + 128 * codes[at, pairs_dev + k]
            total[r] += piece[k * rows : (k + 1) * rows, :].astype(jnp.float32)


def near_sum_kernel(*refs):
    *received, total, codes_v, codes, sem = refs

    def clear():
        total[...] = jnp.zeros_like(total)

    add_received(total, received, codes_v, codes, sem, clear)


def collect_kernel(metric_in, total_in, *refs):
    *received, out, total, metric, codes_v, codes, sem, metric_sem = refs
    occ_local, aux_count = out.shape[:2]
    rows = occ_local * aux_count
    load = pltpu.make_async_copy(metric_in, metric, metric_sem)
    load.start()
    add_received(total, received, codes_v, codes, sem, load.wait)

    row = lax.broadcasted_iota(jnp.int32, (rows, rows), 0)
    column = lax.broadcasted_iota(jnp.int32, (rows, rows), 1)
    left = (
        lax.broadcasted_iota(jnp.int32, (rows, aux_count), 0) % aux_count
        == lax.broadcasted_iota(jnp.int32, (rows, aux_count), 1)
    ).astype(jnp.bfloat16)
    right = (
        lax.broadcasted_iota(jnp.int32, (aux_count, rows), 1) // occ_local
        == lax.broadcasted_iota(jnp.int32, (aux_count, rows), 0)
    ).astype(jnp.bfloat16)
    factor = jnp.dot(left, metric[...], preferred_element_type=jnp.float32).astype(jnp.bfloat16)
    factor = jnp.dot(factor, right, preferred_element_type=jnp.float32)
    mix = jnp.where(row // aux_count == column % occ_local, factor, 0.0).astype(jnp.bfloat16)
    for r in range(0, total.shape[0], 2):
        summed = jnp.concatenate([total[r], total[r + 1]], axis=1).astype(jnp.bfloat16)
        mixed = jnp.dot(mix, summed, preferred_element_type=jnp.float32)
        out[:, :, r * BS : (r + 2) * BS] = mixed.reshape(
            occ_local, aux_count, 2 * BS
        ).astype(jnp.bfloat16)


def flip(value, axis, bits):
    count = lax.axis_size(axis)
    return lax.ppermute(value, axis, [(at, at ^ bits) for at in range(count)])


def after(value, *others):
    return lax.optimization_barrier((value, *others))[0]


def shared(block, *others):
    held, order, bits = [block], [0], lax.axis_size("aux") // 2
    while bits:
        held += [flip(one, "aux", bits) for one in held]
        order += [at ^ bits for at in order]
        bits //= 2
        if others:
            held = [after(one, *others) for one in held]
    return [held[order.index(at)] for at in range(len(held))]


def in_hbm(*operands):
    return [pltpu.with_memory_space_constraint(operand, pltpu.HBM) for operand in operands]


def exchanged_inputs(integrals, pair_list, coef, metric, occ_slot):
    pairs_dev = pair_list.shape[0]
    shell_count = lax.axis_size("shell")
    aux_count = lax.axis_size("aux")
    group = shell_count // 2
    occ_local = coef.shape[1] // (shell_count * aux_count)
    block_count = coef.shape[0] // BS * shell_count
    rows = occ_local * aux_count
    piece = jax.ShapeDtypeStruct((pairs_dev * rows + 16, BS), jnp.bfloat16)
    vmem = pl.BlockSpec(memory_space=pltpu.VMEM)
    hbm = pl.BlockSpec(memory_space=pltpu.HBM)
    params = pltpu.CompilerParams(vmem_limit_bytes=40 * 2**20)

    def transformed(name, coefs, quad, count):
        return pl.pallas_call(
            functools.partial(block_kernel, aux_count),
            out_shape=[piece] * count,
            in_specs=[vmem] * (1 + aux_count),
            out_specs=[vmem] * count,
            compiler_params=params,
            name=name,
        )(coefs, *quad)

    def code_scratch(count):
        return [
            pltpu.VMEM((count, BS), jnp.int32),
            pltpu.SMEM((count, BS), jnp.int32),
            pltpu.SemaphoreType.DMA,
        ]

    blocks = integrals.reshape(pairs_dev, BS, BS)
    far_block = flip(blocks, "shell", group)

    flips = [list(range(group)), list(range(group, shell_count))]
    near_coef, sent_coef, near_block = pl.pallas_call(
        functools.partial(pick_kernel, flips, occ_local, aux_count),
        out_shape=[
            jax.ShapeDtypeStruct((len(f) * occ_local + 16, pairs_dev * BS), jnp.bfloat16)
            for f in flips
        ]
        + [jax.ShapeDtypeStruct(blocks.shape, jnp.bfloat16)],
        in_specs=[hbm] * 4,
        out_specs=[vmem] * (len(flips) + 1),
        scratch_shapes=[
            pltpu.SMEM(pair_list.shape, jnp.int32),
            pltpu.VMEM((1, occ_slot.shape[0]), jnp.int32),
            pltpu.VMEM(coef.shape, jnp.bfloat16),
            pltpu.SemaphoreType.DMA((4,)),
        ],
        compiler_params=params,
        name="pick",
    )(*in_hbm(pair_list, occ_slot.reshape(1, -1), coef, blocks))
    near_blocks = shared(blocks, sent_coef)
    near_blocks[0] = near_block
    far_block, near_coef, sent_coef = lax.optimization_barrier((far_block, near_coef, sent_coef))
    far_coef = flip(sent_coef, "shell", group)
    near = transformed("near_blocks", near_coef, near_blocks, group)
    far_blocks = shared(far_block)
    near = [*near[:-1], after(near[-1], far_blocks[1])]
    near = [near[0]] + [flip(near[f], "shell", f) for f in range(1, group)]
    far = transformed("far_blocks", after(far_coef, *near), far_blocks, group)
    far = [far[0]] + [flip(far[f], "shell", f) for f in range(1, group)]
    total_shape = jax.ShapeDtypeStruct((block_count, rows, BS), jnp.float32)
    total = pl.pallas_call(
        near_sum_kernel,
        out_shape=total_shape,
        in_specs=[vmem] * group,
        out_specs=vmem,
        scratch_shapes=code_scratch(group),
        compiler_params=params,
        name="near_sum",
    )(*(after(one, far[0]) for one in near))
    return pl.pallas_call(
        collect_kernel,
        out_shape=[
            jax.ShapeDtypeStruct((occ_local, aux_count, block_count * BS), jnp.bfloat16),
            total_shape,
        ],
        in_specs=[hbm] + [vmem] * (1 + group),
        out_specs=[vmem, vmem],
        input_output_aliases={1: 1},
        scratch_shapes=[pltpu.VMEM(metric.shape, jnp.bfloat16)]
        + code_scratch(group)
        + [pltpu.SemaphoreType.DMA],
        compiler_params=params,
        name="collect",
    )(*in_hbm(metric), total, *far)[0]


def per_device(integrals, pair_list, coef, metric, occ_slot):
    shell_count, aux_count = lax.axis_size("shell"), lax.axis_size("aux")
    occ_local = coef.shape[1] // (shell_count * aux_count)
    if occ_local % 16 or shell_count & (shell_count - 1) or aux_count & (aux_count - 1):
        return relayed_half_blocks(integrals, pair_list, coef, metric, occ_slot)
    return exchanged_inputs(integrals, pair_list, coef, metric, occ_slot)


def solution(mesh):
    placed = (P("shell", None, "aux", None), P("shell", None), P("shell", None), P(), P())
    return jax.shard_map(
        per_device,
        mesh=mesh,
        in_specs=placed,
        out_specs=P(("shell", "aux"), None, None),
        check_vma=False,
    )
```

```python
import functools

import jax
import jax.numpy as jnp
from jax import lax
from jax.experimental import pallas as pl
from jax.experimental.pallas import tpu as pltpu
from jax.sharding import PartitionSpec as P

BS = 128


def relayed_half_blocks(integrals, pair_list, coef, metric, occ_slot):
    pairs_dev = pair_list.shape[0]
    rows_local = coef.shape[0]
    occ_count = coef.shape[1]
    blocks_dev = rows_local // BS
    shell_count = lax.axis_size("shell")
    block_count = blocks_dev * shell_count
    slot_count = occ_slot.shape[0]
    aux_dev = integrals.shape[2]
    inverse = (
        jnp.zeros((slot_count,), jnp.int32)
        .at[occ_slot]
        .set(jnp.arange(slot_count, dtype=jnp.int32))
    )
    ordered = jnp.take(
        coef.reshape(rows_local, slot_count, occ_count // slot_count), inverse, axis=1
    )
    ordered = ordered.reshape(rows_local, occ_count)

    def one_slot(item):
        int_block, column_index = item
        start = column_index % blocks_dev * BS
        column = lax.dynamic_slice_in_dim(ordered, start, BS, 0)
        product = lax.dot_general(
            column,
            int_block.reshape(BS, aux_dev * BS),
            (((0,), (0,)), ((), ())),
            preferred_element_type=jnp.float32,
        )
        return product.astype(jnp.bfloat16)

    half_blocks = lax.map(one_slot, (integrals, pair_list[:, 1]))
    half_blocks = half_blocks.reshape(pairs_dev, occ_count, aux_dev, BS)
    listing = lax.all_gather(pair_list, "shell", axis=0, tiled=True)
    targets = jnp.arange(block_count, dtype=jnp.int32)[:, None]
    selector = ((listing[:, 0][None, :] == targets) & (listing[:, 2][None, :] == 1)).astype(
        jnp.bfloat16
    )
    relayed = lax.all_to_all(
        lax.all_to_all(half_blocks, "shell", split_axis=1, concat_axis=0, tiled=True),
        "aux",
        split_axis=1,
        concat_axis=2,
        tiled=True,
    )
    summed = jnp.dot(
        selector, relayed.reshape(relayed.shape[0], -1), preferred_element_type=jnp.float32
    )
    blocks = summed.astype(jnp.bfloat16).reshape((block_count,) + relayed.shape[1:])
    result = jnp.einsum("qp,bipm->iqbm", metric, blocks, preferred_element_type=jnp.float32)
    return result.reshape(result.shape[0], result.shape[1], block_count * BS).astype(jnp.bfloat16)


def targets_of(slot_row, block_total, occ_count):
    width = occ_count // block_total
    spread = (
        lax.broadcasted_iota(jnp.int32, (block_total, occ_count), 1) // width
        == lax.broadcasted_iota(jnp.int32, (block_total, occ_count), 0)
    ).astype(jnp.bfloat16)
    slots = jnp.broadcast_to(slot_row, (8, block_total)).astype(jnp.float32)
    target = jnp.dot(slots.astype(jnp.bfloat16), spread, preferred_element_type=jnp.float32)
    return target.astype(jnp.int32)[:1] * width + (
        lax.broadcasted_iota(jnp.int32, (1, occ_count), 1) % width
    )


def code_tile(pairs):
    pairs_dev = pairs.shape[0]
    lane = lax.broadcasted_iota(jnp.int32, (1, BS), 1)
    code = jnp.zeros((1, BS), jnp.int32)
    for k in range(pairs_dev):
        code = jnp.where(lane == k, pairs[k, 0] % 128, code)
        code = jnp.where(lane == pairs_dev + k, pairs[k, 0] // 128, code)
    return jnp.broadcast_to(code.astype(jnp.float32), (16, BS)).astype(jnp.bfloat16)


def pick_kernel(
    flips,
    occ_local,
    aux_count,
    pairs_in,
    slot_in,
    coef_in,
    *refs,
):
    *outs, pairs, slot_row, coef, sems = refs
    pairs_dev = pairs.shape[0]
    blocks_dev = coef.shape[0] // BS
    occ_count = coef.shape[1]
    loads = [
        pltpu.make_async_copy(source, target, sems.at[at])
        for at, (source, target) in enumerate(
            ((slot_in, slot_row), (pairs_in, pairs), (coef_in, coef))
        )
    ]
    for load in loads:
        load.start()
    me = lax.axis_index("shell")
    mine = lax.axis_index("aux")
    every = sum(flips, [])
    row = lax.broadcasted_iota(jnp.int32, (len(every) * occ_local, 1), 0)
    owner = sum(jnp.where(row // occ_local == at, f, 0) for at, f in enumerate(every))
    wanted = (jnp.bitwise_xor(owner, me) * aux_count + mine) * occ_local + row % occ_local
    loads[0].wait()
    target = targets_of(slot_row[...], slot_row.shape[1], occ_count)
    pick = (wanted == target).astype(jnp.bfloat16)
    for load in loads[1:]:
        load.wait()
    code = code_tile(pairs)
    for k in range(pairs_dev):
        start = pl.multiple_of(lax.rem(pairs[k, 1], blocks_dev) * BS, BS)
        live = (pairs[k, 2] == 1).astype(jnp.float32)
        piece = lax.dot_general(
            pick,
            coef[pl.ds(start, BS), :],
            (((1,), (1,)), ((), ())),
            preferred_element_type=jnp.float32,
        )
        piece = (piece * live).astype(jnp.bfloat16)
        first = 0
        for out in outs:
            rows = out.shape[0] - 16
            out[:rows, k * BS : (k + 1) * BS] = piece[first : first + rows]
            out[rows:, k * BS : (k + 1) * BS] = code
            first += rows


def near_kernel(
    occ_local,
    aux_count,
    pairs_in,
    slot_in,
    coef_in,
    blocks_in,
    *refs,
):
    *outs, pairs, slot_row, coef, blocks, sems = refs
    pairs_dev = pairs.shape[0]
    blocks_dev = coef.shape[0] // BS
    occ_count = coef.shape[1]
    loads = [
        pltpu.make_async_copy(source, target, sems.at[at])
        for at, (source, target) in enumerate(
            ((slot_in, slot_row), (pairs_in, pairs), (coef_in, coef), (blocks_in, blocks))
        )
    ]
    for load in loads:
        load.start()
    me = lax.axis_index("shell")
    mine = lax.axis_index("aux")
    owned = aux_count * occ_local
    row = lax.broadcasted_iota(jnp.int32, (len(outs) * owned, 1), 0)
    owner = jnp.bitwise_xor(row // owned, me) * aux_count + jnp.bitwise_xor(
        row // occ_local % aux_count, mine
    )
    wanted = owner * occ_local + row % occ_local
    loads[0].wait()
    target = targets_of(slot_row[...], slot_row.shape[1], occ_count)
    pick = (wanted == target).astype(jnp.bfloat16)
    for load in loads[1:]:
        load.wait()
    code = code_tile(pairs)
    rows = [
        coef[pl.ds(pl.multiple_of(lax.rem(pairs[k, 1], blocks_dev) * BS, BS), BS), :]
        for k in range(pairs_dev)
    ]
    ordered = lax.dot_general(
        pick,
        jnp.concatenate(rows, axis=0),
        (((1,), (1,)), ((), ())),
        preferred_element_type=jnp.float32,
    ).astype(jnp.bfloat16)
    for k in range(pairs_dev):
        block = jnp.dot(
            ordered[:, k * BS : (k + 1) * BS], blocks[k], preferred_element_type=jnp.float32
        )
        block = (block * (pairs[k, 2] == 1).astype(jnp.float32)).astype(jnp.bfloat16)
        for f, out in enumerate(outs):
            for j in range(aux_count):
                first = f * owned + j * occ_local
                at = (j * pairs_dev + k) * occ_local
                out[at : at + occ_local, :] = block[first : first + occ_local, :]
    for out in outs:
        out[pairs_dev * owned :, :] = code


def regroup_kernel(count, *refs):
    received, outs = refs[:count], refs[count:]
    rows = outs[0].shape[0] // count
    for j, out in enumerate(outs, 1):
        for f, piece in enumerate(received):
            out[f * rows : (f + 1) * rows, :] = piece[j * rows : (j + 1) * rows, :]


def block_kernel(aux_count, coefs, *refs):
    blocks, pieces = refs[:aux_count], refs[aux_count:]
    pairs_dev = blocks[0].shape[0]
    rows = coefs.shape[0] - 16
    occ_local = rows // len(pieces)
    mine = lax.axis_index("aux")
    for k in range(pairs_dev):
        left = coefs[:rows, k * BS : (k + 1) * BS]
        for j in range(0, aux_count, 2):
            right = jnp.concatenate([blocks[j][k], blocks[j + 1][k]], axis=1)
            half = jnp.dot(left, right, preferred_element_type=jnp.float32).astype(jnp.bfloat16)
            for side in range(2):
                at = k * aux_count + jnp.bitwise_xor(mine, j + side)
                start = pl.multiple_of(at * occ_local, occ_local)
                for f, piece in enumerate(pieces):
                    piece[pl.ds(start, occ_local), :] = half[
                        f * occ_local : (f + 1) * occ_local, side * BS : (side + 1) * BS
                    ]
    for piece in pieces:
        piece[pairs_dev * aux_count * occ_local :, :] = coefs[rows:, :BS]


def load_codes(received, codes_v, codes, sem):
    for at, piece in enumerate(received):
        digits = piece[piece.shape[0] - 16 :, :].astype(jnp.float32).astype(jnp.int32)
        codes_v[at : at + 1, :] = digits[:1]
    load = pltpu.make_async_copy(codes_v, codes, sem)
    load.start()
    return load


def near_sum_kernel(occ_local, count, *refs):
    *received, total, codes_v, codes, sem = refs
    received, others = received[:count], received[count:]
    load = load_codes(received, codes_v, codes, sem)
    total[...] = jnp.zeros_like(total)
    mine = lax.axis_index("aux")
    pairs_dev = others[0].shape[0] // (count * occ_local)
    load.wait()
    for f in range(count):
        for k in range(pairs_dev):
            r = codes[f, k] + 128 * codes[f, pairs_dev + k]
            for j in range(len(others) + 1):
                source, first = (others[j - 1], f * pairs_dev + k) if j else (received[f], k)
                start = pl.multiple_of(jnp.bitwise_xor(mine, j) * occ_local, occ_local)
                part = source[first * occ_local : (first + 1) * occ_local, :]
                total[r, pl.ds(start, occ_local), :] += part.astype(jnp.float32)


def collect_kernel(metric_in, total_in, *refs):
    *received, out, total, metric, codes_v, codes, sem, metric_sem = refs
    occ_local, aux_count = out.shape[:2]
    rows = occ_local * aux_count
    load = pltpu.make_async_copy(metric_in, metric, metric_sem)
    load.start()
    code_load = load_codes(received, codes_v, codes, sem)
    pairs_dev = (received[0].shape[0] - 16) // rows
    code_load.wait()
    for at, piece in enumerate(received):
        for k in range(pairs_dev):
            r = codes[at, k] + 128 * codes[at, pairs_dev + k]
            total[r] += piece[k * rows : (k + 1) * rows, :].astype(jnp.float32)
    load.wait()

    row = lax.broadcasted_iota(jnp.int32, (rows, rows), 0)
    column = lax.broadcasted_iota(jnp.int32, (rows, rows), 1)
    left = (
        lax.broadcasted_iota(jnp.int32, (rows, aux_count), 0) % aux_count
        == lax.broadcasted_iota(jnp.int32, (rows, aux_count), 1)
    ).astype(jnp.bfloat16)
    right = (
        lax.broadcasted_iota(jnp.int32, (aux_count, rows), 1) // occ_local
        == lax.broadcasted_iota(jnp.int32, (aux_count, rows), 0)
    ).astype(jnp.bfloat16)
    factor = jnp.dot(left, metric[...], preferred_element_type=jnp.float32).astype(jnp.bfloat16)
    factor = jnp.dot(factor, right, preferred_element_type=jnp.float32)
    mix = jnp.where(row // aux_count == column % occ_local, factor, 0.0).astype(jnp.bfloat16)
    for r in range(0, total.shape[0], 2):
        summed = jnp.concatenate([total[r], total[r + 1]], axis=1).astype(jnp.bfloat16)
        mixed = jnp.dot(mix, summed, preferred_element_type=jnp.float32)
        out[:, :, r * BS : (r + 2) * BS] = mixed.reshape(
            occ_local, aux_count, 2 * BS
        ).astype(jnp.bfloat16)


def flip(value, axis, bits):
    count = lax.axis_size(axis)
    return lax.ppermute(value, axis, [(at, at ^ bits) for at in range(count)])


def after(value, *others):
    return lax.optimization_barrier((value, *others))[0]


def shared(block, *others):
    held, order, bits = [block], [0], lax.axis_size("aux") // 2
    while bits:
        held += [flip(one, "aux", bits) for one in held]
        order += [at ^ bits for at in order]
        bits //= 2
        if others:
            held = [after(one, *others) for one in held]
    return [held[order.index(at)] for at in range(len(held))]


def in_hbm(*operands):
    return [pltpu.with_memory_space_constraint(operand, pltpu.HBM) for operand in operands]


def exchanged_inputs(integrals, pair_list, coef, metric, occ_slot):
    pairs_dev = pair_list.shape[0]
    shell_count = lax.axis_size("shell")
    aux_count = lax.axis_size("aux")
    group = shell_count // 2
    occ_local = coef.shape[1] // (shell_count * aux_count)
    block_count = coef.shape[0] // BS * shell_count
    rows = occ_local * aux_count
    piece = jax.ShapeDtypeStruct((pairs_dev * rows + 16, BS), jnp.bfloat16)
    vmem = pl.BlockSpec(memory_space=pltpu.VMEM)
    hbm = pl.BlockSpec(memory_space=pltpu.HBM)
    params = pltpu.CompilerParams(vmem_limit_bytes=40 * 2**20)

    def transformed(name, coefs, quad, count):
        return pl.pallas_call(
            functools.partial(block_kernel, aux_count),
            out_shape=[piece] * count,
            in_specs=[vmem] * (1 + aux_count),
            out_specs=[vmem] * count,
            compiler_params=params,
            name=name,
        )(coefs, *quad)

    def code_scratch(count):
        return [
            pltpu.VMEM((count, BS), jnp.int32),
            pltpu.SMEM((count, BS), jnp.int32),
            pltpu.SemaphoreType.DMA,
        ]

    blocks = integrals.reshape(pairs_dev, BS, BS)
    far_block = flip(blocks, "shell", group)
    operands = (pair_list, occ_slot.reshape(1, -1), coef)
    loaded = [
        pltpu.SMEM(pair_list.shape, jnp.int32),
        pltpu.VMEM((1, occ_slot.shape[0]), jnp.int32),
        pltpu.VMEM(coef.shape, jnp.bfloat16),
    ]
    near = pl.pallas_call(
        functools.partial(near_kernel, occ_local, aux_count),
        out_shape=[piece] * group,
        in_specs=[hbm] * 4,
        out_specs=[vmem] * group,
        scratch_shapes=loaded
        + [pltpu.VMEM(blocks.shape, jnp.bfloat16), pltpu.SemaphoreType.DMA((4,))],
        compiler_params=params,
        name="near_blocks",
    )(*in_hbm(*operands, blocks))
    near = [near[0]] + [flip(near[f], "shell", f) for f in range(1, group)]
    (sent_coef,) = pl.pallas_call(
        functools.partial(
            pick_kernel, [list(range(group, shell_count))], occ_local, aux_count
        ),
        out_shape=[
            jax.ShapeDtypeStruct((group * occ_local + 16, pairs_dev * BS), jnp.bfloat16)
        ],
        in_specs=[hbm] * 3,
        out_specs=[vmem],
        scratch_shapes=loaded + [pltpu.SemaphoreType.DMA((3,))],
        compiler_params=params,
        name="pick",
    )(*in_hbm(*operands))
    far_block = after(far_block, sent_coef)
    far_coef = flip(after(sent_coef, far_block), "shell", group)
    far_blocks = shared(far_block)
    regrouped = pl.pallas_call(
        functools.partial(regroup_kernel, group),
        out_shape=[jax.ShapeDtypeStruct((group * pairs_dev * occ_local, BS), jnp.bfloat16)]
        * (aux_count - 1),
        in_specs=[vmem] * group,
        out_specs=[vmem] * (aux_count - 1),
        compiler_params=params,
        name="regroup",
    )(*near)
    others = [flip(one, "aux", j) for j, one in enumerate(regrouped, 1)]
    far = transformed("far_blocks", far_coef, far_blocks, group)
    total_shape = jax.ShapeDtypeStruct((block_count, rows, BS), jnp.float32)
    total = pl.pallas_call(
        functools.partial(near_sum_kernel, occ_local, group),
        out_shape=total_shape,
        in_specs=[vmem] * (group + aux_count - 1),
        out_specs=vmem,
        scratch_shapes=code_scratch(group),
        compiler_params=params,
        name="near_sum",
    )(*(after(one, far[0]) for one in near), *others)
    far = [far[0]] + [flip(far[f], "shell", f) for f in range(1, group)]
    return pl.pallas_call(
        collect_kernel,
        out_shape=[
            jax.ShapeDtypeStruct((occ_local, aux_count, block_count * BS), jnp.bfloat16),
            total_shape,
        ],
        in_specs=[hbm] + [vmem] * (1 + group),
        out_specs=[vmem, vmem],
        input_output_aliases={1: 1},
        scratch_shapes=[pltpu.VMEM(metric.shape, jnp.bfloat16)]
        + code_scratch(group)
        + [pltpu.SemaphoreType.DMA],
        compiler_params=params,
        name="collect",
    )(*in_hbm(metric), total, *far)[0]


def per_device(integrals, pair_list, coef, metric, occ_slot):
    shell_count, aux_count = lax.axis_size("shell"), lax.axis_size("aux")
    occ_local = coef.shape[1] // (shell_count * aux_count)
    if occ_local % 16 or shell_count & (shell_count - 1) or aux_count & (aux_count - 1):
        return relayed_half_blocks(integrals, pair_list, coef, metric, occ_slot)
    return exchanged_inputs(integrals, pair_list, coef, metric, occ_slot)


def solution(mesh):
    placed = (P("shell", None, "aux", None), P("shell", None), P("shell", None), P(), P())
    return jax.shard_map(
        per_device,
        mesh=mesh,
        in_specs=placed,
        out_specs=P(("shell", "aux"), None, None),
        check_vma=False,
    )
```

```python
import functools

import jax
import jax.numpy as jnp
from jax import lax
from jax.experimental import pallas as pl
from jax.experimental.pallas import tpu as pltpu
from jax.sharding import PartitionSpec as P

BS = 128


def relayed_half_blocks(integrals, pair_list, coef, metric, occ_slot):
    pairs_dev = pair_list.shape[0]
    rows_local = coef.shape[0]
    occ_count = coef.shape[1]
    blocks_dev = rows_local // BS
    shell_count = lax.axis_size("shell")
    block_count = blocks_dev * shell_count
    slot_count = occ_slot.shape[0]
    aux_dev = integrals.shape[2]
    inverse = (
        jnp.zeros((slot_count,), jnp.int32)
        .at[occ_slot]
        .set(jnp.arange(slot_count, dtype=jnp.int32))
    )
    ordered = jnp.take(
        coef.reshape(rows_local, slot_count, occ_count // slot_count), inverse, axis=1
    )
    ordered = ordered.reshape(rows_local, occ_count)

    def one_slot(item):
        int_block, column_index = item
        start = column_index % blocks_dev * BS
        column = lax.dynamic_slice_in_dim(ordered, start, BS, 0)
        product = lax.dot_general(
            column,
            int_block.reshape(BS, aux_dev * BS),
            (((0,), (0,)), ((), ())),
            preferred_element_type=jnp.float32,
        )
        return product.astype(jnp.bfloat16)

    half_blocks = lax.map(one_slot, (integrals, pair_list[:, 1]))
    half_blocks = half_blocks.reshape(pairs_dev, occ_count, aux_dev, BS)
    listing = lax.all_gather(pair_list, "shell", axis=0, tiled=True)
    targets = jnp.arange(block_count, dtype=jnp.int32)[:, None]
    selector = ((listing[:, 0][None, :] == targets) & (listing[:, 2][None, :] == 1)).astype(
        jnp.bfloat16
    )
    relayed = lax.all_to_all(
        lax.all_to_all(half_blocks, "shell", split_axis=1, concat_axis=0, tiled=True),
        "aux",
        split_axis=1,
        concat_axis=2,
        tiled=True,
    )
    summed = jnp.dot(
        selector, relayed.reshape(relayed.shape[0], -1), preferred_element_type=jnp.float32
    )
    blocks = summed.astype(jnp.bfloat16).reshape((block_count,) + relayed.shape[1:])
    result = jnp.einsum("qp,bipm->iqbm", metric, blocks, preferred_element_type=jnp.float32)
    return result.reshape(result.shape[0], result.shape[1], block_count * BS).astype(jnp.bfloat16)


def targets_of(slot_row, block_total, occ_count):
    width = occ_count // block_total
    spread = (
        lax.broadcasted_iota(jnp.int32, (block_total, occ_count), 1) // width
        == lax.broadcasted_iota(jnp.int32, (block_total, occ_count), 0)
    ).astype(jnp.bfloat16)
    slots = jnp.broadcast_to(slot_row, (8, block_total)).astype(jnp.float32)
    target = jnp.dot(slots.astype(jnp.bfloat16), spread, preferred_element_type=jnp.float32)
    return target.astype(jnp.int32)[:1] * width + (
        lax.broadcasted_iota(jnp.int32, (1, occ_count), 1) % width
    )


def code_tile(pairs):
    pairs_dev = pairs.shape[0]
    lane = lax.broadcasted_iota(jnp.int32, (1, BS), 1)
    code = jnp.zeros((1, BS), jnp.int32)
    for k in range(pairs_dev):
        code = jnp.where(lane == k, pairs[k, 0] % 128, code)
        code = jnp.where(lane == pairs_dev + k, pairs[k, 0] // 128, code)
    return jnp.broadcast_to(code.astype(jnp.float32), (16, BS)).astype(jnp.bfloat16)


def pick_kernel(
    flips,
    occ_local,
    aux_count,
    pairs_in,
    slot_in,
    coef_in,
    *refs,
):
    *outs, pairs, slot_row, coef, sems = refs
    pairs_dev = pairs.shape[0]
    blocks_dev = coef.shape[0] // BS
    occ_count = coef.shape[1]
    loads = [
        pltpu.make_async_copy(source, target, sems.at[at])
        for at, (source, target) in enumerate(
            ((slot_in, slot_row), (pairs_in, pairs), (coef_in, coef))
        )
    ]
    for load in loads:
        load.start()
    me = lax.axis_index("shell")
    mine = lax.axis_index("aux")
    every = sum(flips, [])
    row = lax.broadcasted_iota(jnp.int32, (len(every) * occ_local, 1), 0)
    owner = sum(jnp.where(row // occ_local == at, f, 0) for at, f in enumerate(every))
    wanted = (jnp.bitwise_xor(owner, me) * aux_count + mine) * occ_local + row % occ_local
    loads[0].wait()
    target = targets_of(slot_row[...], slot_row.shape[1], occ_count)
    pick = (wanted == target).astype(jnp.bfloat16)
    for load in loads[1:]:
        load.wait()
    code = code_tile(pairs)
    for k in range(pairs_dev):
        start = pl.multiple_of(lax.rem(pairs[k, 1], blocks_dev) * BS, BS)
        live = (pairs[k, 2] == 1).astype(jnp.float32)
        piece = lax.dot_general(
            pick,
            coef[pl.ds(start, BS), :],
            (((1,), (1,)), ((), ())),
            preferred_element_type=jnp.float32,
        )
        piece = (piece * live).astype(jnp.bfloat16)
        first = 0
        for out in outs:
            rows = out.shape[0] - 16
            out[:rows, k * BS : (k + 1) * BS] = piece[first : first + rows]
            out[rows:, k * BS : (k + 1) * BS] = code
            first += rows


def near_kernel(
    occ_local,
    aux_count,
    pairs_in,
    slot_in,
    coef_in,
    blocks_in,
    *refs,
):
    *outs, pairs, slot_row, coef, blocks, sems = refs
    pairs_dev = pairs.shape[0]
    blocks_dev = coef.shape[0] // BS
    occ_count = coef.shape[1]
    loads = [
        pltpu.make_async_copy(source, target, sems.at[at])
        for at, (source, target) in enumerate(
            ((slot_in, slot_row), (pairs_in, pairs), (coef_in, coef), (blocks_in, blocks))
        )
    ]
    for load in loads:
        load.start()
    me = lax.axis_index("shell")
    mine = lax.axis_index("aux")
    owned = aux_count * occ_local
    row = lax.broadcasted_iota(jnp.int32, (len(outs) * owned, 1), 0)
    owner = jnp.bitwise_xor(row // owned, me) * aux_count + jnp.bitwise_xor(
        row // occ_local % aux_count, mine
    )
    wanted = owner * occ_local + row % occ_local
    loads[0].wait()
    target = targets_of(slot_row[...], slot_row.shape[1], occ_count)
    pick = (wanted == target).astype(jnp.bfloat16)
    for load in loads[1:]:
        load.wait()
    code = code_tile(pairs)
    rows = [
        coef[pl.ds(pl.multiple_of(lax.rem(pairs[k, 1], blocks_dev) * BS, BS), BS), :]
        for k in range(pairs_dev)
    ]
    ordered = lax.dot_general(
        pick,
        jnp.concatenate(rows, axis=0),
        (((1,), (1,)), ((), ())),
        preferred_element_type=jnp.float32,
    ).astype(jnp.bfloat16)
    for k in range(pairs_dev):
        block = jnp.dot(
            ordered[:, k * BS : (k + 1) * BS], blocks[k], preferred_element_type=jnp.float32
        )
        block = (block * (pairs[k, 2] == 1).astype(jnp.float32)).astype(jnp.bfloat16)
        for f, out in enumerate(outs):
            for j in range(aux_count):
                first = f * owned + j * occ_local
                at = (j * pairs_dev + k) * occ_local
                out[at : at + occ_local, :] = block[first : first + occ_local, :]
    for out in outs:
        out[pairs_dev * owned :, :] = code


def regroup_kernel(count, *refs):
    received, outs = refs[:count], refs[count:]
    rows = outs[0].shape[0] // count
    for j, out in enumerate(outs, 1):
        for f, piece in enumerate(received):
            out[f * rows : (f + 1) * rows, :] = piece[j * rows : (j + 1) * rows, :]


def block_kernel(aux_count, coefs, *refs):
    blocks, pieces = refs[:aux_count], refs[aux_count:]
    pairs_dev = blocks[0].shape[0]
    rows = coefs.shape[0] - 16
    occ_local = rows // len(pieces)
    mine = lax.axis_index("aux")
    for k in range(pairs_dev):
        left = coefs[:rows, k * BS : (k + 1) * BS]
        for j in range(0, aux_count, 2):
            right = jnp.concatenate([blocks[j][k], blocks[j + 1][k]], axis=1)
            half = jnp.dot(left, right, preferred_element_type=jnp.float32).astype(jnp.bfloat16)
            for side in range(2):
                at = k * aux_count + jnp.bitwise_xor(mine, j + side)
                start = pl.multiple_of(at * occ_local, occ_local)
                for f, piece in enumerate(pieces):
                    piece[pl.ds(start, occ_local), :] = half[
                        f * occ_local : (f + 1) * occ_local, side * BS : (side + 1) * BS
                    ]
    for piece in pieces:
        piece[pairs_dev * aux_count * occ_local :, :] = coefs[rows:, :BS]


def load_codes(received, codes_v, codes, sem):
    for at, piece in enumerate(received):
        digits = piece[piece.shape[0] - 16 :, :].astype(jnp.float32).astype(jnp.int32)
        codes_v[at : at + 1, :] = digits[:1]
    load = pltpu.make_async_copy(codes_v, codes, sem)
    load.start()
    return load


def near_sum_kernel(occ_local, count, *refs):
    *received, total, codes_v, codes, sem = refs
    received, others = received[:count], received[count:]
    load = load_codes(received, codes_v, codes, sem)
    total[...] = jnp.zeros_like(total)
    mine = lax.axis_index("aux")
    pairs_dev = others[0].shape[0] // (count * occ_local)
    load.wait()
    for f in range(count):
        for k in range(pairs_dev):
            r = codes[f, k] + 128 * codes[f, pairs_dev + k]
            for j in range(len(others) + 1):
                source, first = (others[j - 1], f * pairs_dev + k) if j else (received[f], k)
                start = pl.multiple_of(jnp.bitwise_xor(mine, j) * occ_local, occ_local)
                part = source[first * occ_local : (first + 1) * occ_local, :]
                total[r, pl.ds(start, occ_local), :] += part.astype(jnp.float32)


def collect_kernel(metric_in, total_in, *refs):
    *received, out, total, metric, codes_v, codes, sem, metric_sem = refs
    occ_local, aux_count = out.shape[:2]
    rows = occ_local * aux_count
    load = pltpu.make_async_copy(metric_in, metric, metric_sem)
    load.start()
    code_load = load_codes(received, codes_v, codes, sem)
    pairs_dev = (received[0].shape[0] - 16) // rows
    code_load.wait()
    for at, piece in enumerate(received):
        for k in range(pairs_dev):
            r = codes[at, k] + 128 * codes[at, pairs_dev + k]
            total[r] += piece[k * rows : (k + 1) * rows, :].astype(jnp.float32)
    load.wait()

    row = lax.broadcasted_iota(jnp.int32, (rows, rows), 0)
    column = lax.broadcasted_iota(jnp.int32, (rows, rows), 1)
    left = (
        lax.broadcasted_iota(jnp.int32, (rows, aux_count), 0) % aux_count
        == lax.broadcasted_iota(jnp.int32, (rows, aux_count), 1)
    ).astype(jnp.bfloat16)
    right = (
        lax.broadcasted_iota(jnp.int32, (aux_count, rows), 1) // occ_local
        == lax.broadcasted_iota(jnp.int32, (aux_count, rows), 0)
    ).astype(jnp.bfloat16)
    factor = jnp.dot(left, metric[...], preferred_element_type=jnp.float32).astype(jnp.bfloat16)
    factor = jnp.dot(factor, right, preferred_element_type=jnp.float32)
    mix = jnp.where(row // aux_count == column % occ_local, factor, 0.0).astype(jnp.bfloat16)
    for r in range(0, total.shape[0], 2):
        summed = jnp.concatenate([total[r], total[r + 1]], axis=1).astype(jnp.bfloat16)
        mixed = jnp.dot(mix, summed, preferred_element_type=jnp.float32)
        out[:, :, r * BS : (r + 2) * BS] = mixed.reshape(
            occ_local, aux_count, 2 * BS
        ).astype(jnp.bfloat16)


def flip(value, axis, bits):
    count = lax.axis_size(axis)
    return lax.ppermute(value, axis, [(at, at ^ bits) for at in range(count)])


def after(value, *others):
    return lax.optimization_barrier((value, *others))[0]


def shared(block, *others):
    held, order, bits = [block], [0], lax.axis_size("aux") // 2
    while bits:
        held += [flip(one, "aux", bits) for one in held]
        order += [at ^ bits for at in order]
        bits //= 2
        if others:
            held = [after(one, *others) for one in held]
    return [held[order.index(at)] for at in range(len(held))]


def in_hbm(*operands):
    return [pltpu.with_memory_space_constraint(operand, pltpu.HBM) for operand in operands]


def exchanged_inputs(integrals, pair_list, coef, metric, occ_slot):
    pairs_dev = pair_list.shape[0]
    shell_count = lax.axis_size("shell")
    aux_count = lax.axis_size("aux")
    group = shell_count // 2
    occ_local = coef.shape[1] // (shell_count * aux_count)
    block_count = coef.shape[0] // BS * shell_count
    rows = occ_local * aux_count
    piece = jax.ShapeDtypeStruct((pairs_dev * rows + 16, BS), jnp.bfloat16)
    vmem = pl.BlockSpec(memory_space=pltpu.VMEM)
    hbm = pl.BlockSpec(memory_space=pltpu.HBM)
    params = pltpu.CompilerParams(vmem_limit_bytes=40 * 2**20)

    def transformed(name, coefs, quad, count):
        return pl.pallas_call(
            functools.partial(block_kernel, aux_count),
            out_shape=[piece] * count,
            in_specs=[vmem] * (1 + aux_count),
            out_specs=[vmem] * count,
            compiler_params=params,
            name=name,
        )(coefs, *quad)

    def code_scratch(count):
        return [
            pltpu.VMEM((count, BS), jnp.int32),
            pltpu.SMEM((count, BS), jnp.int32),
            pltpu.SemaphoreType.DMA,
        ]

    blocks = integrals.reshape(pairs_dev, BS, BS)
    far_block = flip(blocks, "shell", group)
    operands = (pair_list, occ_slot.reshape(1, -1), coef)
    loaded = [
        pltpu.SMEM(pair_list.shape, jnp.int32),
        pltpu.VMEM((1, occ_slot.shape[0]), jnp.int32),
        pltpu.VMEM(coef.shape, jnp.bfloat16),
    ]
    near = pl.pallas_call(
        functools.partial(near_kernel, occ_local, aux_count),
        out_shape=[piece] * group,
        in_specs=[hbm] * 4,
        out_specs=[vmem] * group,
        scratch_shapes=loaded
        + [pltpu.VMEM(blocks.shape, jnp.bfloat16), pltpu.SemaphoreType.DMA((4,))],
        compiler_params=params,
        name="near_blocks",
    )(*in_hbm(*operands, blocks))
    near = [near[0]] + [flip(near[f], "shell", f) for f in range(1, group)]
    (sent_coef,) = pl.pallas_call(
        functools.partial(
            pick_kernel, [list(range(group, shell_count))], occ_local, aux_count
        ),
        out_shape=[
            jax.ShapeDtypeStruct((group * occ_local + 16, pairs_dev * BS), jnp.bfloat16)
        ],
        in_specs=[hbm] * 3,
        out_specs=[vmem],
        scratch_shapes=loaded + [pltpu.SemaphoreType.DMA((3,))],
        compiler_params=params,
        name="pick",
    )(*in_hbm(*operands))
    far_block = after(far_block, sent_coef)
    far_coef = flip(after(sent_coef, far_block), "shell", group)
    far_blocks = shared(far_block)
    regrouped = pl.pallas_call(
        functools.partial(regroup_kernel, group),
        out_shape=[jax.ShapeDtypeStruct((group * pairs_dev * occ_local, BS), jnp.bfloat16)]
        * (aux_count - 1),
        in_specs=[vmem] * group,
        out_specs=[vmem] * (aux_count - 1),
        compiler_params=params,
        name="regroup",
    )(*near)
    others = [flip(one, "aux", j) for j, one in enumerate(regrouped, 1)]
    far = transformed("far_blocks", far_coef, far_blocks, group)
    total_shape = jax.ShapeDtypeStruct((block_count, rows, BS), jnp.float32)
    total = pl.pallas_call(
        functools.partial(near_sum_kernel, occ_local, group),
        out_shape=total_shape,
        in_specs=[vmem] * (group + aux_count - 1),
        out_specs=vmem,
        scratch_shapes=code_scratch(group),
        compiler_params=params,
        cost_estimate=pl.CostEstimate(
            flops=10**10, transcendentals=0, bytes_accessed=20 * 2**20
        ),
        name="near_sum",
    )(*(after(one, far[0]) for one in near), *others)
    far = [far[0]] + [flip(far[f], "shell", f) for f in range(1, group)]
    return pl.pallas_call(
        collect_kernel,
        out_shape=[
            jax.ShapeDtypeStruct((occ_local, aux_count, block_count * BS), jnp.bfloat16),
            total_shape,
        ],
        in_specs=[hbm] + [vmem] * (1 + group),
        out_specs=[vmem, vmem],
        input_output_aliases={1: 1},
        scratch_shapes=[pltpu.VMEM(metric.shape, jnp.bfloat16)]
        + code_scratch(group)
        + [pltpu.SemaphoreType.DMA],
        compiler_params=params,
        name="collect",
    )(*in_hbm(metric), total, *far)[0]


def per_device(integrals, pair_list, coef, metric, occ_slot):
    shell_count, aux_count = lax.axis_size("shell"), lax.axis_size("aux")
    occ_local = coef.shape[1] // (shell_count * aux_count)
    if occ_local % 16 or shell_count & (shell_count - 1) or aux_count & (aux_count - 1):
        return relayed_half_blocks(integrals, pair_list, coef, metric, occ_slot)
    return exchanged_inputs(integrals, pair_list, coef, metric, occ_slot)


def solution(mesh):
    placed = (P("shell", None, "aux", None), P("shell", None), P("shell", None), P(), P())
    return jax.shard_map(
        per_device,
        mesh=mesh,
        in_specs=placed,
        out_specs=P(("shell", "aux"), None, None),
        check_vma=False,
    )
```

```python
import functools

import jax
import jax.numpy as jnp
from jax import lax
from jax.experimental import pallas as pl
from jax.experimental.pallas import tpu as pltpu
from jax.sharding import PartitionSpec as P

BS = 128


def relayed_half_blocks(integrals, pair_list, coef, metric, occ_slot):
    pairs_dev = pair_list.shape[0]
    rows_local = coef.shape[0]
    occ_count = coef.shape[1]
    blocks_dev = rows_local // BS
    shell_count = lax.axis_size("shell")
    block_count = blocks_dev * shell_count
    slot_count = occ_slot.shape[0]
    aux_dev = integrals.shape[2]
    inverse = (
        jnp.zeros((slot_count,), jnp.int32)
        .at[occ_slot]
        .set(jnp.arange(slot_count, dtype=jnp.int32))
    )
    ordered = jnp.take(
        coef.reshape(rows_local, slot_count, occ_count // slot_count), inverse, axis=1
    )
    ordered = ordered.reshape(rows_local, occ_count)

    def one_slot(item):
        int_block, column_index = item
        start = column_index % blocks_dev * BS
        column = lax.dynamic_slice_in_dim(ordered, start, BS, 0)
        product = lax.dot_general(
            column,
            int_block.reshape(BS, aux_dev * BS),
            (((0,), (0,)), ((), ())),
            preferred_element_type=jnp.float32,
        )
        return product.astype(jnp.bfloat16)

    half_blocks = lax.map(one_slot, (integrals, pair_list[:, 1]))
    half_blocks = half_blocks.reshape(pairs_dev, occ_count, aux_dev, BS)
    listing = lax.all_gather(pair_list, "shell", axis=0, tiled=True)
    targets = jnp.arange(block_count, dtype=jnp.int32)[:, None]
    selector = ((listing[:, 0][None, :] == targets) & (listing[:, 2][None, :] == 1)).astype(
        jnp.bfloat16
    )
    relayed = lax.all_to_all(
        lax.all_to_all(half_blocks, "shell", split_axis=1, concat_axis=0, tiled=True),
        "aux",
        split_axis=1,
        concat_axis=2,
        tiled=True,
    )
    summed = jnp.dot(
        selector, relayed.reshape(relayed.shape[0], -1), preferred_element_type=jnp.float32
    )
    blocks = summed.astype(jnp.bfloat16).reshape((block_count,) + relayed.shape[1:])
    result = jnp.einsum("qp,bipm->iqbm", metric, blocks, preferred_element_type=jnp.float32)
    return result.reshape(result.shape[0], result.shape[1], block_count * BS).astype(jnp.bfloat16)


def targets_of(slot_row, block_total, occ_count):
    width = occ_count // block_total
    spread = (
        lax.broadcasted_iota(jnp.int32, (block_total, occ_count), 1) // width
        == lax.broadcasted_iota(jnp.int32, (block_total, occ_count), 0)
    ).astype(jnp.bfloat16)
    slots = jnp.broadcast_to(slot_row, (8, block_total)).astype(jnp.float32)
    target = jnp.dot(slots.astype(jnp.bfloat16), spread, preferred_element_type=jnp.float32)
    return target.astype(jnp.int32)[:1] * width + (
        lax.broadcasted_iota(jnp.int32, (1, occ_count), 1) % width
    )


def code_tile(pairs):
    pairs_dev = pairs.shape[0]
    lane = lax.broadcasted_iota(jnp.int32, (1, BS), 1)
    code = jnp.zeros((1, BS), jnp.int32)
    for k in range(pairs_dev):
        code = jnp.where(lane == k, pairs[k, 0] % 128, code)
        code = jnp.where(lane == pairs_dev + k, pairs[k, 0] // 128, code)
    return jnp.broadcast_to(code.astype(jnp.float32), (16, BS)).astype(jnp.bfloat16)


def pick_kernel(
    flips,
    occ_local,
    aux_count,
    pairs_in,
    slot_in,
    coef_in,
    *refs,
):
    *outs, pairs, slot_row, coef, sems = refs
    pairs_dev = pairs.shape[0]
    blocks_dev = coef.shape[0] // BS
    occ_count = coef.shape[1]
    loads = [
        pltpu.make_async_copy(source, target, sems.at[at])
        for at, (source, target) in enumerate(
            ((slot_in, slot_row), (pairs_in, pairs), (coef_in, coef))
        )
    ]
    for load in loads:
        load.start()
    me = lax.axis_index("shell")
    mine = lax.axis_index("aux")
    every = sum(flips, [])
    row = lax.broadcasted_iota(jnp.int32, (len(every) * occ_local, 1), 0)
    owner = sum(jnp.where(row // occ_local == at, f, 0) for at, f in enumerate(every))
    wanted = (jnp.bitwise_xor(owner, me) * aux_count + mine) * occ_local + row % occ_local
    loads[0].wait()
    target = targets_of(slot_row[...], slot_row.shape[1], occ_count)
    pick = (wanted == target).astype(jnp.bfloat16)
    for load in loads[1:]:
        load.wait()
    code = code_tile(pairs)
    for k in range(pairs_dev):
        start = pl.multiple_of(lax.rem(pairs[k, 1], blocks_dev) * BS, BS)
        live = (pairs[k, 2] == 1).astype(jnp.float32)
        piece = lax.dot_general(
            pick,
            coef[pl.ds(start, BS), :],
            (((1,), (1,)), ((), ())),
            preferred_element_type=jnp.float32,
        )
        piece = (piece * live).astype(jnp.bfloat16)
        first = 0
        for out in outs:
            rows = out.shape[0] - 16
            out[:rows, k * BS : (k + 1) * BS] = piece[first : first + rows]
            out[rows:, k * BS : (k + 1) * BS] = code
            first += rows


def near_kernel(
    occ_local,
    aux_count,
    pairs_in,
    slot_in,
    coef_in,
    blocks_in,
    *refs,
):
    *outs, pairs, slot_row, coef, blocks, sems = refs
    pairs_dev = pairs.shape[0]
    blocks_dev = coef.shape[0] // BS
    occ_count = coef.shape[1]
    loads = [
        pltpu.make_async_copy(source, target, sems.at[at])
        for at, (source, target) in enumerate(
            ((slot_in, slot_row), (pairs_in, pairs), (coef_in, coef), (blocks_in, blocks))
        )
    ]
    for load in loads:
        load.start()
    me = lax.axis_index("shell")
    mine = lax.axis_index("aux")
    owned = aux_count * occ_local
    row = lax.broadcasted_iota(jnp.int32, (len(outs) * owned, 1), 0)
    owner = jnp.bitwise_xor(row // owned, me) * aux_count + jnp.bitwise_xor(
        row // occ_local % aux_count, mine
    )
    wanted = owner * occ_local + row % occ_local
    loads[0].wait()
    target = targets_of(slot_row[...], slot_row.shape[1], occ_count)
    pick = (wanted == target).astype(jnp.bfloat16)
    for load in loads[1:]:
        load.wait()
    code = code_tile(pairs)
    rows = [
        coef[pl.ds(pl.multiple_of(lax.rem(pairs[k, 1], blocks_dev) * BS, BS), BS), :]
        for k in range(pairs_dev)
    ]
    ordered = lax.dot_general(
        pick,
        jnp.concatenate(rows, axis=0),
        (((1,), (1,)), ((), ())),
        preferred_element_type=jnp.float32,
    ).astype(jnp.bfloat16)
    for k in range(pairs_dev):
        block = jnp.dot(
            ordered[:, k * BS : (k + 1) * BS], blocks[k], preferred_element_type=jnp.float32
        )
        block = (block * (pairs[k, 2] == 1).astype(jnp.float32)).astype(jnp.bfloat16)
        for f, out in enumerate(outs):
            for j in range(aux_count):
                first = f * owned + j * occ_local
                at = (j * pairs_dev + k) * occ_local
                out[at : at + occ_local, :] = block[first : first + occ_local, :]
    for out in outs:
        out[pairs_dev * owned :, :] = code


def regroup_kernel(count, *refs):
    received, outs = refs[:count], refs[count:]
    rows = outs[0].shape[0] // count
    for j, out in enumerate(outs, 1):
        for f, piece in enumerate(received):
            out[f * rows : (f + 1) * rows, :] = piece[j * rows : (j + 1) * rows, :]


def block_kernel(aux_count, coefs, *refs):
    blocks, pieces = refs[:aux_count], refs[aux_count:]
    pairs_dev = blocks[0].shape[0]
    rows = coefs.shape[0] - 16
    occ_local = rows // len(pieces)
    mine = lax.axis_index("aux")
    for k in range(pairs_dev):
        left = coefs[:rows, k * BS : (k + 1) * BS]
        for j in range(0, aux_count, 2):
            right = jnp.concatenate([blocks[j][k], blocks[j + 1][k]], axis=1)
            half = jnp.dot(left, right, preferred_element_type=jnp.float32).astype(jnp.bfloat16)
            for side in range(2):
                at = k * aux_count + jnp.bitwise_xor(mine, j + side)
                start = pl.multiple_of(at * occ_local, occ_local)
                for f, piece in enumerate(pieces):
                    piece[pl.ds(start, occ_local), :] = half[
                        f * occ_local : (f + 1) * occ_local, side * BS : (side + 1) * BS
                    ]
    for piece in pieces:
        piece[pairs_dev * aux_count * occ_local :, :] = coefs[rows:, :BS]


def load_codes(received, codes_v, codes, sem):
    for at, piece in enumerate(received):
        digits = piece[piece.shape[0] - 16 :, :].astype(jnp.float32).astype(jnp.int32)
        codes_v[at : at + 1, :] = digits[:1]
    load = pltpu.make_async_copy(codes_v, codes, sem)
    load.start()
    return load


def near_sum_kernel(occ_local, count, *refs):
    *received, total, codes_v, codes, sem = refs
    received, others = received[:count], received[count:]
    load = load_codes(received, codes_v, codes, sem)
    total[...] = jnp.zeros_like(total)
    mine = lax.axis_index("aux")
    pairs_dev = others[0].shape[0] // (count * occ_local)
    load.wait()
    for f in range(count):
        for k in range(pairs_dev):
            r = codes[f, k] + 128 * codes[f, pairs_dev + k]
            for j in range(len(others) + 1):
                source, first = (others[j - 1], f * pairs_dev + k) if j else (received[f], k)
                start = pl.multiple_of(jnp.bitwise_xor(mine, j) * occ_local, occ_local)
                part = source[first * occ_local : (first + 1) * occ_local, :]
                total[r, pl.ds(start, occ_local), :] += part.astype(jnp.float32)


def collect_kernel(metric_in, total_in, *refs):
    *received, out, total, metric, codes_v, codes, sem, metric_sem = refs
    occ_local, aux_count = out.shape[:2]
    rows = occ_local * aux_count
    load = pltpu.make_async_copy(metric_in, metric, metric_sem)
    load.start()
    code_load = load_codes(received, codes_v, codes, sem)
    pairs_dev = (received[0].shape[0] - 16) // rows
    code_load.wait()
    for at, piece in enumerate(received):
        for k in range(pairs_dev):
            r = codes[at, k] + 128 * codes[at, pairs_dev + k]
            total[r] += piece[k * rows : (k + 1) * rows, :].astype(jnp.float32)
    load.wait()

    row = lax.broadcasted_iota(jnp.int32, (rows, rows), 0)
    column = lax.broadcasted_iota(jnp.int32, (rows, rows), 1)
    left = (
        lax.broadcasted_iota(jnp.int32, (rows, aux_count), 0) % aux_count
        == lax.broadcasted_iota(jnp.int32, (rows, aux_count), 1)
    ).astype(jnp.bfloat16)
    right = (
        lax.broadcasted_iota(jnp.int32, (aux_count, rows), 1) // occ_local
        == lax.broadcasted_iota(jnp.int32, (aux_count, rows), 0)
    ).astype(jnp.bfloat16)
    factor = jnp.dot(left, metric[...], preferred_element_type=jnp.float32).astype(jnp.bfloat16)
    factor = jnp.dot(factor, right, preferred_element_type=jnp.float32)
    mix = jnp.where(row // aux_count == column % occ_local, factor, 0.0).astype(jnp.bfloat16)
    for r in range(0, total.shape[0], 2):
        summed = jnp.concatenate([total[r], total[r + 1]], axis=1).astype(jnp.bfloat16)
        mixed = jnp.dot(mix, summed, preferred_element_type=jnp.float32)
        out[:, :, r * BS : (r + 2) * BS] = mixed.reshape(
            occ_local, aux_count, 2 * BS
        ).astype(jnp.bfloat16)


def flip(value, axis, bits):
    count = lax.axis_size(axis)
    return lax.ppermute(value, axis, [(at, at ^ bits) for at in range(count)])


def after(value, *others):
    return lax.optimization_barrier((value, *others))[0]


def shared(block, *others):
    held, order, bits = [block], [0], lax.axis_size("aux") // 2
    while bits:
        held += [flip(one, "aux", bits) for one in held]
        order += [at ^ bits for at in order]
        bits //= 2
        if others:
            held = [after(one, *others) for one in held]
    return [held[order.index(at)] for at in range(len(held))]


def cost(flops):
    return pl.CostEstimate(flops=int(flops), transcendentals=0, bytes_accessed=2**20)


def in_hbm(*operands):
    return [pltpu.with_memory_space_constraint(operand, pltpu.HBM) for operand in operands]


def exchanged_inputs(integrals, pair_list, coef, metric, occ_slot):
    pairs_dev = pair_list.shape[0]
    shell_count = lax.axis_size("shell")
    aux_count = lax.axis_size("aux")
    group = shell_count // 2
    occ_local = coef.shape[1] // (shell_count * aux_count)
    block_count = coef.shape[0] // BS * shell_count
    rows = occ_local * aux_count
    piece = jax.ShapeDtypeStruct((pairs_dev * rows + 16, BS), jnp.bfloat16)
    vmem = pl.BlockSpec(memory_space=pltpu.VMEM)
    hbm = pl.BlockSpec(memory_space=pltpu.HBM)
    params = pltpu.CompilerParams(vmem_limit_bytes=40 * 2**20)

    def transformed(name, coefs, quad, count):
        return pl.pallas_call(
            functools.partial(block_kernel, aux_count),
            out_shape=[piece] * count,
            in_specs=[vmem] * (1 + aux_count),
            out_specs=[vmem] * count,
            compiler_params=params,
            cost_estimate=cost(3e9) if name == "far_blocks" else None,
            name=name,
        )(coefs, *quad)

    def code_scratch(count):
        return [
            pltpu.VMEM((count, BS), jnp.int32),
            pltpu.SMEM((count, BS), jnp.int32),
            pltpu.SemaphoreType.DMA,
        ]

    blocks = integrals.reshape(pairs_dev, BS, BS)
    far_block = flip(blocks, "shell", group)
    operands = (pair_list, occ_slot.reshape(1, -1), coef)
    loaded = [
        pltpu.SMEM(pair_list.shape, jnp.int32),
        pltpu.VMEM((1, occ_slot.shape[0]), jnp.int32),
        pltpu.VMEM(coef.shape, jnp.bfloat16),
    ]
    near = pl.pallas_call(
        functools.partial(near_kernel, occ_local, aux_count),
        out_shape=[piece] * group,
        in_specs=[hbm] * 4,
        out_specs=[vmem] * group,
        scratch_shapes=loaded
        + [pltpu.VMEM(blocks.shape, jnp.bfloat16), pltpu.SemaphoreType.DMA((4,))],
        compiler_params=params,
        name="near_blocks",
    )(*in_hbm(*operands, blocks))
    sent = near
    near = [sent[0]] + [flip(sent[f], "shell", f) for f in range(1, group - 1)]
    (sent_coef,) = pl.pallas_call(
        functools.partial(
            pick_kernel, [list(range(group, shell_count))], occ_local, aux_count
        ),
        out_shape=[
            jax.ShapeDtypeStruct((group * occ_local + 16, pairs_dev * BS), jnp.bfloat16)
        ],
        in_specs=[hbm] * 3,
        out_specs=[vmem],
        scratch_shapes=loaded + [pltpu.SemaphoreType.DMA((3,))],
        compiler_params=params,
        name="pick",
    )(*in_hbm(*operands))
    far_block = after(far_block, sent_coef)
    far_coef = flip(after(sent_coef, far_block), "shell", group)
    far_blocks = shared(far_block)
    near.append(flip(after(sent[-1], near[-1],sent_coef), "shell", group - 1))
    regrouped = pl.pallas_call(
        functools.partial(regroup_kernel, group),
        out_shape=[jax.ShapeDtypeStruct((group * pairs_dev * occ_local, BS), jnp.bfloat16)]
        * (aux_count - 1),
        in_specs=[vmem] * group,
        out_specs=[vmem] * (aux_count - 1),
        compiler_params=params,
        name="regroup",
    )(*near)
    others = [flip(one, "aux", j) for j, one in enumerate(regrouped, 1)]
    far = transformed("far_blocks", far_coef, far_blocks, group)
    total_shape = jax.ShapeDtypeStruct((block_count, rows, BS), jnp.float32)
    total = pl.pallas_call(
        functools.partial(near_sum_kernel, occ_local, group),
        out_shape=total_shape,
        in_specs=[vmem] * (group + aux_count - 1),
        out_specs=vmem,
        scratch_shapes=code_scratch(group),
        compiler_params=params,
        cost_estimate=cost(3e9),
        name="near_sum",
    )(*(after(one, far[0]) for one in near), *others)
    far = [far[0]] + [flip(far[f], "shell", f) for f in range(1, group)]
    return pl.pallas_call(
        collect_kernel,
        out_shape=[
            jax.ShapeDtypeStruct((occ_local, aux_count, block_count * BS), jnp.bfloat16),
            total_shape,
        ],
        in_specs=[hbm] + [vmem] * (1 + group),
        out_specs=[vmem, vmem],
        input_output_aliases={1: 1},
        scratch_shapes=[pltpu.VMEM(metric.shape, jnp.bfloat16)]
        + code_scratch(group)
        + [pltpu.SemaphoreType.DMA],
        compiler_params=params,
        name="collect",
    )(*in_hbm(metric), total, *far)[0]


def per_device(integrals, pair_list, coef, metric, occ_slot):
    shell_count, aux_count = lax.axis_size("shell"), lax.axis_size("aux")
    occ_local = coef.shape[1] // (shell_count * aux_count)
    if occ_local % 16 or shell_count & (shell_count - 1) or aux_count & (aux_count - 1):
        return relayed_half_blocks(integrals, pair_list, coef, metric, occ_slot)
    return exchanged_inputs(integrals, pair_list, coef, metric, occ_slot)


def solution(mesh):
    placed = (P("shell", None, "aux", None), P("shell", None), P("shell", None), P(), P())
    return jax.shard_map(
        per_device,
        mesh=mesh,
        in_specs=placed,
        out_specs=P(("shell", "aux"), None, None),
        check_vma=False,
    )
```

```python
import functools

import jax
import jax.numpy as jnp
from jax import lax
from jax.experimental import pallas as pl
from jax.experimental.pallas import tpu as pltpu
from jax.sharding import PartitionSpec as P

BS = 128


def relayed_half_blocks(integrals, pair_list, coef, metric, occ_slot):
    pairs_dev = pair_list.shape[0]
    rows_local = coef.shape[0]
    occ_count = coef.shape[1]
    blocks_dev = rows_local // BS
    shell_count = lax.axis_size("shell")
    block_count = blocks_dev * shell_count
    slot_count = occ_slot.shape[0]
    aux_dev = integrals.shape[2]
    inverse = (
        jnp.zeros((slot_count,), jnp.int32)
        .at[occ_slot]
        .set(jnp.arange(slot_count, dtype=jnp.int32))
    )
    ordered = jnp.take(
        coef.reshape(rows_local, slot_count, occ_count // slot_count), inverse, axis=1
    )
    ordered = ordered.reshape(rows_local, occ_count)

    def one_slot(item):
        int_block, column_index = item
        start = column_index % blocks_dev * BS
        column = lax.dynamic_slice_in_dim(ordered, start, BS, 0)
        product = lax.dot_general(
            column,
            int_block.reshape(BS, aux_dev * BS),
            (((0,), (0,)), ((), ())),
            preferred_element_type=jnp.float32,
        )
        return product.astype(jnp.bfloat16)

    half_blocks = lax.map(one_slot, (integrals, pair_list[:, 1]))
    half_blocks = half_blocks.reshape(pairs_dev, occ_count, aux_dev, BS)
    listing = lax.all_gather(pair_list, "shell", axis=0, tiled=True)
    targets = jnp.arange(block_count, dtype=jnp.int32)[:, None]
    selector = ((listing[:, 0][None, :] == targets) & (listing[:, 2][None, :] == 1)).astype(
        jnp.bfloat16
    )
    relayed = lax.all_to_all(
        lax.all_to_all(half_blocks, "shell", split_axis=1, concat_axis=0, tiled=True),
        "aux",
        split_axis=1,
        concat_axis=2,
        tiled=True,
    )
    summed = jnp.dot(
        selector, relayed.reshape(relayed.shape[0], -1), preferred_element_type=jnp.float32
    )
    blocks = summed.astype(jnp.bfloat16).reshape((block_count,) + relayed.shape[1:])
    result = jnp.einsum("qp,bipm->iqbm", metric, blocks, preferred_element_type=jnp.float32)
    return result.reshape(result.shape[0], result.shape[1], block_count * BS).astype(jnp.bfloat16)


def targets_of(slot_row, block_total, occ_count):
    width = occ_count // block_total
    spread = (
        lax.broadcasted_iota(jnp.int32, (block_total, occ_count), 1) // width
        == lax.broadcasted_iota(jnp.int32, (block_total, occ_count), 0)
    ).astype(jnp.bfloat16)
    slots = jnp.broadcast_to(slot_row, (8, block_total)).astype(jnp.float32)
    target = jnp.dot(slots.astype(jnp.bfloat16), spread, preferred_element_type=jnp.float32)
    return target.astype(jnp.int32)[:1] * width + (
        lax.broadcasted_iota(jnp.int32, (1, occ_count), 1) % width
    )


def code_tile(pairs):
    pairs_dev = pairs.shape[0]
    lane = lax.broadcasted_iota(jnp.int32, (1, BS), 1)
    code = jnp.zeros((1, BS), jnp.int32)
    for k in range(pairs_dev):
        code = jnp.where(lane == k, pairs[k, 0] % 128, code)
        code = jnp.where(lane == pairs_dev + k, pairs[k, 0] // 128, code)
    return jnp.broadcast_to(code.astype(jnp.float32), (16, BS)).astype(jnp.bfloat16)


def pick_kernel(
    flips,
    occ_local,
    aux_count,
    pairs_in,
    slot_in,
    coef_in,
    *refs,
):
    *outs, pairs, slot_row, coef, sems = refs
    pairs_dev = pairs.shape[0]
    blocks_dev = coef.shape[0] // BS
    occ_count = coef.shape[1]
    loads = [
        pltpu.make_async_copy(source, target, sems.at[at])
        for at, (source, target) in enumerate(
            ((slot_in, slot_row), (pairs_in, pairs), (coef_in, coef))
        )
    ]
    for load in loads:
        load.start()
    me = lax.axis_index("shell")
    mine = lax.axis_index("aux")
    every = sum(flips, [])
    row = lax.broadcasted_iota(jnp.int32, (len(every) * occ_local, 1), 0)
    owner = sum(jnp.where(row // occ_local == at, f, 0) for at, f in enumerate(every))
    wanted = (jnp.bitwise_xor(owner, me) * aux_count + mine) * occ_local + row % occ_local
    loads[0].wait()
    target = targets_of(slot_row[...], slot_row.shape[1], occ_count)
    pick = (wanted == target).astype(jnp.bfloat16)
    for load in loads[1:]:
        load.wait()
    code = code_tile(pairs)
    for k in range(pairs_dev):
        start = pl.multiple_of(lax.rem(pairs[k, 1], blocks_dev) * BS, BS)
        live = (pairs[k, 2] == 1).astype(jnp.float32)
        piece = lax.dot_general(
            pick,
            coef[pl.ds(start, BS), :],
            (((1,), (1,)), ((), ())),
            preferred_element_type=jnp.float32,
        )
        piece = (piece * live).astype(jnp.bfloat16)
        first = 0
        for out in outs:
            rows = out.shape[0] - 16
            out[:rows, k * BS : (k + 1) * BS] = piece[first : first + rows]
            out[rows:, k * BS : (k + 1) * BS] = code
            first += rows


def near_kernel(
    occ_local,
    aux_count,
    pairs_in,
    slot_in,
    coef_in,
    blocks_in,
    *refs,
):
    *outs, pairs, slot_row, coef, blocks, sems = refs
    pairs_dev = pairs.shape[0]
    blocks_dev = coef.shape[0] // BS
    occ_count = coef.shape[1]
    loads = [
        pltpu.make_async_copy(source, target, sems.at[at])
        for at, (source, target) in enumerate(
            ((slot_in, slot_row), (pairs_in, pairs), (coef_in, coef), (blocks_in, blocks))
        )
    ]
    for load in loads:
        load.start()
    me = lax.axis_index("shell")
    mine = lax.axis_index("aux")
    owned = aux_count * occ_local
    row = lax.broadcasted_iota(jnp.int32, (len(outs) * owned, 1), 0)
    owner = jnp.bitwise_xor(row // owned, me) * aux_count + jnp.bitwise_xor(
        row // occ_local % aux_count, mine
    )
    wanted = owner * occ_local + row % occ_local
    loads[0].wait()
    target = targets_of(slot_row[...], slot_row.shape[1], occ_count)
    pick = (wanted == target).astype(jnp.bfloat16)
    for load in loads[1:]:
        load.wait()
    code = code_tile(pairs)
    rows = [
        coef[pl.ds(pl.multiple_of(lax.rem(pairs[k, 1], blocks_dev) * BS, BS), BS), :]
        for k in range(pairs_dev)
    ]
    ordered = lax.dot_general(
        pick,
        jnp.concatenate(rows, axis=0),
        (((1,), (1,)), ((), ())),
        preferred_element_type=jnp.float32,
    ).astype(jnp.bfloat16)
    for k in range(pairs_dev):
        block = jnp.dot(
            ordered[:, k * BS : (k + 1) * BS], blocks[k], preferred_element_type=jnp.float32
        )
        block = (block * (pairs[k, 2] == 1).astype(jnp.float32)).astype(jnp.bfloat16)
        for f, out in enumerate(outs):
            for j in range(aux_count):
                first = f * owned + j * occ_local
                at = (j * pairs_dev + k) * occ_local
                out[at : at + occ_local, :] = block[first : first + occ_local, :]
    for out in outs:
        out[pairs_dev * owned :, :] = code


def regroup_kernel(count, *refs):
    received, outs = refs[:count], refs[count:]
    rows = outs[0].shape[0] // count
    for j, out in enumerate(outs, 1):
        for f, piece in enumerate(received):
            out[f * rows : (f + 1) * rows, :] = piece[j * rows : (j + 1) * rows, :]


def block_kernel(aux_count, coefs, *refs):
    blocks, pieces = refs[:aux_count], refs[aux_count:]
    pairs_dev = blocks[0].shape[0]
    rows = coefs.shape[0] - 16
    occ_local = rows // len(pieces)
    mine = lax.axis_index("aux")
    for k in range(pairs_dev):
        left = coefs[:rows, k * BS : (k + 1) * BS]
        for j in range(0, aux_count, 2):
            right = jnp.concatenate([blocks[j][k], blocks[j + 1][k]], axis=1)
            half = jnp.dot(left, right, preferred_element_type=jnp.float32).astype(jnp.bfloat16)
            for side in range(2):
                at = k * aux_count + jnp.bitwise_xor(mine, j + side)
                start = pl.multiple_of(at * occ_local, occ_local)
                for f, piece in enumerate(pieces):
                    piece[pl.ds(start, occ_local), :] = half[
                        f * occ_local : (f + 1) * occ_local, side * BS : (side + 1) * BS
                    ]
    for piece in pieces:
        piece[pairs_dev * aux_count * occ_local :, :] = coefs[rows:, :BS]


def load_codes(received, codes_v, codes, sem):
    for at, piece in enumerate(received):
        digits = piece[piece.shape[0] - 16 :, :].astype(jnp.float32).astype(jnp.int32)
        codes_v[at : at + 1, :] = digits[:1]
    load = pltpu.make_async_copy(codes_v, codes, sem)
    load.start()
    return load


def near_sum_kernel(occ_local, count, *refs):
    *received, total, codes_v, codes, sem = refs
    received, others = received[:count], received[count:]
    load = load_codes(received, codes_v, codes, sem)
    total[...] = jnp.zeros_like(total)
    mine = lax.axis_index("aux")
    pairs_dev = others[0].shape[0] // (count * occ_local)
    load.wait()
    for f in range(count):
        for k in range(pairs_dev):
            r = codes[f, k] + 128 * codes[f, pairs_dev + k]
            for j in range(len(others) + 1):
                source, first = (others[j - 1], f * pairs_dev + k) if j else (received[f], k)
                start = pl.multiple_of(jnp.bitwise_xor(mine, j) * occ_local, occ_local)
                part = source[first * occ_local : (first + 1) * occ_local, :]
                total[r, pl.ds(start, occ_local), :] += part.astype(jnp.float32)


def collect_kernel(metric_in, total_in, *refs):
    *received, out, total, metric, codes_v, codes, sem, metric_sem = refs
    occ_local, aux_count = out.shape[:2]
    rows = occ_local * aux_count
    load = pltpu.make_async_copy(metric_in, metric, metric_sem)
    load.start()
    code_load = load_codes(received, codes_v, codes, sem)
    pairs_dev = (received[0].shape[0] - 16) // rows
    code_load.wait()
    for at, piece in enumerate(received):
        for k in range(pairs_dev):
            r = codes[at, k] + 128 * codes[at, pairs_dev + k]
            total[r] += piece[k * rows : (k + 1) * rows, :].astype(jnp.float32)
    load.wait()

    row = lax.broadcasted_iota(jnp.int32, (rows, rows), 0)
    column = lax.broadcasted_iota(jnp.int32, (rows, rows), 1)
    left = (
        lax.broadcasted_iota(jnp.int32, (rows, aux_count), 0) % aux_count
        == lax.broadcasted_iota(jnp.int32, (rows, aux_count), 1)
    ).astype(jnp.bfloat16)
    right = (
        lax.broadcasted_iota(jnp.int32, (aux_count, rows), 1) // occ_local
        == lax.broadcasted_iota(jnp.int32, (aux_count, rows), 0)
    ).astype(jnp.bfloat16)
    factor = jnp.dot(left, metric[...], preferred_element_type=jnp.float32).astype(jnp.bfloat16)
    factor = jnp.dot(factor, right, preferred_element_type=jnp.float32)
    mix = jnp.where(row // aux_count == column % occ_local, factor, 0.0).astype(jnp.bfloat16)
    for r in range(0, total.shape[0], 2):
        summed = jnp.concatenate([total[r], total[r + 1]], axis=1).astype(jnp.bfloat16)
        mixed = jnp.dot(mix, summed, preferred_element_type=jnp.float32)
        out[:, :, r * BS : (r + 2) * BS] = mixed.reshape(
            occ_local, aux_count, 2 * BS
        ).astype(jnp.bfloat16)


def flip(value, axis, bits):
    count = lax.axis_size(axis)
    return lax.ppermute(value, axis, [(at, at ^ bits) for at in range(count)])


def after(value, *others):
    return lax.optimization_barrier((value, *others))[0]


def shared(block, *others):
    held, order, bits = [block], [0], lax.axis_size("aux") // 2
    while bits:
        held += [flip(one, "aux", bits) for one in held]
        order += [at ^ bits for at in order]
        bits //= 2
        if others:
            held = [after(one, *others) for one in held]
    return [held[order.index(at)] for at in range(len(held))]


def cost(flops):
    return pl.CostEstimate(flops=int(flops), transcendentals=0, bytes_accessed=2**20)


def in_hbm(*operands):
    return [pltpu.with_memory_space_constraint(operand, pltpu.HBM) for operand in operands]


def exchanged_inputs(integrals, pair_list, coef, metric, occ_slot):
    pairs_dev = pair_list.shape[0]
    shell_count = lax.axis_size("shell")
    aux_count = lax.axis_size("aux")
    group = shell_count // 2
    occ_local = coef.shape[1] // (shell_count * aux_count)
    block_count = coef.shape[0] // BS * shell_count
    rows = occ_local * aux_count
    piece = jax.ShapeDtypeStruct((pairs_dev * rows + 16, BS), jnp.bfloat16)
    vmem = pl.BlockSpec(memory_space=pltpu.VMEM)
    hbm = pl.BlockSpec(memory_space=pltpu.HBM)
    params = pltpu.CompilerParams(vmem_limit_bytes=40 * 2**20)

    def transformed(name, coefs, quad, count):
        return pl.pallas_call(
            functools.partial(block_kernel, aux_count),
            out_shape=[piece] * count,
            in_specs=[vmem] * (1 + aux_count),
            out_specs=[vmem] * count,
            compiler_params=params,
            cost_estimate=cost(3e9) if name == "far_blocks" else None,
            name=name,
        )(coefs, *quad)

    def code_scratch(count):
        return [
            pltpu.VMEM((count, BS), jnp.int32),
            pltpu.SMEM((count, BS), jnp.int32),
            pltpu.SemaphoreType.DMA,
        ]

    blocks = integrals.reshape(pairs_dev, BS, BS)
    far_block = flip(blocks, "shell", group)
    operands = (pair_list, occ_slot.reshape(1, -1), coef)
    loaded = [
        pltpu.SMEM(pair_list.shape, jnp.int32),
        pltpu.VMEM((1, occ_slot.shape[0]), jnp.int32),
        pltpu.VMEM(coef.shape, jnp.bfloat16),
    ]
    near = pl.pallas_call(
        functools.partial(near_kernel, occ_local, aux_count),
        out_shape=[piece] * group,
        in_specs=[hbm] * 4,
        out_specs=[vmem] * group,
        scratch_shapes=loaded
        + [pltpu.VMEM(blocks.shape, jnp.bfloat16), pltpu.SemaphoreType.DMA((4,))],
        compiler_params=params,
        name="near_blocks",
    )(*in_hbm(*operands, blocks))
    near = [near[0]] + [flip(near[f], "shell", f) for f in range(1, group)]
    (sent_coef,) = pl.pallas_call(
        functools.partial(
            pick_kernel, [list(range(group, shell_count))], occ_local, aux_count
        ),
        out_shape=[
            jax.ShapeDtypeStruct((group * occ_local + 16, pairs_dev * BS), jnp.bfloat16)
        ],
        in_specs=[hbm] * 3,
        out_specs=[vmem],
        scratch_shapes=loaded + [pltpu.SemaphoreType.DMA((3,))],
        compiler_params=params,
        name="pick",
    )(*in_hbm(*operands))
    far_block = after(far_block, sent_coef)
    far_coef = flip(after(sent_coef, far_block), "shell", group)
    far_blocks = shared(far_block, near[1],near[2])
    regrouped = pl.pallas_call(
        functools.partial(regroup_kernel, group),
        out_shape=[jax.ShapeDtypeStruct((group * pairs_dev * occ_local, BS), jnp.bfloat16)]
        * (aux_count - 1),
        in_specs=[vmem] * group,
        out_specs=[vmem] * (aux_count - 1),
        compiler_params=params,
        name="regroup",
    )(*near)
    others = [flip(one, "aux", j) for j, one in enumerate(regrouped, 1)]
    far = transformed("far_blocks", far_coef, far_blocks, group)
    total_shape = jax.ShapeDtypeStruct((block_count, rows, BS), jnp.float32)
    total = pl.pallas_call(
        functools.partial(near_sum_kernel, occ_local, group),
        out_shape=total_shape,
        in_specs=[vmem] * (group + aux_count - 1),
        out_specs=vmem,
        scratch_shapes=code_scratch(group),
        compiler_params=params,
        cost_estimate=cost(3e9),
        name="near_sum",
    )(*(after(one, far[0]) for one in near), *others)
    far = [far[0]] + [flip(far[f], "shell", f) for f in range(1, group)]
    return pl.pallas_call(
        collect_kernel,
        out_shape=[
            jax.ShapeDtypeStruct((occ_local, aux_count, block_count * BS), jnp.bfloat16),
            total_shape,
        ],
        in_specs=[hbm] + [vmem] * (1 + group),
        out_specs=[vmem, vmem],
        input_output_aliases={1: 1},
        scratch_shapes=[pltpu.VMEM(metric.shape, jnp.bfloat16)]
        + code_scratch(group)
        + [pltpu.SemaphoreType.DMA],
        compiler_params=params,
        name="collect",
    )(*in_hbm(metric), total, *far)[0]


def per_device(integrals, pair_list, coef, metric, occ_slot):
    shell_count, aux_count = lax.axis_size("shell"), lax.axis_size("aux")
    occ_local = coef.shape[1] // (shell_count * aux_count)
    if occ_local % 16 or shell_count & (shell_count - 1) or aux_count & (aux_count - 1):
        return relayed_half_blocks(integrals, pair_list, coef, metric, occ_slot)
    return exchanged_inputs(integrals, pair_list, coef, metric, occ_slot)


def solution(mesh):
    placed = (P("shell", None, "aux", None), P("shell", None), P("shell", None), P(), P())
    return jax.shard_map(
        per_device,
        mesh=mesh,
        in_specs=placed,
        out_specs=P(("shell", "aux"), None, None),
        check_vma=False,
    )
```

```python
import functools

import jax
import jax.numpy as jnp
from jax import lax
from jax.experimental import pallas as pl
from jax.experimental.pallas import tpu as pltpu
from jax.sharding import PartitionSpec as P

BS = 128


def relayed_half_blocks(integrals, pair_list, coef, metric, occ_slot):
    pairs_dev = pair_list.shape[0]
    rows_local = coef.shape[0]
    occ_count = coef.shape[1]
    blocks_dev = rows_local // BS
    shell_count = lax.axis_size("shell")
    block_count = blocks_dev * shell_count
    slot_count = occ_slot.shape[0]
    aux_dev = integrals.shape[2]
    inverse = (
        jnp.zeros((slot_count,), jnp.int32)
        .at[occ_slot]
        .set(jnp.arange(slot_count, dtype=jnp.int32))
    )
    ordered = jnp.take(
        coef.reshape(rows_local, slot_count, occ_count // slot_count), inverse, axis=1
    )
    ordered = ordered.reshape(rows_local, occ_count)

    def one_slot(item):
        int_block, column_index = item
        start = column_index % blocks_dev * BS
        column = lax.dynamic_slice_in_dim(ordered, start, BS, 0)
        product = lax.dot_general(
            column,
            int_block.reshape(BS, aux_dev * BS),
            (((0,), (0,)), ((), ())),
            preferred_element_type=jnp.float32,
        )
        return product.astype(jnp.bfloat16)

    half_blocks = lax.map(one_slot, (integrals, pair_list[:, 1]))
    half_blocks = half_blocks.reshape(pairs_dev, occ_count, aux_dev, BS)
    listing = lax.all_gather(pair_list, "shell", axis=0, tiled=True)
    targets = jnp.arange(block_count, dtype=jnp.int32)[:, None]
    selector = ((listing[:, 0][None, :] == targets) & (listing[:, 2][None, :] == 1)).astype(
        jnp.bfloat16
    )
    relayed = lax.all_to_all(
        lax.all_to_all(half_blocks, "shell", split_axis=1, concat_axis=0, tiled=True),
        "aux",
        split_axis=1,
        concat_axis=2,
        tiled=True,
    )
    summed = jnp.dot(
        selector, relayed.reshape(relayed.shape[0], -1), preferred_element_type=jnp.float32
    )
    blocks = summed.astype(jnp.bfloat16).reshape((block_count,) + relayed.shape[1:])
    result = jnp.einsum("qp,bipm->iqbm", metric, blocks, preferred_element_type=jnp.float32)
    return result.reshape(result.shape[0], result.shape[1], block_count * BS).astype(jnp.bfloat16)


def targets_of(slot_row, block_total, occ_count):
    width = occ_count // block_total
    spread = (
        lax.broadcasted_iota(jnp.int32, (block_total, occ_count), 1) // width
        == lax.broadcasted_iota(jnp.int32, (block_total, occ_count), 0)
    ).astype(jnp.bfloat16)
    slots = jnp.broadcast_to(slot_row, (8, block_total)).astype(jnp.float32)
    target = jnp.dot(slots.astype(jnp.bfloat16), spread, preferred_element_type=jnp.float32)
    return target.astype(jnp.int32)[:1] * width + (
        lax.broadcasted_iota(jnp.int32, (1, occ_count), 1) % width
    )


def code_tile(pairs):
    pairs_dev = pairs.shape[0]
    lane = lax.broadcasted_iota(jnp.int32, (1, BS), 1)
    code = jnp.zeros((1, BS), jnp.int32)
    for k in range(pairs_dev):
        code = jnp.where(lane == k, pairs[k, 0] % 128, code)
        code = jnp.where(lane == pairs_dev + k, pairs[k, 0] // 128, code)
    return jnp.broadcast_to(code.astype(jnp.float32), (16, BS)).astype(jnp.bfloat16)


def pick_kernel(
    flips,
    occ_local,
    aux_count,
    pairs_in,
    slot_in,
    coef_in,
    *refs,
):
    *outs, pairs, slot_row, coef, sems = refs
    pairs_dev = pairs.shape[0]
    blocks_dev = coef.shape[0] // BS
    occ_count = coef.shape[1]
    loads = [
        pltpu.make_async_copy(source, target, sems.at[at])
        for at, (source, target) in enumerate(
            ((slot_in, slot_row), (pairs_in, pairs), (coef_in, coef))
        )
    ]
    for load in loads:
        load.start()
    me = lax.axis_index("shell")
    mine = lax.axis_index("aux")
    every = sum(flips, [])
    row = lax.broadcasted_iota(jnp.int32, (len(every) * occ_local, 1), 0)
    owner = sum(jnp.where(row // occ_local == at, f, 0) for at, f in enumerate(every))
    wanted = (jnp.bitwise_xor(owner, me) * aux_count + mine) * occ_local + row % occ_local
    loads[0].wait()
    target = targets_of(slot_row[...], slot_row.shape[1], occ_count)
    pick = (wanted == target).astype(jnp.bfloat16)
    for load in loads[1:]:
        load.wait()
    code = code_tile(pairs)
    for k in range(pairs_dev):
        start = pl.multiple_of(lax.rem(pairs[k, 1], blocks_dev) * BS, BS)
        live = (pairs[k, 2] == 1).astype(jnp.float32)
        piece = lax.dot_general(
            pick,
            coef[pl.ds(start, BS), :],
            (((1,), (1,)), ((), ())),
            preferred_element_type=jnp.float32,
        )
        piece = (piece * live).astype(jnp.bfloat16)
        first = 0
        for out in outs:
            rows = out.shape[0] - 16
            out[:rows, k * BS : (k + 1) * BS] = piece[first : first + rows]
            out[rows:, k * BS : (k + 1) * BS] = code
            first += rows


def near_kernel(
    occ_local,
    aux_count,
    pairs_in,
    slot_in,
    coef_in,
    blocks_in,
    *refs,
):
    *outs, pairs, slot_row, coef, blocks, sems = refs
    pairs_dev = pairs.shape[0]
    blocks_dev = coef.shape[0] // BS
    occ_count = coef.shape[1]
    loads = [
        pltpu.make_async_copy(source, target, sems.at[at])
        for at, (source, target) in enumerate(
            ((slot_in, slot_row), (pairs_in, pairs), (coef_in, coef), (blocks_in, blocks))
        )
    ]
    for load in loads:
        load.start()
    me = lax.axis_index("shell")
    mine = lax.axis_index("aux")
    owned = aux_count * occ_local
    row = lax.broadcasted_iota(jnp.int32, (len(outs) * owned, 1), 0)
    owner = jnp.bitwise_xor(row // owned, me) * aux_count + jnp.bitwise_xor(
        row // occ_local % aux_count, mine
    )
    wanted = owner * occ_local + row % occ_local
    loads[0].wait()
    target = targets_of(slot_row[...], slot_row.shape[1], occ_count)
    pick = (wanted == target).astype(jnp.bfloat16)
    for load in loads[1:]:
        load.wait()
    code = code_tile(pairs)
    rows = [
        coef[pl.ds(pl.multiple_of(lax.rem(pairs[k, 1], blocks_dev) * BS, BS), BS), :]
        for k in range(pairs_dev)
    ]
    ordered = lax.dot_general(
        pick,
        jnp.concatenate(rows, axis=0),
        (((1,), (1,)), ((), ())),
        preferred_element_type=jnp.float32,
    ).astype(jnp.bfloat16)
    for k in range(pairs_dev):
        block = jnp.dot(
            ordered[:, k * BS : (k + 1) * BS], blocks[k], preferred_element_type=jnp.float32
        )
        block = (block * (pairs[k, 2] == 1).astype(jnp.float32)).astype(jnp.bfloat16)
        for f, out in enumerate(outs):
            for j in range(aux_count):
                first = f * owned + j * occ_local
                at = (j * pairs_dev + k) * occ_local
                out[at : at + occ_local, :] = block[first : first + occ_local, :]
    for out in outs:
        out[pairs_dev * owned :, :] = code


def regroup_kernel(count, *refs):
    received, outs = refs[:count], refs[count:]
    rows = outs[0].shape[0] // count
    for j, out in enumerate(outs, 1):
        for f, piece in enumerate(received):
            out[f * rows : (f + 1) * rows, :] = piece[j * rows : (j + 1) * rows, :]


def merge_kernel(first, second, out, sems):
    count = first.shape[0]
    skip = second.shape[0] - count
    loads = [
        pltpu.make_async_copy(first, out.at[:count], sems.at[0]),
        pltpu.make_async_copy(second.at[skip:], out.at[count:], sems.at[1]),
    ]
    for load in loads:
        load.start()
    for load in loads:
        load.wait()


def block_kernel(aux_count, low, coefs, blocks, *refs):
    pieces = refs[len(refs) // 2 :] if low else refs
    pairs_dev = blocks.shape[0] // 2
    rows = coefs.shape[0] - 16
    occ_local = rows // len(pieces)
    mine = lax.axis_index("aux")
    for k in range(pairs_dev):
        left = coefs[:rows, k * BS : (k + 1) * BS]
        right = jnp.concatenate([blocks[k], blocks[pairs_dev + k]], axis=1)
        half = jnp.dot(left, right, preferred_element_type=jnp.float32).astype(jnp.bfloat16)
        for side in range(2):
            flipped = low + side * (aux_count // 2)
            at = k * aux_count + jnp.bitwise_xor(mine, flipped)
            start = pl.multiple_of(at * occ_local, occ_local)
            for f, piece in enumerate(pieces):
                piece[pl.ds(start, occ_local), :] = half[
                    f * occ_local : (f + 1) * occ_local, side * BS : (side + 1) * BS
                ]
    if low == 0:
        for piece in pieces:
            piece[pairs_dev * aux_count * occ_local :, :] = coefs[rows:, :BS]


def read_codes(received, pairs_dev, codes):
    for at, piece in enumerate(received):
        digits = piece[piece.shape[0] - 16 :, :].astype(jnp.float32)[:1]
        high = pltpu.roll(digits, BS - pairs_dev, 1)
        codes[at : at + 1, :] = (digits + 128.0 * high).astype(jnp.int32)


def near_sum_kernel(count, metric_in, *refs):
    *received, total, mix, metric, codes, sem = refs
    received, others = received[:count], received[count:]
    load = pltpu.make_async_copy(metric_in, metric, sem)
    load.start()
    total[...] = jnp.zeros_like(total)
    mine = lax.axis_index("aux")
    rows = total.shape[1]
    occ_local = rows // metric.shape[0]
    pairs_dev = (received[0].shape[0] - 16) // rows
    read_codes(received, pairs_dev, codes)
    for f in range(count):
        for k in range(pairs_dev):
            r = codes[f, k]
            for j in range(len(others) + 1):
                source, first = (others[j - 1], f * pairs_dev + k) if j else (received[f], k)
                start = pl.multiple_of(jnp.bitwise_xor(mine, j) * occ_local, occ_local)
                part = source[first * occ_local : (first + 1) * occ_local, :]
                total[r, pl.ds(start, occ_local), :] += part.astype(jnp.float32)
    load.wait()
    aux_count = metric.shape[0]
    row = lax.broadcasted_iota(jnp.int32, (rows, rows), 0)
    column = lax.broadcasted_iota(jnp.int32, (rows, rows), 1)
    left = (
        lax.broadcasted_iota(jnp.int32, (rows, aux_count), 0) % aux_count
        == lax.broadcasted_iota(jnp.int32, (rows, aux_count), 1)
    ).astype(jnp.bfloat16)
    right = (
        lax.broadcasted_iota(jnp.int32, (aux_count, rows), 1) // occ_local
        == lax.broadcasted_iota(jnp.int32, (aux_count, rows), 0)
    ).astype(jnp.bfloat16)
    factor = jnp.dot(left, metric[...], preferred_element_type=jnp.float32).astype(jnp.bfloat16)
    factor = jnp.dot(factor, right, preferred_element_type=jnp.float32)
    mix[...] = jnp.where(row // aux_count == column % occ_local, factor, 0.0).astype(jnp.bfloat16)


def collect_kernel(mix, total_in, *refs):
    *received, out, total, staged, codes, sems = refs
    occ_local, aux_count = out.shape[:2]
    rows = total.shape[1]
    pairs_dev = (received[0].shape[0] - 16) // rows
    read_codes(received, pairs_dev, codes)
    for at, piece in enumerate(received):
        for k in range(pairs_dev):
            total[codes[at, k]] += piece[k * rows : (k + 1) * rows, :].astype(jnp.float32)
    stores = []
    parts = sems.shape[0]
    each = total.shape[0] // parts
    for part in range(parts):
        for r in range(part * each, (part + 1) * each, 2):
            summed = jnp.concatenate([total[r], total[r + 1]], axis=1).astype(jnp.bfloat16)
            mixed = jnp.dot(mix[...], summed, preferred_element_type=jnp.float32)
            staged[:, :, r * BS : (r + 2) * BS] = mixed.reshape(
                occ_local, aux_count, 2 * BS
            ).astype(jnp.bfloat16)
        lanes = pl.ds(part * each * BS, each * BS)
        store = pltpu.make_async_copy(
            staged.at[:, :, lanes], out.at[:, :, lanes], sems.at[part]
        )
        store.start()
        stores.append(store)
    for store in stores:
        store.wait()

def flip(value, axis, bits):
    count = lax.axis_size(axis)
    return lax.ppermute(value, axis, [(at, at ^ bits) for at in range(count)])


def after(value, *others):
    return lax.optimization_barrier((value, *others))[0]


def cost(flops):
    return pl.CostEstimate(flops=int(flops), transcendentals=0, bytes_accessed=2**20)


def in_hbm(*operands):
    return [pltpu.with_memory_space_constraint(operand, pltpu.HBM) for operand in operands]


def exchanged_inputs(integrals, pair_list, coef, metric, occ_slot):
    pairs_dev = pair_list.shape[0]
    shell_count = lax.axis_size("shell")
    aux_count = lax.axis_size("aux")
    group = shell_count // 2
    occ_local = coef.shape[1] // (shell_count * aux_count)
    block_count = coef.shape[0] // BS * shell_count
    rows = occ_local * aux_count
    piece = jax.ShapeDtypeStruct((pairs_dev * rows + 16, BS), jnp.bfloat16)
    vmem = pl.BlockSpec(memory_space=pltpu.VMEM)
    hbm = pl.BlockSpec(memory_space=pltpu.HBM)
    params = pltpu.CompilerParams(vmem_limit_bytes=40 * 2**20)

    def merged(name, first, second):
        return pl.pallas_call(
            merge_kernel,
            out_shape=jax.ShapeDtypeStruct(
                (2 * first.shape[0],) + first.shape[1:], jnp.bfloat16
            ),
            in_specs=[vmem] * 2,
            out_specs=vmem,
            scratch_shapes=[pltpu.SemaphoreType.DMA((2,))],
            compiler_params=params,
            name=name,
        )(first, second)

    blocks = integrals.reshape(pairs_dev, BS, BS)
    far_block = flip(blocks, "shell", group)
    operands = (pair_list, occ_slot.reshape(1, -1), coef)
    loaded = [
        pltpu.SMEM(pair_list.shape, jnp.int32),
        pltpu.VMEM((1, occ_slot.shape[0]), jnp.int32),
        pltpu.VMEM(coef.shape, jnp.bfloat16),
    ]
    near = pl.pallas_call(
        functools.partial(near_kernel, occ_local, aux_count),
        out_shape=[piece] * group,
        in_specs=[hbm] * 4,
        out_specs=[vmem] * group,
        scratch_shapes=loaded
        + [pltpu.VMEM(blocks.shape, jnp.bfloat16), pltpu.SemaphoreType.DMA((4,))],
        compiler_params=params,
        name="near_blocks",
    )(*in_hbm(*operands, blocks))
    near = [near[0]] + [flip(near[f], "shell", f) for f in range(1, group)]
    (sent_coef,) = pl.pallas_call(
        functools.partial(
            pick_kernel, [list(range(group, shell_count))], occ_local, aux_count
        ),
        out_shape=[
            jax.ShapeDtypeStruct((group * occ_local + 16, pairs_dev * BS), jnp.bfloat16)
        ],
        in_specs=[hbm] * 3,
        out_specs=[vmem],
        scratch_shapes=loaded + [pltpu.SemaphoreType.DMA((3,))],
        compiler_params=params,
        name="pick",
    )(*in_hbm(*operands))
    far_block = after(far_block, sent_coef)
    far_coef = flip(after(sent_coef, far_block), "shell", group)
    far_pair = merged("far_pair", far_block, after(flip(far_block, "aux", 2), *near))
    far_pairs = [far_pair, flip(far_pair, "aux", 1)]
    regrouped = pl.pallas_call(
        functools.partial(regroup_kernel, group),
        out_shape=[jax.ShapeDtypeStruct((group * pairs_dev * occ_local, BS), jnp.bfloat16)]
        * (aux_count - 1),
        in_specs=[vmem] * group,
        out_specs=[vmem] * (aux_count - 1),
        compiler_params=params,
        name="regroup",
    )(*near)
    others = [flip(one, "aux", j) for j, one in enumerate(regrouped, 1)]
    far = []
    for low in range(2):
        far = pl.pallas_call(
            functools.partial(block_kernel, aux_count, low),
            out_shape=[piece] * group,
            in_specs=[vmem] * (2 + len(far)),
            out_specs=[vmem] * group,
            input_output_aliases={2 + f: f for f in range(len(far))},
            compiler_params=params,
            cost_estimate=cost(2e9) if low == 0 else None,
            name=f"far_blocks_{low}",
        )(far_coef, far_pairs[low], *far)
    total_shape = jax.ShapeDtypeStruct((block_count, rows, BS), jnp.float32)
    total, mix = pl.pallas_call(
        functools.partial(near_sum_kernel, group),
        out_shape=[total_shape, jax.ShapeDtypeStruct((rows, rows), jnp.bfloat16)],
        in_specs=[hbm] + [vmem] * (group + aux_count - 1),
        out_specs=[vmem] * 2,
        scratch_shapes=[
            pltpu.VMEM(metric.shape, jnp.bfloat16),
            pltpu.VMEM((8, BS), jnp.int32),
            pltpu.SemaphoreType.DMA,
        ],
        compiler_params=params,
        cost_estimate=cost(3e9),
        name="near_sum",
    )(*in_hbm(metric), *(after(one, far[0]) for one in near), *others)
    far = [far[0]] + [flip(far[f], "shell", f) for f in range(1, group)]
    return pl.pallas_call(
        collect_kernel,
        out_shape=[
            jax.ShapeDtypeStruct((occ_local, aux_count, block_count * BS), jnp.bfloat16),
            total_shape,
        ],
        in_specs=[vmem] * (2 + group),
        out_specs=[hbm, vmem],
        input_output_aliases={1: 1},
        scratch_shapes=[
            pltpu.VMEM((occ_local, aux_count, block_count * BS), jnp.bfloat16),
            pltpu.VMEM((8, BS), jnp.int32),
            pltpu.SemaphoreType.DMA((4,)),
        ],
        compiler_params=params,
        name="collect",
    )(mix, total, *far)[0]


def per_device(integrals, pair_list, coef, metric, occ_slot):
    shell_count, aux_count = lax.axis_size("shell"), lax.axis_size("aux")
    occ_local = coef.shape[1] // (shell_count * aux_count)
    if occ_local % 16 or shell_count & (shell_count - 1) or aux_count != 4:
        return relayed_half_blocks(integrals, pair_list, coef, metric, occ_slot)
    return exchanged_inputs(integrals, pair_list, coef, metric, occ_slot)


def solution(mesh):
    placed = (P("shell", None, "aux", None), P("shell", None), P("shell", None), P(), P())
    return jax.shard_map(
        per_device,
        mesh=mesh,
        in_specs=placed,
        out_specs=P(("shell", "aux"), None, None),
        check_vma=False,
    )
```

```python
import functools

import jax
import jax.numpy as jnp
from jax import lax
from jax.experimental import pallas as pl
from jax.experimental.pallas import tpu as pltpu
from jax.sharding import PartitionSpec as P

BS = 128


def relayed_half_blocks(integrals, pair_list, coef, metric, occ_slot):
    pairs_dev = pair_list.shape[0]
    rows_local = coef.shape[0]
    occ_count = coef.shape[1]
    blocks_dev = rows_local // BS
    shell_count = lax.axis_size("shell")
    block_count = blocks_dev * shell_count
    slot_count = occ_slot.shape[0]
    aux_dev = integrals.shape[2]
    inverse = (
        jnp.zeros((slot_count,), jnp.int32)
        .at[occ_slot]
        .set(jnp.arange(slot_count, dtype=jnp.int32))
    )
    ordered = jnp.take(
        coef.reshape(rows_local, slot_count, occ_count // slot_count), inverse, axis=1
    )
    ordered = ordered.reshape(rows_local, occ_count)

    def one_slot(item):
        int_block, column_index = item
        start = column_index % blocks_dev * BS
        column = lax.dynamic_slice_in_dim(ordered, start, BS, 0)
        product = lax.dot_general(
            column,
            int_block.reshape(BS, aux_dev * BS),
            (((0,), (0,)), ((), ())),
            preferred_element_type=jnp.float32,
        )
        return product.astype(jnp.bfloat16)

    half_blocks = lax.map(one_slot, (integrals, pair_list[:, 1]))
    half_blocks = half_blocks.reshape(pairs_dev, occ_count, aux_dev, BS)
    listing = lax.all_gather(pair_list, "shell", axis=0, tiled=True)
    targets = jnp.arange(block_count, dtype=jnp.int32)[:, None]
    selector = ((listing[:, 0][None, :] == targets) & (listing[:, 2][None, :] == 1)).astype(
        jnp.bfloat16
    )
    relayed = lax.all_to_all(
        lax.all_to_all(half_blocks, "shell", split_axis=1, concat_axis=0, tiled=True),
        "aux",
        split_axis=1,
        concat_axis=2,
        tiled=True,
    )
    summed = jnp.dot(
        selector, relayed.reshape(relayed.shape[0], -1), preferred_element_type=jnp.float32
    )
    blocks = summed.astype(jnp.bfloat16).reshape((block_count,) + relayed.shape[1:])
    result = jnp.einsum("qp,bipm->iqbm", metric, blocks, preferred_element_type=jnp.float32)
    return result.reshape(result.shape[0], result.shape[1], block_count * BS).astype(jnp.bfloat16)


def targets_of(slot_row, block_total, occ_count):
    width = occ_count // block_total
    spread = (
        lax.broadcasted_iota(jnp.int32, (block_total, occ_count), 1) // width
        == lax.broadcasted_iota(jnp.int32, (block_total, occ_count), 0)
    ).astype(jnp.bfloat16)
    slots = jnp.broadcast_to(slot_row, (8, block_total)).astype(jnp.float32)
    target = jnp.dot(slots.astype(jnp.bfloat16), spread, preferred_element_type=jnp.float32)
    return target.astype(jnp.int32)[:1] * width + (
        lax.broadcasted_iota(jnp.int32, (1, occ_count), 1) % width
    )


def code_tile(pairs):
    pairs_dev = pairs.shape[0]
    lane = lax.broadcasted_iota(jnp.int32, (1, BS), 1)
    code = jnp.zeros((1, BS), jnp.int32)
    for k in range(pairs_dev):
        code = jnp.where(lane == k, pairs[k, 0] % 128, code)
        code = jnp.where(lane == pairs_dev + k, pairs[k, 0] // 128, code)
    return jnp.broadcast_to(code.astype(jnp.float32), (16, BS)).astype(jnp.bfloat16)


def pick_kernel(
    flips,
    occ_local,
    aux_count,
    pairs_in,
    slot_in,
    coef_in,
    *refs,
):
    *outs, pairs, slot_row, coef, sems = refs
    pairs_dev = pairs.shape[0]
    blocks_dev = coef.shape[0] // BS
    occ_count = coef.shape[1]
    loads = [
        pltpu.make_async_copy(source, target, sems.at[at])
        for at, (source, target) in enumerate(
            ((slot_in, slot_row), (pairs_in, pairs), (coef_in, coef))
        )
    ]
    for load in loads:
        load.start()
    me = lax.axis_index("shell")
    mine = lax.axis_index("aux")
    every = sum(flips, [])
    row = lax.broadcasted_iota(jnp.int32, (len(every) * occ_local, 1), 0)
    owner = sum(jnp.where(row // occ_local == at, f, 0) for at, f in enumerate(every))
    wanted = (jnp.bitwise_xor(owner, me) * aux_count + mine) * occ_local + row % occ_local
    loads[0].wait()
    target = targets_of(slot_row[...], slot_row.shape[1], occ_count)
    pick = (wanted == target).astype(jnp.bfloat16)
    for load in loads[1:]:
        load.wait()
    code = code_tile(pairs)
    for k in range(pairs_dev):
        start = pl.multiple_of(lax.rem(pairs[k, 1], blocks_dev) * BS, BS)
        live = (pairs[k, 2] == 1).astype(jnp.float32)
        piece = lax.dot_general(
            pick,
            coef[pl.ds(start, BS), :],
            (((1,), (1,)), ((), ())),
            preferred_element_type=jnp.float32,
        )
        piece = (piece * live).astype(jnp.bfloat16)
        first = 0
        for out in outs:
            rows = out.shape[0] - 16
            out[:rows, k * BS : (k + 1) * BS] = piece[first : first + rows]
            out[rows:, k * BS : (k + 1) * BS] = code
            first += rows


def near_kernel(
    occ_local,
    aux_count,
    pairs_in,
    slot_in,
    coef_in,
    blocks_in,
    *refs,
):
    *outs, pairs, slot_row, coef, blocks, sems = refs
    pairs_dev = pairs.shape[0]
    blocks_dev = coef.shape[0] // BS
    occ_count = coef.shape[1]
    loads = [
        pltpu.make_async_copy(source, target, sems.at[at])
        for at, (source, target) in enumerate(
            ((slot_in, slot_row), (pairs_in, pairs), (coef_in, coef), (blocks_in, blocks))
        )
    ]
    for load in loads:
        load.start()
    me = lax.axis_index("shell")
    mine = lax.axis_index("aux")
    owned = aux_count * occ_local
    row = lax.broadcasted_iota(jnp.int32, (len(outs) * owned, 1), 0)
    owner = jnp.bitwise_xor(row // owned, me) * aux_count + jnp.bitwise_xor(
        row // occ_local % aux_count, mine
    )
    wanted = owner * occ_local + row % occ_local
    loads[0].wait()
    target = targets_of(slot_row[...], slot_row.shape[1], occ_count)
    pick = (wanted == target).astype(jnp.bfloat16)
    for load in loads[1:]:
        load.wait()
    code = code_tile(pairs)
    rows = [
        coef[pl.ds(pl.multiple_of(lax.rem(pairs[k, 1], blocks_dev) * BS, BS), BS), :]
        for k in range(pairs_dev)
    ]
    ordered = lax.dot_general(
        pick,
        jnp.concatenate(rows, axis=0),
        (((1,), (1,)), ((), ())),
        preferred_element_type=jnp.float32,
    ).astype(jnp.bfloat16)
    for k in range(pairs_dev):
        block = jnp.dot(
            ordered[:, k * BS : (k + 1) * BS], blocks[k], preferred_element_type=jnp.float32
        )
        block = (block * (pairs[k, 2] == 1).astype(jnp.float32)).astype(jnp.bfloat16)
        for f, out in enumerate(outs):
            for j in range(aux_count):
                first = f * owned + j * occ_local
                at = (j * pairs_dev + k) * occ_local
                out[at : at + occ_local, :] = block[first : first + occ_local, :]
    for out in outs:
        out[pairs_dev * owned :, :] = code


def regroup_kernel(count, *refs):
    received, outs = refs[:count], refs[count:]
    rows = outs[0].shape[0] // count
    for j, out in enumerate(outs, 1):
        for f, piece in enumerate(received):
            out[f * rows : (f + 1) * rows, :] = piece[j * rows : (j + 1) * rows, :]


def merge_kernel(first, second, out, sems):
    count = first.shape[0]
    skip = second.shape[0] - count
    loads = [
        pltpu.make_async_copy(first, out.at[:count], sems.at[0]),
        pltpu.make_async_copy(second.at[skip:], out.at[count:], sems.at[1]),
    ]
    for load in loads:
        load.start()
    for load in loads:
        load.wait()


def block_kernel(aux_count, low, coefs, blocks, *refs):
    pieces = refs[len(refs) // 2 :] if low else refs
    pairs_dev = blocks.shape[0] // 2
    rows = coefs.shape[0] - 16
    occ_local = rows // len(pieces)
    mine = lax.axis_index("aux")
    for k in range(pairs_dev):
        left = coefs[:rows, k * BS : (k + 1) * BS]
        right = jnp.concatenate([blocks[k], blocks[pairs_dev + k]], axis=1)
        half = jnp.dot(left, right, preferred_element_type=jnp.float32).astype(jnp.bfloat16)
        for side in range(2):
            flipped = low + side * (aux_count // 2)
            at = k * aux_count + jnp.bitwise_xor(mine, flipped)
            start = pl.multiple_of(at * occ_local, occ_local)
            for f, piece in enumerate(pieces):
                piece[pl.ds(start, occ_local), :] = half[
                    f * occ_local : (f + 1) * occ_local, side * BS : (side + 1) * BS
                ]
    if low == 0:
        for piece in pieces:
            piece[pairs_dev * aux_count * occ_local :, :] = coefs[rows:, :BS]


def read_codes(received, pairs_dev, codes):
    for at, piece in enumerate(received):
        digits = piece[piece.shape[0] - 16 :, :].astype(jnp.float32)[:1]
        high = pltpu.roll(digits, BS - pairs_dev, 1)
        codes[at : at + 1, :] = (digits + 128.0 * high).astype(jnp.int32)


def near_sum_kernel(count, metric_in, *refs):
    *received, total, mix, metric, codes, sem = refs
    received, others = received[:count], received[count:]
    load = pltpu.make_async_copy(metric_in, metric, sem)
    load.start()
    total[...] = jnp.zeros_like(total)
    mine = lax.axis_index("aux")
    rows = total.shape[1]
    occ_local = rows // metric.shape[0]
    pairs_dev = (received[0].shape[0] - 16) // rows
    read_codes(received, pairs_dev, codes)
    for f in range(count):
        for k in range(pairs_dev):
            r = codes[f, k]
            for j in range(len(others) + 1):
                source, first = (others[j - 1], f * pairs_dev + k) if j else (received[f], k)
                start = pl.multiple_of(jnp.bitwise_xor(mine, j) * occ_local, occ_local)
                part = source[first * occ_local : (first + 1) * occ_local, :]
                total[r, pl.ds(start, occ_local), :] += part.astype(jnp.float32)
    load.wait()
    aux_count = metric.shape[0]
    row = lax.broadcasted_iota(jnp.int32, (rows, rows), 0)
    column = lax.broadcasted_iota(jnp.int32, (rows, rows), 1)
    left = (
        lax.broadcasted_iota(jnp.int32, (rows, aux_count), 0) % aux_count
        == lax.broadcasted_iota(jnp.int32, (rows, aux_count), 1)
    ).astype(jnp.bfloat16)
    right = (
        lax.broadcasted_iota(jnp.int32, (aux_count, rows), 1) // occ_local
        == lax.broadcasted_iota(jnp.int32, (aux_count, rows), 0)
    ).astype(jnp.bfloat16)
    factor = jnp.dot(left, metric[...], preferred_element_type=jnp.float32).astype(jnp.bfloat16)
    factor = jnp.dot(factor, right, preferred_element_type=jnp.float32)
    mix[...] = jnp.where(row // aux_count == column % occ_local, factor, 0.0).astype(jnp.bfloat16)


def collect_kernel(mix, total_in, *refs):
    *received, out, total, staged, codes, sems = refs
    occ_local, aux_count = out.shape[:2]
    rows = total.shape[1]
    pairs_dev = (received[0].shape[0] - 16) // rows
    read_codes(received, pairs_dev, codes)
    for at, piece in enumerate(received):
        for k in range(pairs_dev):
            total[codes[at, k]] += piece[k * rows : (k + 1) * rows, :].astype(jnp.float32)
    stores = []
    parts = sems.shape[0]
    each = total.shape[0] // parts
    for part in range(parts):
        for r in range(part * each, (part + 1) * each, 2):
            summed = jnp.concatenate([total[r], total[r + 1]], axis=1).astype(jnp.bfloat16)
            mixed = jnp.dot(mix[...], summed, preferred_element_type=jnp.float32)
            staged[:, :, r * BS : (r + 2) * BS] = mixed.reshape(
                occ_local, aux_count, 2 * BS
            ).astype(jnp.bfloat16)
        lanes = pl.ds(part * each * BS, each * BS)
        store = pltpu.make_async_copy(
            staged.at[:, :, lanes], out.at[:, :, lanes], sems.at[part]
        )
        store.start()
        stores.append(store)
    for store in stores:
        store.wait()

def flip(value, axis, bits):
    count = lax.axis_size(axis)
    return lax.ppermute(value, axis, [(at, at ^ bits) for at in range(count)])


def after(value, *others):
    return lax.optimization_barrier((value, *others))[0]


def cost(flops):
    return pl.CostEstimate(flops=int(flops), transcendentals=0, bytes_accessed=2**20)


def in_hbm(*operands):
    return [pltpu.with_memory_space_constraint(operand, pltpu.HBM) for operand in operands]


def exchanged_inputs(integrals, pair_list, coef, metric, occ_slot):
    pairs_dev = pair_list.shape[0]
    shell_count = lax.axis_size("shell")
    aux_count = lax.axis_size("aux")
    group = shell_count // 2
    occ_local = coef.shape[1] // (shell_count * aux_count)
    block_count = coef.shape[0] // BS * shell_count
    rows = occ_local * aux_count
    piece = jax.ShapeDtypeStruct((pairs_dev * rows + 16, BS), jnp.bfloat16)
    vmem = pl.BlockSpec(memory_space=pltpu.VMEM)
    hbm = pl.BlockSpec(memory_space=pltpu.HBM)
    params = pltpu.CompilerParams(vmem_limit_bytes=40 * 2**20)

    def merged(name, first, second):
        return pl.pallas_call(
            merge_kernel,
            out_shape=jax.ShapeDtypeStruct(
                (2 * first.shape[0],) + first.shape[1:], jnp.bfloat16
            ),
            in_specs=[vmem] * 2,
            out_specs=vmem,
            scratch_shapes=[pltpu.SemaphoreType.DMA((2,))],
            compiler_params=params,
            name=name,
        )(first, second)

    blocks = integrals.reshape(pairs_dev, BS, BS)
    far_block = flip(blocks, "shell", group)
    operands = (pair_list, occ_slot.reshape(1, -1), coef)
    loaded = [
        pltpu.SMEM(pair_list.shape, jnp.int32),
        pltpu.VMEM((1, occ_slot.shape[0]), jnp.int32),
        pltpu.VMEM(coef.shape, jnp.bfloat16),
    ]
    near = pl.pallas_call(
        functools.partial(near_kernel, occ_local, aux_count),
        out_shape=[piece] * group,
        in_specs=[hbm] * 4,
        out_specs=[vmem] * group,
        scratch_shapes=loaded
        + [pltpu.VMEM(blocks.shape, jnp.bfloat16), pltpu.SemaphoreType.DMA((4,))],
        compiler_params=params,
        name="near_blocks",
    )(*in_hbm(*operands, blocks))
    near = [near[0]] + [flip(near[f], "shell", f) for f in range(1, group)]
    (sent_coef,) = pl.pallas_call(
        functools.partial(
            pick_kernel, [list(range(group, shell_count))], occ_local, aux_count
        ),
        out_shape=[
            jax.ShapeDtypeStruct((group * occ_local + 16, pairs_dev * BS), jnp.bfloat16)
        ],
        in_specs=[hbm] * 3,
        out_specs=[vmem],
        scratch_shapes=loaded + [pltpu.SemaphoreType.DMA((3,))],
        compiler_params=params,
        name="pick",
    )(*in_hbm(*operands))
    far_block = after(far_block, sent_coef)
    far_coef = flip(after(sent_coef, far_block), "shell", group)
    far_pair = merged("far_pair", far_block, after(flip(far_block, "aux", 2), *near[:3]))
    far_pairs = [far_pair, flip(far_pair, "aux", 1)]
    regrouped = pl.pallas_call(
        functools.partial(regroup_kernel, group),
        out_shape=[jax.ShapeDtypeStruct((group * pairs_dev * occ_local, BS), jnp.bfloat16)]
        * (aux_count - 1),
        in_specs=[vmem] * group,
        out_specs=[vmem] * (aux_count - 1),
        compiler_params=params,
        name="regroup",
    )(*near)
    others = [flip(one, "aux", j) for j, one in enumerate(regrouped, 1)]
    far = []
    for low in range(2):
        far = pl.pallas_call(
            functools.partial(block_kernel, aux_count, low),
            out_shape=[piece] * group,
            in_specs=[vmem] * (2 + len(far)),
            out_specs=[vmem] * group,
            input_output_aliases={2 + f: f for f in range(len(far))},
            compiler_params=params,
            cost_estimate=cost(2e9) if low == 0 else None,
            name=f"far_blocks_{low}",
        )(far_coef, far_pairs[low], *far)
    total_shape = jax.ShapeDtypeStruct((block_count, rows, BS), jnp.float32)
    total, mix = pl.pallas_call(
        functools.partial(near_sum_kernel, group),
        out_shape=[total_shape, jax.ShapeDtypeStruct((rows, rows), jnp.bfloat16)],
        in_specs=[hbm] + [vmem] * (group + aux_count - 1),
        out_specs=[vmem] * 2,
        scratch_shapes=[
            pltpu.VMEM(metric.shape, jnp.bfloat16),
            pltpu.VMEM((8, BS), jnp.int32),
            pltpu.SemaphoreType.DMA,
        ],
        compiler_params=params,
        cost_estimate=cost(3e9),
        name="near_sum",
    )(*in_hbm(metric), *(after(one, far[0]) for one in near), *others)
    far = [far[0]] + [flip(far[f], "shell", f) for f in range(1, group)]
    return pl.pallas_call(
        collect_kernel,
        out_shape=[
            jax.ShapeDtypeStruct((occ_local, aux_count, block_count * BS), jnp.bfloat16),
            total_shape,
        ],
        in_specs=[vmem] * (2 + group),
        out_specs=[hbm, vmem],
        input_output_aliases={1: 1},
        scratch_shapes=[
            pltpu.VMEM((occ_local, aux_count, block_count * BS), jnp.bfloat16),
            pltpu.VMEM((8, BS), jnp.int32),
            pltpu.SemaphoreType.DMA((4,)),
        ],
        compiler_params=params,
        name="collect",
    )(mix, total, *far)[0]


def per_device(integrals, pair_list, coef, metric, occ_slot):
    shell_count, aux_count = lax.axis_size("shell"), lax.axis_size("aux")
    occ_local = coef.shape[1] // (shell_count * aux_count)
    if occ_local % 16 or shell_count & (shell_count - 1) or aux_count != 4:
        return relayed_half_blocks(integrals, pair_list, coef, metric, occ_slot)
    return exchanged_inputs(integrals, pair_list, coef, metric, occ_slot)


def solution(mesh):
    placed = (P("shell", None, "aux", None), P("shell", None), P("shell", None), P(), P())
    return jax.shard_map(
        per_device,
        mesh=mesh,
        in_specs=placed,
        out_specs=P(("shell", "aux"), None, None),
        check_vma=False,
    )
```

```python
import functools

import jax
import jax.numpy as jnp
from jax import lax
from jax.experimental import pallas as pl
from jax.experimental.pallas import tpu as pltpu
from jax.sharding import PartitionSpec as P

BS = 128


def relayed_half_blocks(integrals, pair_list, coef, metric, occ_slot):
    pairs_dev = pair_list.shape[0]
    rows_local = coef.shape[0]
    occ_count = coef.shape[1]
    blocks_dev = rows_local // BS
    shell_count = lax.axis_size("shell")
    block_count = blocks_dev * shell_count
    slot_count = occ_slot.shape[0]
    aux_dev = integrals.shape[2]
    inverse = (
        jnp.zeros((slot_count,), jnp.int32)
        .at[occ_slot]
        .set(jnp.arange(slot_count, dtype=jnp.int32))
    )
    ordered = jnp.take(
        coef.reshape(rows_local, slot_count, occ_count // slot_count), inverse, axis=1
    )
    ordered = ordered.reshape(rows_local, occ_count)

    def one_slot(item):
        int_block, column_index = item
        start = column_index % blocks_dev * BS
        column = lax.dynamic_slice_in_dim(ordered, start, BS, 0)
        product = lax.dot_general(
            column,
            int_block.reshape(BS, aux_dev * BS),
            (((0,), (0,)), ((), ())),
            preferred_element_type=jnp.float32,
        )
        return product.astype(jnp.bfloat16)

    half_blocks = lax.map(one_slot, (integrals, pair_list[:, 1]))
    half_blocks = half_blocks.reshape(pairs_dev, occ_count, aux_dev, BS)
    listing = lax.all_gather(pair_list, "shell", axis=0, tiled=True)
    targets = jnp.arange(block_count, dtype=jnp.int32)[:, None]
    selector = ((listing[:, 0][None, :] == targets) & (listing[:, 2][None, :] == 1)).astype(
        jnp.bfloat16
    )
    relayed = lax.all_to_all(
        lax.all_to_all(half_blocks, "shell", split_axis=1, concat_axis=0, tiled=True),
        "aux",
        split_axis=1,
        concat_axis=2,
        tiled=True,
    )
    summed = jnp.dot(
        selector, relayed.reshape(relayed.shape[0], -1), preferred_element_type=jnp.float32
    )
    blocks = summed.astype(jnp.bfloat16).reshape((block_count,) + relayed.shape[1:])
    result = jnp.einsum("qp,bipm->iqbm", metric, blocks, preferred_element_type=jnp.float32)
    return result.reshape(result.shape[0], result.shape[1], block_count * BS).astype(jnp.bfloat16)


def targets_of(slot_row, block_total, occ_count):
    width = occ_count // block_total
    spread = (
        lax.broadcasted_iota(jnp.int32, (block_total, occ_count), 1) // width
        == lax.broadcasted_iota(jnp.int32, (block_total, occ_count), 0)
    ).astype(jnp.bfloat16)
    slots = jnp.broadcast_to(slot_row, (8, block_total)).astype(jnp.float32)
    target = jnp.dot(slots.astype(jnp.bfloat16), spread, preferred_element_type=jnp.float32)
    return target.astype(jnp.int32)[:1] * width + (
        lax.broadcasted_iota(jnp.int32, (1, occ_count), 1) % width
    )


def code_tile(pairs):
    pairs_dev = pairs.shape[0]
    lane = lax.broadcasted_iota(jnp.int32, (1, BS), 1)
    code = jnp.zeros((1, BS), jnp.int32)
    for k in range(pairs_dev):
        code = jnp.where(lane == k, pairs[k, 0] % 128, code)
        code = jnp.where(lane == pairs_dev + k, pairs[k, 0] // 128, code)
    return jnp.broadcast_to(code.astype(jnp.float32), (16, BS)).astype(jnp.bfloat16)


def pick_kernel(
    flips,
    occ_local,
    aux_count,
    pairs_in,
    slot_in,
    coef_in,
    *refs,
):
    *outs, pairs, slot_row, coef, sems = refs
    pairs_dev = pairs.shape[0]
    blocks_dev = coef.shape[0] // BS
    occ_count = coef.shape[1]
    loads = [
        pltpu.make_async_copy(source, target, sems.at[at])
        for at, (source, target) in enumerate(
            ((slot_in, slot_row), (pairs_in, pairs), (coef_in, coef))
        )
    ]
    for load in loads:
        load.start()
    me = lax.axis_index("shell")
    mine = lax.axis_index("aux")
    every = sum(flips, [])
    row = lax.broadcasted_iota(jnp.int32, (len(every) * occ_local, 1), 0)
    owner = sum(jnp.where(row // occ_local == at, f, 0) for at, f in enumerate(every))
    wanted = (jnp.bitwise_xor(owner, me) * aux_count + mine) * occ_local + row % occ_local
    loads[0].wait()
    target = targets_of(slot_row[...], slot_row.shape[1], occ_count)
    pick = (wanted == target).astype(jnp.bfloat16)
    for load in loads[1:]:
        load.wait()
    code = code_tile(pairs)
    for k in range(pairs_dev):
        start = pl.multiple_of(lax.rem(pairs[k, 1], blocks_dev) * BS, BS)
        live = (pairs[k, 2] == 1).astype(jnp.float32)
        piece = lax.dot_general(
            pick,
            coef[pl.ds(start, BS), :],
            (((1,), (1,)), ((), ())),
            preferred_element_type=jnp.float32,
        )
        piece = (piece * live).astype(jnp.bfloat16)
        first = 0
        for out in outs:
            rows = out.shape[0] - 16
            out[:rows, k * BS : (k + 1) * BS] = piece[first : first + rows]
            out[rows:, k * BS : (k + 1) * BS] = code
            first += rows


def near_kernel(
    occ_local,
    aux_count,
    pairs_in,
    slot_in,
    coef_in,
    blocks_in,
    *refs,
):
    *outs, pairs, slot_row, coef, blocks, sems = refs
    pairs_dev = pairs.shape[0]
    blocks_dev = coef.shape[0] // BS
    occ_count = coef.shape[1]
    loads = [
        pltpu.make_async_copy(source, target, sems.at[at])
        for at, (source, target) in enumerate(
            ((slot_in, slot_row), (pairs_in, pairs), (coef_in, coef), (blocks_in, blocks))
        )
    ]
    for load in loads:
        load.start()
    me = lax.axis_index("shell")
    mine = lax.axis_index("aux")
    owned = aux_count * occ_local
    row = lax.broadcasted_iota(jnp.int32, (len(outs) * owned, 1), 0)
    owner = jnp.bitwise_xor(row // owned, me) * aux_count + jnp.bitwise_xor(
        row // occ_local % aux_count, mine
    )
    wanted = owner * occ_local + row % occ_local
    loads[0].wait()
    target = targets_of(slot_row[...], slot_row.shape[1], occ_count)
    pick = (wanted == target).astype(jnp.bfloat16)
    for load in loads[1:]:
        load.wait()
    code = code_tile(pairs)
    rows = [
        coef[pl.ds(pl.multiple_of(lax.rem(pairs[k, 1], blocks_dev) * BS, BS), BS), :]
        for k in range(pairs_dev)
    ]
    ordered = lax.dot_general(
        pick,
        jnp.concatenate(rows, axis=0),
        (((1,), (1,)), ((), ())),
        preferred_element_type=jnp.float32,
    ).astype(jnp.bfloat16)
    for k in range(pairs_dev):
        block = jnp.dot(
            ordered[:, k * BS : (k + 1) * BS], blocks[k], preferred_element_type=jnp.float32
        )
        block = (block * (pairs[k, 2] == 1).astype(jnp.float32)).astype(jnp.bfloat16)
        for f, out in enumerate(outs):
            for j in range(aux_count):
                first = f * owned + j * occ_local
                at = (j * pairs_dev + k) * occ_local
                out[at : at + occ_local, :] = block[first : first + occ_local, :]
    for out in outs:
        out[pairs_dev * owned :, :] = code


def regroup_kernel(count, *refs):
    received, outs = refs[:count], refs[count:]
    rows = outs[0].shape[0] // count
    for j, out in enumerate(outs, 1):
        for f, piece in enumerate(received):
            out[f * rows : (f + 1) * rows, :] = piece[j * rows : (j + 1) * rows, :]


def merge_kernel(first, second, out, sems):
    count = first.shape[0]
    skip = second.shape[0] - count
    loads = [
        pltpu.make_async_copy(first, out.at[:count], sems.at[0]),
        pltpu.make_async_copy(second.at[skip:], out.at[count:], sems.at[1]),
    ]
    for load in loads:
        load.start()
    for load in loads:
        load.wait()


def block_kernel(aux_count, low, coefs, blocks, *refs):
    pieces = refs[len(refs) // 2 :] if low else refs
    pairs_dev = blocks.shape[0] // 2
    rows = coefs.shape[0] - 16
    occ_local = rows // len(pieces)
    mine = lax.axis_index("aux")
    for k in range(pairs_dev):
        left = coefs[:rows, k * BS : (k + 1) * BS]
        right = jnp.concatenate([blocks[k], blocks[pairs_dev + k]], axis=1)
        half = jnp.dot(left, right, preferred_element_type=jnp.float32).astype(jnp.bfloat16)
        for side in range(2):
            flipped = low + side * (aux_count // 2)
            at = k * aux_count + jnp.bitwise_xor(mine, flipped)
            start = pl.multiple_of(at * occ_local, occ_local)
            for f, piece in enumerate(pieces):
                piece[pl.ds(start, occ_local), :] = half[
                    f * occ_local : (f + 1) * occ_local, side * BS : (side + 1) * BS
                ]
    if low == 0:
        for piece in pieces:
            piece[pairs_dev * aux_count * occ_local :, :] = coefs[rows:, :BS]


def read_codes(received, pairs_dev, codes):
    for at, piece in enumerate(received):
        digits = piece[piece.shape[0] - 16 :, :].astype(jnp.float32)[:1]
        high = pltpu.roll(digits, BS - pairs_dev, 1)
        codes[at : at + 1, :] = (digits + 128.0 * high).astype(jnp.int32)


def near_sum_kernel(count, metric_in, *refs):
    *received, total, mix, metric, codes, sem = refs
    received, others = received[:count], received[count:]
    load = pltpu.make_async_copy(metric_in, metric, sem)
    load.start()
    total[...] = jnp.zeros_like(total)
    mine = lax.axis_index("aux")
    rows = total.shape[1]
    occ_local = rows // metric.shape[0]
    pairs_dev = (received[0].shape[0] - 16) // rows
    read_codes(received, pairs_dev, codes)
    for f in range(count):
        for k in range(pairs_dev):
            r = codes[f, k]
            for j in range(len(others) + 1):
                source, first = (others[j - 1], f * pairs_dev + k) if j else (received[f], k)
                start = pl.multiple_of(jnp.bitwise_xor(mine, j) * occ_local, occ_local)
                part = source[first * occ_local : (first + 1) * occ_local, :]
                total[r, pl.ds(start, occ_local), :] += part.astype(jnp.float32)
    load.wait()
    aux_count = metric.shape[0]
    row = lax.broadcasted_iota(jnp.int32, (rows, rows), 0)
    column = lax.broadcasted_iota(jnp.int32, (rows, rows), 1)
    left = (
        lax.broadcasted_iota(jnp.int32, (rows, aux_count), 0) % aux_count
        == lax.broadcasted_iota(jnp.int32, (rows, aux_count), 1)
    ).astype(jnp.bfloat16)
    right = (
        lax.broadcasted_iota(jnp.int32, (aux_count, rows), 1) // occ_local
        == lax.broadcasted_iota(jnp.int32, (aux_count, rows), 0)
    ).astype(jnp.bfloat16)
    factor = jnp.dot(left, metric[...], preferred_element_type=jnp.float32).astype(jnp.bfloat16)
    factor = jnp.dot(factor, right, preferred_element_type=jnp.float32)
    mix[...] = jnp.where(row // aux_count == column % occ_local, factor, 0.0).astype(jnp.bfloat16)


def collect_kernel(mix, total_in, *refs):
    *received, out, total, staged, codes, sems = refs
    occ_local, aux_count = out.shape[:2]
    rows = total.shape[1]
    pairs_dev = (received[0].shape[0] - 16) // rows
    read_codes(received, pairs_dev, codes)
    for at, piece in enumerate(received):
        for k in range(pairs_dev):
            total[codes[at, k]] += piece[k * rows : (k + 1) * rows, :].astype(jnp.float32)
    stores = []
    parts = sems.shape[0]
    each = total.shape[0] // parts
    for part in range(parts):
        for r in range(part * each, (part + 1) * each, 2):
            summed = jnp.concatenate([total[r], total[r + 1]], axis=1).astype(jnp.bfloat16)
            mixed = jnp.dot(mix[...], summed, preferred_element_type=jnp.float32)
            staged[:, :, r * BS : (r + 2) * BS] = mixed.reshape(
                occ_local, aux_count, 2 * BS
            ).astype(jnp.bfloat16)
        lanes = pl.ds(part * each * BS, each * BS)
        store = pltpu.make_async_copy(
            staged.at[:, :, lanes], out.at[:, :, lanes], sems.at[part]
        )
        store.start()
        stores.append(store)
    for store in stores:
        store.wait()

def flip(value, axis, bits):
    count = lax.axis_size(axis)
    return lax.ppermute(value, axis, [(at, at ^ bits) for at in range(count)])


def after(value, *others):
    return lax.optimization_barrier((value, *others))[0]


def cost(flops):
    return pl.CostEstimate(flops=int(flops), transcendentals=0, bytes_accessed=2**20)


def in_hbm(*operands):
    return [pltpu.with_memory_space_constraint(operand, pltpu.HBM) for operand in operands]


def exchanged_inputs(integrals, pair_list, coef, metric, occ_slot):
    pairs_dev = pair_list.shape[0]
    shell_count = lax.axis_size("shell")
    aux_count = lax.axis_size("aux")
    group = shell_count // 2
    occ_local = coef.shape[1] // (shell_count * aux_count)
    block_count = coef.shape[0] // BS * shell_count
    rows = occ_local * aux_count
    piece = jax.ShapeDtypeStruct((pairs_dev * rows + 16, BS), jnp.bfloat16)
    vmem = pl.BlockSpec(memory_space=pltpu.VMEM)
    hbm = pl.BlockSpec(memory_space=pltpu.HBM)
    params = pltpu.CompilerParams(vmem_limit_bytes=40 * 2**20)

    def merged(name, first, second):
        return pl.pallas_call(
            merge_kernel,
            out_shape=jax.ShapeDtypeStruct(
                (2 * first.shape[0],) + first.shape[1:], jnp.bfloat16
            ),
            in_specs=[vmem] * 2,
            out_specs=vmem,
            scratch_shapes=[pltpu.SemaphoreType.DMA((2,))],
            compiler_params=params,
            name=name,
        )(first, second)

    blocks = integrals.reshape(pairs_dev, BS, BS)
    far_block = flip(blocks, "shell", group)
    operands = (pair_list, occ_slot.reshape(1, -1), coef)
    loaded = [
        pltpu.SMEM(pair_list.shape, jnp.int32),
        pltpu.VMEM((1, occ_slot.shape[0]), jnp.int32),
        pltpu.VMEM(coef.shape, jnp.bfloat16),
    ]
    near = pl.pallas_call(
        functools.partial(near_kernel, occ_local, aux_count),
        out_shape=[piece] * group,
        in_specs=[hbm] * 4,
        out_specs=[vmem] * group,
        scratch_shapes=loaded
        + [pltpu.VMEM(blocks.shape, jnp.bfloat16), pltpu.SemaphoreType.DMA((4,))],
        compiler_params=params,
        name="near_blocks",
    )(*in_hbm(*operands, blocks))
    near = [near[0]] + [flip(near[f], "shell", f) for f in range(1, group)]
    (sent_coef,) = pl.pallas_call(
        functools.partial(
            pick_kernel, [list(range(group, shell_count))], occ_local, aux_count
        ),
        out_shape=[
            jax.ShapeDtypeStruct((group * occ_local + 16, pairs_dev * BS), jnp.bfloat16)
        ],
        in_specs=[hbm] * 3,
        out_specs=[vmem],
        scratch_shapes=loaded + [pltpu.SemaphoreType.DMA((3,))],
        compiler_params=params,
        name="pick",
    )(*in_hbm(*operands))
    far_block = after(far_block, sent_coef)
    far_coef = flip(after(sent_coef, far_block), "shell", group)
    far_pair = merged("far_pair", far_block, after(flip(far_block, "aux", 2), near[2],near[3]))
    far_pairs = [far_pair, flip(far_pair, "aux", 1)]
    regrouped = pl.pallas_call(
        functools.partial(regroup_kernel, group),
        out_shape=[jax.ShapeDtypeStruct((group * pairs_dev * occ_local, BS), jnp.bfloat16)]
        * (aux_count - 1),
        in_specs=[vmem] * group,
        out_specs=[vmem] * (aux_count - 1),
        compiler_params=params,
        name="regroup",
    )(*near)
    others = [flip(one, "aux", j) for j, one in enumerate(regrouped, 1)]
    far = []
    for low in range(2):
        far = pl.pallas_call(
            functools.partial(block_kernel, aux_count, low),
            out_shape=[piece] * group,
            in_specs=[vmem] * (2 + len(far)),
            out_specs=[vmem] * group,
            input_output_aliases={2 + f: f for f in range(len(far))},
            compiler_params=params,
            cost_estimate=cost(2e9) if low == 0 else None,
            name=f"far_blocks_{low}",
        )(far_coef, far_pairs[low], *far)
    total_shape = jax.ShapeDtypeStruct((block_count, rows, BS), jnp.float32)
    total, mix = pl.pallas_call(
        functools.partial(near_sum_kernel, group),
        out_shape=[total_shape, jax.ShapeDtypeStruct((rows, rows), jnp.bfloat16)],
        in_specs=[hbm] + [vmem] * (group + aux_count - 1),
        out_specs=[vmem] * 2,
        scratch_shapes=[
            pltpu.VMEM(metric.shape, jnp.bfloat16),
            pltpu.VMEM((8, BS), jnp.int32),
            pltpu.SemaphoreType.DMA,
        ],
        compiler_params=params,
        cost_estimate=cost(3e9),
        name="near_sum",
    )(*in_hbm(metric), *(after(one, far[0]) for one in near), *others)
    far = [far[0]] + [flip(far[f], "shell", f) for f in range(1, group)]
    return pl.pallas_call(
        collect_kernel,
        out_shape=[
            jax.ShapeDtypeStruct((occ_local, aux_count, block_count * BS), jnp.bfloat16),
            total_shape,
        ],
        in_specs=[vmem] * (2 + group),
        out_specs=[hbm, vmem],
        input_output_aliases={1: 1},
        scratch_shapes=[
            pltpu.VMEM((occ_local, aux_count, block_count * BS), jnp.bfloat16),
            pltpu.VMEM((8, BS), jnp.int32),
            pltpu.SemaphoreType.DMA((4,)),
        ],
        compiler_params=params,
        name="collect",
    )(mix, total, *far)[0]


def per_device(integrals, pair_list, coef, metric, occ_slot):
    shell_count, aux_count = lax.axis_size("shell"), lax.axis_size("aux")
    occ_local = coef.shape[1] // (shell_count * aux_count)
    if occ_local % 16 or shell_count & (shell_count - 1) or aux_count != 4:
        return relayed_half_blocks(integrals, pair_list, coef, metric, occ_slot)
    return exchanged_inputs(integrals, pair_list, coef, metric, occ_slot)


def solution(mesh):
    placed = (P("shell", None, "aux", None), P("shell", None), P("shell", None), P(), P())
    return jax.shard_map(
        per_device,
        mesh=mesh,
        in_specs=placed,
        out_specs=P(("shell", "aux"), None, None),
        check_vma=False,
    )
```

```python
import functools

import jax
import jax.numpy as jnp
from jax import lax
from jax.experimental import pallas as pl
from jax.experimental.pallas import tpu as pltpu
from jax.sharding import PartitionSpec as P

BS = 128


def relayed_half_blocks(integrals, pair_list, coef, metric, occ_slot):
    pairs_dev = pair_list.shape[0]
    rows_local = coef.shape[0]
    occ_count = coef.shape[1]
    blocks_dev = rows_local // BS
    shell_count = lax.axis_size("shell")
    block_count = blocks_dev * shell_count
    slot_count = occ_slot.shape[0]
    aux_dev = integrals.shape[2]
    inverse = (
        jnp.zeros((slot_count,), jnp.int32)
        .at[occ_slot]
        .set(jnp.arange(slot_count, dtype=jnp.int32))
    )
    ordered = jnp.take(
        coef.reshape(rows_local, slot_count, occ_count // slot_count), inverse, axis=1
    )
    ordered = ordered.reshape(rows_local, occ_count)

    def one_slot(item):
        int_block, column_index = item
        start = column_index % blocks_dev * BS
        column = lax.dynamic_slice_in_dim(ordered, start, BS, 0)
        product = lax.dot_general(
            column,
            int_block.reshape(BS, aux_dev * BS),
            (((0,), (0,)), ((), ())),
            preferred_element_type=jnp.float32,
        )
        return product.astype(jnp.bfloat16)

    half_blocks = lax.map(one_slot, (integrals, pair_list[:, 1]))
    half_blocks = half_blocks.reshape(pairs_dev, occ_count, aux_dev, BS)
    listing = lax.all_gather(pair_list, "shell", axis=0, tiled=True)
    targets = jnp.arange(block_count, dtype=jnp.int32)[:, None]
    selector = ((listing[:, 0][None, :] == targets) & (listing[:, 2][None, :] == 1)).astype(
        jnp.bfloat16
    )
    relayed = lax.all_to_all(
        lax.all_to_all(half_blocks, "shell", split_axis=1, concat_axis=0, tiled=True),
        "aux",
        split_axis=1,
        concat_axis=2,
        tiled=True,
    )
    summed = jnp.dot(
        selector, relayed.reshape(relayed.shape[0], -1), preferred_element_type=jnp.float32
    )
    blocks = summed.astype(jnp.bfloat16).reshape((block_count,) + relayed.shape[1:])
    result = jnp.einsum("qp,bipm->iqbm", metric, blocks, preferred_element_type=jnp.float32)
    return result.reshape(result.shape[0], result.shape[1], block_count * BS).astype(jnp.bfloat16)


def targets_of(slot_row, block_total, occ_count):
    width = occ_count // block_total
    spread = (
        lax.broadcasted_iota(jnp.int32, (block_total, occ_count), 1) // width
        == lax.broadcasted_iota(jnp.int32, (block_total, occ_count), 0)
    ).astype(jnp.bfloat16)
    slots = jnp.broadcast_to(slot_row, (8, block_total)).astype(jnp.float32)
    target = jnp.dot(slots.astype(jnp.bfloat16), spread, preferred_element_type=jnp.float32)
    return target.astype(jnp.int32)[:1] * width + (
        lax.broadcasted_iota(jnp.int32, (1, occ_count), 1) % width
    )


def code_tile(pairs):
    pairs_dev = pairs.shape[0]
    lane = lax.broadcasted_iota(jnp.int32, (1, BS), 1)
    code = jnp.zeros((1, BS), jnp.int32)
    for k in range(pairs_dev):
        code = jnp.where(lane == k, pairs[k, 0] % 128, code)
        code = jnp.where(lane == pairs_dev + k, pairs[k, 0] // 128, code)
    return jnp.broadcast_to(code.astype(jnp.float32), (16, BS)).astype(jnp.bfloat16)


def pick_kernel(
    flips,
    occ_local,
    aux_count,
    pairs_in,
    slot_in,
    coef_in,
    *refs,
):
    *outs, pairs, slot_row, coef, sems = refs
    pairs_dev = pairs.shape[0]
    blocks_dev = coef.shape[0] // BS
    occ_count = coef.shape[1]
    loads = [
        pltpu.make_async_copy(source, target, sems.at[at])
        for at, (source, target) in enumerate(
            ((slot_in, slot_row), (pairs_in, pairs), (coef_in, coef))
        )
    ]
    for load in loads:
        load.start()
    me = lax.axis_index("shell")
    mine = lax.axis_index("aux")
    every = sum(flips, [])
    row = lax.broadcasted_iota(jnp.int32, (len(every) * occ_local, 1), 0)
    owner = sum(jnp.where(row // occ_local == at, f, 0) for at, f in enumerate(every))
    wanted = (jnp.bitwise_xor(owner, me) * aux_count + mine) * occ_local + row % occ_local
    loads[0].wait()
    target = targets_of(slot_row[...], slot_row.shape[1], occ_count)
    pick = (wanted == target).astype(jnp.bfloat16)
    for load in loads[1:]:
        load.wait()
    code = code_tile(pairs)
    for k in range(pairs_dev):
        start = pl.multiple_of(lax.rem(pairs[k, 1], blocks_dev) * BS, BS)
        live = (pairs[k, 2] == 1).astype(jnp.float32)
        piece = lax.dot_general(
            pick,
            coef[pl.ds(start, BS), :],
            (((1,), (1,)), ((), ())),
            preferred_element_type=jnp.float32,
        )
        piece = (piece * live).astype(jnp.bfloat16)
        first = 0
        for out in outs:
            rows = out.shape[0] - 16
            out[:rows, k * BS : (k + 1) * BS] = piece[first : first + rows]
            out[rows:, k * BS : (k + 1) * BS] = code
            first += rows


def near_kernel(
    occ_local,
    aux_count,
    pairs_in,
    slot_in,
    coef_in,
    blocks_in,
    beside,
    *refs,
):
    *outs, pairs, slot_row, coef, blocks, sems = refs
    pairs_dev = pairs.shape[0]
    blocks_dev = coef.shape[0] // BS
    occ_count = coef.shape[1]
    loads = [
        pltpu.make_async_copy(source, target, sems.at[at])
        for at, (source, target) in enumerate(
            ((slot_in, slot_row), (pairs_in, pairs), (coef_in, coef), (blocks_in, blocks))
        )
    ]
    for load in loads:
        load.start()
    me = lax.axis_index("shell")
    mine = lax.axis_index("aux")
    owned = aux_count // 2 * occ_local
    row = lax.broadcasted_iota(jnp.int32, (len(outs) * owned, 1), 0)
    owner = jnp.bitwise_xor(row // owned, me) * aux_count + jnp.bitwise_xor(
        row // occ_local % (aux_count // 2) * 2, mine
    )
    wanted = owner * occ_local + row % occ_local
    loads[0].wait()
    target = targets_of(slot_row[...], slot_row.shape[1], occ_count)
    pick = (wanted == target).astype(jnp.bfloat16)
    for load in loads[1:]:
        load.wait()
    code = code_tile(pairs)
    rows = [
        coef[pl.ds(pl.multiple_of(lax.rem(pairs[k, 1], blocks_dev) * BS, BS), BS), :]
        for k in range(pairs_dev)
    ]
    ordered = lax.dot_general(
        pick,
        jnp.concatenate(rows, axis=0),
        (((1,), (1,)), ((), ())),
        preferred_element_type=jnp.float32,
    ).astype(jnp.bfloat16)
    for k in range(pairs_dev):
        block = jnp.dot(
            ordered[:, k * BS : (k + 1) * BS],
            jnp.concatenate([blocks[k], beside[k]], axis=1),
            preferred_element_type=jnp.float32,
        )
        block = (block * (pairs[k, 2] == 1).astype(jnp.float32)).astype(jnp.bfloat16)
        for f, out in enumerate(outs):
            for j in range(aux_count // 2):
                first = f * owned + j * occ_local
                for c in range(2):
                    at = ((j * 2 + c) * pairs_dev + k) * occ_local
                    out[at : at + occ_local, :] = block[
                        first : first + occ_local, c * BS : (c + 1) * BS
                    ]
    for out in outs:
        out[out.shape[0] - 16 :, :] = code


def regroup_kernel(*refs):
    *received, out = refs
    rows = out.shape[0] // len(received)
    for f, piece in enumerate(received):
        out[f * rows : (f + 1) * rows, :] = piece[rows : 2 * rows, :]


def merge_kernel(first, second, out, sems):
    count = first.shape[0]
    skip = second.shape[0] - count
    loads = [
        pltpu.make_async_copy(first, out.at[:count], sems.at[0]),
        pltpu.make_async_copy(second.at[skip:], out.at[count:], sems.at[1]),
    ]
    for load in loads:
        load.start()
    for load in loads:
        load.wait()


def block_kernel(aux_count, low, coefs, blocks, *refs):
    pieces = refs[len(refs) // 2 :] if low else refs
    pairs_dev = blocks.shape[0] // 2
    rows = coefs.shape[0] - 16
    occ_local = rows // len(pieces)
    mine = lax.axis_index("aux")
    for k in range(pairs_dev):
        left = coefs[:rows, k * BS : (k + 1) * BS]
        right = jnp.concatenate([blocks[k], blocks[pairs_dev + k]], axis=1)
        half = jnp.dot(left, right, preferred_element_type=jnp.float32).astype(jnp.bfloat16)
        for side in range(2):
            flipped = low + side * (aux_count // 2)
            at = k * aux_count + jnp.bitwise_xor(mine, flipped)
            start = pl.multiple_of(at * occ_local, occ_local)
            for f, piece in enumerate(pieces):
                piece[pl.ds(start, occ_local), :] = half[
                    f * occ_local : (f + 1) * occ_local, side * BS : (side + 1) * BS
                ]
    if low == 0:
        for piece in pieces:
            piece[pairs_dev * aux_count * occ_local :, :] = coefs[rows:, :BS]


def read_codes(received, pairs_dev, codes):
    for at, piece in enumerate(received):
        digits = piece[piece.shape[0] - 16 :, :].astype(jnp.float32)[:1]
        high = pltpu.roll(digits, BS - pairs_dev, 1)
        codes[at : at + 1, :] = (digits + 128.0 * high).astype(jnp.int32)


def near_sum_kernel(metric_in, *refs):
    *received, across, total, mix, metric, codes, sem = refs
    load = pltpu.make_async_copy(metric_in, metric, sem)
    load.start()
    total[...] = jnp.zeros_like(total)
    mine = lax.axis_index("aux")
    rows = total.shape[1]
    occ_local = rows // metric.shape[0]
    pairs_dev = (received[0].shape[0] - 16) // rows
    read_codes(received, pairs_dev, codes)
    for f, piece in enumerate(received):
        for k in range(pairs_dev):
            r = codes[f, k]
            for j in range(metric.shape[0]):
                source, first = (across, f * 2 + j - 2) if j >= 2 else (piece, j)
                first = (first * pairs_dev + k) * occ_local
                start = pl.multiple_of(jnp.bitwise_xor(mine, j) * occ_local, occ_local)
                part = source[first : first + occ_local, :]
                total[r, pl.ds(start, occ_local), :] += part.astype(jnp.float32)
    load.wait()
    aux_count = metric.shape[0]
    row = lax.broadcasted_iota(jnp.int32, (rows, rows), 0)
    column = lax.broadcasted_iota(jnp.int32, (rows, rows), 1)
    left = (
        lax.broadcasted_iota(jnp.int32, (rows, aux_count), 0) % aux_count
        == lax.broadcasted_iota(jnp.int32, (rows, aux_count), 1)
    ).astype(jnp.bfloat16)
    right = (
        lax.broadcasted_iota(jnp.int32, (aux_count, rows), 1) // occ_local
        == lax.broadcasted_iota(jnp.int32, (aux_count, rows), 0)
    ).astype(jnp.bfloat16)
    factor = jnp.dot(left, metric[...], preferred_element_type=jnp.float32).astype(jnp.bfloat16)
    factor = jnp.dot(factor, right, preferred_element_type=jnp.float32)
    mix[...] = jnp.where(row // aux_count == column % occ_local, factor, 0.0).astype(jnp.bfloat16)


def collect_kernel(mix, total_in, *refs):
    *received, out, total, staged, codes, sems = refs
    occ_local, aux_count = out.shape[:2]
    rows = total.shape[1]
    pairs_dev = (received[0].shape[0] - 16) // rows
    read_codes(received, pairs_dev, codes)
    for at, piece in enumerate(received):
        for k in range(pairs_dev):
            total[codes[at, k]] += piece[k * rows : (k + 1) * rows, :].astype(jnp.float32)
    stores = []
    parts = sems.shape[0]
    each = total.shape[0] // parts
    for part in range(parts):
        for r in range(part * each, (part + 1) * each, 2):
            summed = jnp.concatenate([total[r], total[r + 1]], axis=1).astype(jnp.bfloat16)
            mixed = jnp.dot(mix[...], summed, preferred_element_type=jnp.float32)
            staged[:, :, r * BS : (r + 2) * BS] = mixed.reshape(
                occ_local, aux_count, 2 * BS
            ).astype(jnp.bfloat16)
        lanes = pl.ds(part * each * BS, each * BS)
        store = pltpu.make_async_copy(
            staged.at[:, :, lanes], out.at[:, :, lanes], sems.at[part]
        )
        store.start()
        stores.append(store)
    for store in stores:
        store.wait()

def flip(value, axis, bits):
    count = lax.axis_size(axis)
    return lax.ppermute(value, axis, [(at, at ^ bits) for at in range(count)])


def after(value, *others):
    return lax.optimization_barrier((value, *others))[0]


def cost(flops):
    return pl.CostEstimate(flops=int(flops), transcendentals=0, bytes_accessed=2**20)


def in_hbm(*operands):
    return [pltpu.with_memory_space_constraint(operand, pltpu.HBM) for operand in operands]


def exchanged_inputs(integrals, pair_list, coef, metric, occ_slot):
    pairs_dev = pair_list.shape[0]
    shell_count = lax.axis_size("shell")
    aux_count = lax.axis_size("aux")
    group = shell_count // 2
    occ_local = coef.shape[1] // (shell_count * aux_count)
    block_count = coef.shape[0] // BS * shell_count
    rows = occ_local * aux_count
    piece = jax.ShapeDtypeStruct((pairs_dev * rows + 16, BS), jnp.bfloat16)
    vmem = pl.BlockSpec(memory_space=pltpu.VMEM)
    hbm = pl.BlockSpec(memory_space=pltpu.HBM)
    params = pltpu.CompilerParams(vmem_limit_bytes=40 * 2**20)

    def merged(name, first, second):
        return pl.pallas_call(
            merge_kernel,
            out_shape=jax.ShapeDtypeStruct(
                (2 * first.shape[0],) + first.shape[1:], jnp.bfloat16
            ),
            in_specs=[vmem] * 2,
            out_specs=vmem,
            scratch_shapes=[pltpu.SemaphoreType.DMA((2,))],
            compiler_params=params,
            name=name,
        )(first, second)

    blocks = integrals.reshape(pairs_dev, BS, BS)
    far_block = flip(blocks, "shell", group)
    operands = (pair_list, occ_slot.reshape(1, -1), coef)
    loaded = [
        pltpu.SMEM(pair_list.shape, jnp.int32),
        pltpu.VMEM((1, occ_slot.shape[0]), jnp.int32),
        pltpu.VMEM(coef.shape, jnp.bfloat16),
    ]
    near = pl.pallas_call(
        functools.partial(near_kernel, occ_local, aux_count),
        out_shape=[piece] * group,
        in_specs=[hbm] * 4 + [vmem],
        out_specs=[vmem] * group,
        scratch_shapes=loaded
        + [pltpu.VMEM(blocks.shape, jnp.bfloat16), pltpu.SemaphoreType.DMA((4,))],
        compiler_params=params,
        name="near_blocks",
    )(*in_hbm(*operands, blocks), flip(blocks, "aux", 1))
    near = [near[0]] + [flip(near[f], "shell", f) for f in range(1, group)]
    (sent_coef,) = pl.pallas_call(
        functools.partial(
            pick_kernel, [list(range(group, shell_count))], occ_local, aux_count
        ),
        out_shape=[
            jax.ShapeDtypeStruct((group * occ_local + 16, pairs_dev * BS), jnp.bfloat16)
        ],
        in_specs=[hbm] * 3,
        out_specs=[vmem],
        scratch_shapes=loaded + [pltpu.SemaphoreType.DMA((3,))],
        compiler_params=params,
        name="pick",
    )(*in_hbm(*operands))
    far_block = after(far_block, sent_coef)
    far_coef = flip(after(sent_coef, far_block), "shell", group)
    far_pair = merged("far_pair", far_block, flip(far_block, "aux", 2))
    far_pairs = [far_pair, flip(far_pair, "aux", 1)]
    across = flip(
        pl.pallas_call(
            regroup_kernel,
            out_shape=jax.ShapeDtypeStruct(
                (group * 2 * pairs_dev * occ_local, BS), jnp.bfloat16
            ),
            in_specs=[vmem] * group,
            out_specs=vmem,
            compiler_params=params,
            name="regroup",
        )(*near),
        "aux",
        2,
    )
    far = []
    for low in range(2):
        far = pl.pallas_call(
            functools.partial(block_kernel, aux_count, low),
            out_shape=[piece] * group,
            in_specs=[vmem] * (2 + len(far)),
            out_specs=[vmem] * group,
            input_output_aliases={2 + f: f for f in range(len(far))},
            compiler_params=params,
            cost_estimate=cost(2e9) if low == 0 else None,
            name=f"far_blocks_{low}",
        )(far_coef, far_pairs[low], *far)
    total_shape = jax.ShapeDtypeStruct((block_count, rows, BS), jnp.float32)
    total, mix = pl.pallas_call(
        near_sum_kernel,
        out_shape=[total_shape, jax.ShapeDtypeStruct((rows, rows), jnp.bfloat16)],
        in_specs=[hbm] + [vmem] * (group + 1),
        out_specs=[vmem] * 2,
        scratch_shapes=[
            pltpu.VMEM(metric.shape, jnp.bfloat16),
            pltpu.VMEM((8, BS), jnp.int32),
            pltpu.SemaphoreType.DMA,
        ],
        compiler_params=params,
        cost_estimate=cost(3e9),
        name="near_sum",
    )(*in_hbm(metric), *(after(one, far[0]) for one in near), across)
    far = [far[0]] + [flip(far[f], "shell", f) for f in range(1, group)]
    return pl.pallas_call(
        collect_kernel,
        out_shape=[
            jax.ShapeDtypeStruct((occ_local, aux_count, block_count * BS), jnp.bfloat16),
            total_shape,
        ],
        in_specs=[vmem] * (2 + group),
        out_specs=[hbm, vmem],
        input_output_aliases={1: 1},
        scratch_shapes=[
            pltpu.VMEM((occ_local, aux_count, block_count * BS), jnp.bfloat16),
            pltpu.VMEM((8, BS), jnp.int32),
            pltpu.SemaphoreType.DMA((4,)),
        ],
        compiler_params=params,
        name="collect",
    )(mix, total, *far)[0]


def per_device(integrals, pair_list, coef, metric, occ_slot):
    shell_count, aux_count = lax.axis_size("shell"), lax.axis_size("aux")
    occ_local = coef.shape[1] // (shell_count * aux_count)
    if occ_local % 16 or shell_count & (shell_count - 1) or aux_count != 4:
        return relayed_half_blocks(integrals, pair_list, coef, metric, occ_slot)
    return exchanged_inputs(integrals, pair_list, coef, metric, occ_slot)


def solution(mesh):
    placed = (P("shell", None, "aux", None), P("shell", None), P("shell", None), P(), P())
    return jax.shard_map(
        per_device,
        mesh=mesh,
        in_specs=placed,
        out_specs=P(("shell", "aux"), None, None),
        check_vma=False,
    )
```

```python
import functools

import jax
import jax.numpy as jnp
from jax import lax
from jax.experimental import pallas as pl
from jax.experimental.pallas import tpu as pltpu
from jax.sharding import PartitionSpec as P

BS = 128


def relayed_half_blocks(integrals, pair_list, coef, metric, occ_slot):
    pairs_dev = pair_list.shape[0]
    rows_local = coef.shape[0]
    occ_count = coef.shape[1]
    blocks_dev = rows_local // BS
    shell_count = lax.axis_size("shell")
    block_count = blocks_dev * shell_count
    slot_count = occ_slot.shape[0]
    aux_dev = integrals.shape[2]
    inverse = (
        jnp.zeros((slot_count,), jnp.int32)
        .at[occ_slot]
        .set(jnp.arange(slot_count, dtype=jnp.int32))
    )
    ordered = jnp.take(
        coef.reshape(rows_local, slot_count, occ_count // slot_count), inverse, axis=1
    )
    ordered = ordered.reshape(rows_local, occ_count)

    def one_slot(item):
        int_block, column_index = item
        start = column_index % blocks_dev * BS
        column = lax.dynamic_slice_in_dim(ordered, start, BS, 0)
        product = lax.dot_general(
            column,
            int_block.reshape(BS, aux_dev * BS),
            (((0,), (0,)), ((), ())),
            preferred_element_type=jnp.float32,
        )
        return product.astype(jnp.bfloat16)

    half_blocks = lax.map(one_slot, (integrals, pair_list[:, 1]))
    half_blocks = half_blocks.reshape(pairs_dev, occ_count, aux_dev, BS)
    listing = lax.all_gather(pair_list, "shell", axis=0, tiled=True)
    targets = jnp.arange(block_count, dtype=jnp.int32)[:, None]
    selector = ((listing[:, 0][None, :] == targets) & (listing[:, 2][None, :] == 1)).astype(
        jnp.bfloat16
    )
    relayed = lax.all_to_all(
        lax.all_to_all(half_blocks, "shell", split_axis=1, concat_axis=0, tiled=True),
        "aux",
        split_axis=1,
        concat_axis=2,
        tiled=True,
    )
    summed = jnp.dot(
        selector, relayed.reshape(relayed.shape[0], -1), preferred_element_type=jnp.float32
    )
    blocks = summed.astype(jnp.bfloat16).reshape((block_count,) + relayed.shape[1:])
    result = jnp.einsum("qp,bipm->iqbm", metric, blocks, preferred_element_type=jnp.float32)
    return result.reshape(result.shape[0], result.shape[1], block_count * BS).astype(jnp.bfloat16)


def targets_of(slot_row, block_total, occ_count):
    width = occ_count // block_total
    spread = (
        lax.broadcasted_iota(jnp.int32, (block_total, occ_count), 1) // width
        == lax.broadcasted_iota(jnp.int32, (block_total, occ_count), 0)
    ).astype(jnp.bfloat16)
    slots = jnp.broadcast_to(slot_row, (8, block_total)).astype(jnp.float32)
    target = jnp.dot(slots.astype(jnp.bfloat16), spread, preferred_element_type=jnp.float32)
    return target.astype(jnp.int32)[:1] * width + (
        lax.broadcasted_iota(jnp.int32, (1, occ_count), 1) % width
    )


def place_bits(at, aux):
    swapped = at - at % 4 + at % 2 * 2 + at // 2 % 2
    return jnp.where(aux % 2 == 1, at, swapped)


def code_tile(pairs):
    pairs_dev = pairs.shape[0]
    lane = lax.broadcasted_iota(jnp.int32, (1, BS), 1)
    code = jnp.zeros((1, BS), jnp.int32)
    for k in range(pairs_dev):
        code = jnp.where(lane == k, pairs[k, 0] % 128, code)
        code = jnp.where(lane == pairs_dev + k, pairs[k, 0] // 128, code)
    return jnp.broadcast_to(code.astype(jnp.float32), (16, BS)).astype(jnp.bfloat16)


def pick_kernel(
    group,
    occ_local,
    aux_count,
    pairs_in,
    slot_in,
    coef_in,
    out,
    pairs,
    slot_row,
    coef,
    sems,
):
    pairs_dev = pairs.shape[0]
    blocks_dev = coef.shape[0] // BS
    occ_count = coef.shape[1]
    loads = [
        pltpu.make_async_copy(source, target, sems.at[at])
        for at, (source, target) in enumerate(
            ((slot_in, slot_row), (pairs_in, pairs), (coef_in, coef))
        )
    ]
    for load in loads:
        load.start()
    me = lax.axis_index("shell")
    mine = lax.axis_index("aux")
    rows = group * occ_local
    row = lax.broadcasted_iota(jnp.int32, (rows, 1), 0)
    owner = group + place_bits(row // occ_local, mine)
    wanted = (jnp.bitwise_xor(owner, me) * aux_count + mine) * occ_local + row % occ_local
    loads[0].wait()
    target = targets_of(slot_row[...], slot_row.shape[1], occ_count)
    pick = (wanted == target).astype(jnp.bfloat16)
    for load in loads[1:]:
        load.wait()
    code = code_tile(pairs)
    for k in range(pairs_dev):
        start = pl.multiple_of(lax.rem(pairs[k, 1], blocks_dev) * BS, BS)
        live = (pairs[k, 2] == 1).astype(jnp.float32)
        piece = lax.dot_general(
            pick,
            coef[pl.ds(start, BS), :],
            (((1,), (1,)), ((), ())),
            preferred_element_type=jnp.float32,
        )
        piece = (piece * live).astype(jnp.bfloat16)
        out[:rows, k * BS : (k + 1) * BS] = piece
        out[rows:, k * BS : (k + 1) * BS] = code


def near_kernel(
    occ_local,
    aux_count,
    pairs_in,
    slot_in,
    coef_in,
    blocks_in,
    beside,
    *refs,
):
    *outs, pairs, slot_row, coef, blocks, sems = refs
    pairs_dev = pairs.shape[0]
    blocks_dev = coef.shape[0] // BS
    occ_count = coef.shape[1]
    loads = [
        pltpu.make_async_copy(source, target, sems.at[at])
        for at, (source, target) in enumerate(
            ((slot_in, slot_row), (pairs_in, pairs), (coef_in, coef), (blocks_in, blocks))
        )
    ]
    for load in loads:
        load.start()
    me = lax.axis_index("shell")
    mine = lax.axis_index("aux")
    owned = aux_count // 2 * occ_local
    row = lax.broadcasted_iota(jnp.int32, (len(outs) * owned, 1), 0)
    owner = jnp.bitwise_xor(place_bits(row // owned, mine), me) * aux_count + jnp.bitwise_xor(
        row // occ_local % (aux_count // 2) * 2, mine
    )
    wanted = owner * occ_local + row % occ_local
    loads[0].wait()
    target = targets_of(slot_row[...], slot_row.shape[1], occ_count)
    pick = (wanted == target).astype(jnp.bfloat16)
    for load in loads[1:]:
        load.wait()
    code = code_tile(pairs)
    rows = [
        coef[pl.ds(pl.multiple_of(lax.rem(pairs[k, 1], blocks_dev) * BS, BS), BS), :]
        for k in range(pairs_dev)
    ]
    ordered = lax.dot_general(
        pick,
        jnp.concatenate(rows, axis=0),
        (((1,), (1,)), ((), ())),
        preferred_element_type=jnp.float32,
    ).astype(jnp.bfloat16)
    for k in range(pairs_dev):
        block = jnp.dot(
            ordered[:, k * BS : (k + 1) * BS],
            jnp.concatenate([blocks[k], beside[k]], axis=1),
            preferred_element_type=jnp.float32,
        )
        block = (block * (pairs[k, 2] == 1).astype(jnp.float32)).astype(jnp.bfloat16)
        for f, out in enumerate(outs):
            for j in range(aux_count // 2):
                first = f * owned + j * occ_local
                for c in range(2):
                    at = ((j * 2 + c) * pairs_dev + k) * occ_local
                    out[at : at + occ_local, :] = block[
                        first : first + occ_local, c * BS : (c + 1) * BS
                    ]
    for out in outs:
        out[out.shape[0] - 16 :, :] = code


def regroup_kernel(*refs):
    *received, out = refs
    rows = out.shape[0] // len(received)
    for f, piece in enumerate(received):
        out[f * rows : (f + 1) * rows, :] = piece[rows : 2 * rows, :]


def merge_kernel(first, second, out, sems):
    count = first.shape[0]
    skip = second.shape[0] - count
    loads = [
        pltpu.make_async_copy(first, out.at[:count], sems.at[0]),
        pltpu.make_async_copy(second.at[skip:], out.at[count:], sems.at[1]),
    ]
    for load in loads:
        load.start()
    for load in loads:
        load.wait()


def block_kernel(aux_count, low, coefs, blocks, *refs):
    pieces = refs[len(refs) // 2 :] if low else refs
    pairs_dev = blocks.shape[0] // 2
    rows = coefs.shape[0] - 16
    occ_local = rows // len(pieces)
    mine = lax.axis_index("aux")
    for k in range(pairs_dev):
        left = coefs[:rows, k * BS : (k + 1) * BS]
        right = jnp.concatenate([blocks[k], blocks[pairs_dev + k]], axis=1)
        half = jnp.dot(left, right, preferred_element_type=jnp.float32).astype(jnp.bfloat16)
        for side in range(2):
            flipped = low + side * (aux_count // 2)
            at = k * aux_count + jnp.bitwise_xor(mine, flipped)
            start = pl.multiple_of(at * occ_local, occ_local)
            for f, piece in enumerate(pieces):
                piece[pl.ds(start, occ_local), :] = half[
                    f * occ_local : (f + 1) * occ_local, side * BS : (side + 1) * BS
                ]
    if low == 0:
        for piece in pieces:
            piece[pairs_dev * aux_count * occ_local :, :] = coefs[rows:, :BS]


def read_codes(received, pairs_dev, codes):
    for at, piece in enumerate(received):
        digits = piece[piece.shape[0] - 16 :, :].astype(jnp.float32)[:1]
        high = pltpu.roll(digits, BS - pairs_dev, 1)
        codes[at : at + 1, :] = (digits + 128.0 * high).astype(jnp.int32)


def near_sum_kernel(metric_in, *refs):
    *received, across, total, mix, metric, codes, sem = refs
    load = pltpu.make_async_copy(metric_in, metric, sem)
    load.start()
    total[...] = jnp.zeros_like(total)
    mine = lax.axis_index("aux")
    rows = total.shape[1]
    occ_local = rows // metric.shape[0]
    pairs_dev = (received[0].shape[0] - 16) // rows
    read_codes(received, pairs_dev, codes)
    for f, piece in enumerate(received):
        for k in range(pairs_dev):
            r = codes[f, k]
            for j in range(metric.shape[0]):
                source, first = (across, f * 2 + j - 2) if j >= 2 else (piece, j)
                first = (first * pairs_dev + k) * occ_local
                start = pl.multiple_of(jnp.bitwise_xor(mine, j) * occ_local, occ_local)
                part = source[first : first + occ_local, :]
                total[r, pl.ds(start, occ_local), :] += part.astype(jnp.float32)
    load.wait()
    aux_count = metric.shape[0]
    row = lax.broadcasted_iota(jnp.int32, (rows, rows), 0)
    column = lax.broadcasted_iota(jnp.int32, (rows, rows), 1)
    left = (
        lax.broadcasted_iota(jnp.int32, (rows, aux_count), 0) % aux_count
        == lax.broadcasted_iota(jnp.int32, (rows, aux_count), 1)
    ).astype(jnp.bfloat16)
    right = (
        lax.broadcasted_iota(jnp.int32, (aux_count, rows), 1) // occ_local
        == lax.broadcasted_iota(jnp.int32, (aux_count, rows), 0)
    ).astype(jnp.bfloat16)
    factor = jnp.dot(left, metric[...], preferred_element_type=jnp.float32).astype(jnp.bfloat16)
    factor = jnp.dot(factor, right, preferred_element_type=jnp.float32)
    mix[...] = jnp.where(row // aux_count == column % occ_local, factor, 0.0).astype(jnp.bfloat16)


def collect_kernel(mix, total_in, *refs):
    *received, out, total, staged, codes, sems = refs
    occ_local, aux_count = out.shape[:2]
    rows = total.shape[1]
    pairs_dev = (received[0].shape[0] - 16) // rows
    read_codes(received, pairs_dev, codes)
    for at, piece in enumerate(received):
        for k in range(pairs_dev):
            total[codes[at, k]] += piece[k * rows : (k + 1) * rows, :].astype(jnp.float32)
    stores = []
    parts = sems.shape[0]
    each = total.shape[0] // parts
    for part in range(parts):
        for r in range(part * each, (part + 1) * each, 2):
            summed = jnp.concatenate([total[r], total[r + 1]], axis=1).astype(jnp.bfloat16)
            mixed = jnp.dot(mix[...], summed, preferred_element_type=jnp.float32)
            staged[:, :, r * BS : (r + 2) * BS] = mixed.reshape(
                occ_local, aux_count, 2 * BS
            ).astype(jnp.bfloat16)
        lanes = pl.ds(part * each * BS, each * BS)
        store = pltpu.make_async_copy(
            staged.at[:, :, lanes], out.at[:, :, lanes], sems.at[part]
        )
        store.start()
        stores.append(store)
    for store in stores:
        store.wait()

def flip(value, axis, bits):
    count = lax.axis_size(axis)
    return lax.ppermute(value, axis, [(at, at ^ bits) for at in range(count)])


def to_place(value, at):
    shell_count, aux_count = lax.axis_size("shell"), lax.axis_size("aux")
    moves = []
    for shell in range(shell_count):
        for aux in range(aux_count):
            bits = at if aux % 2 else at - at % 4 + at % 2 * 2 + at // 2 % 2
            moves.append((shell * aux_count + aux, (shell ^ bits) * aux_count + aux))
    return lax.ppermute(value, ("shell", "aux"), moves)


def after(value, *others):
    return lax.optimization_barrier((value, *others))[0]


def cost(flops):
    return pl.CostEstimate(flops=int(flops), transcendentals=0, bytes_accessed=2**20)


def in_hbm(*operands):
    return [pltpu.with_memory_space_constraint(operand, pltpu.HBM) for operand in operands]


def exchanged_inputs(integrals, pair_list, coef, metric, occ_slot):
    pairs_dev = pair_list.shape[0]
    shell_count = lax.axis_size("shell")
    aux_count = lax.axis_size("aux")
    group = shell_count // 2
    occ_local = coef.shape[1] // (shell_count * aux_count)
    block_count = coef.shape[0] // BS * shell_count
    rows = occ_local * aux_count
    piece = jax.ShapeDtypeStruct((pairs_dev * rows + 16, BS), jnp.bfloat16)
    vmem = pl.BlockSpec(memory_space=pltpu.VMEM)
    hbm = pl.BlockSpec(memory_space=pltpu.HBM)
    params = pltpu.CompilerParams(vmem_limit_bytes=40 * 2**20)

    def merged(name, first, second):
        return pl.pallas_call(
            merge_kernel,
            out_shape=jax.ShapeDtypeStruct(
                (2 * first.shape[0],) + first.shape[1:], jnp.bfloat16
            ),
            in_specs=[vmem] * 2,
            out_specs=vmem,
            scratch_shapes=[pltpu.SemaphoreType.DMA((2,))],
            compiler_params=params,
            name=name,
        )(first, second)

    blocks = integrals.reshape(pairs_dev, BS, BS)
    far_block = flip(blocks, "shell", group)
    operands = (pair_list, occ_slot.reshape(1, -1), coef)
    loaded = [
        pltpu.SMEM(pair_list.shape, jnp.int32),
        pltpu.VMEM((1, occ_slot.shape[0]), jnp.int32),
        pltpu.VMEM(coef.shape, jnp.bfloat16),
    ]
    near = pl.pallas_call(
        functools.partial(near_kernel, occ_local, aux_count),
        out_shape=[piece] * group,
        in_specs=[hbm] * 4 + [vmem],
        out_specs=[vmem] * group,
        scratch_shapes=loaded
        + [pltpu.VMEM(blocks.shape, jnp.bfloat16), pltpu.SemaphoreType.DMA((4,))],
        compiler_params=params,
        name="near_blocks",
    )(*in_hbm(*operands, blocks), flip(blocks, "aux", 1))
    near = [near[0]] + [to_place(near[f], f) for f in range(1, group)]
    sent_coef = pl.pallas_call(
        functools.partial(pick_kernel, group, occ_local, aux_count),
        out_shape=jax.ShapeDtypeStruct(
            (group * occ_local + 16, pairs_dev * BS), jnp.bfloat16
        ),
        in_specs=[hbm] * 3,
        out_specs=vmem,
        scratch_shapes=loaded + [pltpu.SemaphoreType.DMA((3,))],
        compiler_params=params,
        name="pick",
    )(*in_hbm(*operands))
    far_block = after(far_block, sent_coef)
    far_coef = flip(after(sent_coef, far_block), "shell", group)
    far_pair = merged("far_pair", far_block, flip(far_block, "aux", 2))
    far_pairs = [far_pair, flip(far_pair, "aux", 1)]
    across = flip(
        pl.pallas_call(
            regroup_kernel,
            out_shape=jax.ShapeDtypeStruct(
                (group * 2 * pairs_dev * occ_local, BS), jnp.bfloat16
            ),
            in_specs=[vmem] * group,
            out_specs=vmem,
            compiler_params=params,
            name="regroup",
        )(*near),
        "aux",
        2,
    )
    far = []
    for low in range(2):
        far = pl.pallas_call(
            functools.partial(block_kernel, aux_count, low),
            out_shape=[piece] * group,
            in_specs=[vmem] * (2 + len(far)),
            out_specs=[vmem] * group,
            input_output_aliases={2 + f: f for f in range(len(far))},
            compiler_params=params,
            cost_estimate=cost(2e9) if low == 0 else None,
            name=f"far_blocks_{low}",
        )(far_coef, far_pairs[low], *far)
    total_shape = jax.ShapeDtypeStruct((block_count, rows, BS), jnp.float32)
    total, mix = pl.pallas_call(
        near_sum_kernel,
        out_shape=[total_shape, jax.ShapeDtypeStruct((rows, rows), jnp.bfloat16)],
        in_specs=[hbm] + [vmem] * (group + 1),
        out_specs=[vmem] * 2,
        scratch_shapes=[
            pltpu.VMEM(metric.shape, jnp.bfloat16),
            pltpu.VMEM((8, BS), jnp.int32),
            pltpu.SemaphoreType.DMA,
        ],
        compiler_params=params,
        cost_estimate=cost(3e9),
        name="near_sum",
    )(*in_hbm(metric), *(after(one, far[0]) for one in near), across)
    far = [far[0]] + [to_place(far[f], f) for f in range(1, group)]
    return pl.pallas_call(
        collect_kernel,
        out_shape=[
            jax.ShapeDtypeStruct((occ_local, aux_count, block_count * BS), jnp.bfloat16),
            total_shape,
        ],
        in_specs=[vmem] * (2 + group),
        out_specs=[hbm, vmem],
        input_output_aliases={1: 1},
        scratch_shapes=[
            pltpu.VMEM((occ_local, aux_count, block_count * BS), jnp.bfloat16),
            pltpu.VMEM((8, BS), jnp.int32),
            pltpu.SemaphoreType.DMA((4,)),
        ],
        compiler_params=params,
        name="collect",
    )(mix, total, *far)[0]


def per_device(integrals, pair_list, coef, metric, occ_slot):
    shell_count, aux_count = lax.axis_size("shell"), lax.axis_size("aux")
    occ_local = coef.shape[1] // (shell_count * aux_count)
    if occ_local % 16 or shell_count < 8 or shell_count & (shell_count - 1) or aux_count != 4:
        return relayed_half_blocks(integrals, pair_list, coef, metric, occ_slot)
    return exchanged_inputs(integrals, pair_list, coef, metric, occ_slot)


def solution(mesh):
    placed = (P("shell", None, "aux", None), P("shell", None), P("shell", None), P(), P())
    return jax.shard_map(
        per_device,
        mesh=mesh,
        in_specs=placed,
        out_specs=P(("shell", "aux"), None, None),
        check_vma=False,
    )
```

```python
import functools

import jax
import jax.numpy as jnp
from jax import lax
from jax.experimental import pallas as pl
from jax.experimental.pallas import tpu as pltpu
from jax.sharding import PartitionSpec as P

BS = 128
TILE = 8


def relayed_half_blocks(integrals, pair_list, coef, metric, occ_slot):
    pairs_dev = pair_list.shape[0]
    rows_local = coef.shape[0]
    occ_count = coef.shape[1]
    blocks_dev = rows_local // BS
    shell_count = lax.axis_size("shell")
    block_count = blocks_dev * shell_count
    slot_count = occ_slot.shape[0]
    aux_dev = integrals.shape[2]
    inverse = (
        jnp.zeros((slot_count,), jnp.int32)
        .at[occ_slot]
        .set(jnp.arange(slot_count, dtype=jnp.int32))
    )
    ordered = jnp.take(
        coef.reshape(rows_local, slot_count, occ_count // slot_count), inverse, axis=1
    )
    ordered = ordered.reshape(rows_local, occ_count)

    def one_slot(item):
        int_block, column_index = item
        start = column_index % blocks_dev * BS
        column = lax.dynamic_slice_in_dim(ordered, start, BS, 0)
        product = lax.dot_general(
            column,
            int_block.reshape(BS, aux_dev * BS),
            (((0,), (0,)), ((), ())),
            preferred_element_type=jnp.float32,
        )
        return product.astype(jnp.bfloat16)

    half_blocks = lax.map(one_slot, (integrals, pair_list[:, 1]))
    half_blocks = half_blocks.reshape(pairs_dev, occ_count, aux_dev, BS)
    listing = lax.all_gather(pair_list, "shell", axis=0, tiled=True)
    targets = jnp.arange(block_count, dtype=jnp.int32)[:, None]
    selector = ((listing[:, 0][None, :] == targets) & (listing[:, 2][None, :] == 1)).astype(
        jnp.bfloat16
    )
    relayed = lax.all_to_all(
        lax.all_to_all(half_blocks, "shell", split_axis=1, concat_axis=0, tiled=True),
        "aux",
        split_axis=1,
        concat_axis=2,
        tiled=True,
    )
    summed = jnp.dot(
        selector, relayed.reshape(relayed.shape[0], -1), preferred_element_type=jnp.float32
    )
    blocks = summed.astype(jnp.bfloat16).reshape((block_count,) + relayed.shape[1:])
    result = jnp.einsum("qp,bipm->iqbm", metric, blocks, preferred_element_type=jnp.float32)
    return result.reshape(result.shape[0], result.shape[1], block_count * BS).astype(jnp.bfloat16)


def targets_of(slot_row, block_total, occ_count):
    width = occ_count // block_total
    spread = (
        lax.broadcasted_iota(jnp.int32, (block_total, occ_count), 1) // width
        == lax.broadcasted_iota(jnp.int32, (block_total, occ_count), 0)
    ).astype(jnp.bfloat16)
    slots = jnp.broadcast_to(slot_row, (8, block_total)).astype(jnp.float32)
    target = jnp.dot(slots.astype(jnp.bfloat16), spread, preferred_element_type=jnp.float32)
    return target.astype(jnp.int32)[:1] * width + (
        lax.broadcasted_iota(jnp.int32, (1, occ_count), 1) % width
    )


def code_tile(pairs):
    pairs_dev = pairs.shape[0]
    lane = lax.broadcasted_iota(jnp.int32, (1, BS), 1)
    code = jnp.zeros((1, BS), jnp.int32)
    for k in range(pairs_dev):
        code = jnp.where(lane == k, pairs[k, 0] % 128, code)
        code = jnp.where(lane == pairs_dev + k, pairs[k, 0] // 128, code)
    return jnp.broadcast_to(code.astype(jnp.float32), (TILE, BS)).astype(jnp.bfloat16)


def pick_kernel(
    flips,
    occ_local,
    aux_count,
    pairs_in,
    slot_in,
    coef_in,
    *refs,
):
    *outs, pairs, slot_row, coef, sems = refs
    pairs_dev = pairs.shape[0]
    blocks_dev = coef.shape[0] // BS
    occ_count = coef.shape[1]
    loads = [
        pltpu.make_async_copy(source, target, sems.at[at])
        for at, (source, target) in enumerate(
            ((slot_in, slot_row), (pairs_in, pairs), (coef_in, coef))
        )
    ]
    for load in loads:
        load.start()
    me = lax.axis_index("shell")
    mine = lax.axis_index("aux")
    every = sum(flips, [])
    row = lax.broadcasted_iota(jnp.int32, (len(every) * occ_local, 1), 0)
    owner = sum(jnp.where(row // occ_local == at, f, 0) for at, f in enumerate(every))
    wanted = (jnp.bitwise_xor(owner, me) * aux_count + mine) * occ_local + row % occ_local
    loads[0].wait()
    target = targets_of(slot_row[...], slot_row.shape[1], occ_count)
    pick = (wanted == target).astype(jnp.bfloat16)
    for load in loads[1:]:
        load.wait()
    code = code_tile(pairs)
    for k in range(pairs_dev):
        start = pl.multiple_of(lax.rem(pairs[k, 1], blocks_dev) * BS, BS)
        live = (pairs[k, 2] == 1).astype(jnp.float32)
        piece = lax.dot_general(
            pick,
            coef[pl.ds(start, BS), :],
            (((1,), (1,)), ((), ())),
            preferred_element_type=jnp.float32,
        )
        piece = (piece * live).astype(jnp.bfloat16)
        first = 0
        for out in outs:
            rows = out.shape[0] - TILE
            out[:rows, k * BS : (k + 1) * BS] = piece[first : first + rows]
            out[rows:, k * BS : (k + 1) * BS] = code
            first += rows


def near_kernel(
    occ_local,
    aux_count,
    pairs_in,
    slot_in,
    coef_in,
    blocks_in,
    beside,
    *refs,
):
    *outs, pairs, slot_row, coef, blocks, sems = refs
    pairs_dev = pairs.shape[0]
    blocks_dev = coef.shape[0] // BS
    occ_count = coef.shape[1]
    loads = [
        pltpu.make_async_copy(source, target, sems.at[at])
        for at, (source, target) in enumerate(
            ((slot_in, slot_row), (pairs_in, pairs), (coef_in, coef), (blocks_in, blocks))
        )
    ]
    for load in loads:
        load.start()
    me = lax.axis_index("shell")
    mine = lax.axis_index("aux")
    owned = 2 * occ_local
    row = lax.broadcasted_iota(jnp.int32, (len(outs) * owned, 1), 0)
    flips = row // owned % 2 + row // occ_local % 2 * 2
    owner = jnp.bitwise_xor(flips, me) * aux_count + jnp.bitwise_xor(
        row // (2 * owned) * 2, mine
    )
    wanted = owner * occ_local + row % occ_local
    loads[0].wait()
    target = targets_of(slot_row[...], slot_row.shape[1], occ_count)
    pick = (wanted == target).astype(jnp.bfloat16)
    for load in loads[1:]:
        load.wait()
    code = code_tile(pairs)
    rows = [
        coef[pl.ds(pl.multiple_of(lax.rem(pairs[k, 1], blocks_dev) * BS, BS), BS), :]
        for k in range(pairs_dev)
    ]
    ordered = lax.dot_general(
        pick,
        jnp.concatenate(rows, axis=0),
        (((1,), (1,)), ((), ())),
        preferred_element_type=jnp.float32,
    ).astype(jnp.bfloat16)
    for k in range(pairs_dev):
        block = jnp.dot(
            ordered[:, k * BS : (k + 1) * BS],
            jnp.concatenate([blocks[k], beside[k]], axis=1),
            preferred_element_type=jnp.float32,
        )
        block = (block * (pairs[k, 2] == 1).astype(jnp.float32)).astype(jnp.bfloat16)
        for f, out in enumerate(outs):
            for j in range(2):
                first = f * owned + j * occ_local
                for c in range(2):
                    at = ((j * 2 + c) * pairs_dev + k) * occ_local
                    out[at : at + occ_local, :] = block[
                        first : first + occ_local, c * BS : (c + 1) * BS
                    ]
    for out in outs:
        out[out.shape[0] - TILE :, :] = code


def regroup_kernel(*refs):
    *received, out = refs
    rows = (received[0].shape[0] - TILE) // 2
    for f, piece in enumerate(received):
        out[f * rows : (f + 1) * rows, :] = piece[rows : 2 * rows, :]
    tiles = [piece[2 * rows :, :].astype(jnp.float32) for piece in received[:2]]
    out[len(received) * rows :, :] = jnp.concatenate(tiles, axis=0).astype(jnp.bfloat16)


def merge_kernel(first, second, out, sems):
    count = first.shape[0]
    skip = second.shape[0] - count
    loads = [
        pltpu.make_async_copy(first, out.at[:count], sems.at[0]),
        pltpu.make_async_copy(second.at[skip:], out.at[count:], sems.at[1]),
    ]
    for load in loads:
        load.start()
    for load in loads:
        load.wait()


def block_kernel(aux_count, low, coefs, blocks, *refs):
    pieces = refs[len(refs) // 2 :] if low else refs
    pairs_dev = blocks.shape[0] // 2
    rows = coefs.shape[0] - TILE
    occ_local = rows // len(pieces)
    mine = lax.axis_index("aux")
    for k in range(pairs_dev):
        left = coefs[:rows, k * BS : (k + 1) * BS]
        right = jnp.concatenate([blocks[k], blocks[pairs_dev + k]], axis=1)
        half = jnp.dot(left, right, preferred_element_type=jnp.float32).astype(jnp.bfloat16)
        for side in range(2):
            flipped = low + side * (aux_count // 2)
            at = k * aux_count + jnp.bitwise_xor(mine, flipped)
            start = pl.multiple_of(at * occ_local, occ_local)
            for f, piece in enumerate(pieces):
                piece[pl.ds(start, occ_local), :] = half[
                    f * occ_local : (f + 1) * occ_local, side * BS : (side + 1) * BS
                ]
    if low == 0:
        for piece in pieces:
            piece[pairs_dev * aux_count * occ_local :, :] = coefs[rows:, :BS]


def read_codes(tiles, pairs_dev, codes):
    for at, tile in enumerate(tiles):
        digits = tile.astype(jnp.float32)[:1]
        high = pltpu.roll(digits, BS - pairs_dev, 1)
        codes[at : at + 1, :] = (digits + 128.0 * high).astype(jnp.int32)


def near_sum_kernel(metric_in, *refs):
    *received, across, total, mix, metric, codes, sem = refs
    load = pltpu.make_async_copy(metric_in, metric, sem)
    load.start()
    total[...] = jnp.zeros_like(total)
    mine = lax.axis_index("aux")
    rows = total.shape[1]
    occ_local = rows // metric.shape[0]
    pairs_dev = (received[0].shape[0] - TILE) // rows
    each = 2 * pairs_dev * occ_local
    last = across[len(received) * each :, :].astype(jnp.float32)
    tiles = [piece[2 * each :, :] for piece in received[:2]] + [last[:TILE], last[TILE:]]
    read_codes(tiles, pairs_dev, codes)
    for f, piece in enumerate(received):
        for k in range(pairs_dev):
            for source, at, r in (
                (piece, 0, codes[f % 2, k]),
                (across, f * each, codes[2 + f % 2, k]),
            ):
                for c in range(2):
                    first = at + (c * pairs_dev + k) * occ_local
                    flipped = f // 2 * 2 + c
                    start = pl.multiple_of(
                        jnp.bitwise_xor(mine, flipped) * occ_local, occ_local
                    )
                    part = source[first : first + occ_local, :]
                    total[r, pl.ds(start, occ_local), :] += part.astype(jnp.float32)
    load.wait()
    aux_count = metric.shape[0]
    row = lax.broadcasted_iota(jnp.int32, (rows, rows), 0)
    column = lax.broadcasted_iota(jnp.int32, (rows, rows), 1)
    left = (
        lax.broadcasted_iota(jnp.int32, (rows, aux_count), 0) % aux_count
        == lax.broadcasted_iota(jnp.int32, (rows, aux_count), 1)
    ).astype(jnp.bfloat16)
    right = (
        lax.broadcasted_iota(jnp.int32, (aux_count, rows), 1) // occ_local
        == lax.broadcasted_iota(jnp.int32, (aux_count, rows), 0)
    ).astype(jnp.bfloat16)
    factor = jnp.dot(left, metric[...], preferred_element_type=jnp.float32).astype(jnp.bfloat16)
    factor = jnp.dot(factor, right, preferred_element_type=jnp.float32)
    mix[...] = jnp.where(row // aux_count == column % occ_local, factor, 0.0).astype(jnp.bfloat16)


def collect_kernel(mix, total_in, *refs):
    *received, out, total, staged, codes, sems = refs
    occ_local, aux_count = out.shape[:2]
    rows = total.shape[1]
    pairs_dev = (received[0].shape[0] - TILE) // rows
    read_codes([piece[pairs_dev * rows :, :] for piece in received], pairs_dev, codes)
    for at, piece in enumerate(received):
        for k in range(pairs_dev):
            total[codes[at, k]] += piece[k * rows : (k + 1) * rows, :].astype(jnp.float32)
    stores = []
    parts = sems.shape[0]
    each = total.shape[0] // parts
    for part in range(parts):
        for r in range(part * each, (part + 1) * each, 2):
            summed = jnp.concatenate([total[r], total[r + 1]], axis=1).astype(jnp.bfloat16)
            mixed = jnp.dot(mix[...], summed, preferred_element_type=jnp.float32)
            staged[:, :, r * BS : (r + 2) * BS] = mixed.reshape(
                occ_local, aux_count, 2 * BS
            ).astype(jnp.bfloat16)
        lanes = pl.ds(part * each * BS, each * BS)
        store = pltpu.make_async_copy(
            staged.at[:, :, lanes], out.at[:, :, lanes], sems.at[part]
        )
        store.start()
        stores.append(store)
    for store in stores:
        store.wait()

def flip(value, axis, bits):
    count = lax.axis_size(axis)
    return lax.ppermute(value, axis, [(at, at ^ bits) for at in range(count)])


def beyond(value, shell_bits, aux_bits):
    shell_count, aux_count = lax.axis_size("shell"), lax.axis_size("aux")
    moves = [
        (shell * aux_count + aux, (shell ^ shell_bits) * aux_count + (aux ^ aux_bits))
        for shell in range(shell_count)
        for aux in range(aux_count)
    ]
    return lax.ppermute(value, ("shell", "aux"), moves)


def after(value, *others):
    return lax.optimization_barrier((value, *others))[0]


def cost(flops):
    return pl.CostEstimate(flops=int(flops), transcendentals=0, bytes_accessed=2**20)


def in_hbm(*operands):
    return [pltpu.with_memory_space_constraint(operand, pltpu.HBM) for operand in operands]


def exchanged_inputs(integrals, pair_list, coef, metric, occ_slot):
    pairs_dev = pair_list.shape[0]
    shell_count = lax.axis_size("shell")
    aux_count = lax.axis_size("aux")
    group = shell_count // 2
    occ_local = coef.shape[1] // (shell_count * aux_count)
    block_count = coef.shape[0] // BS * shell_count
    rows = occ_local * aux_count
    piece = jax.ShapeDtypeStruct((pairs_dev * rows + TILE, BS), jnp.bfloat16)
    vmem = pl.BlockSpec(memory_space=pltpu.VMEM)
    hbm = pl.BlockSpec(memory_space=pltpu.HBM)
    params = pltpu.CompilerParams(vmem_limit_bytes=40 * 2**20)

    def merged(name, first, second):
        return pl.pallas_call(
            merge_kernel,
            out_shape=jax.ShapeDtypeStruct(
                (2 * first.shape[0],) + first.shape[1:], jnp.bfloat16
            ),
            in_specs=[vmem] * 2,
            out_specs=vmem,
            scratch_shapes=[pltpu.SemaphoreType.DMA((2,))],
            compiler_params=params,
            name=name,
        )(first, second)

    blocks = integrals.reshape(pairs_dev, BS, BS)
    far_block = flip(blocks, "shell", group)
    operands = (pair_list, occ_slot.reshape(1, -1), coef)
    loaded = [
        pltpu.SMEM(pair_list.shape, jnp.int32),
        pltpu.VMEM((1, occ_slot.shape[0]), jnp.int32),
        pltpu.VMEM(coef.shape, jnp.bfloat16),
    ]
    near = pl.pallas_call(
        functools.partial(near_kernel, occ_local, aux_count),
        out_shape=[piece] * 4,
        in_specs=[hbm] * 4 + [vmem],
        out_specs=[vmem] * 4,
        scratch_shapes=loaded
        + [pltpu.VMEM(blocks.shape, jnp.bfloat16), pltpu.SemaphoreType.DMA((4,))],
        compiler_params=params,
        name="near_blocks",
    )(*in_hbm(*operands, blocks), flip(blocks, "aux", 1))
    near = [near[0]] + [beyond(near[f], f % 2, f // 2 * 2) for f in range(1, 4)]
    (sent_coef,) = pl.pallas_call(
        functools.partial(
            pick_kernel, [list(range(group, shell_count))], occ_local, aux_count
        ),
        out_shape=[
            jax.ShapeDtypeStruct((group * occ_local + TILE, pairs_dev * BS), jnp.bfloat16)
        ],
        in_specs=[hbm] * 3,
        out_specs=[vmem],
        scratch_shapes=loaded + [pltpu.SemaphoreType.DMA((3,))],
        compiler_params=params,
        name="pick",
    )(*in_hbm(*operands))
    far_block = after(far_block, sent_coef)
    far_coef = flip(after(sent_coef, far_block), "shell", group)
    far_pair = merged("far_pair", far_block, flip(far_block, "aux", 2))
    far_pairs = [far_pair, flip(far_pair, "aux", 1)]
    across = flip(
        pl.pallas_call(
            regroup_kernel,
            out_shape=jax.ShapeDtypeStruct(
                (4 * 2 * pairs_dev * occ_local + 2 * TILE, BS), jnp.bfloat16
            ),
            in_specs=[vmem] * 4,
            out_specs=vmem,
            compiler_params=params,
            name="regroup",
        )(*near),
        "shell",
        2,
    )
    far = []
    for low in range(2):
        far = pl.pallas_call(
            functools.partial(block_kernel, aux_count, low),
            out_shape=[piece] * group,
            in_specs=[vmem] * (2 + len(far)),
            out_specs=[vmem] * group,
            input_output_aliases={2 + f: f for f in range(len(far))},
            compiler_params=params,
            cost_estimate=cost(2e9) if low == 0 else None,
            name=f"far_blocks_{low}",
        )(far_coef, far_pairs[low], *far)
    total_shape = jax.ShapeDtypeStruct((block_count, rows, BS), jnp.float32)
    total, mix = pl.pallas_call(
        near_sum_kernel,
        out_shape=[total_shape, jax.ShapeDtypeStruct((rows, rows), jnp.bfloat16)],
        in_specs=[hbm] + [vmem] * 5,
        out_specs=[vmem] * 2,
        scratch_shapes=[
            pltpu.VMEM(metric.shape, jnp.bfloat16),
            pltpu.VMEM((8, BS), jnp.int32),
            pltpu.SemaphoreType.DMA,
        ],
        compiler_params=params,
        cost_estimate=cost(3e9),
        name="near_sum",
    )(*in_hbm(metric), *(after(one, far[0]) for one in near), across)
    far = [far[0]] + [flip(far[f], "shell", f) for f in range(1, group)]
    return pl.pallas_call(
        collect_kernel,
        out_shape=[
            jax.ShapeDtypeStruct((occ_local, aux_count, block_count * BS), jnp.bfloat16),
            total_shape,
        ],
        in_specs=[vmem] * (2 + group),
        out_specs=[hbm, vmem],
        input_output_aliases={1: 1},
        scratch_shapes=[
            pltpu.VMEM((occ_local, aux_count, block_count * BS), jnp.bfloat16),
            pltpu.VMEM((8, BS), jnp.int32),
            pltpu.SemaphoreType.DMA((4,)),
        ],
        compiler_params=params,
        name="collect",
    )(mix, total, *far)[0]


def per_device(integrals, pair_list, coef, metric, occ_slot):
    shell_count, aux_count = lax.axis_size("shell"), lax.axis_size("aux")
    occ_local = coef.shape[1] // (shell_count * aux_count)
    if occ_local % 16 or shell_count != 8 or aux_count != 4:
        return relayed_half_blocks(integrals, pair_list, coef, metric, occ_slot)
    return exchanged_inputs(integrals, pair_list, coef, metric, occ_slot)


def solution(mesh):
    placed = (P("shell", None, "aux", None), P("shell", None), P("shell", None), P(), P())
    return jax.shard_map(
        per_device,
        mesh=mesh,
        in_specs=placed,
        out_specs=P(("shell", "aux"), None, None),
        check_vma=False,
    )
```

```python
import functools

import jax
import jax.numpy as jnp
from jax import lax
from jax.experimental import pallas as pl
from jax.experimental.pallas import tpu as pltpu
from jax.sharding import PartitionSpec as P

BS = 128
TILE = 8


def relayed_half_blocks(integrals, pair_list, coef, metric, occ_slot):
    pairs_dev = pair_list.shape[0]
    rows_local = coef.shape[0]
    occ_count = coef.shape[1]
    blocks_dev = rows_local // BS
    shell_count = lax.axis_size("shell")
    block_count = blocks_dev * shell_count
    slot_count = occ_slot.shape[0]
    aux_dev = integrals.shape[2]
    inverse = (
        jnp.zeros((slot_count,), jnp.int32)
        .at[occ_slot]
        .set(jnp.arange(slot_count, dtype=jnp.int32))
    )
    ordered = jnp.take(
        coef.reshape(rows_local, slot_count, occ_count // slot_count), inverse, axis=1
    )
    ordered = ordered.reshape(rows_local, occ_count)

    def one_slot(item):
        int_block, column_index = item
        start = column_index % blocks_dev * BS
        column = lax.dynamic_slice_in_dim(ordered, start, BS, 0)
        product = lax.dot_general(
            column,
            int_block.reshape(BS, aux_dev * BS),
            (((0,), (0,)), ((), ())),
            preferred_element_type=jnp.float32,
        )
        return product.astype(jnp.bfloat16)

    half_blocks = lax.map(one_slot, (integrals, pair_list[:, 1]))
    half_blocks = half_blocks.reshape(pairs_dev, occ_count, aux_dev, BS)
    listing = lax.all_gather(pair_list, "shell", axis=0, tiled=True)
    targets = jnp.arange(block_count, dtype=jnp.int32)[:, None]
    selector = ((listing[:, 0][None, :] == targets) & (listing[:, 2][None, :] == 1)).astype(
        jnp.bfloat16
    )
    relayed = lax.all_to_all(
        lax.all_to_all(half_blocks, "shell", split_axis=1, concat_axis=0, tiled=True),
        "aux",
        split_axis=1,
        concat_axis=2,
        tiled=True,
    )
    summed = jnp.dot(
        selector, relayed.reshape(relayed.shape[0], -1), preferred_element_type=jnp.float32
    )
    blocks = summed.astype(jnp.bfloat16).reshape((block_count,) + relayed.shape[1:])
    result = jnp.einsum("qp,bipm->iqbm", metric, blocks, preferred_element_type=jnp.float32)
    return result.reshape(result.shape[0], result.shape[1], block_count * BS).astype(jnp.bfloat16)


def targets_of(slot_row, block_total, occ_count):
    width = occ_count // block_total
    spread = (
        lax.broadcasted_iota(jnp.int32, (block_total, occ_count), 1) // width
        == lax.broadcasted_iota(jnp.int32, (block_total, occ_count), 0)
    ).astype(jnp.bfloat16)
    slots = jnp.broadcast_to(slot_row, (8, block_total)).astype(jnp.float32)
    target = jnp.dot(slots.astype(jnp.bfloat16), spread, preferred_element_type=jnp.float32)
    return target.astype(jnp.int32)[:1] * width + (
        lax.broadcasted_iota(jnp.int32, (1, occ_count), 1) % width
    )


def code_tile(pairs):
    pairs_dev = pairs.shape[0]
    lane = lax.broadcasted_iota(jnp.int32, (1, BS), 1)
    code = jnp.zeros((1, BS), jnp.int32)
    for k in range(pairs_dev):
        code = jnp.where(lane == k, pairs[k, 0] % 128, code)
        code = jnp.where(lane == pairs_dev + k, pairs[k, 0] // 128, code)
    return jnp.broadcast_to(code.astype(jnp.float32), (TILE, BS)).astype(jnp.bfloat16)


def pick_kernel(
    flips,
    occ_local,
    aux_count,
    pairs_in,
    slot_in,
    coef_in,
    *refs,
):
    *outs, pairs, slot_row, coef, sems = refs
    pairs_dev = pairs.shape[0]
    blocks_dev = coef.shape[0] // BS
    occ_count = coef.shape[1]
    loads = [
        pltpu.make_async_copy(source, target, sems.at[at])
        for at, (source, target) in enumerate(
            ((slot_in, slot_row), (pairs_in, pairs), (coef_in, coef))
        )
    ]
    for load in loads:
        load.start()
    me = lax.axis_index("shell")
    mine = lax.axis_index("aux")
    every = sum(flips, [])
    row = lax.broadcasted_iota(jnp.int32, (len(every) * occ_local, 1), 0)
    owner = sum(jnp.where(row // occ_local == at, f, 0) for at, f in enumerate(every))
    wanted = (jnp.bitwise_xor(owner, me) * aux_count + mine) * occ_local + row % occ_local
    loads[0].wait()
    target = targets_of(slot_row[...], slot_row.shape[1], occ_count)
    pick = (wanted == target).astype(jnp.bfloat16)
    for load in loads[1:]:
        load.wait()
    code = code_tile(pairs)
    for k in range(pairs_dev):
        start = pl.multiple_of(lax.rem(pairs[k, 1], blocks_dev) * BS, BS)
        live = (pairs[k, 2] == 1).astype(jnp.float32)
        piece = lax.dot_general(
            pick,
            coef[pl.ds(start, BS), :],
            (((1,), (1,)), ((), ())),
            preferred_element_type=jnp.float32,
        )
        piece = (piece * live).astype(jnp.bfloat16)
        first = 0
        for out in outs:
            rows = out.shape[0] - TILE
            out[:rows, k * BS : (k + 1) * BS] = piece[first : first + rows]
            out[rows:, k * BS : (k + 1) * BS] = code
            first += rows


def near_kernel(
    occ_local,
    aux_count,
    pairs_in,
    slot_in,
    coef_in,
    blocks_in,
    beside,
    *refs,
):
    *outs, pairs, slot_row, coef, blocks, sems = refs
    pairs_dev = pairs.shape[0]
    blocks_dev = coef.shape[0] // BS
    occ_count = coef.shape[1]
    loads = [
        pltpu.make_async_copy(source, target, sems.at[at])
        for at, (source, target) in enumerate(
            ((slot_in, slot_row), (pairs_in, pairs), (coef_in, coef), (blocks_in, blocks))
        )
    ]
    for load in loads:
        load.start()
    me = lax.axis_index("shell")
    mine = lax.axis_index("aux")
    owned = 2 * occ_local
    row = lax.broadcasted_iota(jnp.int32, (len(outs) * owned, 1), 0)
    flips = row // owned % 2 + row // occ_local % 2 * 2
    owner = jnp.bitwise_xor(flips, me) * aux_count + jnp.bitwise_xor(
        row // (2 * owned) * 2, mine
    )
    wanted = owner * occ_local + row % occ_local
    loads[0].wait()
    target = targets_of(slot_row[...], slot_row.shape[1], occ_count)
    pick = (wanted == target).astype(jnp.bfloat16)
    for load in loads[1:]:
        load.wait()
    code = code_tile(pairs)
    rows = [
        coef[pl.ds(pl.multiple_of(lax.rem(pairs[k, 1], blocks_dev) * BS, BS), BS), :]
        for k in range(pairs_dev)
    ]
    ordered = lax.dot_general(
        pick,
        jnp.concatenate(rows, axis=0),
        (((1,), (1,)), ((), ())),
        preferred_element_type=jnp.float32,
    ).astype(jnp.bfloat16)
    for k in range(pairs_dev):
        block = jnp.dot(
            ordered[:, k * BS : (k + 1) * BS],
            jnp.concatenate([blocks[k], beside[k]], axis=1),
            preferred_element_type=jnp.float32,
        )
        block = (block * (pairs[k, 2] == 1).astype(jnp.float32)).astype(jnp.bfloat16)
        for f, out in enumerate(outs):
            for j in range(2):
                first = f * owned + j * occ_local
                for c in range(2):
                    at = ((j * 2 + c) * pairs_dev + k) * occ_local
                    out[at : at + occ_local, :] = block[
                        first : first + occ_local, c * BS : (c + 1) * BS
                    ]
    for out in outs:
        out[out.shape[0] - TILE :, :] = code


def regroup_kernel(*refs):
    *received, out = refs
    rows = (received[0].shape[0] - TILE) // 2
    for f, piece in enumerate(received):
        out[f * rows : (f + 1) * rows, :] = piece[rows : 2 * rows, :]
    tiles = [piece[2 * rows :, :].astype(jnp.float32) for piece in received[:2]]
    out[len(received) * rows :, :] = jnp.concatenate(tiles, axis=0).astype(jnp.bfloat16)


def merge_kernel(first, second, out, sems):
    count = first.shape[0]
    skip = second.shape[0] - count
    loads = [
        pltpu.make_async_copy(first, out.at[:count], sems.at[0]),
        pltpu.make_async_copy(second.at[skip:], out.at[count:], sems.at[1]),
    ]
    for load in loads:
        load.start()
    for load in loads:
        load.wait()


def block_kernel(aux_count, low, coefs, blocks, *refs):
    pieces = refs[len(refs) // 2 :] if low else refs
    pairs_dev = blocks.shape[0] // 2
    rows = coefs.shape[0] - TILE
    occ_local = rows // len(pieces)
    mine = lax.axis_index("aux")
    for k in range(pairs_dev):
        left = coefs[:rows, k * BS : (k + 1) * BS]
        right = jnp.concatenate([blocks[k], blocks[pairs_dev + k]], axis=1)
        half = jnp.dot(left, right, preferred_element_type=jnp.float32).astype(jnp.bfloat16)
        for side in range(2):
            flipped = low + side * (aux_count // 2)
            at = k * aux_count + jnp.bitwise_xor(mine, flipped)
            start = pl.multiple_of(at * occ_local, occ_local)
            for f, piece in enumerate(pieces):
                piece[pl.ds(start, occ_local), :] = half[
                    f * occ_local : (f + 1) * occ_local, side * BS : (side + 1) * BS
                ]
    if low == 0:
        for piece in pieces:
            piece[pairs_dev * aux_count * occ_local :, :] = coefs[rows:, :BS]


def read_codes(tiles, pairs_dev, codes):
    for at, tile in enumerate(tiles):
        digits = tile.astype(jnp.float32)[:1]
        high = pltpu.roll(digits, BS - pairs_dev, 1)
        codes[at : at + 1, :] = (digits + 128.0 * high).astype(jnp.int32)


def near_sum_kernel(metric_in, *refs):
    *received, across, total, mix, metric, codes, sem = refs
    load = pltpu.make_async_copy(metric_in, metric, sem)
    load.start()
    total[...] = jnp.zeros_like(total)
    mine = lax.axis_index("aux")
    rows = total.shape[1]
    occ_local = rows // metric.shape[0]
    pairs_dev = (received[0].shape[0] - TILE) // rows
    each = 2 * pairs_dev * occ_local
    last = across[len(received) * each :, :].astype(jnp.float32)
    tiles = [piece[2 * each :, :] for piece in received[:2]] + [last[:TILE], last[TILE:]]
    read_codes(tiles, pairs_dev, codes)
    for f, piece in enumerate(received):
        for k in range(pairs_dev):
            for source, at, r in (
                (piece, 0, codes[f % 2, k]),
                (across, f * each, codes[2 + f % 2, k]),
            ):
                for c in range(2):
                    first = at + (c * pairs_dev + k) * occ_local
                    flipped = f // 2 * 2 + c
                    start = pl.multiple_of(
                        jnp.bitwise_xor(mine, flipped) * occ_local, occ_local
                    )
                    part = source[first : first + occ_local, :]
                    total[r, pl.ds(start, occ_local), :] += part.astype(jnp.float32)
    load.wait()
    aux_count = metric.shape[0]
    row = lax.broadcasted_iota(jnp.int32, (rows, rows), 0)
    column = lax.broadcasted_iota(jnp.int32, (rows, rows), 1)
    left = (
        lax.broadcasted_iota(jnp.int32, (rows, aux_count), 0) % aux_count
        == lax.broadcasted_iota(jnp.int32, (rows, aux_count), 1)
    ).astype(jnp.bfloat16)
    right = (
        lax.broadcasted_iota(jnp.int32, (aux_count, rows), 1) // occ_local
        == lax.broadcasted_iota(jnp.int32, (aux_count, rows), 0)
    ).astype(jnp.bfloat16)
    factor = jnp.dot(left, metric[...], preferred_element_type=jnp.float32).astype(jnp.bfloat16)
    factor = jnp.dot(factor, right, preferred_element_type=jnp.float32)
    mix[...] = jnp.where(row // aux_count == column % occ_local, factor, 0.0).astype(jnp.bfloat16)


def collect_kernel(mix, total_in, *refs):
    *received, out, total, staged, codes, sems = refs
    occ_local, aux_count = out.shape[:2]
    rows = total.shape[1]
    pairs_dev = (received[0].shape[0] - TILE) // rows
    read_codes([piece[pairs_dev * rows :, :] for piece in received], pairs_dev, codes)
    for at, piece in enumerate(received):
        for k in range(pairs_dev):
            total[codes[at, k]] += piece[k * rows : (k + 1) * rows, :].astype(jnp.float32)
    stores = []
    parts = sems.shape[0]
    each = total.shape[0] // parts
    for part in range(parts):
        for r in range(part * each, (part + 1) * each, 2):
            summed = jnp.concatenate([total[r], total[r + 1]], axis=1).astype(jnp.bfloat16)
            mixed = jnp.dot(mix[...], summed, preferred_element_type=jnp.float32)
            staged[:, :, r * BS : (r + 2) * BS] = mixed.reshape(
                occ_local, aux_count, 2 * BS
            ).astype(jnp.bfloat16)
        lanes = pl.ds(part * each * BS, each * BS)
        store = pltpu.make_async_copy(
            staged.at[:, :, lanes], out.at[:, :, lanes], sems.at[part]
        )
        store.start()
        stores.append(store)
    for store in stores:
        store.wait()

def flip(value, axis, bits):
    count = lax.axis_size(axis)
    return lax.ppermute(value, axis, [(at, at ^ bits) for at in range(count)])


def beyond(value, shell_bits, aux_bits):
    shell_count, aux_count = lax.axis_size("shell"), lax.axis_size("aux")
    moves = [
        (shell * aux_count + aux, (shell ^ shell_bits) * aux_count + (aux ^ aux_bits))
        for shell in range(shell_count)
        for aux in range(aux_count)
    ]
    return lax.ppermute(value, ("shell", "aux"), moves)


def after(value, *others):
    return lax.optimization_barrier((value, *others))[0]


def cost(flops):
    return pl.CostEstimate(flops=int(flops), transcendentals=0, bytes_accessed=2**20)


def in_hbm(*operands):
    return [pltpu.with_memory_space_constraint(operand, pltpu.HBM) for operand in operands]


def exchanged_inputs(integrals, pair_list, coef, metric, occ_slot):
    pairs_dev = pair_list.shape[0]
    shell_count = lax.axis_size("shell")
    aux_count = lax.axis_size("aux")
    group = shell_count // 2
    occ_local = coef.shape[1] // (shell_count * aux_count)
    block_count = coef.shape[0] // BS * shell_count
    rows = occ_local * aux_count
    piece = jax.ShapeDtypeStruct((pairs_dev * rows + TILE, BS), jnp.bfloat16)
    vmem = pl.BlockSpec(memory_space=pltpu.VMEM)
    hbm = pl.BlockSpec(memory_space=pltpu.HBM)
    params = pltpu.CompilerParams(vmem_limit_bytes=40 * 2**20)

    def merged(name, first, second):
        return pl.pallas_call(
            merge_kernel,
            out_shape=jax.ShapeDtypeStruct(
                (2 * first.shape[0],) + first.shape[1:], jnp.bfloat16
            ),
            in_specs=[vmem] * 2,
            out_specs=vmem,
            scratch_shapes=[pltpu.SemaphoreType.DMA((2,))],
            compiler_params=params,
            name=name,
        )(first, second)

    blocks = integrals.reshape(pairs_dev, BS, BS)
    far_block = flip(blocks, "shell", group)
    operands = (pair_list, occ_slot.reshape(1, -1), coef)
    loaded = [
        pltpu.SMEM(pair_list.shape, jnp.int32),
        pltpu.VMEM((1, occ_slot.shape[0]), jnp.int32),
        pltpu.VMEM(coef.shape, jnp.bfloat16),
    ]
    near = pl.pallas_call(
        functools.partial(near_kernel, occ_local, aux_count),
        out_shape=[piece] * 4,
        in_specs=[hbm] * 4 + [vmem],
        out_specs=[vmem] * 4,
        scratch_shapes=loaded
        + [pltpu.VMEM(blocks.shape, jnp.bfloat16), pltpu.SemaphoreType.DMA((4,))],
        compiler_params=params,
        name="near_blocks",
    )(*in_hbm(*operands, blocks), flip(blocks, "aux", 1))
    near = [near[0]] + [beyond(near[f], f % 2, f // 2 * 2) for f in range(1, 4)]
    (sent_coef,) = pl.pallas_call(
        functools.partial(
            pick_kernel, [list(range(group, shell_count))], occ_local, aux_count
        ),
        out_shape=[
            jax.ShapeDtypeStruct((group * occ_local + TILE, pairs_dev * BS), jnp.bfloat16)
        ],
        in_specs=[hbm] * 3,
        out_specs=[vmem],
        scratch_shapes=loaded + [pltpu.SemaphoreType.DMA((3,))],
        compiler_params=params,
        name="pick",
    )(*in_hbm(*operands))
    far_block = after(far_block, sent_coef)
    far_coef = flip(after(sent_coef, far_block), "shell", group)
    far_pair = merged("far_pair", far_block, flip(far_block, "aux", 2))
    far_pairs = [far_pair, flip(far_pair, "aux", 1)]
    across = flip(
        pl.pallas_call(
            regroup_kernel,
            out_shape=jax.ShapeDtypeStruct(
                (4 * 2 * pairs_dev * occ_local + 2 * TILE, BS), jnp.bfloat16
            ),
            in_specs=[vmem] * 4,
            out_specs=vmem,
            compiler_params=params,
            name="regroup",
        )(*near),
        "shell",
        2,
    )
    far = []
    for low in range(2):
        far = pl.pallas_call(
            functools.partial(block_kernel, aux_count, low),
            out_shape=[piece] * group,
            in_specs=[vmem] * (2 + len(far)),
            out_specs=[vmem] * group,
            input_output_aliases={2 + f: f for f in range(len(far))},
            compiler_params=params,
            cost_estimate=cost(2e9) if low == 0 else None,
            name=f"far_blocks_{low}",
        )(far_coef, far_pairs[low], *far)
    total_shape = jax.ShapeDtypeStruct((block_count, rows, BS), jnp.float32)
    total, mix = pl.pallas_call(
        near_sum_kernel,
        out_shape=[total_shape, jax.ShapeDtypeStruct((rows, rows), jnp.bfloat16)],
        in_specs=[hbm] + [vmem] * 5,
        out_specs=[vmem] * 2,
        scratch_shapes=[
            pltpu.VMEM(metric.shape, jnp.bfloat16),
            pltpu.VMEM((8, BS), jnp.int32),
            pltpu.SemaphoreType.DMA,
        ],
        compiler_params=params,
        cost_estimate=cost(3e9),
        name="near_sum",
    )(*in_hbm(metric), *(after(one, far[0]) for one in near), across)
    far = [far[0]] + [flip(far[f], "shell", f) for f in range(1, group)]
    return pl.pallas_call(
        collect_kernel,
        out_shape=[
            jax.ShapeDtypeStruct((occ_local, aux_count, block_count * BS), jnp.bfloat16),
            total_shape,
        ],
        in_specs=[vmem] * (2 + group),
        out_specs=[hbm, vmem],
        input_output_aliases={1: 1},
        scratch_shapes=[
            pltpu.VMEM((occ_local, aux_count, block_count * BS), jnp.bfloat16),
            pltpu.VMEM((8, BS), jnp.int32),
            pltpu.SemaphoreType.DMA((4,)),
        ],
        compiler_params=params,
        name="collect",
    )(mix, total, *reversed(far))[0]


def per_device(integrals, pair_list, coef, metric, occ_slot):
    shell_count, aux_count = lax.axis_size("shell"), lax.axis_size("aux")
    occ_local = coef.shape[1] // (shell_count * aux_count)
    if occ_local % 16 or shell_count != 8 or aux_count != 4:
        return relayed_half_blocks(integrals, pair_list, coef, metric, occ_slot)
    return exchanged_inputs(integrals, pair_list, coef, metric, occ_slot)


def solution(mesh):
    placed = (P("shell", None, "aux", None), P("shell", None), P("shell", None), P(), P())
    return jax.shard_map(
        per_device,
        mesh=mesh,
        in_specs=placed,
        out_specs=P(("shell", "aux"), None, None),
        check_vma=False,
    )
```

```python
import functools

import jax
import jax.numpy as jnp
from jax import lax
from jax.experimental import pallas as pl
from jax.experimental.pallas import tpu as pltpu
from jax.sharding import PartitionSpec as P

BS = 128
TILE = 8


def relayed_half_blocks(integrals, pair_list, coef, metric, occ_slot):
    pairs_dev = pair_list.shape[0]
    rows_local = coef.shape[0]
    occ_count = coef.shape[1]
    blocks_dev = rows_local // BS
    shell_count = lax.axis_size("shell")
    block_count = blocks_dev * shell_count
    slot_count = occ_slot.shape[0]
    aux_dev = integrals.shape[2]
    inverse = (
        jnp.zeros((slot_count,), jnp.int32)
        .at[occ_slot]
        .set(jnp.arange(slot_count, dtype=jnp.int32))
    )
    ordered = jnp.take(
        coef.reshape(rows_local, slot_count, occ_count // slot_count), inverse, axis=1
    )
    ordered = ordered.reshape(rows_local, occ_count)

    def one_slot(item):
        int_block, column_index = item
        start = column_index % blocks_dev * BS
        column = lax.dynamic_slice_in_dim(ordered, start, BS, 0)
        product = lax.dot_general(
            column,
            int_block.reshape(BS, aux_dev * BS),
            (((0,), (0,)), ((), ())),
            preferred_element_type=jnp.float32,
        )
        return product.astype(jnp.bfloat16)

    half_blocks = lax.map(one_slot, (integrals, pair_list[:, 1]))
    half_blocks = half_blocks.reshape(pairs_dev, occ_count, aux_dev, BS)
    listing = lax.all_gather(pair_list, "shell", axis=0, tiled=True)
    targets = jnp.arange(block_count, dtype=jnp.int32)[:, None]
    selector = ((listing[:, 0][None, :] == targets) & (listing[:, 2][None, :] == 1)).astype(
        jnp.bfloat16
    )
    relayed = lax.all_to_all(
        lax.all_to_all(half_blocks, "shell", split_axis=1, concat_axis=0, tiled=True),
        "aux",
        split_axis=1,
        concat_axis=2,
        tiled=True,
    )
    summed = jnp.dot(
        selector, relayed.reshape(relayed.shape[0], -1), preferred_element_type=jnp.float32
    )
    blocks = summed.astype(jnp.bfloat16).reshape((block_count,) + relayed.shape[1:])
    result = jnp.einsum("qp,bipm->iqbm", metric, blocks, preferred_element_type=jnp.float32)
    return result.reshape(result.shape[0], result.shape[1], block_count * BS).astype(jnp.bfloat16)


def targets_of(slot_row, block_total, occ_count):
    width = occ_count // block_total
    spread = (
        lax.broadcasted_iota(jnp.int32, (block_total, occ_count), 1) // width
        == lax.broadcasted_iota(jnp.int32, (block_total, occ_count), 0)
    ).astype(jnp.bfloat16)
    slots = jnp.broadcast_to(slot_row, (8, block_total)).astype(jnp.float32)
    target = jnp.dot(slots.astype(jnp.bfloat16), spread, preferred_element_type=jnp.float32)
    return target.astype(jnp.int32)[:1] * width + (
        lax.broadcasted_iota(jnp.int32, (1, occ_count), 1) % width
    )


def code_tile(pairs):
    pairs_dev = pairs.shape[0]
    lane = lax.broadcasted_iota(jnp.int32, (1, BS), 1)
    code = jnp.zeros((1, BS), jnp.int32)
    for k in range(pairs_dev):
        code = jnp.where(lane == k, pairs[k, 0] % 128, code)
        code = jnp.where(lane == pairs_dev + k, pairs[k, 0] // 128, code)
    return jnp.broadcast_to(code.astype(jnp.float32), (TILE, BS)).astype(jnp.bfloat16)


def pick_kernel(
    flips,
    occ_local,
    aux_count,
    pairs_in,
    slot_in,
    coef_in,
    *refs,
):
    *outs, pairs, slot_row, coef, sems = refs
    pairs_dev = pairs.shape[0]
    blocks_dev = coef.shape[0] // BS
    occ_count = coef.shape[1]
    loads = [
        pltpu.make_async_copy(source, target, sems.at[at])
        for at, (source, target) in enumerate(
            ((slot_in, slot_row), (pairs_in, pairs), (coef_in, coef))
        )
    ]
    for load in loads:
        load.start()
    me = lax.axis_index("shell")
    mine = lax.axis_index("aux")
    every = sum(flips, [])
    row = lax.broadcasted_iota(jnp.int32, (len(every) * occ_local, 1), 0)
    owner = sum(jnp.where(row // occ_local == at, f, 0) for at, f in enumerate(every))
    wanted = (jnp.bitwise_xor(owner, me) * aux_count + mine) * occ_local + row % occ_local
    loads[0].wait()
    target = targets_of(slot_row[...], slot_row.shape[1], occ_count)
    pick = (wanted == target).astype(jnp.bfloat16)
    for load in loads[1:]:
        load.wait()
    code = code_tile(pairs)
    for k in range(pairs_dev):
        start = pl.multiple_of(lax.rem(pairs[k, 1], blocks_dev) * BS, BS)
        live = (pairs[k, 2] == 1).astype(jnp.float32)
        piece = lax.dot_general(
            pick,
            coef[pl.ds(start, BS), :],
            (((1,), (1,)), ((), ())),
            preferred_element_type=jnp.float32,
        )
        piece = (piece * live).astype(jnp.bfloat16)
        first = 0
        for out in outs:
            rows = out.shape[0] - TILE
            out[:rows, k * BS : (k + 1) * BS] = piece[first : first + rows]
            out[rows:, k * BS : (k + 1) * BS] = code
            first += rows


def near_kernel(
    occ_local,
    aux_count,
    pairs_in,
    slot_in,
    coef_in,
    blocks_in,
    beside,
    *refs,
):
    *outs, pairs, slot_row, coef, blocks, sems = refs
    pairs_dev = pairs.shape[0]
    blocks_dev = coef.shape[0] // BS
    occ_count = coef.shape[1]
    loads = [
        pltpu.make_async_copy(source, target, sems.at[at])
        for at, (source, target) in enumerate(
            ((slot_in, slot_row), (pairs_in, pairs), (coef_in, coef), (blocks_in, blocks))
        )
    ]
    for load in loads:
        load.start()
    me = lax.axis_index("shell")
    mine = lax.axis_index("aux")
    owned = aux_count // 2 * occ_local
    row = lax.broadcasted_iota(jnp.int32, (len(outs) * owned, 1), 0)
    owner = jnp.bitwise_xor(row // owned, me) * aux_count + jnp.bitwise_xor(
        row // occ_local % (aux_count // 2) * 2, mine
    )
    wanted = owner * occ_local + row % occ_local
    loads[0].wait()
    target = targets_of(slot_row[...], slot_row.shape[1], occ_count)
    pick = (wanted == target).astype(jnp.bfloat16)
    for load in loads[1:]:
        load.wait()
    code = code_tile(pairs)
    rows = [
        coef[pl.ds(pl.multiple_of(lax.rem(pairs[k, 1], blocks_dev) * BS, BS), BS), :]
        for k in range(pairs_dev)
    ]
    ordered = lax.dot_general(
        pick,
        jnp.concatenate(rows, axis=0),
        (((1,), (1,)), ((), ())),
        preferred_element_type=jnp.float32,
    ).astype(jnp.bfloat16)
    for k in range(pairs_dev):
        block = jnp.dot(
            ordered[:, k * BS : (k + 1) * BS],
            jnp.concatenate([blocks[k], beside[k]], axis=1),
            preferred_element_type=jnp.float32,
        )
        block = (block * (pairs[k, 2] == 1).astype(jnp.float32)).astype(jnp.bfloat16)
        for f, out in enumerate(outs):
            for j in range(aux_count // 2):
                first = f * owned + j * occ_local
                for c in range(2):
                    at = ((j * 2 + c) * pairs_dev + k) * occ_local
                    out[at : at + occ_local, :] = block[
                        first : first + occ_local, c * BS : (c + 1) * BS
                    ]
    for out in outs:
        out[out.shape[0] - TILE :, :] = code


def regroup_kernel(*refs):
    *received, out = refs
    rows = out.shape[0] // len(received)
    for f, piece in enumerate(received):
        out[f * rows : (f + 1) * rows, :] = piece[rows : 2 * rows, :]


def merge_kernel(first, second, out, sems):
    count = first.shape[0]
    skip = second.shape[0] - count
    loads = [
        pltpu.make_async_copy(first, out.at[:count], sems.at[0]),
        pltpu.make_async_copy(second.at[skip:], out.at[count:], sems.at[1]),
    ]
    for load in loads:
        load.start()
    for load in loads:
        load.wait()


def block_kernel(aux_count, low, coefs, blocks, *refs):
    pieces = refs[len(refs) // 2 :] if low else refs
    pairs_dev = blocks.shape[0] // 2
    rows = coefs.shape[0] - TILE
    occ_local = rows // len(pieces)
    mine = lax.axis_index("aux")
    for k in range(pairs_dev):
        left = coefs[:rows, k * BS : (k + 1) * BS]
        right = jnp.concatenate([blocks[k], blocks[pairs_dev + k]], axis=1)
        half = jnp.dot(left, right, preferred_element_type=jnp.float32).astype(jnp.bfloat16)
        for side in range(2):
            flipped = low + side * (aux_count // 2)
            at = k * aux_count + jnp.bitwise_xor(mine, flipped)
            start = pl.multiple_of(at * occ_local, occ_local)
            for f, piece in enumerate(pieces):
                piece[pl.ds(start, occ_local), :] = half[
                    f * occ_local : (f + 1) * occ_local, side * BS : (side + 1) * BS
                ]
    if low == 0:
        for piece in pieces:
            piece[pairs_dev * aux_count * occ_local :, :] = coefs[rows:, :BS]


def read_codes(received, pairs_dev, codes):
    for at, piece in enumerate(received):
        digits = piece[piece.shape[0] - TILE :, :].astype(jnp.float32)[:1]
        high = pltpu.roll(digits, BS - pairs_dev, 1)
        codes[at : at + 1, :] = (digits + 128.0 * high).astype(jnp.int32)


def near_sum_kernel(metric_in, *refs):
    *received, across, total, mix, metric, codes, sem = refs
    load = pltpu.make_async_copy(metric_in, metric, sem)
    load.start()
    total[...] = jnp.zeros_like(total)
    mine = lax.axis_index("aux")
    rows = total.shape[1]
    occ_local = rows // metric.shape[0]
    pairs_dev = (received[0].shape[0] - TILE) // rows
    read_codes(received, pairs_dev, codes)
    for f, piece in enumerate(received):
        for k in range(pairs_dev):
            r = codes[f, k]
            for j in range(metric.shape[0]):
                source, first = (across, f * 2 + j - 2) if j >= 2 else (piece, j)
                first = (first * pairs_dev + k) * occ_local
                start = pl.multiple_of(jnp.bitwise_xor(mine, j) * occ_local, occ_local)
                part = source[first : first + occ_local, :]
                total[r, pl.ds(start, occ_local), :] += part.astype(jnp.float32)
    load.wait()
    aux_count = metric.shape[0]
    row = lax.broadcasted_iota(jnp.int32, (rows, rows), 0)
    column = lax.broadcasted_iota(jnp.int32, (rows, rows), 1)
    left = (
        lax.broadcasted_iota(jnp.int32, (rows, aux_count), 0) % aux_count
        == lax.broadcasted_iota(jnp.int32, (rows, aux_count), 1)
    ).astype(jnp.bfloat16)
    right = (
        lax.broadcasted_iota(jnp.int32, (aux_count, rows), 1) // occ_local
        == lax.broadcasted_iota(jnp.int32, (aux_count, rows), 0)
    ).astype(jnp.bfloat16)
    factor = jnp.dot(left, metric[...], preferred_element_type=jnp.float32).astype(jnp.bfloat16)
    factor = jnp.dot(factor, right, preferred_element_type=jnp.float32)
    mix[...] = jnp.where(row // aux_count == column % occ_local, factor, 0.0).astype(jnp.bfloat16)


def collect_kernel(mix, total_in, *refs):
    *received, out, total, staged, codes, sems = refs
    occ_local, aux_count = out.shape[:2]
    rows = total.shape[1]
    pairs_dev = (received[0].shape[0] - TILE) // rows
    read_codes(received, pairs_dev, codes)
    for at, piece in enumerate(received):
        for k in range(pairs_dev):
            total[codes[at, k]] += piece[k * rows : (k + 1) * rows, :].astype(jnp.float32)
    stores = []
    parts = sems.shape[0]
    each = total.shape[0] // parts
    for part in range(parts):
        for r in range(part * each, (part + 1) * each, 2):
            summed = jnp.concatenate([total[r], total[r + 1]], axis=1).astype(jnp.bfloat16)
            mixed = jnp.dot(mix[...], summed, preferred_element_type=jnp.float32)
            staged[:, :, r * BS : (r + 2) * BS] = mixed.reshape(
                occ_local, aux_count, 2 * BS
            ).astype(jnp.bfloat16)
        lanes = pl.ds(part * each * BS, each * BS)
        store = pltpu.make_async_copy(
            staged.at[:, :, lanes], out.at[:, :, lanes], sems.at[part]
        )
        store.start()
        stores.append(store)
    for store in stores:
        store.wait()

def flip(value, axis, bits):
    count = lax.axis_size(axis)
    return lax.ppermute(value, axis, [(at, at ^ bits) for at in range(count)])


def after(value, *others):
    return lax.optimization_barrier((value, *others))[0]


def cost(flops):
    return pl.CostEstimate(flops=int(flops), transcendentals=0, bytes_accessed=2**20)


def in_hbm(*operands):
    return [pltpu.with_memory_space_constraint(operand, pltpu.HBM) for operand in operands]


def exchanged_inputs(integrals, pair_list, coef, metric, occ_slot):
    pairs_dev = pair_list.shape[0]
    shell_count = lax.axis_size("shell")
    aux_count = lax.axis_size("aux")
    group = shell_count // 2
    occ_local = coef.shape[1] // (shell_count * aux_count)
    block_count = coef.shape[0] // BS * shell_count
    rows = occ_local * aux_count
    piece = jax.ShapeDtypeStruct((pairs_dev * rows + TILE, BS), jnp.bfloat16)
    vmem = pl.BlockSpec(memory_space=pltpu.VMEM)
    hbm = pl.BlockSpec(memory_space=pltpu.HBM)
    params = pltpu.CompilerParams(vmem_limit_bytes=40 * 2**20)

    def merged(name, first, second):
        return pl.pallas_call(
            merge_kernel,
            out_shape=jax.ShapeDtypeStruct(
                (2 * first.shape[0],) + first.shape[1:], jnp.bfloat16
            ),
            in_specs=[vmem] * 2,
            out_specs=vmem,
            scratch_shapes=[pltpu.SemaphoreType.DMA((2,))],
            compiler_params=params,
            name=name,
        )(first, second)

    blocks = integrals.reshape(pairs_dev, BS, BS)
    far_block = flip(blocks, "shell", group)
    operands = (pair_list, occ_slot.reshape(1, -1), coef)
    loaded = [
        pltpu.SMEM(pair_list.shape, jnp.int32),
        pltpu.VMEM((1, occ_slot.shape[0]), jnp.int32),
        pltpu.VMEM(coef.shape, jnp.bfloat16),
    ]
    near = pl.pallas_call(
        functools.partial(near_kernel, occ_local, aux_count),
        out_shape=[piece] * group,
        in_specs=[hbm] * 4 + [vmem],
        out_specs=[vmem] * group,
        scratch_shapes=loaded
        + [pltpu.VMEM(blocks.shape, jnp.bfloat16), pltpu.SemaphoreType.DMA((4,))],
        compiler_params=params,
        name="near_blocks",
    )(*in_hbm(*operands, blocks), flip(blocks, "aux", 1))
    near = [near[0]] + [flip(near[f], "shell", f) for f in range(1, group)]
    (sent_coef,) = pl.pallas_call(
        functools.partial(
            pick_kernel, [list(range(group, shell_count))], occ_local, aux_count
        ),
        out_shape=[
            jax.ShapeDtypeStruct((group * occ_local + TILE, pairs_dev * BS), jnp.bfloat16)
        ],
        in_specs=[hbm] * 3,
        out_specs=[vmem],
        scratch_shapes=loaded + [pltpu.SemaphoreType.DMA((3,))],
        compiler_params=params,
        name="pick",
    )(*in_hbm(*operands))
    far_block = after(far_block, sent_coef)
    far_coef = flip(after(sent_coef, far_block), "shell", group)
    far_pair = merged("far_pair", far_block, flip(far_block, "aux", 2))
    far_pairs = [far_pair, flip(far_pair, "aux", 1)]
    across = flip(
        pl.pallas_call(
            regroup_kernel,
            out_shape=jax.ShapeDtypeStruct(
                (group * 2 * pairs_dev * occ_local, BS), jnp.bfloat16
            ),
            in_specs=[vmem] * group,
            out_specs=vmem,
            compiler_params=params,
            name="regroup",
        )(*near),
        "aux",
        2,
    )
    far = []
    for low in range(2):
        far = pl.pallas_call(
            functools.partial(block_kernel, aux_count, low),
            out_shape=[piece] * group,
            in_specs=[vmem] * (2 + len(far)),
            out_specs=[vmem] * group,
            input_output_aliases={2 + f: f for f in range(len(far))},
            compiler_params=params,
            cost_estimate=cost(2e9) if low == 0 else None,
            name=f"far_blocks_{low}",
        )(far_coef, far_pairs[low], *far)
    total_shape = jax.ShapeDtypeStruct((block_count, rows, BS), jnp.float32)
    total, mix = pl.pallas_call(
        near_sum_kernel,
        out_shape=[total_shape, jax.ShapeDtypeStruct((rows, rows), jnp.bfloat16)],
        in_specs=[hbm] + [vmem] * (group + 1),
        out_specs=[vmem] * 2,
        scratch_shapes=[
            pltpu.VMEM(metric.shape, jnp.bfloat16),
            pltpu.VMEM((8, BS), jnp.int32),
            pltpu.SemaphoreType.DMA,
        ],
        compiler_params=params,
        cost_estimate=cost(3e9),
        name="near_sum",
    )(*in_hbm(metric), *(after(one, far[0]) for one in near), across)
    far = [far[0]] + [flip(far[f], "shell", f) for f in range(1, group)]
    return pl.pallas_call(
        collect_kernel,
        out_shape=[
            jax.ShapeDtypeStruct((occ_local, aux_count, block_count * BS), jnp.bfloat16),
            total_shape,
        ],
        in_specs=[vmem] * (2 + group),
        out_specs=[hbm, vmem],
        input_output_aliases={1: 1},
        scratch_shapes=[
            pltpu.VMEM((occ_local, aux_count, block_count * BS), jnp.bfloat16),
            pltpu.VMEM((8, BS), jnp.int32),
            pltpu.SemaphoreType.DMA((4,)),
        ],
        compiler_params=params,
        name="collect",
    )(mix, total, *reversed(far))[0]


def per_device(integrals, pair_list, coef, metric, occ_slot):
    shell_count, aux_count = lax.axis_size("shell"), lax.axis_size("aux")
    occ_local = coef.shape[1] // (shell_count * aux_count)
    if occ_local % 16 or shell_count & (shell_count - 1) or aux_count != 4:
        return relayed_half_blocks(integrals, pair_list, coef, metric, occ_slot)
    return exchanged_inputs(integrals, pair_list, coef, metric, occ_slot)


def solution(mesh):
    placed = (P("shell", None, "aux", None), P("shell", None), P("shell", None), P(), P())
    return jax.shard_map(
        per_device,
        mesh=mesh,
        in_specs=placed,
        out_specs=P(("shell", "aux"), None, None),
        check_vma=False,
    )
```

```python
import functools

import jax
import jax.numpy as jnp
from jax import lax
from jax.experimental import pallas as pl
from jax.experimental.pallas import tpu as pltpu
from jax.sharding import PartitionSpec as P

BS = 128
TILE = 8


def relayed_half_blocks(integrals, pair_list, coef, metric, occ_slot):
    pairs_dev = pair_list.shape[0]
    rows_local = coef.shape[0]
    occ_count = coef.shape[1]
    blocks_dev = rows_local // BS
    shell_count = lax.axis_size("shell")
    block_count = blocks_dev * shell_count
    slot_count = occ_slot.shape[0]
    aux_dev = integrals.shape[2]
    inverse = (
        jnp.zeros((slot_count,), jnp.int32)
        .at[occ_slot]
        .set(jnp.arange(slot_count, dtype=jnp.int32))
    )
    ordered = jnp.take(
        coef.reshape(rows_local, slot_count, occ_count // slot_count), inverse, axis=1
    )
    ordered = ordered.reshape(rows_local, occ_count)

    def one_slot(item):
        int_block, column_index = item
        start = column_index % blocks_dev * BS
        column = lax.dynamic_slice_in_dim(ordered, start, BS, 0)
        product = lax.dot_general(
            column,
            int_block.reshape(BS, aux_dev * BS),
            (((0,), (0,)), ((), ())),
            preferred_element_type=jnp.float32,
        )
        return product.astype(jnp.bfloat16)

    half_blocks = lax.map(one_slot, (integrals, pair_list[:, 1]))
    half_blocks = half_blocks.reshape(pairs_dev, occ_count, aux_dev, BS)
    listing = lax.all_gather(pair_list, "shell", axis=0, tiled=True)
    targets = jnp.arange(block_count, dtype=jnp.int32)[:, None]
    selector = ((listing[:, 0][None, :] == targets) & (listing[:, 2][None, :] == 1)).astype(
        jnp.bfloat16
    )
    relayed = lax.all_to_all(
        lax.all_to_all(half_blocks, "shell", split_axis=1, concat_axis=0, tiled=True),
        "aux",
        split_axis=1,
        concat_axis=2,
        tiled=True,
    )
    summed = jnp.dot(
        selector, relayed.reshape(relayed.shape[0], -1), preferred_element_type=jnp.float32
    )
    blocks = summed.astype(jnp.bfloat16).reshape((block_count,) + relayed.shape[1:])
    result = jnp.einsum("qp,bipm->iqbm", metric, blocks, preferred_element_type=jnp.float32)
    return result.reshape(result.shape[0], result.shape[1], block_count * BS).astype(jnp.bfloat16)


def targets_of(slot_row, block_total, occ_count):
    width = occ_count // block_total
    spread = (
        lax.broadcasted_iota(jnp.int32, (block_total, occ_count), 1) // width
        == lax.broadcasted_iota(jnp.int32, (block_total, occ_count), 0)
    ).astype(jnp.bfloat16)
    slots = jnp.broadcast_to(slot_row, (8, block_total)).astype(jnp.float32)
    target = jnp.dot(slots.astype(jnp.bfloat16), spread, preferred_element_type=jnp.float32)
    return target.astype(jnp.int32)[:1] * width + (
        lax.broadcasted_iota(jnp.int32, (1, occ_count), 1) % width
    )


def code_tile(pairs):
    pairs_dev = pairs.shape[0]
    lane = lax.broadcasted_iota(jnp.int32, (1, BS), 1)
    code = jnp.zeros((1, BS), jnp.int32)
    for k in range(pairs_dev):
        code = jnp.where(lane == k, pairs[k, 0] % 128, code)
        code = jnp.where(lane == pairs_dev + k, pairs[k, 0] // 128, code)
    return jnp.broadcast_to(code.astype(jnp.float32), (TILE, BS)).astype(jnp.bfloat16)


def pick_kernel(
    flips,
    occ_local,
    aux_count,
    pairs_in,
    slot_in,
    coef_in,
    *refs,
):
    *outs, pairs, slot_row, coef, sems = refs
    pairs_dev = pairs.shape[0]
    blocks_dev = coef.shape[0] // BS
    occ_count = coef.shape[1]
    loads = [
        pltpu.make_async_copy(source, target, sems.at[at])
        for at, (source, target) in enumerate(
            ((slot_in, slot_row), (pairs_in, pairs), (coef_in, coef))
        )
    ]
    for load in loads:
        load.start()
    me = lax.axis_index("shell")
    mine = lax.axis_index("aux")
    every = sum(flips, [])
    row = lax.broadcasted_iota(jnp.int32, (len(every) * occ_local, 1), 0)
    owner = sum(jnp.where(row // occ_local == at, f, 0) for at, f in enumerate(every))
    wanted = (jnp.bitwise_xor(owner, me) * aux_count + mine) * occ_local + row % occ_local
    loads[0].wait()
    target = targets_of(slot_row[...], slot_row.shape[1], occ_count)
    pick = (wanted == target).astype(jnp.bfloat16)
    for load in loads[1:]:
        load.wait()
    code = code_tile(pairs)
    for k in range(pairs_dev):
        start = pl.multiple_of(lax.rem(pairs[k, 1], blocks_dev) * BS, BS)
        live = (pairs[k, 2] == 1).astype(jnp.float32)
        piece = lax.dot_general(
            pick,
            coef[pl.ds(start, BS), :],
            (((1,), (1,)), ((), ())),
            preferred_element_type=jnp.float32,
        )
        piece = (piece * live).astype(jnp.bfloat16)
        first = 0
        for out in outs:
            rows = out.shape[0] - TILE
            out[:rows, k * BS : (k + 1) * BS] = piece[first : first + rows]
            out[rows:, k * BS : (k + 1) * BS] = code
            first += rows


def near_kernel(
    occ_local,
    aux_count,
    pairs_in,
    slot_in,
    coef_in,
    blocks_in,
    beside,
    *refs,
):
    *outs, pairs, slot_row, coef, blocks, sems = refs
    pairs_dev = pairs.shape[0]
    blocks_dev = coef.shape[0] // BS
    occ_count = coef.shape[1]
    loads = [
        pltpu.make_async_copy(source, target, sems.at[at])
        for at, (source, target) in enumerate(
            ((slot_in, slot_row), (pairs_in, pairs), (coef_in, coef), (blocks_in, blocks))
        )
    ]
    for load in loads:
        load.start()
    me = lax.axis_index("shell")
    mine = lax.axis_index("aux")
    owned = aux_count // 2 * occ_local
    row = lax.broadcasted_iota(jnp.int32, (len(outs) * owned, 1), 0)
    owner = jnp.bitwise_xor(row // owned, me) * aux_count + jnp.bitwise_xor(
        row // occ_local % (aux_count // 2) * 2, mine
    )
    wanted = owner * occ_local + row % occ_local
    loads[0].wait()
    target = targets_of(slot_row[...], slot_row.shape[1], occ_count)
    pick = (wanted == target).astype(jnp.bfloat16)
    for load in loads[1:]:
        load.wait()
    code = code_tile(pairs)
    rows = [
        coef[pl.ds(pl.multiple_of(lax.rem(pairs[k, 1], blocks_dev) * BS, BS), BS), :]
        for k in range(pairs_dev)
    ]
    ordered = lax.dot_general(
        pick,
        jnp.concatenate(rows, axis=0),
        (((1,), (1,)), ((), ())),
        preferred_element_type=jnp.float32,
    ).astype(jnp.bfloat16)
    for k in range(pairs_dev):
        block = jnp.dot(
            ordered[:, k * BS : (k + 1) * BS],
            jnp.concatenate([blocks[k], beside[k]], axis=1),
            preferred_element_type=jnp.float32,
        )
        block = (block * (pairs[k, 2] == 1).astype(jnp.float32)).astype(jnp.bfloat16)
        for f, out in enumerate(outs):
            for j in range(aux_count // 2):
                first = f * owned + j * occ_local
                for c in range(2):
                    at = ((j * 2 + c) * pairs_dev + k) * occ_local
                    out[at : at + occ_local, :] = block[
                        first : first + occ_local, c * BS : (c + 1) * BS
                    ]
    for out in outs:
        out[out.shape[0] - TILE :, :] = code


def regroup_kernel(*refs):
    *received, out = refs
    rows = out.shape[0] // len(received)
    for f, piece in enumerate(received):
        out[f * rows : (f + 1) * rows, :] = piece[rows : 2 * rows, :]


def merge_kernel(first, second, out, sems):
    count = first.shape[0]
    skip = second.shape[0] - count
    loads = [
        pltpu.make_async_copy(first, out.at[:count], sems.at[0]),
        pltpu.make_async_copy(second.at[skip:], out.at[count:], sems.at[1]),
    ]
    for load in loads:
        load.start()
    for load in loads:
        load.wait()


def block_kernel(aux_count, low, coefs, blocks, *refs):
    pieces = refs[len(refs) // 2 :] if low else refs
    pairs_dev = blocks.shape[0] // 2
    rows = coefs.shape[0] - TILE
    occ_local = rows // len(pieces)
    mine = lax.axis_index("aux")
    for k in range(pairs_dev):
        left = coefs[:rows, k * BS : (k + 1) * BS]
        right = jnp.concatenate([blocks[k], blocks[pairs_dev + k]], axis=1)
        half = jnp.dot(left, right, preferred_element_type=jnp.float32).astype(jnp.bfloat16)
        for side in range(2):
            flipped = low + side * (aux_count // 2)
            at = k * aux_count + jnp.bitwise_xor(mine, flipped)
            start = pl.multiple_of(at * occ_local, occ_local)
            for f, piece in enumerate(pieces):
                piece[pl.ds(start, occ_local), :] = half[
                    f * occ_local : (f + 1) * occ_local, side * BS : (side + 1) * BS
                ]
    if low == 0:
        for piece in pieces:
            piece[pairs_dev * aux_count * occ_local :, :] = coefs[rows:, :BS]


def read_codes(received, pairs_dev, codes):
    for at, piece in enumerate(received):
        digits = piece[piece.shape[0] - TILE :, :].astype(jnp.float32)[:1]
        high = pltpu.roll(digits, BS - pairs_dev, 1)
        codes[at : at + 1, :] = (digits + 128.0 * high).astype(jnp.int32)


def near_sum_kernel(metric_in, *refs):
    *received, across, total, mix, metric, codes, sem = refs
    load = pltpu.make_async_copy(metric_in, metric, sem)
    load.start()
    total[...] = jnp.zeros_like(total)
    mine = lax.axis_index("aux")
    rows = total.shape[1]
    occ_local = rows // metric.shape[0]
    pairs_dev = (received[0].shape[0] - TILE) // rows
    read_codes(received, pairs_dev, codes)
    for f, piece in enumerate(received):
        for k in range(pairs_dev):
            r = codes[f, k]
            for j in range(metric.shape[0]):
                source, first = (across, f * 2 + j - 2) if j >= 2 else (piece, j)
                first = (first * pairs_dev + k) * occ_local
                start = pl.multiple_of(jnp.bitwise_xor(mine, j) * occ_local, occ_local)
                part = source[first : first + occ_local, :]
                total[r, pl.ds(start, occ_local), :] += part.astype(jnp.float32)
    load.wait()
    aux_count = metric.shape[0]
    row = lax.broadcasted_iota(jnp.int32, (rows, rows), 0)
    column = lax.broadcasted_iota(jnp.int32, (rows, rows), 1)
    left = (
        lax.broadcasted_iota(jnp.int32, (rows, aux_count), 0) % aux_count
        == lax.broadcasted_iota(jnp.int32, (rows, aux_count), 1)
    ).astype(jnp.bfloat16)
    right = (
        lax.broadcasted_iota(jnp.int32, (aux_count, rows), 1) // occ_local
        == lax.broadcasted_iota(jnp.int32, (aux_count, rows), 0)
    ).astype(jnp.bfloat16)
    factor = jnp.dot(left, metric[...], preferred_element_type=jnp.float32).astype(jnp.bfloat16)
    factor = jnp.dot(factor, right, preferred_element_type=jnp.float32)
    mix[...] = jnp.where(row // aux_count == column % occ_local, factor, 0.0).astype(jnp.bfloat16)


def collect_kernel(mix, total_in, *refs):
    *received, out, total, staged, codes, sems = refs
    occ_local, aux_count = out.shape[:2]
    rows = total.shape[1]
    pairs_dev = (received[0].shape[0] - TILE) // rows
    read_codes(received, pairs_dev, codes)
    for at, piece in enumerate(received):
        for k in range(pairs_dev):
            total[codes[at, k]] += piece[k * rows : (k + 1) * rows, :].astype(jnp.float32)
    stores = []
    parts = sems.shape[0]
    each = total.shape[0] // parts
    for part in range(parts):
        for r in range(part * each, (part + 1) * each, 2):
            summed = jnp.concatenate([total[r], total[r + 1]], axis=1).astype(jnp.bfloat16)
            mixed = jnp.dot(mix[...], summed, preferred_element_type=jnp.float32)
            staged[:, :, r * BS : (r + 2) * BS] = mixed.reshape(
                occ_local, aux_count, 2 * BS
            ).astype(jnp.bfloat16)
        lanes = pl.ds(part * each * BS, each * BS)
        store = pltpu.make_async_copy(
            staged.at[:, :, lanes], out.at[:, :, lanes], sems.at[part]
        )
        store.start()
        stores.append(store)
    for store in stores:
        store.wait()

def flip(value, axis, bits):
    count = lax.axis_size(axis)
    return lax.ppermute(value, axis, [(at, at ^ bits) for at in range(count)])


def after(value, *others):
    return lax.optimization_barrier((value, *others))[0]


def cost(flops):
    return pl.CostEstimate(flops=int(flops), transcendentals=0, bytes_accessed=2**20)


def in_hbm(*operands):
    return [pltpu.with_memory_space_constraint(operand, pltpu.HBM) for operand in operands]


def exchanged_inputs(integrals, pair_list, coef, metric, occ_slot):
    pairs_dev = pair_list.shape[0]
    shell_count = lax.axis_size("shell")
    aux_count = lax.axis_size("aux")
    group = shell_count // 2
    occ_local = coef.shape[1] // (shell_count * aux_count)
    block_count = coef.shape[0] // BS * shell_count
    rows = occ_local * aux_count
    piece = jax.ShapeDtypeStruct((pairs_dev * rows + TILE, BS), jnp.bfloat16)
    vmem = pl.BlockSpec(memory_space=pltpu.VMEM)
    hbm = pl.BlockSpec(memory_space=pltpu.HBM)
    params = pltpu.CompilerParams(vmem_limit_bytes=40 * 2**20)

    def merged(name, first, second):
        return pl.pallas_call(
            merge_kernel,
            out_shape=jax.ShapeDtypeStruct(
                (2 * first.shape[0],) + first.shape[1:], jnp.bfloat16
            ),
            in_specs=[vmem] * 2,
            out_specs=vmem,
            scratch_shapes=[pltpu.SemaphoreType.DMA((2,))],
            compiler_params=params,
            name=name,
        )(first, second)

    blocks = integrals.reshape(pairs_dev, BS, BS)
    far_block = flip(blocks, "shell", group)
    operands = (pair_list, occ_slot.reshape(1, -1), coef)
    loaded = [
        pltpu.SMEM(pair_list.shape, jnp.int32),
        pltpu.VMEM((1, occ_slot.shape[0]), jnp.int32),
        pltpu.VMEM(coef.shape, jnp.bfloat16),
    ]
    near = pl.pallas_call(
        functools.partial(near_kernel, occ_local, aux_count),
        out_shape=[piece] * group,
        in_specs=[hbm] * 4 + [vmem],
        out_specs=[vmem] * group,
        scratch_shapes=loaded
        + [pltpu.VMEM(blocks.shape, jnp.bfloat16), pltpu.SemaphoreType.DMA((4,))],
        compiler_params=params,
        name="near_blocks",
    )(*in_hbm(*operands, blocks), flip(blocks, "aux", 1))
    near = [near[0]] + [flip(near[f], "shell", f) for f in range(1, group)]
    (sent_coef,) = pl.pallas_call(
        functools.partial(
            pick_kernel, [list(range(group, shell_count))], occ_local, aux_count
        ),
        out_shape=[
            jax.ShapeDtypeStruct((group * occ_local + TILE, pairs_dev * BS), jnp.bfloat16)
        ],
        in_specs=[hbm] * 3,
        out_specs=[vmem],
        scratch_shapes=loaded + [pltpu.SemaphoreType.DMA((3,))],
        compiler_params=params,
        name="pick",
    )(*in_hbm(after(pair_list, near[0]), *operands[1:]))
    far_block = after(far_block, sent_coef)
    far_coef = flip(sent_coef, "shell", group)
    far_pair = merged("far_pair", far_block, flip(far_block, "aux", 2))
    far_pairs = [far_pair, flip(far_pair, "aux", 1)]
    across = flip(
        pl.pallas_call(
            regroup_kernel,
            out_shape=jax.ShapeDtypeStruct(
                (group * 2 * pairs_dev * occ_local, BS), jnp.bfloat16
            ),
            in_specs=[vmem] * group,
            out_specs=vmem,
            compiler_params=params,
            name="regroup",
        )(*near),
        "aux",
        2,
    )
    far = []
    for low in range(2):
        far = pl.pallas_call(
            functools.partial(block_kernel, aux_count, low),
            out_shape=[piece] * group,
            in_specs=[vmem] * (2 + len(far)),
            out_specs=[vmem] * group,
            input_output_aliases={2 + f: f for f in range(len(far))},
            compiler_params=params,
            cost_estimate=cost(3e9) if low == 0 else None,
            name=f"far_blocks_{low}",
        )(far_coef, far_pairs[low], *far)
    total_shape = jax.ShapeDtypeStruct((block_count, rows, BS), jnp.float32)
    total, mix = pl.pallas_call(
        near_sum_kernel,
        out_shape=[total_shape, jax.ShapeDtypeStruct((rows, rows), jnp.bfloat16)],
        in_specs=[hbm] + [vmem] * (group + 1),
        out_specs=[vmem] * 2,
        scratch_shapes=[
            pltpu.VMEM(metric.shape, jnp.bfloat16),
            pltpu.VMEM((8, BS), jnp.int32),
            pltpu.SemaphoreType.DMA,
        ],
        compiler_params=params,
        cost_estimate=cost(3e9),
        name="near_sum",
    )(*in_hbm(metric), *(after(one, far[0]) for one in near), across)
    far = [far[0]] + [flip(far[f], "shell", f) for f in range(1, group)]
    return pl.pallas_call(
        collect_kernel,
        out_shape=[
            jax.ShapeDtypeStruct((occ_local, aux_count, block_count * BS), jnp.bfloat16),
            total_shape,
        ],
        in_specs=[vmem] * (2 + group),
        out_specs=[hbm, vmem],
        input_output_aliases={1: 1},
        scratch_shapes=[
            pltpu.VMEM((occ_local, aux_count, block_count * BS), jnp.bfloat16),
            pltpu.VMEM((8, BS), jnp.int32),
            pltpu.SemaphoreType.DMA((4,)),
        ],
        compiler_params=params,
        name="collect",
    )(mix, total, *reversed(far))[0]


def per_device(integrals, pair_list, coef, metric, occ_slot):
    shell_count, aux_count = lax.axis_size("shell"), lax.axis_size("aux")
    occ_local = coef.shape[1] // (shell_count * aux_count)
    if occ_local % 16 or shell_count & (shell_count - 1) or aux_count != 4:
        return relayed_half_blocks(integrals, pair_list, coef, metric, occ_slot)
    return exchanged_inputs(integrals, pair_list, coef, metric, occ_slot)


def solution(mesh):
    placed = (P("shell", None, "aux", None), P("shell", None), P("shell", None), P(), P())
    return jax.shard_map(
        per_device,
        mesh=mesh,
        in_specs=placed,
        out_specs=P(("shell", "aux"), None, None),
        check_vma=False,
    )
```

```python
import functools

import jax
import jax.numpy as jnp
from jax import lax
from jax.experimental import pallas as pl
from jax.experimental.pallas import tpu as pltpu
from jax.sharding import PartitionSpec as P

BS = 128
TILE = 8


def relayed_half_blocks(integrals, pair_list, coef, metric, occ_slot):
    pairs_dev = pair_list.shape[0]
    rows_local = coef.shape[0]
    occ_count = coef.shape[1]
    blocks_dev = rows_local // BS
    shell_count = lax.axis_size("shell")
    block_count = blocks_dev * shell_count
    slot_count = occ_slot.shape[0]
    aux_dev = integrals.shape[2]
    inverse = (
        jnp.zeros((slot_count,), jnp.int32)
        .at[occ_slot]
        .set(jnp.arange(slot_count, dtype=jnp.int32))
    )
    ordered = jnp.take(
        coef.reshape(rows_local, slot_count, occ_count // slot_count), inverse, axis=1
    )
    ordered = ordered.reshape(rows_local, occ_count)

    def one_slot(item):
        int_block, column_index = item
        start = column_index % blocks_dev * BS
        column = lax.dynamic_slice_in_dim(ordered, start, BS, 0)
        product = lax.dot_general(
            column,
            int_block.reshape(BS, aux_dev * BS),
            (((0,), (0,)), ((), ())),
            preferred_element_type=jnp.float32,
        )
        return product.astype(jnp.bfloat16)

    half_blocks = lax.map(one_slot, (integrals, pair_list[:, 1]))
    half_blocks = half_blocks.reshape(pairs_dev, occ_count, aux_dev, BS)
    listing = lax.all_gather(pair_list, "shell", axis=0, tiled=True)
    targets = jnp.arange(block_count, dtype=jnp.int32)[:, None]
    selector = ((listing[:, 0][None, :] == targets) & (listing[:, 2][None, :] == 1)).astype(
        jnp.bfloat16
    )
    relayed = lax.all_to_all(
        lax.all_to_all(half_blocks, "shell", split_axis=1, concat_axis=0, tiled=True),
        "aux",
        split_axis=1,
        concat_axis=2,
        tiled=True,
    )
    summed = jnp.dot(
        selector, relayed.reshape(relayed.shape[0], -1), preferred_element_type=jnp.float32
    )
    blocks = summed.astype(jnp.bfloat16).reshape((block_count,) + relayed.shape[1:])
    result = jnp.einsum("qp,bipm->iqbm", metric, blocks, preferred_element_type=jnp.float32)
    return result.reshape(result.shape[0], result.shape[1], block_count * BS).astype(jnp.bfloat16)


def targets_of(slot_row, block_total, occ_count):
    width = occ_count // block_total
    spread = (
        lax.broadcasted_iota(jnp.int32, (block_total, occ_count), 1) // width
        == lax.broadcasted_iota(jnp.int32, (block_total, occ_count), 0)
    ).astype(jnp.bfloat16)
    slots = jnp.broadcast_to(slot_row, (8, block_total)).astype(jnp.float32)
    target = jnp.dot(slots.astype(jnp.bfloat16), spread, preferred_element_type=jnp.float32)
    return target.astype(jnp.int32)[:1] * width + (
        lax.broadcasted_iota(jnp.int32, (1, occ_count), 1) % width
    )


def code_tile(pairs):
    pairs_dev = pairs.shape[0]
    lane = lax.broadcasted_iota(jnp.int32, (1, BS), 1)
    code = jnp.zeros((1, BS), jnp.int32)
    for k in range(pairs_dev):
        code = jnp.where(lane == k, pairs[k, 0] % 128, code)
        code = jnp.where(lane == pairs_dev + k, pairs[k, 0] // 128, code)
    return jnp.broadcast_to(code.astype(jnp.float32), (TILE, BS)).astype(jnp.bfloat16)


def pick_kernel(
    flips,
    occ_local,
    aux_count,
    pairs_in,
    slot_in,
    coef_in,
    *refs,
):
    *outs, pairs, slot_row, coef, sems = refs
    pairs_dev = pairs.shape[0]
    blocks_dev = coef.shape[0] // BS
    occ_count = coef.shape[1]
    loads = [
        pltpu.make_async_copy(source, target, sems.at[at])
        for at, (source, target) in enumerate(
            ((slot_in, slot_row), (pairs_in, pairs), (coef_in, coef))
        )
    ]
    for load in loads:
        load.start()
    me = lax.axis_index("shell")
    mine = lax.axis_index("aux")
    every = sum(flips, [])
    row = lax.broadcasted_iota(jnp.int32, (len(every) * occ_local, 1), 0)
    owner = sum(jnp.where(row // occ_local == at, f, 0) for at, f in enumerate(every))
    wanted = (jnp.bitwise_xor(owner, me) * aux_count + mine) * occ_local + row % occ_local
    loads[0].wait()
    target = targets_of(slot_row[...], slot_row.shape[1], occ_count)
    pick = (wanted == target).astype(jnp.bfloat16)
    for load in loads[1:]:
        load.wait()
    code = code_tile(pairs)
    for k in range(pairs_dev):
        start = pl.multiple_of(lax.rem(pairs[k, 1], blocks_dev) * BS, BS)
        live = (pairs[k, 2] == 1).astype(jnp.float32)
        piece = lax.dot_general(
            pick,
            coef[pl.ds(start, BS), :],
            (((1,), (1,)), ((), ())),
            preferred_element_type=jnp.float32,
        )
        piece = (piece * live).astype(jnp.bfloat16)
        first = 0
        for out in outs:
            rows = out.shape[0] - TILE
            out[:rows, k * BS : (k + 1) * BS] = piece[first : first + rows]
            out[rows:, k * BS : (k + 1) * BS] = code
            first += rows


def near_kernel(
    occ_local,
    aux_count,
    pairs_in,
    slot_in,
    coef_in,
    blocks_in,
    beside,
    *refs,
):
    *outs, pairs, slot_row, coef, blocks, sems = refs
    pairs_dev = pairs.shape[0]
    blocks_dev = coef.shape[0] // BS
    occ_count = coef.shape[1]
    loads = [
        pltpu.make_async_copy(source, target, sems.at[at])
        for at, (source, target) in enumerate(
            ((slot_in, slot_row), (pairs_in, pairs), (coef_in, coef), (blocks_in, blocks))
        )
    ]
    for load in loads:
        load.start()
    me = lax.axis_index("shell")
    mine = lax.axis_index("aux")
    owned = aux_count // 2 * occ_local
    row = lax.broadcasted_iota(jnp.int32, (len(outs) * owned, 1), 0)
    owner = jnp.bitwise_xor(row // owned, me) * aux_count + jnp.bitwise_xor(
        row // occ_local % (aux_count // 2) * 2, mine
    )
    wanted = owner * occ_local + row % occ_local
    loads[0].wait()
    target = targets_of(slot_row[...], slot_row.shape[1], occ_count)
    pick = (wanted == target).astype(jnp.bfloat16)
    for load in loads[1:]:
        load.wait()
    code = code_tile(pairs)
    rows = [
        coef[pl.ds(pl.multiple_of(lax.rem(pairs[k, 1], blocks_dev) * BS, BS), BS), :]
        for k in range(pairs_dev)
    ]
    ordered = lax.dot_general(
        pick,
        jnp.concatenate(rows, axis=0),
        (((1,), (1,)), ((), ())),
        preferred_element_type=jnp.float32,
    ).astype(jnp.bfloat16)
    for k in range(pairs_dev):
        block = jnp.dot(
            ordered[:, k * BS : (k + 1) * BS],
            jnp.concatenate([blocks[k], beside[k]], axis=1),
            preferred_element_type=jnp.float32,
        )
        block = (block * (pairs[k, 2] == 1).astype(jnp.float32)).astype(jnp.bfloat16)
        for f, out in enumerate(outs):
            for j in range(aux_count // 2):
                first = f * owned + j * occ_local
                for c in range(2):
                    at = ((j * 2 + c) * pairs_dev + k) * occ_local
                    out[at : at + occ_local, :] = block[
                        first : first + occ_local, c * BS : (c + 1) * BS
                    ]
    for out in outs:
        out[out.shape[0] - TILE :, :] = code


def regroup_kernel(*refs):
    *received, out = refs
    rows = out.shape[0] // len(received)
    for f, piece in enumerate(received):
        out[f * rows : (f + 1) * rows, :] = piece[rows : 2 * rows, :]


def merge_kernel(first, second, out, sems):
    count = first.shape[0]
    skip = second.shape[0] - count
    loads = [
        pltpu.make_async_copy(first, out.at[:count], sems.at[0]),
        pltpu.make_async_copy(second.at[skip:], out.at[count:], sems.at[1]),
    ]
    for load in loads:
        load.start()
    for load in loads:
        load.wait()


def block_kernel(aux_count, low, coefs, blocks, *refs):
    pieces = refs[len(refs) // 2 :] if low else refs
    pairs_dev = blocks.shape[0] // 2
    rows = coefs.shape[0] - TILE
    occ_local = rows // len(pieces)
    mine = lax.axis_index("aux")
    for k in range(pairs_dev):
        left = coefs[:rows, k * BS : (k + 1) * BS]
        right = jnp.concatenate([blocks[k], blocks[pairs_dev + k]], axis=1)
        half = jnp.dot(left, right, preferred_element_type=jnp.float32).astype(jnp.bfloat16)
        for side in range(2):
            flipped = low + side * (aux_count // 2)
            at = k * aux_count + jnp.bitwise_xor(mine, flipped)
            start = pl.multiple_of(at * occ_local, occ_local)
            for f, piece in enumerate(pieces):
                piece[pl.ds(start, occ_local), :] = half[
                    f * occ_local : (f + 1) * occ_local, side * BS : (side + 1) * BS
                ]
    if low == 0:
        for piece in pieces:
            piece[pairs_dev * aux_count * occ_local :, :] = coefs[rows:, :BS]


def read_codes(received, pairs_dev, codes):
    for at, piece in enumerate(received):
        digits = piece[piece.shape[0] - TILE :, :].astype(jnp.float32)[:1]
        high = pltpu.roll(digits, BS - pairs_dev, 1)
        codes[at : at + 1, :] = (digits + 128.0 * high).astype(jnp.int32)


def near_sum_kernel(metric_in, own, *refs):
    *received, across, total, mix, metric, codes, sem = refs
    load = pltpu.make_async_copy(metric_in, metric, sem)
    load.start()
    total[...] = jnp.zeros_like(total)
    mine = lax.axis_index("aux")
    rows = total.shape[1]
    occ_local = rows // metric.shape[0]
    pairs_dev = (received[0].shape[0] - TILE) // rows
    read_codes([*received, own], pairs_dev, codes)
    for k in range(pairs_dev):
        part = own[k * rows : (k + 1) * rows, :]
        total[codes[len(received), k]] += part.astype(jnp.float32)
    for f, piece in enumerate(received):
        for k in range(pairs_dev):
            r = codes[f, k]
            for j in range(metric.shape[0]):
                source, first = (across, f * 2 + j - 2) if j >= 2 else (piece, j)
                first = (first * pairs_dev + k) * occ_local
                start = pl.multiple_of(jnp.bitwise_xor(mine, j) * occ_local, occ_local)
                part = source[first : first + occ_local, :]
                total[r, pl.ds(start, occ_local), :] += part.astype(jnp.float32)
    load.wait()
    aux_count = metric.shape[0]
    row = lax.broadcasted_iota(jnp.int32, (rows, rows), 0)
    column = lax.broadcasted_iota(jnp.int32, (rows, rows), 1)
    left = (
        lax.broadcasted_iota(jnp.int32, (rows, aux_count), 0) % aux_count
        == lax.broadcasted_iota(jnp.int32, (rows, aux_count), 1)
    ).astype(jnp.bfloat16)
    right = (
        lax.broadcasted_iota(jnp.int32, (aux_count, rows), 1) // occ_local
        == lax.broadcasted_iota(jnp.int32, (aux_count, rows), 0)
    ).astype(jnp.bfloat16)
    factor = jnp.dot(left, metric[...], preferred_element_type=jnp.float32).astype(jnp.bfloat16)
    factor = jnp.dot(factor, right, preferred_element_type=jnp.float32)
    mix[...] = jnp.where(row // aux_count == column % occ_local, factor, 0.0).astype(jnp.bfloat16)


def collect_kernel(mix, total_in, *refs):
    *received, out, total, staged, codes, sems = refs
    occ_local, aux_count = out.shape[:2]
    rows = total.shape[1]
    pairs_dev = (received[0].shape[0] - TILE) // rows
    read_codes(received, pairs_dev, codes)
    for at, piece in enumerate(received):
        for k in range(pairs_dev):
            total[codes[at, k]] += piece[k * rows : (k + 1) * rows, :].astype(jnp.float32)
    stores = []
    parts = sems.shape[0]
    each = total.shape[0] // parts
    for part in range(parts):
        for r in range(part * each, (part + 1) * each, 2):
            summed = jnp.concatenate([total[r], total[r + 1]], axis=1).astype(jnp.bfloat16)
            mixed = jnp.dot(mix[...], summed, preferred_element_type=jnp.float32)
            staged[:, :, r * BS : (r + 2) * BS] = mixed.reshape(
                occ_local, aux_count, 2 * BS
            ).astype(jnp.bfloat16)
        lanes = pl.ds(part * each * BS, each * BS)
        store = pltpu.make_async_copy(
            staged.at[:, :, lanes], out.at[:, :, lanes], sems.at[part]
        )
        store.start()
        stores.append(store)
    for store in stores:
        store.wait()

def flip(value, axis, bits):
    count = lax.axis_size(axis)
    return lax.ppermute(value, axis, [(at, at ^ bits) for at in range(count)])


def after(value, *others):
    return lax.optimization_barrier((value, *others))[0]


def cost(flops):
    return pl.CostEstimate(flops=int(flops), transcendentals=0, bytes_accessed=2**20)


def in_hbm(*operands):
    return [pltpu.with_memory_space_constraint(operand, pltpu.HBM) for operand in operands]


def exchanged_inputs(integrals, pair_list, coef, metric, occ_slot):
    pairs_dev = pair_list.shape[0]
    shell_count = lax.axis_size("shell")
    aux_count = lax.axis_size("aux")
    group = shell_count // 2
    occ_local = coef.shape[1] // (shell_count * aux_count)
    block_count = coef.shape[0] // BS * shell_count
    rows = occ_local * aux_count
    piece = jax.ShapeDtypeStruct((pairs_dev * rows + TILE, BS), jnp.bfloat16)
    vmem = pl.BlockSpec(memory_space=pltpu.VMEM)
    hbm = pl.BlockSpec(memory_space=pltpu.HBM)
    params = pltpu.CompilerParams(vmem_limit_bytes=40 * 2**20)

    def merged(name, first, second):
        return pl.pallas_call(
            merge_kernel,
            out_shape=jax.ShapeDtypeStruct(
                (2 * first.shape[0],) + first.shape[1:], jnp.bfloat16
            ),
            in_specs=[vmem] * 2,
            out_specs=vmem,
            scratch_shapes=[pltpu.SemaphoreType.DMA((2,))],
            compiler_params=params,
            name=name,
        )(first, second)

    blocks = integrals.reshape(pairs_dev, BS, BS)
    far_block = flip(blocks, "shell", group)
    operands = (pair_list, occ_slot.reshape(1, -1), coef)
    loaded = [
        pltpu.SMEM(pair_list.shape, jnp.int32),
        pltpu.VMEM((1, occ_slot.shape[0]), jnp.int32),
        pltpu.VMEM(coef.shape, jnp.bfloat16),
    ]
    near = pl.pallas_call(
        functools.partial(near_kernel, occ_local, aux_count),
        out_shape=[piece] * group,
        in_specs=[hbm] * 4 + [vmem],
        out_specs=[vmem] * group,
        scratch_shapes=loaded
        + [pltpu.VMEM(blocks.shape, jnp.bfloat16), pltpu.SemaphoreType.DMA((4,))],
        compiler_params=params,
        name="near_blocks",
    )(*in_hbm(*operands, blocks), flip(blocks, "aux", 1))
    near = [near[0]] + [flip(near[f], "shell", f) for f in range(1, group)]
    (sent_coef,) = pl.pallas_call(
        functools.partial(
            pick_kernel, [list(range(group, shell_count))], occ_local, aux_count
        ),
        out_shape=[
            jax.ShapeDtypeStruct((group * occ_local + TILE, pairs_dev * BS), jnp.bfloat16)
        ],
        in_specs=[hbm] * 3,
        out_specs=[vmem],
        scratch_shapes=loaded + [pltpu.SemaphoreType.DMA((3,))],
        compiler_params=params,
        name="pick",
    )(*in_hbm(*operands))
    far_block = after(far_block, sent_coef)
    far_coef = flip(after(sent_coef, far_block), "shell", group)
    far_pair = merged("far_pair", far_block, flip(far_block, "aux", 2))
    far_pairs = [far_pair, flip(far_pair, "aux", 1)]
    across = flip(
        pl.pallas_call(
            regroup_kernel,
            out_shape=jax.ShapeDtypeStruct(
                (group * 2 * pairs_dev * occ_local, BS), jnp.bfloat16
            ),
            in_specs=[vmem] * group,
            out_specs=vmem,
            compiler_params=params,
            name="regroup",
        )(*near),
        "aux",
        2,
    )
    far = []
    for low in range(2):
        far = pl.pallas_call(
            functools.partial(block_kernel, aux_count, low),
            out_shape=[piece] * group,
            in_specs=[vmem] * (2 + len(far)),
            out_specs=[vmem] * group,
            input_output_aliases={2 + f: f for f in range(len(far))},
            compiler_params=params,
            cost_estimate=cost(2e9) if low == 0 else None,
            name=f"far_blocks_{low}",
        )(far_coef, far_pairs[low], *far)
    total_shape = jax.ShapeDtypeStruct((block_count, rows, BS), jnp.float32)
    total, mix = pl.pallas_call(
        near_sum_kernel,
        out_shape=[total_shape, jax.ShapeDtypeStruct((rows, rows), jnp.bfloat16)],
        in_specs=[hbm] + [vmem] * (group + 2),
        out_specs=[vmem] * 2,
        scratch_shapes=[
            pltpu.VMEM(metric.shape, jnp.bfloat16),
            pltpu.VMEM((8, BS), jnp.int32),
            pltpu.SemaphoreType.DMA,
        ],
        compiler_params=params,
        cost_estimate=cost(3e9),
        name="near_sum",
    )(*in_hbm(metric), far[0], *near, across)
    far = [far[0]] + [flip(far[f], "shell", f) for f in range(1, group)]
    return pl.pallas_call(
        collect_kernel,
        out_shape=[
            jax.ShapeDtypeStruct((occ_local, aux_count, block_count * BS), jnp.bfloat16),
            total_shape,
        ],
        in_specs=[vmem] * (1 + group),
        out_specs=[hbm, vmem],
        input_output_aliases={1: 1},
        scratch_shapes=[
            pltpu.VMEM((occ_local, aux_count, block_count * BS), jnp.bfloat16),
            pltpu.VMEM((8, BS), jnp.int32),
            pltpu.SemaphoreType.DMA((4,)),
        ],
        compiler_params=params,
        name="collect",
    )(mix, total, far[3], far[1], far[2])[0]


def per_device(integrals, pair_list, coef, metric, occ_slot):
    shell_count, aux_count = lax.axis_size("shell"), lax.axis_size("aux")
    occ_local = coef.shape[1] // (shell_count * aux_count)
    if occ_local % 16 or shell_count & (shell_count - 1) or aux_count != 4:
        return relayed_half_blocks(integrals, pair_list, coef, metric, occ_slot)
    return exchanged_inputs(integrals, pair_list, coef, metric, occ_slot)


def solution(mesh):
    placed = (P("shell", None, "aux", None), P("shell", None), P("shell", None), P(), P())
    return jax.shard_map(
        per_device,
        mesh=mesh,
        in_specs=placed,
        out_specs=P(("shell", "aux"), None, None),
        check_vma=False,
    )
```

```python
import functools

import jax
import jax.numpy as jnp
from jax import lax
from jax.experimental import pallas as pl
from jax.experimental.pallas import tpu as pltpu
from jax.sharding import PartitionSpec as P

BS = 128
TILE = 8


def relayed_half_blocks(integrals, pair_list, coef, metric, occ_slot):
    pairs_dev = pair_list.shape[0]
    rows_local = coef.shape[0]
    occ_count = coef.shape[1]
    blocks_dev = rows_local // BS
    shell_count = lax.axis_size("shell")
    block_count = blocks_dev * shell_count
    slot_count = occ_slot.shape[0]
    aux_dev = integrals.shape[2]
    inverse = (
        jnp.zeros((slot_count,), jnp.int32)
        .at[occ_slot]
        .set(jnp.arange(slot_count, dtype=jnp.int32))
    )
    ordered = jnp.take(
        coef.reshape(rows_local, slot_count, occ_count // slot_count), inverse, axis=1
    )
    ordered = ordered.reshape(rows_local, occ_count)

    def one_slot(item):
        int_block, column_index = item
        start = column_index % blocks_dev * BS
        column = lax.dynamic_slice_in_dim(ordered, start, BS, 0)
        product = lax.dot_general(
            column,
            int_block.reshape(BS, aux_dev * BS),
            (((0,), (0,)), ((), ())),
            preferred_element_type=jnp.float32,
        )
        return product.astype(jnp.bfloat16)

    half_blocks = lax.map(one_slot, (integrals, pair_list[:, 1]))
    half_blocks = half_blocks.reshape(pairs_dev, occ_count, aux_dev, BS)
    listing = lax.all_gather(pair_list, "shell", axis=0, tiled=True)
    targets = jnp.arange(block_count, dtype=jnp.int32)[:, None]
    selector = ((listing[:, 0][None, :] == targets) & (listing[:, 2][None, :] == 1)).astype(
        jnp.bfloat16
    )
    relayed = lax.all_to_all(
        lax.all_to_all(half_blocks, "shell", split_axis=1, concat_axis=0, tiled=True),
        "aux",
        split_axis=1,
        concat_axis=2,
        tiled=True,
    )
    summed = jnp.dot(
        selector, relayed.reshape(relayed.shape[0], -1), preferred_element_type=jnp.float32
    )
    blocks = summed.astype(jnp.bfloat16).reshape((block_count,) + relayed.shape[1:])
    result = jnp.einsum("qp,bipm->iqbm", metric, blocks, preferred_element_type=jnp.float32)
    return result.reshape(result.shape[0], result.shape[1], block_count * BS).astype(jnp.bfloat16)


def targets_of(slot_row, block_total, occ_count):
    width = occ_count // block_total
    spread = (
        lax.broadcasted_iota(jnp.int32, (block_total, occ_count), 1) // width
        == lax.broadcasted_iota(jnp.int32, (block_total, occ_count), 0)
    ).astype(jnp.bfloat16)
    slots = jnp.broadcast_to(slot_row, (8, block_total)).astype(jnp.float32)
    target = jnp.dot(slots.astype(jnp.bfloat16), spread, preferred_element_type=jnp.float32)
    return target.astype(jnp.int32)[:1] * width + (
        lax.broadcasted_iota(jnp.int32, (1, occ_count), 1) % width
    )


def code_tile(pairs):
    pairs_dev = pairs.shape[0]
    lane = lax.broadcasted_iota(jnp.int32, (1, BS), 1)
    code = jnp.zeros((1, BS), jnp.int32)
    for k in range(pairs_dev):
        code = jnp.where(lane == k, pairs[k, 0] % 128, code)
        code = jnp.where(lane == pairs_dev + k, pairs[k, 0] // 128, code)
    return jnp.broadcast_to(code.astype(jnp.float32), (TILE, BS)).astype(jnp.bfloat16)


def pick_kernel(
    flips,
    occ_local,
    aux_count,
    pairs_in,
    slot_in,
    coef_in,
    *refs,
):
    *outs, pairs, slot_row, coef, sems = refs
    pairs_dev = pairs.shape[0]
    blocks_dev = coef.shape[0] // BS
    occ_count = coef.shape[1]
    loads = [
        pltpu.make_async_copy(source, target, sems.at[at])
        for at, (source, target) in enumerate(
            ((slot_in, slot_row), (pairs_in, pairs), (coef_in, coef))
        )
    ]
    for load in loads:
        load.start()
    me = lax.axis_index("shell")
    mine = lax.axis_index("aux")
    every = sum(flips, [])
    row = lax.broadcasted_iota(jnp.int32, (len(every) * occ_local, 1), 0)
    owner = sum(jnp.where(row // occ_local == at, f, 0) for at, f in enumerate(every))
    wanted = (jnp.bitwise_xor(owner, me) * aux_count + mine) * occ_local + row % occ_local
    loads[0].wait()
    target = targets_of(slot_row[...], slot_row.shape[1], occ_count)
    pick = (wanted == target).astype(jnp.bfloat16)
    for load in loads[1:]:
        load.wait()
    code = code_tile(pairs)
    for k in range(pairs_dev):
        start = pl.multiple_of(lax.rem(pairs[k, 1], blocks_dev) * BS, BS)
        live = (pairs[k, 2] == 1).astype(jnp.float32)
        piece = lax.dot_general(
            pick,
            coef[pl.ds(start, BS), :],
            (((1,), (1,)), ((), ())),
            preferred_element_type=jnp.float32,
        )
        piece = (piece * live).astype(jnp.bfloat16)
        first = 0
        for out in outs:
            rows = out.shape[0] - TILE
            out[:rows, k * BS : (k + 1) * BS] = piece[first : first + rows]
            out[rows:, k * BS : (k + 1) * BS] = code
            first += rows


def near_kernel(
    occ_local,
    aux_count,
    pairs_in,
    slot_in,
    coef_in,
    blocks_in,
    beside,
    *refs,
):
    *outs, pairs, slot_row, coef, blocks, sems = refs
    pairs_dev = pairs.shape[0]
    blocks_dev = coef.shape[0] // BS
    occ_count = coef.shape[1]
    loads = [
        pltpu.make_async_copy(source, target, sems.at[at])
        for at, (source, target) in enumerate(
            ((slot_in, slot_row), (pairs_in, pairs), (coef_in, coef), (blocks_in, blocks))
        )
    ]
    for load in loads:
        load.start()
    me = lax.axis_index("shell")
    mine = lax.axis_index("aux")
    owned = aux_count // 2 * occ_local
    row = lax.broadcasted_iota(jnp.int32, (len(outs) * owned, 1), 0)
    owner = jnp.bitwise_xor(row // owned, me) * aux_count + jnp.bitwise_xor(
        row // occ_local % (aux_count // 2) * 2, mine
    )
    wanted = owner * occ_local + row % occ_local
    loads[0].wait()
    target = targets_of(slot_row[...], slot_row.shape[1], occ_count)
    pick = (wanted == target).astype(jnp.bfloat16)
    for load in loads[1:]:
        load.wait()
    code = code_tile(pairs)
    rows = [
        coef[pl.ds(pl.multiple_of(lax.rem(pairs[k, 1], blocks_dev) * BS, BS), BS), :]
        for k in range(pairs_dev)
    ]
    ordered = lax.dot_general(
        pick,
        jnp.concatenate(rows, axis=0),
        (((1,), (1,)), ((), ())),
        preferred_element_type=jnp.float32,
    ).astype(jnp.bfloat16)
    for k in range(pairs_dev):
        block = jnp.dot(
            ordered[:, k * BS : (k + 1) * BS],
            jnp.concatenate([blocks[k], beside[k]], axis=1),
            preferred_element_type=jnp.float32,
        )
        block = (block * (pairs[k, 2] == 1).astype(jnp.float32)).astype(jnp.bfloat16)
        for f, out in enumerate(outs):
            for j in range(aux_count // 2):
                first = f * owned + j * occ_local
                for c in range(2):
                    at = ((j * 2 + c) * pairs_dev + k) * occ_local
                    out[at : at + occ_local, :] = block[
                        first : first + occ_local, c * BS : (c + 1) * BS
                    ]
    for out in outs:
        out[out.shape[0] - TILE :, :] = code


def regroup_kernel(*refs):
    *received, out = refs
    rows = out.shape[0] // len(received)
    for f, piece in enumerate(received):
        out[f * rows : (f + 1) * rows, :] = piece[rows : 2 * rows, :]


def merge_kernel(first, second, out, sems):
    count = first.shape[0]
    skip = second.shape[0] - count
    loads = [
        pltpu.make_async_copy(first, out.at[:count], sems.at[0]),
        pltpu.make_async_copy(second.at[skip:], out.at[count:], sems.at[1]),
    ]
    for load in loads:
        load.start()
    for load in loads:
        load.wait()


def block_kernel(aux_count, low, coefs, blocks, *refs):
    pieces = refs[len(refs) // 2 :] if low else refs
    pairs_dev = blocks.shape[0] // 2
    rows = coefs.shape[0] - TILE
    occ_local = rows // len(pieces)
    mine = lax.axis_index("aux")
    for k in range(pairs_dev):
        left = coefs[:rows, k * BS : (k + 1) * BS]
        right = jnp.concatenate([blocks[k], blocks[pairs_dev + k]], axis=1)
        half = jnp.dot(left, right, preferred_element_type=jnp.float32).astype(jnp.bfloat16)
        for side in range(2):
            flipped = low + side * (aux_count // 2)
            at = k * aux_count + jnp.bitwise_xor(mine, flipped)
            start = pl.multiple_of(at * occ_local, occ_local)
            for f, piece in enumerate(pieces):
                piece[pl.ds(start, occ_local), :] = half[
                    f * occ_local : (f + 1) * occ_local, side * BS : (side + 1) * BS
                ]
    if low == 0:
        for piece in pieces:
            piece[pairs_dev * aux_count * occ_local :, :] = coefs[rows:, :BS]


def read_codes(received, pairs_dev, codes):
    for at, piece in enumerate(received):
        digits = piece[piece.shape[0] - TILE :, :].astype(jnp.float32)[:1]
        high = pltpu.roll(digits, BS - pairs_dev, 1)
        codes[at : at + 1, :] = (digits + 128.0 * high).astype(jnp.int32)


def near_sum_kernel(metric_in, own, *refs):
    *received, across, total, mix, metric, codes, sem = refs
    load = pltpu.make_async_copy(metric_in, metric, sem)
    load.start()
    total[...] = jnp.zeros_like(total)
    mine = lax.axis_index("aux")
    rows = total.shape[1]
    occ_local = rows // metric.shape[0]
    pairs_dev = (received[0].shape[0] - TILE) // rows
    read_codes([*received, own], pairs_dev, codes)
    for k in range(pairs_dev):
        part = own[k * rows : (k + 1) * rows, :]
        total[codes[len(received), k]] += part.astype(jnp.float32)
    for f, piece in enumerate(received):
        for k in range(pairs_dev):
            r = codes[f, k]
            for j in range(metric.shape[0]):
                source, first = (across, f * 2 + j - 2) if j >= 2 else (piece, j)
                first = (first * pairs_dev + k) * occ_local
                start = pl.multiple_of(jnp.bitwise_xor(mine, j) * occ_local, occ_local)
                part = source[first : first + occ_local, :]
                total[r, pl.ds(start, occ_local), :] += part.astype(jnp.float32)
    load.wait()
    aux_count = metric.shape[0]
    row = lax.broadcasted_iota(jnp.int32, (rows, rows), 0)
    column = lax.broadcasted_iota(jnp.int32, (rows, rows), 1)
    left = (
        lax.broadcasted_iota(jnp.int32, (rows, aux_count), 0) % aux_count
        == lax.broadcasted_iota(jnp.int32, (rows, aux_count), 1)
    ).astype(jnp.bfloat16)
    right = (
        lax.broadcasted_iota(jnp.int32, (aux_count, rows), 1) // occ_local
        == lax.broadcasted_iota(jnp.int32, (aux_count, rows), 0)
    ).astype(jnp.bfloat16)
    factor = jnp.dot(left, metric[...], preferred_element_type=jnp.float32).astype(jnp.bfloat16)
    factor = jnp.dot(factor, right, preferred_element_type=jnp.float32)
    mix[...] = jnp.where(row // aux_count == column % occ_local, factor, 0.0).astype(jnp.bfloat16)


def collect_kernel(mix, total_in, *refs):
    *received, out, total, staged, codes, sems = refs
    occ_local, aux_count = out.shape[:2]
    rows = total.shape[1]
    pairs_dev = (received[0].shape[0] - TILE) // rows
    read_codes(received, pairs_dev, codes)
    for at, piece in enumerate(received):
        for k in range(pairs_dev):
            total[codes[at, k]] += piece[k * rows : (k + 1) * rows, :].astype(jnp.float32)
    stores = []
    parts = sems.shape[0]
    each = total.shape[0] // parts
    for part in range(parts):
        for r in range(part * each, (part + 1) * each, 2):
            summed = jnp.concatenate([total[r], total[r + 1]], axis=1).astype(jnp.bfloat16)
            mixed = jnp.dot(mix[...], summed, preferred_element_type=jnp.float32)
            staged[:, :, r * BS : (r + 2) * BS] = mixed.reshape(
                occ_local, aux_count, 2 * BS
            ).astype(jnp.bfloat16)
        lanes = pl.ds(part * each * BS, each * BS)
        store = pltpu.make_async_copy(
            staged.at[:, :, lanes], out.at[:, :, lanes], sems.at[part]
        )
        store.start()
        stores.append(store)
    for store in stores:
        store.wait()

def flip(value, axis, bits):
    count = lax.axis_size(axis)
    return lax.ppermute(value, axis, [(at, at ^ bits) for at in range(count)])


def after(value, *others):
    return lax.optimization_barrier((value, *others))[0]


def cost(flops):
    return pl.CostEstimate(flops=int(flops), transcendentals=0, bytes_accessed=2**20)


def in_hbm(*operands):
    return [pltpu.with_memory_space_constraint(operand, pltpu.HBM) for operand in operands]


def exchanged_inputs(integrals, pair_list, coef, metric, occ_slot):
    pairs_dev = pair_list.shape[0]
    shell_count = lax.axis_size("shell")
    aux_count = lax.axis_size("aux")
    group = shell_count // 2
    occ_local = coef.shape[1] // (shell_count * aux_count)
    block_count = coef.shape[0] // BS * shell_count
    rows = occ_local * aux_count
    piece = jax.ShapeDtypeStruct((pairs_dev * rows + TILE, BS), jnp.bfloat16)
    vmem = pl.BlockSpec(memory_space=pltpu.VMEM)
    hbm = pl.BlockSpec(memory_space=pltpu.HBM)
    params = pltpu.CompilerParams(vmem_limit_bytes=40 * 2**20)

    def merged(name, first, second):
        return pl.pallas_call(
            merge_kernel,
            out_shape=jax.ShapeDtypeStruct(
                (2 * first.shape[0],) + first.shape[1:], jnp.bfloat16
            ),
            in_specs=[vmem] * 2,
            out_specs=vmem,
            scratch_shapes=[pltpu.SemaphoreType.DMA((2,))],
            compiler_params=params,
            name=name,
        )(first, second)

    blocks = integrals.reshape(pairs_dev, BS, BS)
    far_block = flip(blocks, "shell", group)
    operands = (pair_list, occ_slot.reshape(1, -1), coef)
    loaded = [
        pltpu.SMEM(pair_list.shape, jnp.int32),
        pltpu.VMEM((1, occ_slot.shape[0]), jnp.int32),
        pltpu.VMEM(coef.shape, jnp.bfloat16),
    ]
    near = pl.pallas_call(
        functools.partial(near_kernel, occ_local, aux_count),
        out_shape=[piece] * group,
        in_specs=[hbm] * 4 + [vmem],
        out_specs=[vmem] * group,
        scratch_shapes=loaded
        + [pltpu.VMEM(blocks.shape, jnp.bfloat16), pltpu.SemaphoreType.DMA((4,))],
        compiler_params=params,
        name="near_blocks",
    )(*in_hbm(*operands, blocks), flip(blocks, "aux", 1))
    near = [near[0]] + [flip(near[f], "shell", f) for f in range(1, group)]
    (sent_coef,) = pl.pallas_call(
        functools.partial(
            pick_kernel, [list(range(group, shell_count))], occ_local, aux_count
        ),
        out_shape=[
            jax.ShapeDtypeStruct((group * occ_local + TILE, pairs_dev * BS), jnp.bfloat16)
        ],
        in_specs=[hbm] * 3,
        out_specs=[vmem],
        scratch_shapes=loaded + [pltpu.SemaphoreType.DMA((3,))],
        compiler_params=params,
        name="pick",
    )(*in_hbm(*operands))
    far_block = after(far_block, sent_coef)
    far_coef = flip(after(sent_coef, far_block), "shell", group)
    far_pair = merged("far_pair", far_block, flip(far_block, "aux", 2))
    far_pairs = [far_pair, flip(far_pair, "aux", 1)]
    across = flip(
        pl.pallas_call(
            regroup_kernel,
            out_shape=jax.ShapeDtypeStruct(
                (group * 2 * pairs_dev * occ_local, BS), jnp.bfloat16
            ),
            in_specs=[vmem] * group,
            out_specs=vmem,
            compiler_params=params,
            name="regroup",
        )(*near),
        "aux",
        2,
    )
    far = []
    for low in range(2):
        far = pl.pallas_call(
            functools.partial(block_kernel, aux_count, low),
            out_shape=[piece] * group,
            in_specs=[vmem] * (2 + len(far)),
            out_specs=[vmem] * group,
            input_output_aliases={2 + f: f for f in range(len(far))},
            compiler_params=params,
            cost_estimate=cost(2e9) if low == 0 else None,
            name=f"far_blocks_{low}",
        )(far_coef, far_pairs[low], *far)
    total_shape = jax.ShapeDtypeStruct((block_count, rows, BS), jnp.float32)
    total, mix = pl.pallas_call(
        near_sum_kernel,
        out_shape=[total_shape, jax.ShapeDtypeStruct((rows, rows), jnp.bfloat16)],
        in_specs=[hbm] + [vmem] * (group + 2),
        out_specs=[vmem] * 2,
        scratch_shapes=[
            pltpu.VMEM(metric.shape, jnp.bfloat16),
            pltpu.VMEM((8, BS), jnp.int32),
            pltpu.SemaphoreType.DMA,
        ],
        compiler_params=params,
        cost_estimate=cost(3e9),
        name="near_sum",
    )(*in_hbm(metric), far[0], *near, across)
    far = [far[0]] + [flip(far[f], "shell", f) for f in range(1, group)]
    return pl.pallas_call(
        collect_kernel,
        out_shape=[
            jax.ShapeDtypeStruct((occ_local, aux_count, block_count * BS), jnp.bfloat16),
            total_shape,
        ],
        in_specs=[vmem] * (1 + group),
        out_specs=[hbm, vmem],
        input_output_aliases={1: 1},
        scratch_shapes=[
            pltpu.VMEM((occ_local, aux_count, block_count * BS), jnp.bfloat16),
            pltpu.VMEM((8, BS), jnp.int32),
            pltpu.SemaphoreType.DMA((4,)),
        ],
        compiler_params=params,
        name="collect",
    )(mix, total, far[1], far[3], far[2])[0]


def per_device(integrals, pair_list, coef, metric, occ_slot):
    shell_count, aux_count = lax.axis_size("shell"), lax.axis_size("aux")
    occ_local = coef.shape[1] // (shell_count * aux_count)
    if occ_local % 16 or shell_count & (shell_count - 1) or aux_count != 4:
        return relayed_half_blocks(integrals, pair_list, coef, metric, occ_slot)
    return exchanged_inputs(integrals, pair_list, coef, metric, occ_slot)


def solution(mesh):
    placed = (P("shell", None, "aux", None), P("shell", None), P("shell", None), P(), P())
    return jax.shard_map(
        per_device,
        mesh=mesh,
        in_specs=placed,
        out_specs=P(("shell", "aux"), None, None),
        check_vma=False,
    )
```

```python
import functools

import jax
import jax.numpy as jnp
from jax import lax
from jax.experimental import pallas as pl
from jax.experimental.pallas import tpu as pltpu
from jax.sharding import PartitionSpec as P

BS = 128
TILE = 8


def relayed_half_blocks(integrals, pair_list, coef, metric, occ_slot):
    pairs_dev = pair_list.shape[0]
    rows_local = coef.shape[0]
    occ_count = coef.shape[1]
    blocks_dev = rows_local // BS
    shell_count = lax.axis_size("shell")
    block_count = blocks_dev * shell_count
    slot_count = occ_slot.shape[0]
    aux_dev = integrals.shape[2]
    inverse = (
        jnp.zeros((slot_count,), jnp.int32)
        .at[occ_slot]
        .set(jnp.arange(slot_count, dtype=jnp.int32))
    )
    ordered = jnp.take(
        coef.reshape(rows_local, slot_count, occ_count // slot_count), inverse, axis=1
    )
    ordered = ordered.reshape(rows_local, occ_count)

    def one_slot(item):
        int_block, column_index = item
        start = column_index % blocks_dev * BS
        column = lax.dynamic_slice_in_dim(ordered, start, BS, 0)
        product = lax.dot_general(
            column,
            int_block.reshape(BS, aux_dev * BS),
            (((0,), (0,)), ((), ())),
            preferred_element_type=jnp.float32,
        )
        return product.astype(jnp.bfloat16)

    half_blocks = lax.map(one_slot, (integrals, pair_list[:, 1]))
    half_blocks = half_blocks.reshape(pairs_dev, occ_count, aux_dev, BS)
    listing = lax.all_gather(pair_list, "shell", axis=0, tiled=True)
    targets = jnp.arange(block_count, dtype=jnp.int32)[:, None]
    selector = ((listing[:, 0][None, :] == targets) & (listing[:, 2][None, :] == 1)).astype(
        jnp.bfloat16
    )
    relayed = lax.all_to_all(
        lax.all_to_all(half_blocks, "shell", split_axis=1, concat_axis=0, tiled=True),
        "aux",
        split_axis=1,
        concat_axis=2,
        tiled=True,
    )
    summed = jnp.dot(
        selector, relayed.reshape(relayed.shape[0], -1), preferred_element_type=jnp.float32
    )
    blocks = summed.astype(jnp.bfloat16).reshape((block_count,) + relayed.shape[1:])
    result = jnp.einsum("qp,bipm->iqbm", metric, blocks, preferred_element_type=jnp.float32)
    return result.reshape(result.shape[0], result.shape[1], block_count * BS).astype(jnp.bfloat16)


def targets_of(slot_row, block_total, occ_count):
    width = occ_count // block_total
    spread = (
        lax.broadcasted_iota(jnp.int32, (block_total, occ_count), 1) // width
        == lax.broadcasted_iota(jnp.int32, (block_total, occ_count), 0)
    ).astype(jnp.bfloat16)
    slots = jnp.broadcast_to(slot_row, (8, block_total)).astype(jnp.float32)
    target = jnp.dot(slots.astype(jnp.bfloat16), spread, preferred_element_type=jnp.float32)
    return target.astype(jnp.int32)[:1] * width + (
        lax.broadcasted_iota(jnp.int32, (1, occ_count), 1) % width
    )


def code_tile(pairs):
    pairs_dev = pairs.shape[0]
    lane = lax.broadcasted_iota(jnp.int32, (1, BS), 1)
    code = jnp.zeros((1, BS), jnp.int32)
    for k in range(pairs_dev):
        code = jnp.where(lane == k, pairs[k, 0] % 128, code)
        code = jnp.where(lane == pairs_dev + k, pairs[k, 0] // 128, code)
    return jnp.broadcast_to(code.astype(jnp.float32), (TILE, BS)).astype(jnp.bfloat16)


def near_kernel(
    occ_local,
    aux_count,
    pairs_in,
    slot_in,
    coef_in,
    blocks_in,
    beside,
    *refs,
):
    *outs, far, pairs, slot_row, coef, blocks, sems = refs
    pairs_dev = pairs.shape[0]
    blocks_dev = coef.shape[0] // BS
    occ_count = coef.shape[1]
    loads = [
        pltpu.make_async_copy(source, target, sems.at[at])
        for at, (source, target) in enumerate(
            ((slot_in, slot_row), (pairs_in, pairs), (coef_in, coef), (blocks_in, blocks))
        )
    ]
    for load in loads:
        load.start()
    me = lax.axis_index("shell")
    mine = lax.axis_index("aux")
    owned = aux_count // 2 * occ_local
    row = lax.broadcasted_iota(jnp.int32, (len(outs) * owned, 1), 0)
    owner = jnp.bitwise_xor(row // owned, me) * aux_count + jnp.bitwise_xor(
        row // occ_local % (aux_count // 2) * 2, mine
    )
    wanted = owner * occ_local + row % occ_local
    far_rows = far.shape[0] - TILE
    row = lax.broadcasted_iota(jnp.int32, (far_rows, 1), 0)
    owner = jnp.bitwise_xor(len(outs) + row // occ_local, me) * aux_count + mine
    far_wanted = owner * occ_local + row % occ_local
    loads[0].wait()
    target = targets_of(slot_row[...], slot_row.shape[1], occ_count)
    pick = (wanted == target).astype(jnp.bfloat16)
    far_pick = (far_wanted == target).astype(jnp.bfloat16)
    for load in loads[1:]:
        load.wait()
    code = code_tile(pairs)
    rows = [
        coef[pl.ds(pl.multiple_of(lax.rem(pairs[k, 1], blocks_dev) * BS, BS), BS), :]
        for k in range(pairs_dev)
    ]
    rows = jnp.concatenate(rows, axis=0)
    contract = (((1,), (1,)), ((), ()))
    ordered = lax.dot_general(pick, rows, contract, preferred_element_type=jnp.float32)
    ordered = ordered.astype(jnp.bfloat16)
    far_coef = lax.dot_general(far_pick, rows, contract, preferred_element_type=jnp.float32)
    for k in range(pairs_dev):
        block = jnp.dot(
            ordered[:, k * BS : (k + 1) * BS],
            jnp.concatenate([blocks[k], beside[k]], axis=1),
            preferred_element_type=jnp.float32,
        )
        live = (pairs[k, 2] == 1).astype(jnp.float32)
        block = (block * live).astype(jnp.bfloat16)
        lanes = slice(k * BS, (k + 1) * BS)
        far[:far_rows, lanes] = (far_coef[:, lanes] * live).astype(jnp.bfloat16)
        far[far_rows:, lanes] = code
        for f, out in enumerate(outs):
            for j in range(aux_count // 2):
                first = f * owned + j * occ_local
                for c in range(2):
                    at = ((j * 2 + c) * pairs_dev + k) * occ_local
                    out[at : at + occ_local, :] = block[
                        first : first + occ_local, c * BS : (c + 1) * BS
                    ]
    for out in outs:
        out[out.shape[0] - TILE :, :] = code


def regroup_kernel(*refs):
    *received, out = refs
    rows = out.shape[0] // len(received)
    for f, piece in enumerate(received):
        out[f * rows : (f + 1) * rows, :] = piece[rows : 2 * rows, :]


def merge_kernel(first, second, out, sems):
    count = first.shape[0]
    skip = second.shape[0] - count
    loads = [
        pltpu.make_async_copy(first, out.at[:count], sems.at[0]),
        pltpu.make_async_copy(second.at[skip:], out.at[count:], sems.at[1]),
    ]
    for load in loads:
        load.start()
    for load in loads:
        load.wait()


def block_kernel(aux_count, low, coefs, blocks, *refs):
    pieces = refs[len(refs) // 2 :] if low else refs
    pairs_dev = blocks.shape[0] // 2
    rows = coefs.shape[0] - TILE
    occ_local = rows // len(pieces)
    mine = lax.axis_index("aux")
    for k in range(pairs_dev):
        left = coefs[:rows, k * BS : (k + 1) * BS]
        right = jnp.concatenate([blocks[k], blocks[pairs_dev + k]], axis=1)
        half = jnp.dot(left, right, preferred_element_type=jnp.float32).astype(jnp.bfloat16)
        for side in range(2):
            flipped = low + side * (aux_count // 2)
            at = k * aux_count + jnp.bitwise_xor(mine, flipped)
            start = pl.multiple_of(at * occ_local, occ_local)
            for f, piece in enumerate(pieces):
                piece[pl.ds(start, occ_local), :] = half[
                    f * occ_local : (f + 1) * occ_local, side * BS : (side + 1) * BS
                ]
    if low == 0:
        for piece in pieces:
            piece[pairs_dev * aux_count * occ_local :, :] = coefs[rows:, :BS]


def read_codes(received, pairs_dev, codes):
    for at, piece in enumerate(received):
        digits = piece[piece.shape[0] - TILE :, :].astype(jnp.float32)[:1]
        high = pltpu.roll(digits, BS - pairs_dev, 1)
        codes[at : at + 1, :] = (digits + 128.0 * high).astype(jnp.int32)


def near_sum_kernel(metric_in, own, *refs):
    *received, across, total, mix, metric, codes, sem = refs
    load = pltpu.make_async_copy(metric_in, metric, sem)
    load.start()
    total[...] = jnp.zeros_like(total)
    mine = lax.axis_index("aux")
    rows = total.shape[1]
    occ_local = rows // metric.shape[0]
    pairs_dev = (received[0].shape[0] - TILE) // rows
    read_codes([*received, own], pairs_dev, codes)
    for k in range(pairs_dev):
        part = own[k * rows : (k + 1) * rows, :]
        total[codes[len(received), k]] += part.astype(jnp.float32)
    for f, piece in enumerate(received):
        for k in range(pairs_dev):
            r = codes[f, k]
            for j in range(metric.shape[0]):
                source, first = (across, f * 2 + j - 2) if j >= 2 else (piece, j)
                first = (first * pairs_dev + k) * occ_local
                start = pl.multiple_of(jnp.bitwise_xor(mine, j) * occ_local, occ_local)
                part = source[first : first + occ_local, :]
                total[r, pl.ds(start, occ_local), :] += part.astype(jnp.float32)
    load.wait()
    aux_count = metric.shape[0]
    row = lax.broadcasted_iota(jnp.int32, (rows, rows), 0)
    column = lax.broadcasted_iota(jnp.int32, (rows, rows), 1)
    left = (
        lax.broadcasted_iota(jnp.int32, (rows, aux_count), 0) % aux_count
        == lax.broadcasted_iota(jnp.int32, (rows, aux_count), 1)
    ).astype(jnp.bfloat16)
    right = (
        lax.broadcasted_iota(jnp.int32, (aux_count, rows), 1) // occ_local
        == lax.broadcasted_iota(jnp.int32, (aux_count, rows), 0)
    ).astype(jnp.bfloat16)
    factor = jnp.dot(left, metric[...], preferred_element_type=jnp.float32).astype(jnp.bfloat16)
    factor = jnp.dot(factor, right, preferred_element_type=jnp.float32)
    mix[...] = jnp.where(row // aux_count == column % occ_local, factor, 0.0).astype(jnp.bfloat16)


def collect_kernel(mix, total_in, *refs):
    *received, out, total, staged, codes, sems = refs
    occ_local, aux_count = out.shape[:2]
    rows = total.shape[1]
    pairs_dev = (received[0].shape[0] - TILE) // rows
    read_codes(received, pairs_dev, codes)
    for at, piece in enumerate(received):
        for k in range(pairs_dev):
            total[codes[at, k]] += piece[k * rows : (k + 1) * rows, :].astype(jnp.float32)
    stores = []
    parts = sems.shape[0]
    each = total.shape[0] // parts
    for part in range(parts):
        for r in range(part * each, (part + 1) * each, 2):
            summed = jnp.concatenate([total[r], total[r + 1]], axis=1).astype(jnp.bfloat16)
            mixed = jnp.dot(mix[...], summed, preferred_element_type=jnp.float32)
            staged[:, :, r * BS : (r + 2) * BS] = mixed.reshape(
                occ_local, aux_count, 2 * BS
            ).astype(jnp.bfloat16)
        lanes = pl.ds(part * each * BS, each * BS)
        store = pltpu.make_async_copy(
            staged.at[:, :, lanes], out.at[:, :, lanes], sems.at[part]
        )
        store.start()
        stores.append(store)
    for store in stores:
        store.wait()

def flip(value, axis, bits):
    count = lax.axis_size(axis)
    return lax.ppermute(value, axis, [(at, at ^ bits) for at in range(count)])


def after(value, *others):
    return lax.optimization_barrier((value, *others))[0]


def cost(flops):
    return pl.CostEstimate(flops=int(flops), transcendentals=0, bytes_accessed=2**20)


def in_hbm(*operands):
    return [pltpu.with_memory_space_constraint(operand, pltpu.HBM) for operand in operands]


def exchanged_inputs(integrals, pair_list, coef, metric, occ_slot):
    pairs_dev = pair_list.shape[0]
    shell_count = lax.axis_size("shell")
    aux_count = lax.axis_size("aux")
    group = shell_count // 2
    occ_local = coef.shape[1] // (shell_count * aux_count)
    block_count = coef.shape[0] // BS * shell_count
    rows = occ_local * aux_count
    piece = jax.ShapeDtypeStruct((pairs_dev * rows + TILE, BS), jnp.bfloat16)
    vmem = pl.BlockSpec(memory_space=pltpu.VMEM)
    hbm = pl.BlockSpec(memory_space=pltpu.HBM)
    params = pltpu.CompilerParams(vmem_limit_bytes=40 * 2**20)

    def merged(name, first, second):
        return pl.pallas_call(
            merge_kernel,
            out_shape=jax.ShapeDtypeStruct(
                (2 * first.shape[0],) + first.shape[1:], jnp.bfloat16
            ),
            in_specs=[vmem] * 2,
            out_specs=vmem,
            scratch_shapes=[pltpu.SemaphoreType.DMA((2,))],
            compiler_params=params,
            name=name,
        )(first, second)

    blocks = integrals.reshape(pairs_dev, BS, BS)
    far_block = flip(blocks, "shell", group)
    operands = (pair_list, occ_slot.reshape(1, -1), coef)
    loaded = [
        pltpu.SMEM(pair_list.shape, jnp.int32),
        pltpu.VMEM((1, occ_slot.shape[0]), jnp.int32),
        pltpu.VMEM(coef.shape, jnp.bfloat16),
    ]
    *near, sent_coef = pl.pallas_call(
        functools.partial(near_kernel, occ_local, aux_count),
        out_shape=[piece] * group
        + [jax.ShapeDtypeStruct((group * occ_local + TILE, pairs_dev * BS), jnp.bfloat16)],
        in_specs=[hbm] * 4 + [vmem],
        out_specs=[vmem] * (group + 1),
        scratch_shapes=loaded
        + [pltpu.VMEM(blocks.shape, jnp.bfloat16), pltpu.SemaphoreType.DMA((4,))],
        compiler_params=params,
        name="near_blocks",
    )(*in_hbm(*operands, blocks), flip(blocks, "aux", 1))
    near = [near[0]] + [flip(near[f], "shell", f) for f in range(1, group)]
    far_block = after(far_block, sent_coef)
    far_coef = flip(after(sent_coef, far_block), "shell", group)
    far_pair = merged("far_pair", far_block, flip(far_block, "aux", 2))
    far_pairs = [far_pair, flip(far_pair, "aux", 1)]
    across = flip(
        pl.pallas_call(
            regroup_kernel,
            out_shape=jax.ShapeDtypeStruct(
                (group * 2 * pairs_dev * occ_local, BS), jnp.bfloat16
            ),
            in_specs=[vmem] * group,
            out_specs=vmem,
            compiler_params=params,
            name="regroup",
        )(*near),
        "aux",
        2,
    )
    far = []
    for low in range(2):
        far = pl.pallas_call(
            functools.partial(block_kernel, aux_count, low),
            out_shape=[piece] * group,
            in_specs=[vmem] * (2 + len(far)),
            out_specs=[vmem] * group,
            input_output_aliases={2 + f: f for f in range(len(far))},
            compiler_params=params,
            cost_estimate=cost(2e9) if low == 0 else None,
            name=f"far_blocks_{low}",
        )(far_coef, far_pairs[low], *far)
    total_shape = jax.ShapeDtypeStruct((block_count, rows, BS), jnp.float32)
    total, mix = pl.pallas_call(
        near_sum_kernel,
        out_shape=[total_shape, jax.ShapeDtypeStruct((rows, rows), jnp.bfloat16)],
        in_specs=[hbm] + [vmem] * (group + 2),
        out_specs=[vmem] * 2,
        scratch_shapes=[
            pltpu.VMEM(metric.shape, jnp.bfloat16),
            pltpu.VMEM((8, BS), jnp.int32),
            pltpu.SemaphoreType.DMA,
        ],
        compiler_params=params,
        cost_estimate=cost(3e9),
        name="near_sum",
    )(*in_hbm(metric), far[0], *near, across)
    far = [far[0]] + [flip(far[f], "shell", f) for f in range(1, group)]
    return pl.pallas_call(
        collect_kernel,
        out_shape=[
            jax.ShapeDtypeStruct((occ_local, aux_count, block_count * BS), jnp.bfloat16),
            total_shape,
        ],
        in_specs=[vmem] * (1 + group),
        out_specs=[hbm, vmem],
        input_output_aliases={1: 1},
        scratch_shapes=[
            pltpu.VMEM((occ_local, aux_count, block_count * BS), jnp.bfloat16),
            pltpu.VMEM((8, BS), jnp.int32),
            pltpu.SemaphoreType.DMA((4,)),
        ],
        compiler_params=params,
        name="collect",
    )(mix, total, far[3], far[1], far[2])[0]


def per_device(integrals, pair_list, coef, metric, occ_slot):
    shell_count, aux_count = lax.axis_size("shell"), lax.axis_size("aux")
    occ_local = coef.shape[1] // (shell_count * aux_count)
    if occ_local % 16 or shell_count & (shell_count - 1) or aux_count != 4:
        return relayed_half_blocks(integrals, pair_list, coef, metric, occ_slot)
    return exchanged_inputs(integrals, pair_list, coef, metric, occ_slot)


def solution(mesh):
    placed = (P("shell", None, "aux", None), P("shell", None), P("shell", None), P(), P())
    return jax.shard_map(
        per_device,
        mesh=mesh,
        in_specs=placed,
        out_specs=P(("shell", "aux"), None, None),
        check_vma=False,
    )
```

```python
import functools

import jax
import jax.numpy as jnp
from jax import lax
from jax.experimental import pallas as pl
from jax.experimental.pallas import tpu as pltpu
from jax.sharding import PartitionSpec as P

BS = 128
TILE = 8


def relayed_half_blocks(integrals, pair_list, coef, metric, occ_slot):
    pairs_dev = pair_list.shape[0]
    rows_local = coef.shape[0]
    occ_count = coef.shape[1]
    blocks_dev = rows_local // BS
    shell_count = lax.axis_size("shell")
    block_count = blocks_dev * shell_count
    slot_count = occ_slot.shape[0]
    aux_dev = integrals.shape[2]
    inverse = (
        jnp.zeros((slot_count,), jnp.int32)
        .at[occ_slot]
        .set(jnp.arange(slot_count, dtype=jnp.int32))
    )
    ordered = jnp.take(
        coef.reshape(rows_local, slot_count, occ_count // slot_count), inverse, axis=1
    )
    ordered = ordered.reshape(rows_local, occ_count)

    def one_slot(item):
        int_block, column_index = item
        start = column_index % blocks_dev * BS
        column = lax.dynamic_slice_in_dim(ordered, start, BS, 0)
        product = lax.dot_general(
            column,
            int_block.reshape(BS, aux_dev * BS),
            (((0,), (0,)), ((), ())),
            preferred_element_type=jnp.float32,
        )
        return product.astype(jnp.bfloat16)

    half_blocks = lax.map(one_slot, (integrals, pair_list[:, 1]))
    half_blocks = half_blocks.reshape(pairs_dev, occ_count, aux_dev, BS)
    listing = lax.all_gather(pair_list, "shell", axis=0, tiled=True)
    targets = jnp.arange(block_count, dtype=jnp.int32)[:, None]
    selector = ((listing[:, 0][None, :] == targets) & (listing[:, 2][None, :] == 1)).astype(
        jnp.bfloat16
    )
    relayed = lax.all_to_all(
        lax.all_to_all(half_blocks, "shell", split_axis=1, concat_axis=0, tiled=True),
        "aux",
        split_axis=1,
        concat_axis=2,
        tiled=True,
    )
    summed = jnp.dot(
        selector, relayed.reshape(relayed.shape[0], -1), preferred_element_type=jnp.float32
    )
    blocks = summed.astype(jnp.bfloat16).reshape((block_count,) + relayed.shape[1:])
    result = jnp.einsum("qp,bipm->iqbm", metric, blocks, preferred_element_type=jnp.float32)
    return result.reshape(result.shape[0], result.shape[1], block_count * BS).astype(jnp.bfloat16)


def targets_of(slot_row, block_total, occ_count):
    width = occ_count // block_total
    spread = (
        lax.broadcasted_iota(jnp.int32, (block_total, occ_count), 1) // width
        == lax.broadcasted_iota(jnp.int32, (block_total, occ_count), 0)
    ).astype(jnp.bfloat16)
    slots = jnp.broadcast_to(slot_row, (8, block_total)).astype(jnp.float32)
    target = jnp.dot(slots.astype(jnp.bfloat16), spread, preferred_element_type=jnp.float32)
    return target.astype(jnp.int32)[:1] * width + (
        lax.broadcasted_iota(jnp.int32, (1, occ_count), 1) % width
    )


def code_tile(pairs):
    pairs_dev = pairs.shape[0]
    lane = lax.broadcasted_iota(jnp.int32, (1, BS), 1)
    code = jnp.zeros((1, BS), jnp.int32)
    for k in range(pairs_dev):
        code = jnp.where(lane == k, pairs[k, 0] % 128, code)
        code = jnp.where(lane == pairs_dev + k, pairs[k, 0] // 128, code)
    return jnp.broadcast_to(code.astype(jnp.float32), (TILE, BS)).astype(jnp.bfloat16)


def near_kernel(
    occ_local,
    aux_count,
    pairs_in,
    slot_in,
    coef_in,
    blocks_in,
    beside,
    *refs,
):
    *outs, far, pairs, slot_row, coef, blocks, sems = refs
    pairs_dev = pairs.shape[0]
    blocks_dev = coef.shape[0] // BS
    occ_count = coef.shape[1]
    loads = [
        pltpu.make_async_copy(source, target, sems.at[at])
        for at, (source, target) in enumerate(
            ((slot_in, slot_row), (pairs_in, pairs), (coef_in, coef), (blocks_in, blocks))
        )
    ]
    for load in loads:
        load.start()
    me = lax.axis_index("shell")
    mine = lax.axis_index("aux")
    owned = aux_count // 2 * occ_local
    row = lax.broadcasted_iota(jnp.int32, (len(outs) * owned, 1), 0)
    owner = jnp.bitwise_xor(row // owned, me) * aux_count + jnp.bitwise_xor(
        row // occ_local % (aux_count // 2) * 2, mine
    )
    wanted = owner * occ_local + row % occ_local
    far_rows = far.shape[0] - TILE
    row = lax.broadcasted_iota(jnp.int32, (far_rows, 1), 0)
    owner = jnp.bitwise_xor(len(outs) + row // occ_local, me) * aux_count + mine
    far_wanted = owner * occ_local + row % occ_local
    loads[0].wait()
    target = targets_of(slot_row[...], slot_row.shape[1], occ_count)
    pick = (wanted == target).astype(jnp.bfloat16)
    far_pick = (far_wanted == target).astype(jnp.bfloat16)
    for load in loads[1:]:
        load.wait()
    code = code_tile(pairs)
    rows = [
        coef[pl.ds(pl.multiple_of(lax.rem(pairs[k, 1], blocks_dev) * BS, BS), BS), :]
        for k in range(pairs_dev)
    ]
    rows = jnp.concatenate(rows, axis=0)
    contract = (((1,), (1,)), ((), ()))
    ordered = lax.dot_general(pick, rows, contract, preferred_element_type=jnp.float32)
    ordered = ordered.astype(jnp.bfloat16)
    far_coef = lax.dot_general(far_pick, rows, contract, preferred_element_type=jnp.float32)
    for k in range(pairs_dev):
        block = jnp.dot(
            ordered[:, k * BS : (k + 1) * BS],
            jnp.concatenate([blocks[k], beside[k]], axis=1),
            preferred_element_type=jnp.float32,
        )
        live = (pairs[k, 2] == 1).astype(jnp.float32)
        block = (block * live).astype(jnp.bfloat16)
        lanes = slice(k * BS, (k + 1) * BS)
        far[:far_rows, lanes] = (far_coef[:, lanes] * live).astype(jnp.bfloat16)
        far[far_rows:, lanes] = code
        for f, out in enumerate(outs):
            for j in range(aux_count // 2):
                first = f * owned + j * occ_local
                for c in range(2):
                    at = ((j * 2 + c) * pairs_dev + k) * occ_local
                    out[at : at + occ_local, :] = block[
                        first : first + occ_local, c * BS : (c + 1) * BS
                    ]
    for out in outs:
        out[out.shape[0] - TILE :, :] = code


def regroup_kernel(*refs):
    *received, out = refs
    received = received[::-1]
    rows = out.shape[0] // len(received)
    for f, piece in enumerate(received):
        out[f * rows : (f + 1) * rows, :] = piece[rows : 2 * rows, :]


def merge_kernel(first, second, out, sems):
    count = first.shape[0]
    skip = second.shape[0] - count
    loads = [
        pltpu.make_async_copy(first, out.at[:count], sems.at[0]),
        pltpu.make_async_copy(second.at[skip:], out.at[count:], sems.at[1]),
    ]
    for load in loads:
        load.start()
    for load in loads:
        load.wait()


def block_kernel(aux_count, low, coefs, blocks, *refs):
    pieces = refs[len(refs) // 2 :] if low else refs
    pairs_dev = blocks.shape[0] // 2
    rows = coefs.shape[0] - TILE
    occ_local = rows // len(pieces)
    mine = lax.axis_index("aux")
    for k in range(pairs_dev):
        left = coefs[:rows, k * BS : (k + 1) * BS]
        right = jnp.concatenate([blocks[k], blocks[pairs_dev + k]], axis=1)
        half = jnp.dot(left, right, preferred_element_type=jnp.float32).astype(jnp.bfloat16)
        for side in range(2):
            flipped = low + side * (aux_count // 2)
            at = k * aux_count + jnp.bitwise_xor(mine, flipped)
            start = pl.multiple_of(at * occ_local, occ_local)
            for f, piece in enumerate(pieces):
                piece[pl.ds(start, occ_local), :] = half[
                    f * occ_local : (f + 1) * occ_local, side * BS : (side + 1) * BS
                ]
    if low == 0:
        for piece in pieces:
            piece[pairs_dev * aux_count * occ_local :, :] = coefs[rows:, :BS]


def read_codes(received, pairs_dev, codes):
    for at, piece in enumerate(received):
        digits = piece[piece.shape[0] - TILE :, :].astype(jnp.float32)[:1]
        high = pltpu.roll(digits, BS - pairs_dev, 1)
        codes[at : at + 1, :] = (digits + 128.0 * high).astype(jnp.int32)


def near_sum_kernel(metric_in, own, *refs):
    *received, across, total, mix, metric, codes, sem = refs
    received = received[::-1]
    load = pltpu.make_async_copy(metric_in, metric, sem)
    load.start()
    total[...] = jnp.zeros_like(total)
    mine = lax.axis_index("aux")
    rows = total.shape[1]
    occ_local = rows // metric.shape[0]
    pairs_dev = (received[0].shape[0] - TILE) // rows
    read_codes([*received, own], pairs_dev, codes)
    for k in range(pairs_dev):
        part = own[k * rows : (k + 1) * rows, :]
        total[codes[len(received), k]] += part.astype(jnp.float32)
    for f, piece in enumerate(received):
        for k in range(pairs_dev):
            r = codes[f, k]
            for j in range(metric.shape[0]):
                source, first = (across, f * 2 + j - 2) if j >= 2 else (piece, j)
                first = (first * pairs_dev + k) * occ_local
                start = pl.multiple_of(jnp.bitwise_xor(mine, j) * occ_local, occ_local)
                part = source[first : first + occ_local, :]
                total[r, pl.ds(start, occ_local), :] += part.astype(jnp.float32)
    load.wait()
    aux_count = metric.shape[0]
    row = lax.broadcasted_iota(jnp.int32, (rows, rows), 0)
    column = lax.broadcasted_iota(jnp.int32, (rows, rows), 1)
    left = (
        lax.broadcasted_iota(jnp.int32, (rows, aux_count), 0) % aux_count
        == lax.broadcasted_iota(jnp.int32, (rows, aux_count), 1)
    ).astype(jnp.bfloat16)
    right = (
        lax.broadcasted_iota(jnp.int32, (aux_count, rows), 1) // occ_local
        == lax.broadcasted_iota(jnp.int32, (aux_count, rows), 0)
    ).astype(jnp.bfloat16)
    factor = jnp.dot(left, metric[...], preferred_element_type=jnp.float32).astype(jnp.bfloat16)
    factor = jnp.dot(factor, right, preferred_element_type=jnp.float32)
    mix[...] = jnp.where(row // aux_count == column % occ_local, factor, 0.0).astype(jnp.bfloat16)


def collect_kernel(mix, total_in, *refs):
    *received, out, total, staged, codes, sems = refs
    occ_local, aux_count = out.shape[:2]
    rows = total.shape[1]
    pairs_dev = (received[0].shape[0] - TILE) // rows
    read_codes(received, pairs_dev, codes)
    for at, piece in enumerate(received):
        for k in range(pairs_dev):
            total[codes[at, k]] += piece[k * rows : (k + 1) * rows, :].astype(jnp.float32)
    stores = []
    parts = sems.shape[0]
    each = total.shape[0] // parts
    for part in range(parts):
        for r in range(part * each, (part + 1) * each, 2):
            summed = jnp.concatenate([total[r], total[r + 1]], axis=1).astype(jnp.bfloat16)
            mixed = jnp.dot(mix[...], summed, preferred_element_type=jnp.float32)
            staged[:, :, r * BS : (r + 2) * BS] = mixed.reshape(
                occ_local, aux_count, 2 * BS
            ).astype(jnp.bfloat16)
        lanes = pl.ds(part * each * BS, each * BS)
        store = pltpu.make_async_copy(
            staged.at[:, :, lanes], out.at[:, :, lanes], sems.at[part]
        )
        store.start()
        stores.append(store)
    for store in stores:
        store.wait()

def flip(value, axis, bits):
    count = lax.axis_size(axis)
    return lax.ppermute(value, axis, [(at, at ^ bits) for at in range(count)])


def after(value, *others):
    return lax.optimization_barrier((value, *others))[0]


def cost(flops):
    return pl.CostEstimate(flops=int(flops), transcendentals=0, bytes_accessed=2**20)


def in_hbm(*operands):
    return [pltpu.with_memory_space_constraint(operand, pltpu.HBM) for operand in operands]


def exchanged_inputs(integrals, pair_list, coef, metric, occ_slot):
    pairs_dev = pair_list.shape[0]
    shell_count = lax.axis_size("shell")
    aux_count = lax.axis_size("aux")
    group = shell_count // 2
    occ_local = coef.shape[1] // (shell_count * aux_count)
    block_count = coef.shape[0] // BS * shell_count
    rows = occ_local * aux_count
    piece = jax.ShapeDtypeStruct((pairs_dev * rows + TILE, BS), jnp.bfloat16)
    vmem = pl.BlockSpec(memory_space=pltpu.VMEM)
    hbm = pl.BlockSpec(memory_space=pltpu.HBM)
    params = pltpu.CompilerParams(vmem_limit_bytes=40 * 2**20)

    def merged(name, first, second):
        return pl.pallas_call(
            merge_kernel,
            out_shape=jax.ShapeDtypeStruct(
                (2 * first.shape[0],) + first.shape[1:], jnp.bfloat16
            ),
            in_specs=[vmem] * 2,
            out_specs=vmem,
            scratch_shapes=[pltpu.SemaphoreType.DMA((2,))],
            compiler_params=params,
            name=name,
        )(first, second)

    blocks = integrals.reshape(pairs_dev, BS, BS)
    far_block = flip(blocks, "shell", group)
    operands = (pair_list, occ_slot.reshape(1, -1), coef)
    loaded = [
        pltpu.SMEM(pair_list.shape, jnp.int32),
        pltpu.VMEM((1, occ_slot.shape[0]), jnp.int32),
        pltpu.VMEM(coef.shape, jnp.bfloat16),
    ]
    *near, sent_coef = pl.pallas_call(
        functools.partial(near_kernel, occ_local, aux_count),
        out_shape=[piece] * group
        + [jax.ShapeDtypeStruct((group * occ_local + TILE, pairs_dev * BS), jnp.bfloat16)],
        in_specs=[hbm] * 4 + [vmem],
        out_specs=[vmem] * (group + 1),
        scratch_shapes=loaded
        + [pltpu.VMEM(blocks.shape, jnp.bfloat16), pltpu.SemaphoreType.DMA((4,))],
        compiler_params=params,
        name="near_blocks",
    )(*in_hbm(*operands, blocks), flip(blocks, "aux", 1))
    near = [near[0]] + [flip(near[f], "shell", f) for f in range(1, group)]
    far_block = after(far_block, sent_coef)
    far_coef = flip(after(sent_coef, far_block), "shell", group)
    far_pair = merged("far_pair", far_block, flip(far_block, "aux", 2))
    far_pairs = [far_pair, flip(far_pair, "aux", 1)]
    across = flip(
        pl.pallas_call(
            regroup_kernel,
            out_shape=jax.ShapeDtypeStruct(
                (group * 2 * pairs_dev * occ_local, BS), jnp.bfloat16
            ),
            in_specs=[vmem] * group,
            out_specs=vmem,
            compiler_params=params,
            name="regroup",
        )(*reversed(near)),
        "aux",
        2,
    )
    far = []
    for low in range(2):
        far = pl.pallas_call(
            functools.partial(block_kernel, aux_count, low),
            out_shape=[piece] * group,
            in_specs=[vmem] * (2 + len(far)),
            out_specs=[vmem] * group,
            input_output_aliases={2 + f: f for f in range(len(far))},
            compiler_params=params,
            cost_estimate=cost(2e9) if low == 0 else None,
            name=f"far_blocks_{low}",
        )(far_coef, far_pairs[low], *far)
    total_shape = jax.ShapeDtypeStruct((block_count, rows, BS), jnp.float32)
    total, mix = pl.pallas_call(
        near_sum_kernel,
        out_shape=[total_shape, jax.ShapeDtypeStruct((rows, rows), jnp.bfloat16)],
        in_specs=[hbm] + [vmem] * (group + 2),
        out_specs=[vmem] * 2,
        scratch_shapes=[
            pltpu.VMEM(metric.shape, jnp.bfloat16),
            pltpu.VMEM((8, BS), jnp.int32),
            pltpu.SemaphoreType.DMA,
        ],
        compiler_params=params,
        cost_estimate=cost(3e9),
        name="near_sum",
    )(*in_hbm(metric), far[0], *reversed(near), across)
    far = [far[0]] + [flip(far[f], "shell", f) for f in range(1, group)]
    return pl.pallas_call(
        collect_kernel,
        out_shape=[
            jax.ShapeDtypeStruct((occ_local, aux_count, block_count * BS), jnp.bfloat16),
            total_shape,
        ],
        in_specs=[vmem] * (1 + group),
        out_specs=[hbm, vmem],
        input_output_aliases={1: 1},
        scratch_shapes=[
            pltpu.VMEM((occ_local, aux_count, block_count * BS), jnp.bfloat16),
            pltpu.VMEM((8, BS), jnp.int32),
            pltpu.SemaphoreType.DMA((4,)),
        ],
        compiler_params=params,
        name="collect",
    )(mix, total, far[3], far[1], far[2])[0]


def per_device(integrals, pair_list, coef, metric, occ_slot):
    shell_count, aux_count = lax.axis_size("shell"), lax.axis_size("aux")
    occ_local = coef.shape[1] // (shell_count * aux_count)
    if occ_local % 16 or shell_count & (shell_count - 1) or aux_count != 4:
        return relayed_half_blocks(integrals, pair_list, coef, metric, occ_slot)
    return exchanged_inputs(integrals, pair_list, coef, metric, occ_slot)


def solution(mesh):
    placed = (P("shell", None, "aux", None), P("shell", None), P("shell", None), P(), P())
    return jax.shard_map(
        per_device,
        mesh=mesh,
        in_specs=placed,
        out_specs=P(("shell", "aux"), None, None),
        check_vma=False,
    )
```

```python
import functools

import jax
import jax.numpy as jnp
from jax import lax
from jax.experimental import pallas as pl
from jax.experimental.pallas import tpu as pltpu
from jax.sharding import PartitionSpec as P

BS = 128
TILE = 8


def relayed_half_blocks(integrals, pair_list, coef, metric, occ_slot):
    pairs_dev = pair_list.shape[0]
    rows_local = coef.shape[0]
    occ_count = coef.shape[1]
    blocks_dev = rows_local // BS
    shell_count = lax.axis_size("shell")
    block_count = blocks_dev * shell_count
    slot_count = occ_slot.shape[0]
    aux_dev = integrals.shape[2]
    inverse = (
        jnp.zeros((slot_count,), jnp.int32)
        .at[occ_slot]
        .set(jnp.arange(slot_count, dtype=jnp.int32))
    )
    ordered = jnp.take(
        coef.reshape(rows_local, slot_count, occ_count // slot_count), inverse, axis=1
    )
    ordered = ordered.reshape(rows_local, occ_count)

    def one_slot(item):
        int_block, column_index = item
        start = column_index % blocks_dev * BS
        column = lax.dynamic_slice_in_dim(ordered, start, BS, 0)
        product = lax.dot_general(
            column,
            int_block.reshape(BS, aux_dev * BS),
            (((0,), (0,)), ((), ())),
            preferred_element_type=jnp.float32,
        )
        return product.astype(jnp.bfloat16)

    half_blocks = lax.map(one_slot, (integrals, pair_list[:, 1]))
    half_blocks = half_blocks.reshape(pairs_dev, occ_count, aux_dev, BS)
    listing = lax.all_gather(pair_list, "shell", axis=0, tiled=True)
    targets = jnp.arange(block_count, dtype=jnp.int32)[:, None]
    selector = ((listing[:, 0][None, :] == targets) & (listing[:, 2][None, :] == 1)).astype(
        jnp.bfloat16
    )
    relayed = lax.all_to_all(
        lax.all_to_all(half_blocks, "shell", split_axis=1, concat_axis=0, tiled=True),
        "aux",
        split_axis=1,
        concat_axis=2,
        tiled=True,
    )
    summed = jnp.dot(
        selector, relayed.reshape(relayed.shape[0], -1), preferred_element_type=jnp.float32
    )
    blocks = summed.astype(jnp.bfloat16).reshape((block_count,) + relayed.shape[1:])
    result = jnp.einsum("qp,bipm->iqbm", metric, blocks, preferred_element_type=jnp.float32)
    return result.reshape(result.shape[0], result.shape[1], block_count * BS).astype(jnp.bfloat16)


def targets_of(slot_row, block_total, occ_count):
    width = occ_count // block_total
    spread = (
        lax.broadcasted_iota(jnp.int32, (block_total, occ_count), 1) // width
        == lax.broadcasted_iota(jnp.int32, (block_total, occ_count), 0)
    ).astype(jnp.bfloat16)
    slots = jnp.broadcast_to(slot_row, (8, block_total)).astype(jnp.float32)
    target = jnp.dot(slots.astype(jnp.bfloat16), spread, preferred_element_type=jnp.float32)
    return target.astype(jnp.int32)[:1] * width + (
        lax.broadcasted_iota(jnp.int32, (1, occ_count), 1) % width
    )


def code_tile(pairs):
    pairs_dev = pairs.shape[0]
    lane = lax.broadcasted_iota(jnp.int32, (1, BS), 1)
    code = jnp.zeros((1, BS), jnp.int32)
    for k in range(pairs_dev):
        code = jnp.where(lane == k, pairs[k, 0] % 128, code)
        code = jnp.where(lane == pairs_dev + k, pairs[k, 0] // 128, code)
    return jnp.broadcast_to(code.astype(jnp.float32), (TILE, BS)).astype(jnp.bfloat16)


def near_kernel(
    occ_local,
    aux_count,
    pairs_in,
    slot_in,
    coef_in,
    blocks_in,
    beside,
    *refs,
):
    *outs, far, pairs, slot_row, coef, blocks, sems = refs
    pairs_dev = pairs.shape[0]
    blocks_dev = coef.shape[0] // BS
    occ_count = coef.shape[1]
    loads = [
        pltpu.make_async_copy(source, target, sems.at[at])
        for at, (source, target) in enumerate(
            ((slot_in, slot_row), (pairs_in, pairs), (coef_in, coef), (blocks_in, blocks))
        )
    ]
    for load in loads:
        load.start()
    me = lax.axis_index("shell")
    mine = lax.axis_index("aux")
    owned = aux_count // 2 * occ_local
    row = lax.broadcasted_iota(jnp.int32, (len(outs) * owned, 1), 0)
    owner = jnp.bitwise_xor(row // owned, me) * aux_count + jnp.bitwise_xor(
        row // occ_local % (aux_count // 2) * 2, mine
    )
    wanted = owner * occ_local + row % occ_local
    far_rows = far.shape[0]
    row = lax.broadcasted_iota(jnp.int32, (far_rows, 1), 0)
    owner = jnp.bitwise_xor(len(outs) + row // occ_local, me) * aux_count + mine
    far_wanted = owner * occ_local + row % occ_local
    loads[0].wait()
    target = targets_of(slot_row[...], slot_row.shape[1], occ_count)
    pick = (wanted == target).astype(jnp.bfloat16)
    far_pick = (far_wanted == target).astype(jnp.bfloat16)
    for load in loads[1:]:
        load.wait()
    code = code_tile(pairs)
    rows = [
        coef[pl.ds(pl.multiple_of(lax.rem(pairs[k, 1], blocks_dev) * BS, BS), BS), :]
        for k in range(pairs_dev)
    ]
    rows = jnp.concatenate(rows, axis=0)
    contract = (((1,), (1,)), ((), ()))
    ordered = lax.dot_general(pick, rows, contract, preferred_element_type=jnp.float32)
    ordered = ordered.astype(jnp.bfloat16)
    far_coef = lax.dot_general(far_pick, rows, contract, preferred_element_type=jnp.float32)
    for k in range(pairs_dev):
        block = jnp.dot(
            ordered[:, k * BS : (k + 1) * BS],
            jnp.concatenate([blocks[k], beside[k]], axis=1),
            preferred_element_type=jnp.float32,
        )
        live = (pairs[k, 2] == 1).astype(jnp.float32)
        block = (block * live).astype(jnp.bfloat16)
        lanes = slice(k * BS, (k + 1) * BS)
        far[:, lanes] = (far_coef[:, lanes] * live).astype(jnp.bfloat16)
        for f, out in enumerate(outs):
            for j in range(aux_count // 2):
                first = f * owned + j * occ_local
                for c in range(2):
                    at = ((j * 2 + c) * pairs_dev + k) * occ_local
                    out[at : at + occ_local, :] = block[
                        first : first + occ_local, c * BS : (c + 1) * BS
                    ]
    for out in outs:
        out[out.shape[0] - TILE :, :] = code


def regroup_kernel(*refs):
    *received, out = refs
    rows = out.shape[0] // len(received)
    for f, piece in enumerate(received):
        out[f * rows : (f + 1) * rows, :] = piece[rows : 2 * rows, :]


def merge_kernel(first, second, out, sems):
    count = first.shape[0]
    skip = second.shape[0] - count
    loads = [
        pltpu.make_async_copy(first, out.at[:count], sems.at[0]),
        pltpu.make_async_copy(second.at[skip:], out.at[count:], sems.at[1]),
    ]
    for load in loads:
        load.start()
    for load in loads:
        load.wait()


def tile_kernel(pairs, out):
    out[...] = code_tile(pairs)


def block_kernel(aux_count, low, coefs, blocks, tile, *refs):
    pieces = refs[len(refs) // 2 :] if low else refs
    pairs_dev = blocks.shape[0] // 2
    rows = coefs.shape[0]
    occ_local = rows // len(pieces)
    mine = lax.axis_index("aux")
    for k in range(pairs_dev):
        left = coefs[:rows, k * BS : (k + 1) * BS]
        right = jnp.concatenate([blocks[k], blocks[pairs_dev + k]], axis=1)
        half = jnp.dot(left, right, preferred_element_type=jnp.float32).astype(jnp.bfloat16)
        for side in range(2):
            flipped = low + side * (aux_count // 2)
            at = k * aux_count + jnp.bitwise_xor(mine, flipped)
            start = pl.multiple_of(at * occ_local, occ_local)
            for f, piece in enumerate(pieces):
                piece[pl.ds(start, occ_local), :] = half[
                    f * occ_local : (f + 1) * occ_local, side * BS : (side + 1) * BS
                ]
    if low == 0:
        for piece in pieces:
            piece[pairs_dev * aux_count * occ_local :, :] = tile[...]


def read_codes(received, pairs_dev, codes):
    for at, piece in enumerate(received):
        digits = piece[piece.shape[0] - TILE :, :].astype(jnp.float32)[:1]
        high = pltpu.roll(digits, BS - pairs_dev, 1)
        codes[at : at + 1, :] = (digits + 128.0 * high).astype(jnp.int32)


def near_sum_kernel(metric_in, own, *refs):
    *received, across, total, mix, metric, codes, sem = refs
    load = pltpu.make_async_copy(metric_in, metric, sem)
    load.start()
    total[...] = jnp.zeros_like(total)
    mine = lax.axis_index("aux")
    rows = total.shape[1]
    occ_local = rows // metric.shape[0]
    pairs_dev = (received[0].shape[0] - TILE) // rows
    read_codes([*received, own], pairs_dev, codes)
    for k in range(pairs_dev):
        part = own[k * rows : (k + 1) * rows, :]
        total[codes[len(received), k]] += part.astype(jnp.float32)
    for f, piece in enumerate(received):
        for k in range(pairs_dev):
            r = codes[f, k]
            for j in range(metric.shape[0]):
                source, first = (across, f * 2 + j - 2) if j >= 2 else (piece, j)
                first = (first * pairs_dev + k) * occ_local
                start = pl.multiple_of(jnp.bitwise_xor(mine, j) * occ_local, occ_local)
                part = source[first : first + occ_local, :]
                total[r, pl.ds(start, occ_local), :] += part.astype(jnp.float32)
    load.wait()
    aux_count = metric.shape[0]
    row = lax.broadcasted_iota(jnp.int32, (rows, rows), 0)
    column = lax.broadcasted_iota(jnp.int32, (rows, rows), 1)
    left = (
        lax.broadcasted_iota(jnp.int32, (rows, aux_count), 0) % aux_count
        == lax.broadcasted_iota(jnp.int32, (rows, aux_count), 1)
    ).astype(jnp.bfloat16)
    right = (
        lax.broadcasted_iota(jnp.int32, (aux_count, rows), 1) // occ_local
        == lax.broadcasted_iota(jnp.int32, (aux_count, rows), 0)
    ).astype(jnp.bfloat16)
    factor = jnp.dot(left, metric[...], preferred_element_type=jnp.float32).astype(jnp.bfloat16)
    factor = jnp.dot(factor, right, preferred_element_type=jnp.float32)
    mix[...] = jnp.where(row // aux_count == column % occ_local, factor, 0.0).astype(jnp.bfloat16)


def collect_kernel(mix, total_in, *refs):
    *received, out, total, staged, codes, sems = refs
    occ_local, aux_count = out.shape[:2]
    rows = total.shape[1]
    pairs_dev = (received[0].shape[0] - TILE) // rows
    read_codes(received, pairs_dev, codes)
    for at, piece in enumerate(received):
        for k in range(pairs_dev):
            total[codes[at, k]] += piece[k * rows : (k + 1) * rows, :].astype(jnp.float32)
    stores = []
    parts = sems.shape[0]
    each = total.shape[0] // parts
    for part in range(parts):
        for r in range(part * each, (part + 1) * each, 2):
            summed = jnp.concatenate([total[r], total[r + 1]], axis=1).astype(jnp.bfloat16)
            mixed = jnp.dot(mix[...], summed, preferred_element_type=jnp.float32)
            staged[:, :, r * BS : (r + 2) * BS] = mixed.reshape(
                occ_local, aux_count, 2 * BS
            ).astype(jnp.bfloat16)
        lanes = pl.ds(part * each * BS, each * BS)
        store = pltpu.make_async_copy(
            staged.at[:, :, lanes], out.at[:, :, lanes], sems.at[part]
        )
        store.start()
        stores.append(store)
    for store in stores:
        store.wait()

def flip(value, axis, bits):
    count = lax.axis_size(axis)
    return lax.ppermute(value, axis, [(at, at ^ bits) for at in range(count)])


def after(value, *others):
    return lax.optimization_barrier((value, *others))[0]


def cost(flops):
    return pl.CostEstimate(flops=int(flops), transcendentals=0, bytes_accessed=2**20)


def in_hbm(*operands):
    return [pltpu.with_memory_space_constraint(operand, pltpu.HBM) for operand in operands]


def exchanged_inputs(integrals, pair_list, coef, metric, occ_slot):
    pairs_dev = pair_list.shape[0]
    shell_count = lax.axis_size("shell")
    aux_count = lax.axis_size("aux")
    group = shell_count // 2
    occ_local = coef.shape[1] // (shell_count * aux_count)
    block_count = coef.shape[0] // BS * shell_count
    rows = occ_local * aux_count
    piece = jax.ShapeDtypeStruct((pairs_dev * rows + TILE, BS), jnp.bfloat16)
    vmem = pl.BlockSpec(memory_space=pltpu.VMEM)
    hbm = pl.BlockSpec(memory_space=pltpu.HBM)
    params = pltpu.CompilerParams(vmem_limit_bytes=40 * 2**20)

    def merged(name, first, second):
        return pl.pallas_call(
            merge_kernel,
            out_shape=jax.ShapeDtypeStruct(
                (2 * first.shape[0],) + first.shape[1:], jnp.bfloat16
            ),
            in_specs=[vmem] * 2,
            out_specs=vmem,
            scratch_shapes=[pltpu.SemaphoreType.DMA((2,))],
            compiler_params=params,
            name=name,
        )(first, second)

    blocks = integrals.reshape(pairs_dev, BS, BS)
    far_list = flip(pair_list, "shell", group)
    far_block = flip(blocks, "shell", group)
    operands = (pair_list, occ_slot.reshape(1, -1), coef)
    loaded = [
        pltpu.SMEM(pair_list.shape, jnp.int32),
        pltpu.VMEM((1, occ_slot.shape[0]), jnp.int32),
        pltpu.VMEM(coef.shape, jnp.bfloat16),
    ]
    *near, sent_coef = pl.pallas_call(
        functools.partial(near_kernel, occ_local, aux_count),
        out_shape=[piece] * group
        + [jax.ShapeDtypeStruct((group * occ_local, pairs_dev * BS), jnp.bfloat16)],
        in_specs=[hbm] * 4 + [vmem],
        out_specs=[vmem] * (group + 1),
        scratch_shapes=loaded
        + [pltpu.VMEM(blocks.shape, jnp.bfloat16), pltpu.SemaphoreType.DMA((4,))],
        compiler_params=params,
        name="near_blocks",
    )(*in_hbm(*operands, blocks), flip(blocks, "aux", 1))
    near = [near[0]] + [flip(near[f], "shell", f) for f in range(1, group)]
    far_tile = pl.pallas_call(
        tile_kernel,
        out_shape=jax.ShapeDtypeStruct((TILE, BS), jnp.bfloat16),
        in_specs=[pl.BlockSpec(memory_space=pltpu.SMEM)],
        out_specs=vmem,
        name="far_tile",
    )(far_list)
    far_block = after(far_block, sent_coef, far_tile)
    far_coef = flip(after(sent_coef, far_block), "shell", group)
    far_pair = merged("far_pair", far_block, flip(far_block, "aux", 2))
    far_pairs = [far_pair, flip(far_pair, "aux", 1)]
    across = flip(
        pl.pallas_call(
            regroup_kernel,
            out_shape=jax.ShapeDtypeStruct(
                (group * 2 * pairs_dev * occ_local, BS), jnp.bfloat16
            ),
            in_specs=[vmem] * group,
            out_specs=vmem,
            compiler_params=params,
            name="regroup",
        )(*near),
        "aux",
        2,
    )
    far = []
    for low in range(2):
        far = pl.pallas_call(
            functools.partial(block_kernel, aux_count, low),
            out_shape=[piece] * group,
            in_specs=[vmem] * (3 + len(far)),
            out_specs=[vmem] * group,
            input_output_aliases={3 + f: f for f in range(len(far))},
            compiler_params=params,
            cost_estimate=cost(2e9) if low == 0 else None,
            name=f"far_blocks_{low}",
        )(far_coef, far_pairs[low], far_tile, *far)
    total_shape = jax.ShapeDtypeStruct((block_count, rows, BS), jnp.float32)
    total, mix = pl.pallas_call(
        near_sum_kernel,
        out_shape=[total_shape, jax.ShapeDtypeStruct((rows, rows), jnp.bfloat16)],
        in_specs=[hbm] + [vmem] * (group + 2),
        out_specs=[vmem] * 2,
        scratch_shapes=[
            pltpu.VMEM(metric.shape, jnp.bfloat16),
            pltpu.VMEM((8, BS), jnp.int32),
            pltpu.SemaphoreType.DMA,
        ],
        compiler_params=params,
        cost_estimate=cost(3e9),
        name="near_sum",
    )(*in_hbm(metric), far[0], *near, across)
    far = [far[0]] + [flip(far[f], "shell", f) for f in range(1, group)]
    return pl.pallas_call(
        collect_kernel,
        out_shape=[
            jax.ShapeDtypeStruct((occ_local, aux_count, block_count * BS), jnp.bfloat16),
            total_shape,
        ],
        in_specs=[vmem] * (1 + group),
        out_specs=[hbm, vmem],
        input_output_aliases={1: 1},
        scratch_shapes=[
            pltpu.VMEM((occ_local, aux_count, block_count * BS), jnp.bfloat16),
            pltpu.VMEM((8, BS), jnp.int32),
            pltpu.SemaphoreType.DMA((4,)),
        ],
        compiler_params=params,
        name="collect",
    )(mix, total, far[3], far[1], far[2])[0]


def per_device(integrals, pair_list, coef, metric, occ_slot):
    shell_count, aux_count = lax.axis_size("shell"), lax.axis_size("aux")
    occ_local = coef.shape[1] // (shell_count * aux_count)
    if occ_local % 16 or shell_count & (shell_count - 1) or aux_count != 4:
        return relayed_half_blocks(integrals, pair_list, coef, metric, occ_slot)
    return exchanged_inputs(integrals, pair_list, coef, metric, occ_slot)


def solution(mesh):
    placed = (P("shell", None, "aux", None), P("shell", None), P("shell", None), P(), P())
    return jax.shard_map(
        per_device,
        mesh=mesh,
        in_specs=placed,
        out_specs=P(("shell", "aux"), None, None),
        check_vma=False,
    )
```

```python
import functools

import jax
import jax.numpy as jnp
from jax import lax
from jax.experimental import pallas as pl
from jax.experimental.pallas import tpu as pltpu
from jax.sharding import PartitionSpec as P

BS = 128
TILE = 8


def relayed_half_blocks(integrals, pair_list, coef, metric, occ_slot):
    pairs_dev = pair_list.shape[0]
    rows_local = coef.shape[0]
    occ_count = coef.shape[1]
    blocks_dev = rows_local // BS
    shell_count = lax.axis_size("shell")
    block_count = blocks_dev * shell_count
    slot_count = occ_slot.shape[0]
    aux_dev = integrals.shape[2]
    inverse = (
        jnp.zeros((slot_count,), jnp.int32)
        .at[occ_slot]
        .set(jnp.arange(slot_count, dtype=jnp.int32))
    )
    ordered = jnp.take(
        coef.reshape(rows_local, slot_count, occ_count // slot_count), inverse, axis=1
    )
    ordered = ordered.reshape(rows_local, occ_count)

    def one_slot(item):
        int_block, column_index = item
        start = column_index % blocks_dev * BS
        column = lax.dynamic_slice_in_dim(ordered, start, BS, 0)
        product = lax.dot_general(
            column,
            int_block.reshape(BS, aux_dev * BS),
            (((0,), (0,)), ((), ())),
            preferred_element_type=jnp.float32,
        )
        return product.astype(jnp.bfloat16)

    half_blocks = lax.map(one_slot, (integrals, pair_list[:, 1]))
    half_blocks = half_blocks.reshape(pairs_dev, occ_count, aux_dev, BS)
    listing = lax.all_gather(pair_list, "shell", axis=0, tiled=True)
    targets = jnp.arange(block_count, dtype=jnp.int32)[:, None]
    selector = ((listing[:, 0][None, :] == targets) & (listing[:, 2][None, :] == 1)).astype(
        jnp.bfloat16
    )
    relayed = lax.all_to_all(
        lax.all_to_all(half_blocks, "shell", split_axis=1, concat_axis=0, tiled=True),
        "aux",
        split_axis=1,
        concat_axis=2,
        tiled=True,
    )
    summed = jnp.dot(
        selector, relayed.reshape(relayed.shape[0], -1), preferred_element_type=jnp.float32
    )
    blocks = summed.astype(jnp.bfloat16).reshape((block_count,) + relayed.shape[1:])
    result = jnp.einsum("qp,bipm->iqbm", metric, blocks, preferred_element_type=jnp.float32)
    return result.reshape(result.shape[0], result.shape[1], block_count * BS).astype(jnp.bfloat16)


def targets_of(slot_row, block_total, occ_count):
    width = occ_count // block_total
    spread = (
        lax.broadcasted_iota(jnp.int32, (block_total, occ_count), 1) // width
        == lax.broadcasted_iota(jnp.int32, (block_total, occ_count), 0)
    ).astype(jnp.bfloat16)
    slots = jnp.broadcast_to(slot_row, (8, block_total)).astype(jnp.float32)
    target = jnp.dot(slots.astype(jnp.bfloat16), spread, preferred_element_type=jnp.float32)
    return target.astype(jnp.int32)[:1] * width + (
        lax.broadcasted_iota(jnp.int32, (1, occ_count), 1) % width
    )


def code_tile(pairs):
    pairs_dev = pairs.shape[0]
    lane = lax.broadcasted_iota(jnp.int32, (1, BS), 1)
    code = jnp.zeros((1, BS), jnp.int32)
    for k in range(pairs_dev):
        code = jnp.where(lane == k, pairs[k, 0] % 128, code)
        code = jnp.where(lane == pairs_dev + k, pairs[k, 0] // 128, code)
    return jnp.broadcast_to(code.astype(jnp.float32), (TILE, BS)).astype(jnp.bfloat16)


def near_kernel(
    occ_local,
    aux_count,
    pairs_in,
    slot_in,
    coef_in,
    blocks_in,
    beside,
    *refs,
):
    *outs, far, pairs, slot_row, coef, blocks, sems = refs
    pairs_dev = pairs.shape[0]
    blocks_dev = coef.shape[0] // BS
    occ_count = coef.shape[1]
    loads = [
        pltpu.make_async_copy(source, target, sems.at[at])
        for at, (source, target) in enumerate(
            ((slot_in, slot_row), (pairs_in, pairs), (coef_in, coef), (blocks_in, blocks))
        )
    ]
    for load in loads:
        load.start()
    me = lax.axis_index("shell")
    mine = lax.axis_index("aux")
    owned = aux_count // 2 * occ_local
    row = lax.broadcasted_iota(jnp.int32, (len(outs) * owned, 1), 0)
    owner = jnp.bitwise_xor(row // owned, me) * aux_count + jnp.bitwise_xor(
        row // occ_local % (aux_count // 2) * 2, mine
    )
    wanted = owner * occ_local + row % occ_local
    far_rows = far.shape[0] - TILE
    row = lax.broadcasted_iota(jnp.int32, (far_rows, 1), 0)
    owner = jnp.bitwise_xor(len(outs) + row // occ_local, me) * aux_count + mine
    far_wanted = owner * occ_local + row % occ_local
    loads[0].wait()
    target = targets_of(slot_row[...], slot_row.shape[1], occ_count)
    pick = (wanted == target).astype(jnp.bfloat16)
    far_pick = (far_wanted == target).astype(jnp.bfloat16)
    for load in loads[1:]:
        load.wait()
    code = code_tile(pairs)
    rows = [
        coef[pl.ds(pl.multiple_of(lax.rem(pairs[k, 1], blocks_dev) * BS, BS), BS), :]
        for k in range(pairs_dev)
    ]
    rows = jnp.concatenate(rows, axis=0)
    contract = (((1,), (1,)), ((), ()))
    ordered = lax.dot_general(pick, rows, contract, preferred_element_type=jnp.float32)
    ordered = ordered.astype(jnp.bfloat16)
    far_coef = lax.dot_general(far_pick, rows, contract, preferred_element_type=jnp.float32)
    for k in range(pairs_dev):
        block = jnp.dot(
            ordered[:, k * BS : (k + 1) * BS],
            jnp.concatenate([blocks[k], beside[k]], axis=1),
            preferred_element_type=jnp.float32,
        )
        live = (pairs[k, 2] == 1).astype(jnp.float32)
        block = (block * live).astype(jnp.bfloat16)
        lanes = slice(k * BS, (k + 1) * BS)
        far[:far_rows, lanes] = (far_coef[:, lanes] * live).astype(jnp.bfloat16)
        far[far_rows:, lanes] = code
        for f, out in enumerate(outs):
            for j in range(aux_count // 2):
                first = f * owned + j * occ_local
                for c in range(2):
                    at = ((j * 2 + c) * pairs_dev + k) * occ_local
                    out[at : at + occ_local, :] = block[
                        first : first + occ_local, c * BS : (c + 1) * BS
                    ]
    for out in outs:
        out[out.shape[0] - TILE :, :] = code


def regroup_kernel(*refs):
    *received, out = refs
    rows = out.shape[0] // len(received)
    for f, piece in enumerate(received):
        out[f * rows : (f + 1) * rows, :] = piece[rows : 2 * rows, :]


def merge_kernel(first, second, out, sems):
    count = first.shape[0]
    skip = second.shape[0] - count
    loads = [
        pltpu.make_async_copy(first, out.at[:count], sems.at[0]),
        pltpu.make_async_copy(second.at[skip:], out.at[count:], sems.at[1]),
    ]
    for load in loads:
        load.start()
    for load in loads:
        load.wait()


def block_kernel(aux_count, low, coefs, blocks, *refs):
    pieces = refs[len(refs) // 2 :] if low else refs
    pairs_dev = blocks.shape[0] // 2
    rows = coefs.shape[0] - TILE
    occ_local = rows // len(pieces)
    mine = lax.axis_index("aux")
    for k in range(pairs_dev):
        left = coefs[:rows, k * BS : (k + 1) * BS]
        right = jnp.concatenate([blocks[k], blocks[pairs_dev + k]], axis=1)
        half = jnp.dot(left, right, preferred_element_type=jnp.float32).astype(jnp.bfloat16)
        for side in range(2):
            flipped = low + side * (aux_count // 2)
            at = k * aux_count + jnp.bitwise_xor(mine, flipped)
            start = pl.multiple_of(at * occ_local, occ_local)
            for f, piece in enumerate(pieces):
                piece[pl.ds(start, occ_local), :] = half[
                    f * occ_local : (f + 1) * occ_local, side * BS : (side + 1) * BS
                ]
    if low == 0:
        for piece in pieces:
            piece[pairs_dev * aux_count * occ_local :, :] = coefs[rows:, :BS]


def read_codes(received, pairs_dev, codes):
    for at, piece in enumerate(received):
        digits = piece[piece.shape[0] - TILE :, :].astype(jnp.float32)[:1]
        high = pltpu.roll(digits, BS - pairs_dev, 1)
        codes[at : at + 1, :] = (digits + 128.0 * high).astype(jnp.int32)


def near_sum_kernel(metric_in, own, *refs):
    *received, across, total, mix, metric, codes, sem = refs
    load = pltpu.make_async_copy(metric_in, metric, sem)
    load.start()
    total[...] = jnp.zeros_like(total)
    mine = lax.axis_index("aux")
    rows = total.shape[1]
    occ_local = rows // metric.shape[0]
    pairs_dev = (received[0].shape[0] - TILE) // rows
    read_codes([*received, own], pairs_dev, codes)
    for k in range(pairs_dev):
        part = own[k * rows : (k + 1) * rows, :]
        total[codes[len(received), k]] += part.astype(jnp.float32)
    for f, piece in enumerate(received):
        for k in range(pairs_dev):
            r = codes[f, k]
            for j in range(metric.shape[0]):
                source, first = (across, f * 2 + j - 2) if j >= 2 else (piece, j)
                first = (first * pairs_dev + k) * occ_local
                start = pl.multiple_of(jnp.bitwise_xor(mine, j) * occ_local, occ_local)
                part = source[first : first + occ_local, :]
                total[r, pl.ds(start, occ_local), :] += part.astype(jnp.float32)
    load.wait()
    aux_count = metric.shape[0]
    row = lax.broadcasted_iota(jnp.int32, (rows, rows), 0)
    column = lax.broadcasted_iota(jnp.int32, (rows, rows), 1)
    left = (
        lax.broadcasted_iota(jnp.int32, (rows, aux_count), 0) % aux_count
        == lax.broadcasted_iota(jnp.int32, (rows, aux_count), 1)
    ).astype(jnp.bfloat16)
    right = (
        lax.broadcasted_iota(jnp.int32, (aux_count, rows), 1) // occ_local
        == lax.broadcasted_iota(jnp.int32, (aux_count, rows), 0)
    ).astype(jnp.bfloat16)
    factor = jnp.dot(left, metric[...], preferred_element_type=jnp.float32).astype(jnp.bfloat16)
    factor = jnp.dot(factor, right, preferred_element_type=jnp.float32)
    mix[...] = jnp.where(row // aux_count == column % occ_local, factor, 0.0).astype(jnp.bfloat16)


def collect_kernel(mix, total_in, *refs):
    *received, out, total, staged, codes, sems = refs
    occ_local, aux_count = out.shape[:2]
    rows = total.shape[1]
    pairs_dev = (received[0].shape[0] - TILE) // rows
    read_codes(received, pairs_dev, codes)
    for at, piece in enumerate(received):
        for k in range(pairs_dev):
            total[codes[at, k]] += piece[k * rows : (k + 1) * rows, :].astype(jnp.float32)
    stores = []
    parts = sems.shape[0]
    each = total.shape[0] // parts
    for part in range(parts):
        for r in range(part * each, (part + 1) * each, 2):
            summed = jnp.concatenate([total[r], total[r + 1]], axis=1).astype(jnp.bfloat16)
            mixed = jnp.dot(mix[...], summed, preferred_element_type=jnp.float32)
            staged[:, :, r * BS : (r + 2) * BS] = mixed.reshape(
                occ_local, aux_count, 2 * BS
            ).astype(jnp.bfloat16)
        lanes = pl.ds(part * each * BS, each * BS)
        store = pltpu.make_async_copy(
            staged.at[:, :, lanes], out.at[:, :, lanes], sems.at[part]
        )
        store.start()
        stores.append(store)
    for store in stores:
        store.wait()

def flip(value, axis, bits):
    count = lax.axis_size(axis)
    return lax.ppermute(value, axis, [(at, at ^ bits) for at in range(count)])


def after(value, *others):
    return lax.optimization_barrier((value, *others))[0]


def cost(flops):
    return pl.CostEstimate(flops=int(flops), transcendentals=0, bytes_accessed=2**20)


def in_hbm(*operands):
    return [pltpu.with_memory_space_constraint(operand, pltpu.HBM) for operand in operands]


def exchanged_inputs(integrals, pair_list, coef, metric, occ_slot):
    pairs_dev = pair_list.shape[0]
    shell_count = lax.axis_size("shell")
    aux_count = lax.axis_size("aux")
    group = shell_count // 2
    occ_local = coef.shape[1] // (shell_count * aux_count)
    block_count = coef.shape[0] // BS * shell_count
    rows = occ_local * aux_count
    piece = jax.ShapeDtypeStruct((pairs_dev * rows + TILE, BS), jnp.bfloat16)
    vmem = pl.BlockSpec(memory_space=pltpu.VMEM)
    hbm = pl.BlockSpec(memory_space=pltpu.HBM)
    params = pltpu.CompilerParams(vmem_limit_bytes=40 * 2**20)

    def merged(name, first, second):
        return pl.pallas_call(
            merge_kernel,
            out_shape=jax.ShapeDtypeStruct(
                (2 * first.shape[0],) + first.shape[1:], jnp.bfloat16
            ),
            in_specs=[vmem] * 2,
            out_specs=vmem,
            scratch_shapes=[pltpu.SemaphoreType.DMA((2,))],
            compiler_params=params,
            name=name,
        )(first, second)

    blocks = integrals.reshape(pairs_dev, BS, BS)
    far_block = flip(blocks, "shell", group)
    operands = (pair_list, occ_slot.reshape(1, -1), coef)
    loaded = [
        pltpu.SMEM(pair_list.shape, jnp.int32),
        pltpu.VMEM((1, occ_slot.shape[0]), jnp.int32),
        pltpu.VMEM(coef.shape, jnp.bfloat16),
    ]
    *near, sent_coef = pl.pallas_call(
        functools.partial(near_kernel, occ_local, aux_count),
        out_shape=[piece] * group
        + [jax.ShapeDtypeStruct((group * occ_local + TILE, pairs_dev * BS), jnp.bfloat16)],
        in_specs=[hbm] * 4 + [vmem],
        out_specs=[vmem] * (group + 1),
        scratch_shapes=loaded
        + [pltpu.VMEM(blocks.shape, jnp.bfloat16), pltpu.SemaphoreType.DMA((4,))],
        compiler_params=params,
        name="near_blocks",
    )(*in_hbm(*operands, blocks), flip(blocks, "aux", 1))
    near = [near[0]] + [flip(near[f], "shell", f) for f in range(1, group)]
    far_block = after(far_block, sent_coef)
    far_coef = flip(after(sent_coef, far_block), "shell", group)
    far_pair = merged("far_pair", far_block, flip(far_block, "aux", 2))
    far_pairs = [far_pair, flip(far_pair, "aux", 1)]
    across = flip(
        pl.pallas_call(
            regroup_kernel,
            out_shape=jax.ShapeDtypeStruct(
                (group * 2 * pairs_dev * occ_local, BS), jnp.bfloat16
            ),
            in_specs=[vmem] * group,
            out_specs=vmem,
            compiler_params=params,
            name="regroup",
        )(*near),
        "aux",
        2,
    )
    far = []
    for low in range(2):
        far = pl.pallas_call(
            functools.partial(block_kernel, aux_count, low),
            out_shape=[piece] * group,
            in_specs=[vmem] * (2 + len(far)),
            out_specs=[vmem] * group,
            input_output_aliases={2 + f: f for f in range(len(far))},
            compiler_params=params,
            cost_estimate=cost(2e9) if low == 0 else None,
            name=f"far_blocks_{low}",
        )(far_coef, far_pairs[low], *far)
    total_shape = jax.ShapeDtypeStruct((block_count, rows, BS), jnp.float32)
    total, mix = pl.pallas_call(
        near_sum_kernel,
        out_shape=[total_shape, jax.ShapeDtypeStruct((rows, rows), jnp.bfloat16)],
        in_specs=[hbm] + [vmem] * (group + 2),
        out_specs=[vmem] * 2,
        scratch_shapes=[
            pltpu.VMEM(metric.shape, jnp.bfloat16),
            pltpu.VMEM((8, BS), jnp.int32),
            pltpu.SemaphoreType.DMA,
        ],
        compiler_params=params,
        cost_estimate=cost(3e9),
        name="near_sum",
    )(*in_hbm(metric), far[0], *near, across)
    far = [far[0]] + [flip(far[f], "shell", f) for f in range(1, group)]
    return pl.pallas_call(
        collect_kernel,
        out_shape=[
            jax.ShapeDtypeStruct((occ_local, aux_count, block_count * BS), jnp.bfloat16),
            total_shape,
        ],
        in_specs=[vmem] * (1 + group),
        out_specs=[hbm, vmem],
        input_output_aliases={1: 1},
        scratch_shapes=[
            pltpu.VMEM((occ_local, aux_count, block_count * BS), jnp.bfloat16),
            pltpu.VMEM((8, BS), jnp.int32),
            pltpu.SemaphoreType.DMA((8,)),
        ],
        compiler_params=params,
        name="collect",
    )(mix, total, far[3], far[1], far[2])[0]


def per_device(integrals, pair_list, coef, metric, occ_slot):
    shell_count, aux_count = lax.axis_size("shell"), lax.axis_size("aux")
    occ_local = coef.shape[1] // (shell_count * aux_count)
    if occ_local % 16 or shell_count & (shell_count - 1) or aux_count != 4:
        return relayed_half_blocks(integrals, pair_list, coef, metric, occ_slot)
    return exchanged_inputs(integrals, pair_list, coef, metric, occ_slot)


def solution(mesh):
    placed = (P("shell", None, "aux", None), P("shell", None), P("shell", None), P(), P())
    return jax.shard_map(
        per_device,
        mesh=mesh,
        in_specs=placed,
        out_specs=P(("shell", "aux"), None, None),
        check_vma=False,
    )
```
